32 devices in a mesh: dx: 4 (over x, core), dy: 8 (over z, y).
Axes of the slice: x: 2, y: 2, z: 4, core: 2. Of those that a mesh axis runs over, the one named last changes fastest.
Arguments:
- features: bfloat16 [4, 8, 384, 128], P('dx', 'dy'), may hold values from -6 to 6
- positions: bfloat16 [4, 8, 3, 384], P('dx', 'dy'), may hold values from 0 to 1
- atom_count: int32 [4, 8], P('dx', 'dy'), may hold values from 192 to 384, as said below
- ghost_index: int32 [4, 8, 256], P('dx', 'dy'), may hold values from 0 to 383, as said below
- neighbour_list: int32 [4, 8, 384, 32], P('dx', 'dy'), may hold values from 0 to 2687, as said below
- cell_index: int32 [4, 8, 384], P('dx', 'dy'), may hold values from 0 to 65535
- w_self: bfloat16 [128, 128], replicated, may hold values from -0.5 to 0.5
- w_pair: bfloat16 [128, 256], replicated, may hold values from -0.5 to 0.5
- w_radial: float32 [8, 128], replicated, may hold values from -2 to 2
- w_expand: bfloat16 [128, 1024], replicated, may hold values from -0.5 to 0.5
- w_contract: bfloat16 [1024, 128], replicated, may hold values from -0.1875 to 0.1875
- w_final: bfloat16 [128, 128], replicated, may hold values from -0.5 to 0.5
- w_charge: bfloat16 [128], replicated, may hold values from -0.5 to 0.5
Outputs:
- forces: float32 [4, 8, 3, 384], P('dx', 'dy')
The draws below stay inside these ranges and needn't reach their ends.
Inputs may be any that keep to these rules, and one draw needn't show every extreme that they name: `atom_count`: each domain holds at least half of 384 live atoms in its first slots, and some domain is full. `ghost_index`: each entry is a live slot of the same domain. `neighbour_list`: each entry is a live slot of the domain itself or a slot of a ghost block other than block 4 (the domain's own exports).
All inputs are finite; a program needn't handle non-finite values.
Results may differ from the reference program's by a relative error of at most 0.0049.
Values may be sent and summed in bfloat16 or wider, within the bound.
No kernel may reach another device: no remote copies, remote signals or barrier semaphores. Data moves between devices by JAX's collectives and lax.ppermute only.
A program may use at most 128 MiB of HBM per device.

```python
import math
import jax
import jax.numpy as jnp
from jax import lax

WIDTH = 128
LATENT = 1024
BASIS = 8
NEIGHBOURS = 32
ATOM_BLOCK = 64
ATOMS = 384
GHOSTS = 256
GRID_X = 8
GRID_Y = 8
GRID_Z = 1024
N_DX = 4
N_DY = 8


def live_counts(key):
    sub = jax.random.fold_in(key, 11)
    first, second = jax.random.split(sub)
    base = jax.random.randint(first, (N_DX * N_DY,), ATOMS // 2, ATOMS + 1)
    chosen = jax.random.randint(second, (), 0, N_DX * N_DY)
    filled = jnp.where(jnp.arange(N_DX * N_DY) == chosen, ATOMS, base)
    return filled.reshape(N_DX, N_DY).astype(jnp.int32)


def draw_atom_count(key, part):
    return live_counts(key)


def draw_ghost_index(key, part):
    counts = live_counts(key)
    sub = jax.random.fold_in(key, 12)
    return jax.random.randint(sub, (N_DX, N_DY, GHOSTS), 0, counts[:, :, None]).astype(jnp.int32)


def draw_neighbour_list(key, part):
    counts = live_counts(key)
    sub = jax.random.fold_in(key, 13)
    key_local, key_block, key_slot, key_side = jax.random.split(sub, 4)
    shape = (N_DX, N_DY, ATOMS, NEIGHBOURS)
    local_slot = jax.random.randint(key_local, shape, 0, counts[:, :, None, None])
    which = jax.random.randint(key_block, shape, 0, 8)
    block_id = which + (which >= 4).astype(jnp.int32)
    ghost_slot = jax.random.randint(key_slot, shape, 0, GHOSTS)
    ghost_entry = ATOMS + block_id * GHOSTS + ghost_slot
    side = jax.random.randint(key_side, shape, 0, 2)
    result = jnp.where(side == 0, local_slot, ghost_entry).astype(jnp.int32)
    result = result.at[0, 0, 0, 0].set(0)
    result = result.at[0, 0, 0, 1].set(ATOMS + 9 * GHOSTS - 1)
    return result.astype(jnp.int32)


def with_ends(drawn, key, least, top_value):
    longest = drawn.shape.index(max(drawn.shape))
    spots = []
    for shift in (0, 1):
        where = [jax.random.randint(jax.random.fold_in(key, axis), (), 0, length) for axis, length in enumerate(drawn.shape)]
        where[longest] = (where[longest] + shift) % drawn.shape[longest]
        spots.append(tuple(where))
    return drawn.at[spots[0]].set(least).at[spots[1]].set(top_value)


def block_levels(rng, extent, shards, low, largest):
    gain = 1.0
    for dim, parts in shards:
        draws = jax.random.uniform(jax.random.fold_in(jax.random.fold_in(rng, 6), dim), (parts,), jnp.float32, low / len(shards), largest / len(shards))
        gain = gain * jnp.repeat(jnp.exp(draws), extent[dim] // parts).reshape((-1,) + (1,) * (len(extent) - 1 - dim))
    return gain


def bell_draw(key, shape, scale, limit, cuts=(), kind=jnp.bfloat16):
    drawn = jax.random.normal(key, shape, jnp.float32) * scale
    if len(cuts) > 0:
        drawn = block_levels(key, shape, cuts, -0.22, 0.18) * drawn
    return jnp.clip(drawn, min=-limit, max=limit).astype(kind)


def setup_inputs(seed: int = 0) -> dict:
    keys = jax.random.split(jax.random.key(seed), 14)
    return {
        "features": bell_draw(keys[0], (N_DX, N_DY, ATOMS, WIDTH), 1.0, 6.0, ((0, 4), (1, 8))),
        "positions": jnp.clip(1.0 * jax.random.uniform(keys[1], (N_DX, N_DY, 3, ATOMS), jnp.float32) ** block_levels(keys[1], (N_DX, N_DY, 3, ATOMS), ((0, 4), (1, 8)), -0.2, 0.2), 0.0, 1.0).astype(jnp.bfloat16),
        "atom_count": draw_atom_count(jax.random.fold_in(keys[13], 71), 0),
        "ghost_index": draw_ghost_index(jax.random.fold_in(keys[13], 71), 0),
        "neighbour_list": draw_neighbour_list(jax.random.fold_in(keys[13], 71), 0),
        "cell_index": with_ends(jax.random.randint(keys[5], (N_DX, N_DY, ATOMS), 0, GRID_X * GRID_Y * GRID_Z), jax.random.fold_in(keys[5], 1), 0, (GRID_X * GRID_Y * GRID_Z) - 1).astype(jnp.int32),
        "w_self": bell_draw(keys[6], (WIDTH, WIDTH), WIDTH ** -0.5, 0.5),
        "w_pair": bell_draw(keys[7], (WIDTH, 2 * WIDTH), WIDTH ** -0.5, 0.5),
        "w_radial": bell_draw(keys[8], (BASIS, WIDTH), BASIS ** -0.5, 2.0, (), jnp.float32),
        "w_expand": bell_draw(keys[9], (WIDTH, LATENT), WIDTH ** -0.5, 0.5),
        "w_contract": bell_draw(keys[10], (LATENT, WIDTH), LATENT ** -0.5, 0.1875),
        "w_final": bell_draw(keys[11], (WIDTH, WIDTH), WIDTH ** -0.5, 0.5),
        "w_charge": bell_draw(keys[12], (WIDTH,), WIDTH ** -0.5, 0.5),
    }


box_side = 1.0
cutoff_sq = 6.25
smearing = 1.0

def short_range(features, projected, own_coords, ext_coords, block_lists_all, w_self, w_radial, w_expand, w_contract, w_final):
    channels = features.shape[1]
    atom_rows = features.shape[0]
    per_atom = block_lists_all.shape[1]
    basis_count = w_radial.shape[0]
    block_count = atom_rows // ATOM_BLOCK
    own_term = jnp.dot(features, w_self, preferred_element_type=jnp.float32)
    spacing = cutoff_sq / (basis_count - 1)
    centers = jnp.arange(basis_count, dtype=jnp.float32) * spacing
    edge_scale = 1.0 / math.sqrt(per_atom)

    def one_block(inputs):
        own_rows, near_coords, block_lists = inputs
        flat_list = block_lists.reshape(-1)
        gathered = jnp.take(projected, flat_list, axis=0)
        bias_rows = gathered[:, :channels].astype(jnp.float32)
        value_rows = gathered[:, channels:].astype(jnp.float32)
        far_coords = jnp.take(ext_coords, flat_list, axis=1)
        start_coords = jnp.broadcast_to(near_coords[:, :, None], (3, near_coords.shape[1], per_atom)).reshape(3, -1)
        displace = far_coords - start_coords
        dist_sq = lax.optimization_barrier(jnp.sum(displace * displace, axis=0))
        basis_rows = jnp.exp(-jnp.square((dist_sq[None, :] - centers[:, None]) / spacing))
        envelope = jnp.square(jnp.maximum(0.0, 1.0 - dist_sq / cutoff_sq))
        radial = lax.dot_general(basis_rows, w_radial, (((0,), (0,)), ((), ())), precision=lax.Precision.HIGHEST, preferred_element_type=jnp.float32)
        own_edges = jnp.broadcast_to(own_rows[:, None, :], (own_rows.shape[0], per_atom, channels)).reshape(-1, channels)
        edge_in = jax.nn.silu(radial + own_edges + bias_rows).astype(jnp.bfloat16)
        latent = jax.nn.silu(jnp.dot(edge_in, w_expand, preferred_element_type=jnp.float32)).astype(jnp.bfloat16)
        mixed_out = jnp.dot(latent, w_contract, preferred_element_type=jnp.float32)
        weight = mixed_out * envelope[:, None] * value_rows
        scalar = weight.reshape(-1, per_atom, channels).sum(axis=1) * edge_scale
        vector = (displace[:, :, None] * weight[None]).reshape(3, -1, per_atom, channels).sum(axis=2) * edge_scale
        invariant = (scalar + lax.optimization_barrier(jnp.sum(vector * vector, axis=0)) / 3.0).astype(jnp.bfloat16)
        gating = jax.nn.silu(jnp.dot(invariant, w_final, preferred_element_type=jnp.float32))
        return lax.optimization_barrier(jnp.sum(vector * gating[None], axis=2)) / math.sqrt(channels)
    own_blocks = own_term.reshape(block_count, ATOM_BLOCK, channels)
    coord_blocks = own_coords.reshape(3, block_count, ATOM_BLOCK).transpose(1, 0, 2)
    list_blocks = block_lists_all.reshape(block_count, ATOM_BLOCK, per_atom)
    result = lax.map(one_block, (own_blocks, coord_blocks, list_blocks))
    return result.transpose(1, 0, 2).reshape(3, atom_rows)

def signed_modes(count):
    modes = jnp.arange(count, dtype=jnp.int32)
    return jnp.where(modes < count // 2, modes, modes - count)

def reference(features, positions, atom_count, ghost_index, neighbour_list, cell_index, w_self, w_pair, w_radial, w_expand, w_contract, w_final, w_charge):
    exported_feat = jnp.take_along_axis(features, ghost_index[:, :, :, None], axis=2)
    exported_coords = jnp.take_along_axis(positions, ghost_index[:, :, None, :], axis=3).astype(jnp.float32)
    feat_blocks = []
    coord_blocks = []
    for shift_x in range(3):
        for shift_y in range(3):
            moved_feat = jnp.roll(exported_feat, (1 - shift_x, 1 - shift_y), axis=(0, 1))
            moved_coords = jnp.roll(exported_coords, (1 - shift_x, 1 - shift_y), axis=(0, 1))
            offsets = jnp.array([(shift_x - 1) * box_side, (shift_y - 1) * box_side, 0.0], dtype=jnp.float32)
            feat_blocks.append(moved_feat)
            coord_blocks.append(moved_coords + offsets[None, None, :, None])
    ghost_feat = jnp.stack(feat_blocks, axis=2).reshape(N_DX, N_DY, 9 * GHOSTS, WIDTH)
    ghost_coords = jnp.stack(coord_blocks, axis=3).reshape(N_DX, N_DY, 3, 9 * GHOSTS)
    own_coords = positions.astype(jnp.float32)
    ext_feat = jnp.concatenate([features, ghost_feat], axis=2)
    ext_coords = jnp.concatenate([own_coords, ghost_coords], axis=3)
    devices_all = N_DX * N_DY

    def per_domain(inputs):
        feat_one, ext_one, coords_one, ext_coords_one, lists_one = inputs
        projected = jnp.dot(ext_one, w_pair, preferred_element_type=jnp.float32).astype(jnp.bfloat16)
        return short_range(feat_one, projected, coords_one, ext_coords_one, lists_one, w_self, w_radial, w_expand, w_contract, w_final)
    short = lax.map(per_domain, (features.reshape(devices_all, ATOMS, WIDTH), ext_feat.reshape(devices_all, ATOMS + 9 * GHOSTS, WIDTH), own_coords.reshape(devices_all, 3, ATOMS), ext_coords.reshape(devices_all, 3, ATOMS + 9 * GHOSTS), neighbour_list.reshape(devices_all, ATOMS, NEIGHBOURS))).reshape(N_DX, N_DY, 3, ATOMS)
    live = jnp.arange(ATOMS, dtype=jnp.int32)[None, None, :] < atom_count[:, :, None]
    charge = lax.optimization_barrier(jnp.sum(features.astype(jnp.float32) * w_charge.astype(jnp.float32), axis=-1))
    charge = jnp.where(live, charge, jnp.zeros_like(charge))
    mesh_x = GRID_X * N_DX
    mesh_y = GRID_Y * N_DY
    local_x = cell_index // (GRID_Y * GRID_Z)
    local_y = cell_index // GRID_Z % GRID_Y
    local_z = cell_index % GRID_Z
    row_dev = jnp.arange(N_DX, dtype=jnp.int32)[:, None, None]
    col_dev = jnp.arange(N_DY, dtype=jnp.int32)[None, :, None]
    global_flat = ((row_dev * GRID_X + local_x) * mesh_y + col_dev * GRID_Y + local_y) * GRID_Z + local_z
    density = jax.ops.segment_sum(charge.reshape(-1), global_flat.reshape(-1).astype(jnp.int32), num_segments=mesh_x * mesh_y * GRID_Z)
    density = density.reshape(mesh_x, mesh_y, GRID_Z)
    sig_x = signed_modes(mesh_x)[:, None, None]
    sig_y = signed_modes(mesh_y)[None, :, None]
    sig_z = signed_modes(GRID_Z)[None, None, :]
    wave_x = sig_x.astype(jnp.float32) * (2.0 * math.pi / mesh_x)
    wave_y = sig_y.astype(jnp.float32) * (2.0 * math.pi / mesh_y)
    wave_z = sig_z.astype(jnp.float32) * (2.0 * math.pi / GRID_Z)
    wave_sq = wave_x * wave_x + wave_y * wave_y + wave_z * wave_z
    is_zero = (sig_x == 0) & (sig_y == 0) & (sig_z == 0)
    safe_sq = jnp.where(is_zero, jnp.ones_like(wave_sq), wave_sq)
    green = jnp.where(is_zero, jnp.zeros_like(wave_sq), 4.0 * math.pi * jnp.exp(-0.5 * smearing * smearing * wave_sq) / safe_sq)
    spectrum = jnp.fft.fftn(density) * green
    derivatives = []
    for signed, wave, count in ((sig_x, wave_x, mesh_x), (sig_y, wave_y, mesh_y), (sig_z, wave_z, GRID_Z)):
        derivatives.append(jnp.where(signed * 2 == -count, jnp.zeros_like(wave), wave))
    samples = []
    for wave in derivatives:
        field = jnp.real(jnp.fft.ifftn(-1j * wave * spectrum))
        samples.append(jnp.take(field.reshape(-1), global_flat.reshape(-1).astype(jnp.int32)).reshape(N_DX, N_DY, ATOMS))
    sampled = jnp.stack(samples, axis=2)
    total = short + charge[:, :, None, :] * sampled
    return jnp.where(live[:, :, None, :], total, jnp.zeros_like(total))
```

```python
import functools
import math

import jax
import jax.numpy as jnp
import numpy as np
from jax import lax
from jax.experimental import pallas as pl
from jax.experimental.pallas import tpu as pltpu
from jax.sharding import PartitionSpec as P

GRID_X = 8
GRID_Y = 8
GRID_Z = 1024
BOX = 1.0
CUTOFF_SQ = 6.25
SMEARING = 1.0

LANES = 128
EXTRA = 16
ROWS = 32
CHUNK_ATOMS = 16
HIGHEST = lax.Precision.HIGHEST
F32 = jnp.float32
BF16 = jnp.bfloat16


def contract_first(a, b, precision=None):
    return lax.dot_general(
        a, b, (((0,), (0,)), ((), ())), precision=precision, preferred_element_type=F32
    )


def contract_last(a, b, precision=None):
    return lax.dot_general(
        a, b, (((1,), (1,)), ((), ())), precision=precision, preferred_element_type=F32
    )


def prepare_kernel(count_ref, feat_ref, pos_ref, export_ref, cell_ref, wq_ref, out_ref, qc_ref):
    atoms = feat_ref.shape[0]
    ghosts = export_ref.shape[1]
    pick = lax.broadcasted_iota(jnp.int32, (atoms, ghosts), 0) == export_ref[...]
    pick = jnp.where(pick, 1.0, 0.0).astype(BF16)
    out_ref[pl.ds(0, ghosts), :] = contract_first(pick, feat_ref[...]).astype(BF16)
    pos = jnp.concatenate([pos_ref[...].astype(F32), jnp.zeros((13, atoms), F32)], axis=0)
    coords = jnp.dot(pos.astype(BF16), pick, preferred_element_type=F32)
    tail = [coords[:8, h * LANES : (h + 1) * LANES] for h in range(ghosts // LANES)]
    out_ref[pl.ds(ghosts, EXTRA), :] = jnp.concatenate(tail, axis=0).astype(BF16)
    weights = jnp.broadcast_to(wq_ref[...].astype(F32), (16, LANES)).astype(BF16)
    charge = contract_last(weights, feat_ref[...])[:1]
    live = lax.broadcasted_iota(jnp.int32, (1, atoms), 1) < count_ref[0, 0]
    qc_ref[...] = jnp.concatenate(
        [jnp.where(live, charge, 0.0), cell_ref[...].astype(F32)], axis=0
    )


def prepare(count, feat, pos, exports, cells, w_charge):
    atoms, ghosts = (feat.shape[0], exports.shape[0])
    vmem = pl.BlockSpec(memory_space=pltpu.VMEM)
    return pl.pallas_call(
        prepare_kernel,
        in_specs=[pl.BlockSpec(memory_space=pltpu.SMEM)] + [vmem] * 5,
        out_specs=[vmem, vmem],
        out_shape=[
            jax.ShapeDtypeStruct((ghosts + EXTRA, feat.shape[1]), BF16),
            jax.ShapeDtypeStruct((2, atoms), F32),
        ],
        name="prepare",
    )(count, feat, pos, exports[None], cells[None], w_charge[None])


def real_tables(count):
    half = count // 2
    index = np.arange(count)
    freq = np.where(index <= half, index, index - half)
    place = np.arange(count)
    angle = 2.0 * np.pi * (freq[:, None] * place[None, :] % count) / count
    is_cos = (index <= half)[:, None]
    basis = np.where(is_cos, np.cos(angle), np.sin(angle))
    weight = np.where((index == 0) | (index == half), 1.0, 2.0)[:, None] / count
    wave = np.where(index == half, 0.0, 2.0 * np.pi * freq / count)[:, None]
    slope = np.where(is_cos, np.sin(angle), -np.cos(angle)) * wave
    return (basis, (weight * basis).T, (weight * slope).T)


def split_table(table, copies):
    whole = np.kron(np.eye(copies), table).astype(np.float32)
    high = whole.astype(BF16)
    low = (whole - high.astype(np.float32)).astype(BF16)
    return np.concatenate([high, low], axis=1)


def sine_half(t):
    x = t * (math.pi / 512.0)
    s = x * x
    p = -2.50521084e-08
    p = p * s + 2.75573192e-06
    p = p * s - 1.98412698e-04
    p = p * s + 8.33333333e-03
    p = p * s - 1.66666667e-01
    return x + x * (s * p)


def grid_kernel(
    cycle_x, cycle_y, place_ref, qc_ref, fy_ref, fx_ref, ix_ref, iy_ref, dy_ref, out_ref,
    buf_a, buf_b, buf_c, buf_d, buf_e, trig_ref,
):
    mesh_x, mesh_y, mesh_z = (GRID_X * cycle_x, GRID_Y * cycle_y, GRID_Z)
    devices = cycle_x * cycle_y
    modes = mesh_z // 2 // devices
    coefs = 2 * modes
    first = place_ref[0] * modes
    columns = GRID_X * GRID_Y
    group_y = max(1, 256 // mesh_y)
    group_x = max(1, 256 // mesh_x)
    atoms = qc_ref.shape[2]

    row = lax.broadcasted_iota(jnp.int32, (ROWS, 1), 0) % coefs
    row_mode = first + row % modes
    row_sine = row >= modes
    row_edge = row_sine & (row_mode == 0)
    row_factor = jnp.where(row_edge, mesh_z // 2, row_mode)
    row_shift = jnp.where(row_sine & (row_mode != 0), mesh_z // 4, 0)
    column_iota = lax.broadcasted_iota(jnp.int32, (columns, atoms), 0)

    def columns_of(device):
        cell = qc_ref[device, 1:2, :].astype(jnp.int32)
        return cell, column_iota == lax.shift_right_logical(cell, 10)

    def spread(device, carry):
        cell, match = columns_of(device)
        depth = cell & (mesh_z - 1)
        turn = (row_factor * depth - row_shift) & (mesh_z - 1)
        trig = sine_half((jnp.abs(turn - mesh_z // 2) - mesh_z // 4).astype(F32))
        high = trig.astype(BF16)
        trig_ref[device, pl.ds(0, ROWS), :] = high
        trig_ref[device, pl.ds(ROWS, ROWS), :] = (trig - high.astype(F32)).astype(BF16)
        charged = trig * qc_ref[device, 0:1, :]
        high = charged.astype(BF16)
        low = (charged - high.astype(F32)).astype(BF16)
        pick = jnp.where(match, 1.0, 0.0).astype(BF16)
        copies = LANES // ROWS
        total = contract_last(pick, jnp.concatenate([high] * copies, axis=0))
        total += contract_last(pick, jnp.concatenate([low] * copies, axis=0))
        buf_a[pl.ds(device * columns, columns), :] = total
        return carry

    lax.fori_loop(0, devices, spread, 0)

    lane = lax.broadcasted_iota(jnp.int32, (1, LANES), 1)
    low_half = lane >= LANES // 2

    def apply(table_ref, data):
        high = data.astype(BF16).astype(F32)
        mixed = jnp.where(low_half, data - high, high).astype(BF16)
        both = jnp.concatenate([mixed, mixed], axis=0)
        result = jnp.dot(table_ref[...], both, preferred_element_type=F32)
        return result + pltpu.roll(result, LANES // 2, 1)

    def forward_y(step, carry):
        parts = []
        for i in range(group_y):
            place = step * group_y + i
            for sy in range(cycle_y):
                start = ((place // GRID_X) * cycle_y + sy) * columns + (place % GRID_X) * GRID_Y
                parts.append(buf_a[pl.ds(pl.multiple_of(start, 8), GRID_Y), :])
        size = group_y * mesh_y
        start = pl.multiple_of(step * size, 8)
        buf_b[pl.ds(start, size), :] = apply(fy_ref, jnp.concatenate(parts, axis=0))
        return carry

    lax.fori_loop(0, mesh_x // group_y, forward_y, 0)

    size_x = group_x * mesh_x
    lane_coef = lane % coefs
    lane_mode = first + lane_coef % modes
    lane_sine = lane_coef >= modes
    lane_freq = jnp.where(lane_sine & (lane_mode == 0), mesh_z // 2, lane_mode)
    wave_z = lane_freq.astype(F32) * (2.0 * math.pi / mesh_z)
    lane_weight = jnp.where(lane_mode == 0, 1.0, 2.0) / mesh_z
    slope_z = jnp.where(lane_mode == 0, 0.0, wave_z) * jnp.where(lane_sine, 1.0, -1.0)
    index_x = lax.broadcasted_iota(jnp.int32, (size_x, 1), 0)
    freq_x = index_x % mesh_x
    freq_x = jnp.where(freq_x <= mesh_x // 2, freq_x, freq_x - mesh_x // 2)
    wave_x = freq_x.astype(F32) * (2.0 * math.pi / mesh_x)
    near = wave_x * wave_x + wave_z * wave_z

    def middle(step, carry):
        parts = []
        for i in range(group_x):
            parts.append(buf_b[pl.ds(step * group_x + i, mesh_x, stride=mesh_y), :])
        spectrum = apply(fx_ref, jnp.concatenate(parts, axis=0))
        freq_y = step * group_x + index_x // mesh_x
        freq_y = jnp.where(freq_y <= mesh_y // 2, freq_y, freq_y - mesh_y // 2)
        wave_y = freq_y.astype(F32) * (2.0 * math.pi / mesh_y)
        wave_sq = near + wave_y * wave_y
        zero = wave_sq == 0.0
        green = jnp.exp(-0.5 * SMEARING * SMEARING * wave_sq) / jnp.where(zero, 1.0, wave_sq)
        green = jnp.where(zero, 0.0, 4.0 * math.pi * green)
        both = apply(ix_ref, spectrum * (green * lane_weight))
        start = pl.multiple_of(step * size_x, 8)
        buf_a[pl.ds(start, size_x), :] = both[:size_x]
        buf_c[pl.ds(start, size_x), :] = both[size_x:]
        return carry

    lax.fori_loop(0, mesh_y // group_x, middle, 0)

    def backward_y(step, carry):
        plain, sloped = ([], [])
        for i in range(group_y):
            place = step * group_y + i
            plain.append(buf_a[pl.ds(place, mesh_y, stride=mesh_x), :])
            sloped.append(buf_c[pl.ds(place, mesh_y, stride=mesh_x), :])
        plain = jnp.concatenate(plain, axis=0)
        size = group_y * mesh_y
        start = pl.multiple_of(step * size, 8)
        potential = apply(iy_ref, plain)
        buf_b[pl.ds(start, size), :] = apply(iy_ref, jnp.concatenate(sloped, axis=0))
        buf_d[pl.ds(start, size), :] = apply(dy_ref, plain)
        buf_e[pl.ds(start, size), :] = pltpu.roll(potential, modes, 1) * slope_z
        return carry

    lax.fori_loop(0, mesh_x // group_y, backward_y, 0)

    use_low = (lane // ROWS) == 1
    use_none = (lane % ROWS) >= coefs

    def sample(device, carry):
        _, match = columns_of(device)
        rows = []
        for buf in (buf_b, buf_d, buf_e):
            for lx in range(GRID_X):
                place = (device // cycle_y) * GRID_X + lx
                start = place * mesh_y + (device % cycle_y) * GRID_Y
                rows.append(buf[pl.ds(pl.multiple_of(start, 8), GRID_Y), :])
        data = jnp.concatenate(rows, axis=0)
        high = data.astype(BF16).astype(F32)
        mixed = jnp.where(use_low, data - high, high)
        mixed = jnp.where(use_none, 0.0, mixed).astype(BF16)
        high = trig_ref[device, pl.ds(0, ROWS), :]
        low = trig_ref[device, pl.ds(ROWS, ROWS), :]
        waves = jnp.concatenate([high, high, low, jnp.zeros_like(low)], axis=0)
        fields = jnp.dot(mixed, waves, preferred_element_type=F32)
        picked = []
        for a in range(3):
            part = jnp.where(match, fields[a * columns : (a + 1) * columns], 0.0)
            picked.append(jnp.sum(part, axis=0, keepdims=True))
        out_ref[device] = jnp.concatenate(picked, axis=0)
        return carry

    lax.fori_loop(0, devices, sample, 0)


def grid_fields(place, gathered, cycle_x, cycle_y):
    mesh_x, mesh_y = (GRID_X * cycle_x, GRID_Y * cycle_y)
    devices, _, atoms = gathered.shape
    group_y = max(1, 256 // mesh_y)
    group_x = max(1, 256 // mesh_x)
    ax, bx, cx = real_tables(mesh_x)
    ay, by, cy = real_tables(mesh_y)
    tables = [
        split_table(ay, group_y),
        split_table(ax, group_x),
        np.concatenate([split_table(bx, group_x), split_table(cx, group_x)], axis=0),
        split_table(by, group_y),
        split_table(cy, group_y),
    ]
    plane = pltpu.VMEM((mesh_x * mesh_y, LANES), F32)
    vmem = pl.BlockSpec(memory_space=pltpu.VMEM)
    return pl.pallas_call(
        functools.partial(grid_kernel, cycle_x, cycle_y),
        in_specs=[pl.BlockSpec(memory_space=pltpu.SMEM)] + [vmem] * 6,
        out_specs=vmem,
        out_shape=jax.ShapeDtypeStruct((devices, 3, atoms), F32),
        scratch_shapes=[plane] * 5 + [pltpu.VMEM((devices, 2 * ROWS, atoms), BF16)],
        compiler_params=pltpu.CompilerParams(vmem_limit_bytes=60 << 20),
        cost_estimate=pl.CostEstimate(
            flops=8_000_000_000, bytes_accessed=4_000_000, transcendentals=100_000
        ),
        name="grid_fields",
    )(place, gathered, *[jnp.asarray(t) for t in tables])


def edge_kernel(
    list_ref, feat_ref, pos_ref, mid_ref, up_ref, down_ref, w_self_ref, w_pair_ref, w_radial_ref,
    w_expand_ref, w_contract_ref, w_final_ref, out_ref,
    table, near_a, near_b, own_ref, sums_ref,
):
    atoms, channels = feat_ref.shape
    ghosts = mid_ref.shape[1] - EXTRA
    per_atom = list_ref.shape[0] // atoms
    chunk = CHUNK_ATOMS * per_atom
    chunks = atoms // CHUNK_ATOMS
    basis_count = w_radial_ref.shape[0]
    spacing = CUTOFF_SQ / (basis_count - 1)

    def column_of(index, size):
        rows = lax.broadcasted_iota(jnp.int32, (8, 3 * LANES), 0)
        cols = lax.broadcasted_iota(jnp.int32, (8, 3 * LANES), 1) // LANES
        return jnp.where(rows == cols, 1.0, 0.0)

    spread = column_of(0, 0)

    def fill(start, rows, coords, shift):
        projected = jnp.dot(rows, w_pair_ref[...], preferred_element_type=F32)
        projected = projected.astype(BF16).astype(F32)
        count = rows.shape[0]
        wide = contract_first(coords, spread, HIGHEST)
        parts = [projected[:, :channels] * 0.5, projected[:, channels:]]
        for a in range(3):
            part = wide[:, a * LANES : (a + 1) * LANES]
            parts.append(part + shift[a] if shift[a] != 0.0 else part)
        for s, part in enumerate(parts):
            table[pl.ds(start * 8 + s, count, stride=8), :] = part
        return parts

    pos = jnp.concatenate([pos_ref[...].astype(F32), jnp.zeros((5, atoms), F32)], axis=0)
    for i in range(atoms // LANES):
        rows = feat_ref[pl.ds(i * LANES, LANES), :]
        parts = fill(i * LANES, rows, pos[:, i * LANES : (i + 1) * LANES], (0.0, 0.0, 0.0))
        own = jnp.dot(rows, w_self_ref[...], preferred_element_type=F32)
        own_ref[0, pl.ds(i * LANES, LANES), :] = own * 0.5
        for a in range(3):
            own_ref[1 + a, pl.ds(i * LANES, LANES), :] = parts[2 + a]
    for sx in range(3):
        for sy, ref in enumerate((up_ref, mid_ref, down_ref)):
            block = 3 * sx + sy
            if block == 4:
                continue
            tail = ref[sx, pl.ds(ghosts, EXTRA), :].astype(F32)
            shift = ((sx - 1) * BOX, (sy - 1) * BOX, 0.0)
            for h in range(ghosts // LANES):
                rows = ref[sx, pl.ds(h * LANES, LANES), :]
                start = atoms + block * ghosts + h * LANES
                fill(start, rows, tail[h * 8 : (h + 1) * 8], shift)

    w_radial = w_radial_ref[...] * 0.5
    high = w_radial.astype(BF16).astype(F32)
    w_basis = jnp.concatenate(
        [high, high, w_radial - high, jnp.zeros((LANES - 3 * basis_count, channels), F32)], axis=0
    ).astype(BF16)
    lane = lax.broadcasted_iota(jnp.int32, (1, LANES), 1)
    center = (lane % basis_count).astype(F32)
    use_low = (lane // basis_count) == 1

    def gather(index, near):
        for a in range(CHUNK_ATOMS):
            for k in range(per_atom):
                j = pl.multiple_of(list_ref[(index * CHUNK_ATOMS + a) * per_atom + k], 8)
                e = k * CHUNK_ATOMS + a
                near[pl.ds(e * 8, 8), :] = table[pl.ds(j, 8), :]

    def work(index, near):
        first = pl.multiple_of(index * CHUNK_ATOMS, 8)

        def per_edge(s):
            return near[pl.ds(s, chunk, stride=8), :].reshape(per_atom, CHUNK_ATOMS, LANES)

        def own(s):
            return own_ref[s, pl.ds(first, CHUNK_ATOMS), :][None]

        disp = [per_edge(2 + a) - own(1 + a) for a in range(3)]
        d2 = disp[0] * disp[0] + disp[1] * disp[1] + disp[2] * disp[2]
        t = (d2 * (1.0 / spacing)).reshape(chunk, LANES) - center
        basis = jnp.exp(-(t * t))
        basis_high = basis.astype(BF16).astype(F32)
        mixed = jnp.where(use_low, basis - basis_high, basis_high).astype(BF16)
        radial = jnp.dot(mixed, w_basis, preferred_element_type=F32)
        half = radial.reshape(per_atom, CHUNK_ATOMS, LANES) + own(0) + per_edge(0)
        edge_in = (half + half * jnp.tanh(half)).astype(BF16).reshape(chunk, LANES)
        half = jnp.dot(edge_in, w_expand_ref[...], preferred_element_type=F32)
        latent = (half + half * jnp.tanh(half)).astype(BF16)
        out = jnp.dot(latent, w_contract_ref[...], preferred_element_type=F32)
        envelope = jnp.maximum(0.0, 1.0 - d2 * (1.0 / CUTOFF_SQ))
        envelope = envelope * envelope
        weight = out.reshape(per_atom, CHUNK_ATOMS, LANES) * envelope * per_edge(1)
        sums_ref[0, pl.ds(first, CHUNK_ATOMS), :] = jnp.sum(weight, axis=0)
        for a in range(3):
            sums_ref[1 + a, pl.ds(first, CHUNK_ATOMS), :] = jnp.sum(disp[a] * weight, axis=0)

    gather(0, near_a)

    def pair(step, carry):
        gather(2 * step + 1, near_b)
        work(2 * step, near_a)
        gather(jnp.minimum(2 * step + 2, chunks - 1), near_a)
        work(2 * step + 1, near_b)
        return carry

    lax.fori_loop(0, chunks // 2, pair, 0)

    scale = 1.0 / math.sqrt(per_atom)
    vector = [sums_ref[1 + a] * scale for a in range(3)]
    square = vector[0] * vector[0] + vector[1] * vector[1] + vector[2] * vector[2]
    invariant = (sums_ref[0] * scale + square * (1.0 / 3.0)).astype(BF16)
    gate = jnp.dot(invariant, w_final_ref[...], preferred_element_type=F32)
    gate = gate * (0.5 + 0.5 * jnp.tanh(0.5 * gate)) * (1.0 / math.sqrt(channels))
    ones = jnp.ones((8, channels), F32)
    short = [contract_last(ones, vector[a] * gate, HIGHEST)[:1] for a in range(3)]
    out_ref[...] = jnp.concatenate(short, axis=0)


def edge_forces(lists, feat, pos, mid, up, down, w_self, w_pair, w_radial, w_expand, w_contract, w_final):
    atoms, channels = feat.shape
    per_atom = lists.shape[1]
    ghosts = mid.shape[1] - EXTRA
    chunk = CHUNK_ATOMS * per_atom
    vmem = pl.BlockSpec(memory_space=pltpu.VMEM)
    near = pltpu.VMEM((chunk * 8, LANES), F32)
    edges = atoms * per_atom
    latent = w_expand.shape[1]
    return pl.pallas_call(
        edge_kernel,
        in_specs=[pl.BlockSpec(memory_space=pltpu.SMEM)] + [vmem] * 11,
        out_specs=vmem,
        out_shape=jax.ShapeDtypeStruct((3, atoms), F32),
        scratch_shapes=[
            pltpu.VMEM(((atoms + 9 * ghosts) * 8, LANES), F32),
            near,
            near,
            pltpu.VMEM((4, atoms, LANES), F32),
            pltpu.VMEM((4, atoms, LANES), F32),
        ],
        compiler_params=pltpu.CompilerParams(vmem_limit_bytes=56 << 20),
        cost_estimate=pl.CostEstimate(
            flops=4 * edges * channels * latent,
            bytes_accessed=4_000_000,
            transcendentals=edges * latent,
        ),
        name="edge_forces",
    )(
        (lists * 8).reshape(-1), feat, pos, mid, up, down, w_self, w_pair, w_radial,
        w_expand * 0.5, w_contract, w_final,
    )


def ring(array, axis, step):
    size = lax.axis_size(axis)
    return lax.ppermute(array, axis, [(i, (i + step) % size) for i in range(size)])


def shards(
    features, positions, atom_count, ghost_index, neighbour_list, cell_index, w_self, w_pair,
    w_radial, w_expand, w_contract, w_final, w_charge,
):
    feat = features[0, 0]
    pos = positions[0, 0]
    cycle_x, cycle_y = (lax.axis_size("dx"), lax.axis_size("dy"))
    exported, charge_cell = prepare(
        atom_count, feat, pos, ghost_index[0, 0], cell_index[0, 0], w_charge
    )
    gathered = lax.all_gather(charge_cell, ("dx", "dy"))
    mid = jnp.stack([ring(exported, "dx", 1), exported, ring(exported, "dx", -1)])
    up = ring(mid, "dy", 1)
    down = ring(mid, "dy", -1)
    place = lax.axis_index("dx") * cycle_y + lax.axis_index("dy")
    partial = grid_fields(place[None].astype(jnp.int32), gathered, cycle_x, cycle_y)
    received = lax.all_to_all(partial, ("dx", "dy"), split_axis=0, concat_axis=0, tiled=True)
    short = edge_forces(
        neighbour_list[0, 0], feat, pos, mid, up, down, w_self, w_pair, w_radial, w_expand,
        w_contract, w_final,
    )
    field = jnp.sum(received, axis=0)
    total = short + charge_cell[:1] * field
    live = lax.broadcasted_iota(jnp.int32, (1, feat.shape[0]), 1) < atom_count[0, 0]
    return jnp.where(live, total, jnp.zeros_like(total))[None, None]


def solution(mesh):
    placed = (
        P("dx", "dy", None, None),
        P("dx", "dy", None, None),
        P("dx", "dy"),
        P("dx", "dy", None),
        P("dx", "dy", None, None),
        P("dx", "dy", None),
    ) + (P(),) * 7
    return jax.shard_map(
        shards, mesh=mesh, in_specs=placed, out_specs=P("dx", "dy", None, None), check_vma=False
    )
```

```python
import functools
import math

import jax
import jax.numpy as jnp
import numpy as np
from jax import lax
from jax.experimental import pallas as pl
from jax.experimental.pallas import tpu as pltpu
from jax.sharding import PartitionSpec as P

GRID_X = 8
GRID_Y = 8
GRID_Z = 1024
BOX = 1.0
CUTOFF_SQ = 6.25
SMEARING = 1.0

LANES = 128
EXTRA = 16
ROWS = 32
CHUNK_ATOMS = 16
PIECES = 4
HIGHEST = lax.Precision.HIGHEST
F32 = jnp.float32
BF16 = jnp.bfloat16


def contract_first(a, b, precision=None):
    return lax.dot_general(
        a, b, (((0,), (0,)), ((), ())), precision=precision, preferred_element_type=F32
    )


def contract_last(a, b, precision=None):
    return lax.dot_general(
        a, b, (((1,), (1,)), ((), ())), precision=precision, preferred_element_type=F32
    )


def prepare_kernel(count_ref, feat_ref, pos_ref, export_ref, cell_ref, wq_ref, out_ref, qc_ref):
    atoms = feat_ref.shape[0]
    ghosts = export_ref.shape[1]
    pick = lax.broadcasted_iota(jnp.int32, (atoms, ghosts), 0) == export_ref[...]
    pick = jnp.where(pick, 1.0, 0.0).astype(BF16)
    out_ref[pl.ds(0, ghosts), :] = contract_first(pick, feat_ref[...]).astype(BF16)
    pos = jnp.concatenate([pos_ref[...].astype(F32), jnp.zeros((13, atoms), F32)], axis=0)
    coords = jnp.dot(pos.astype(BF16), pick, preferred_element_type=F32)
    tail = [coords[:8, h * LANES : (h + 1) * LANES] for h in range(ghosts // LANES)]
    out_ref[pl.ds(ghosts, EXTRA), :] = jnp.concatenate(tail, axis=0).astype(BF16)
    weights = jnp.broadcast_to(wq_ref[...].astype(F32), (16, LANES)).astype(BF16)
    charge = contract_last(weights, feat_ref[...])[:1]
    live = lax.broadcasted_iota(jnp.int32, (1, atoms), 1) < count_ref[0, 0]
    qc_ref[...] = jnp.concatenate(
        [jnp.where(live, charge, 0.0), cell_ref[...].astype(F32)], axis=0
    )


def prepare(count, feat, pos, exports, cells, w_charge):
    atoms, ghosts = (feat.shape[0], exports.shape[0])
    vmem = pl.BlockSpec(memory_space=pltpu.VMEM)
    return pl.pallas_call(
        prepare_kernel,
        in_specs=[pl.BlockSpec(memory_space=pltpu.SMEM)] + [vmem] * 5,
        out_specs=[vmem, vmem],
        out_shape=[
            jax.ShapeDtypeStruct((ghosts + EXTRA, feat.shape[1]), BF16),
            jax.ShapeDtypeStruct((2, atoms), F32),
        ],
        name="prepare",
    )(count, feat, pos, exports[None], cells[None], w_charge[None])


def real_tables(count):
    half = count // 2
    index = np.arange(count)
    freq = np.where(index <= half, index, index - half)
    place = np.arange(count)
    angle = 2.0 * np.pi * (freq[:, None] * place[None, :] % count) / count
    is_cos = (index <= half)[:, None]
    basis = np.where(is_cos, np.cos(angle), np.sin(angle))
    weight = np.where((index == 0) | (index == half), 1.0, 2.0)[:, None] / count
    wave = np.where(index == half, 0.0, 2.0 * np.pi * freq / count)[:, None]
    slope = np.where(is_cos, np.sin(angle), -np.cos(angle)) * wave
    return (basis, (weight * basis).T, (weight * slope).T)


def block_table(table, copies):
    return np.kron(np.eye(copies), table).astype(np.float32)


def sine_half(t):
    x = t * (math.pi / 512.0)
    s = x * x
    p = -2.50521084e-08
    p = p * s + 2.75573192e-06
    p = p * s - 1.98412698e-04
    p = p * s + 8.33333333e-03
    p = p * s - 1.66666667e-01
    return x + x * (s * p)


def grid_kernel(
    cycle_x, cycle_y, place_ref, qc_ref, fy_table, fx_table, ix_table, iy_table, dy_table, out_ref,
    buf_a, buf_b, buf_c, buf_d, buf_e, trig_ref, fy_ref, fx_ref, ix_ref, iy_ref, dy_ref,
):
    tables = (fy_table, fx_table, ix_table, iy_table, dy_table)
    for whole, halves in zip(tables, (fy_ref, fx_ref, ix_ref, iy_ref, dy_ref)):
        high = whole[...].astype(BF16)
        halves[:, : whole.shape[1]] = high
        halves[:, whole.shape[1] :] = (whole[...] - high.astype(F32)).astype(BF16)
    mesh_x, mesh_y, mesh_z = (GRID_X * cycle_x, GRID_Y * cycle_y, GRID_Z)
    devices = cycle_x * cycle_y
    modes = mesh_z // 2 // devices
    coefs = 2 * modes
    first = place_ref[0] * modes
    columns = GRID_X * GRID_Y
    group_y = max(1, 256 // mesh_y)
    group_x = max(1, 256 // mesh_x)
    atoms = qc_ref.shape[2]

    row = lax.broadcasted_iota(jnp.int32, (ROWS, 1), 0) % coefs
    row_mode = first + row % modes
    row_sine = row >= modes
    row_edge = row_sine & (row_mode == 0)
    row_factor = jnp.where(row_edge, mesh_z // 2, row_mode)
    row_shift = jnp.where(row_sine & (row_mode != 0), mesh_z // 4, 0)
    column_iota = lax.broadcasted_iota(jnp.int32, (columns, atoms), 0)

    def columns_of(device):
        cell = qc_ref[device, 1:2, :].astype(jnp.int32)
        return cell, column_iota == lax.shift_right_logical(cell, 10)

    def spread(device, carry):
        cell, match = columns_of(device)
        depth = cell & (mesh_z - 1)
        turn = (row_factor * depth - row_shift) & (mesh_z - 1)
        trig = sine_half((jnp.abs(turn - mesh_z // 2) - mesh_z // 4).astype(F32))
        high = trig.astype(BF16)
        trig_ref[device, pl.ds(0, ROWS), :] = high
        trig_ref[device, pl.ds(ROWS, ROWS), :] = (trig - high.astype(F32)).astype(BF16)
        charged = trig * qc_ref[device, 0:1, :]
        high = charged.astype(BF16)
        low = (charged - high.astype(F32)).astype(BF16)
        pick = jnp.where(match, 1.0, 0.0).astype(BF16)
        total = contract_last(pick, jnp.concatenate([high, low] * (LANES // ROWS // 2), axis=0))
        total = total + pltpu.roll(total, ROWS, 1)
        buf_a[pl.ds(pl.multiple_of(device * columns, 8), columns), :] = total
        return carry

    lax.fori_loop(0, devices, spread, 0, unroll=4)

    lane = lax.broadcasted_iota(jnp.int32, (1, LANES), 1)
    low_half = lane >= LANES // 2

    def apply(table_ref, data):
        high = data.astype(BF16).astype(F32)
        mixed = jnp.where(low_half, data - high, high).astype(BF16)
        both = jnp.concatenate([mixed, mixed], axis=0)
        result = jnp.dot(table_ref[...], both, preferred_element_type=F32)
        return result + pltpu.roll(result, LANES // 2, 1)

    def forward_y(step, carry):
        parts = []
        for i in range(group_y):
            place = step * group_y + i
            for sy in range(cycle_y):
                start = ((place // GRID_X) * cycle_y + sy) * columns + (place % GRID_X) * GRID_Y
                parts.append(buf_a[pl.ds(pl.multiple_of(start, 8), GRID_Y), :])
        size = group_y * mesh_y
        start = pl.multiple_of(step * size, 8)
        buf_b[pl.ds(start, size), :] = apply(fy_ref, jnp.concatenate(parts, axis=0))
        return carry

    lax.fori_loop(0, mesh_x // group_y, forward_y, 0, unroll=2)

    size_x = group_x * mesh_x
    lane_coef = lane % coefs
    lane_mode = first + lane_coef % modes
    lane_sine = lane_coef >= modes
    lane_freq = jnp.where(lane_sine & (lane_mode == 0), mesh_z // 2, lane_mode)
    wave_z = lane_freq.astype(F32) * (2.0 * math.pi / mesh_z)
    lane_weight = jnp.where(lane_mode == 0, 1.0, 2.0) / mesh_z
    slope_z = jnp.where(lane_mode == 0, 0.0, wave_z) * jnp.where(lane_sine, 1.0, -1.0)
    index_x = lax.broadcasted_iota(jnp.int32, (size_x, 1), 0)
    freq_x = index_x % mesh_x
    freq_x = jnp.where(freq_x <= mesh_x // 2, freq_x, freq_x - mesh_x // 2)
    wave_x = freq_x.astype(F32) * (2.0 * math.pi / mesh_x)
    near = wave_x * wave_x + wave_z * wave_z

    def middle(step, carry):
        parts = []
        for i in range(group_x):
            parts.append(buf_b[pl.ds(step * group_x + i, mesh_x, stride=mesh_y), :])
        spectrum = apply(fx_ref, jnp.concatenate(parts, axis=0))
        freq_y = step * group_x + index_x // mesh_x
        freq_y = jnp.where(freq_y <= mesh_y // 2, freq_y, freq_y - mesh_y // 2)
        wave_y = freq_y.astype(F32) * (2.0 * math.pi / mesh_y)
        wave_sq = near + wave_y * wave_y
        zero = wave_sq == 0.0
        green = jnp.exp(-0.5 * SMEARING * SMEARING * wave_sq) / jnp.where(zero, 1.0, wave_sq)
        green = jnp.where(zero, 0.0, 4.0 * math.pi * green)
        both = apply(ix_ref, spectrum * (green * lane_weight))
        start = pl.multiple_of(step * size_x, 8)
        buf_a[pl.ds(start, size_x), :] = both[:size_x]
        buf_c[pl.ds(start, size_x), :] = both[size_x:]
        return carry

    lax.fori_loop(0, mesh_y // group_x, middle, 0, unroll=2)

    def backward_y(step, carry):
        plain, sloped = ([], [])
        for i in range(group_y):
            place = step * group_y + i
            plain.append(buf_a[pl.ds(place, mesh_y, stride=mesh_x), :])
            sloped.append(buf_c[pl.ds(place, mesh_y, stride=mesh_x), :])
        plain = jnp.concatenate(plain, axis=0)
        size = group_y * mesh_y
        start = pl.multiple_of(step * size, 8)
        potential = apply(iy_ref, plain)
        buf_b[pl.ds(start, size), :] = apply(iy_ref, jnp.concatenate(sloped, axis=0))
        buf_d[pl.ds(start, size), :] = apply(dy_ref, plain)
        buf_e[pl.ds(start, size), :] = pltpu.roll(potential, modes, 1) * slope_z
        return carry

    lax.fori_loop(0, mesh_x // group_y, backward_y, 0, unroll=2)

    use_low = (lane // ROWS) == 1
    use_none = (lane % ROWS) >= coefs

    def sample(device, carry):
        _, match = columns_of(device)
        rows = []
        for buf in (buf_b, buf_d, buf_e):
            for lx in range(GRID_X):
                place = (device // cycle_y) * GRID_X + lx
                start = place * mesh_y + (device % cycle_y) * GRID_Y
                rows.append(buf[pl.ds(pl.multiple_of(start, 8), GRID_Y), :])
        data = jnp.concatenate(rows, axis=0)
        high = data.astype(BF16).astype(F32)
        mixed = jnp.where(use_low, data - high, high)
        mixed = jnp.where(use_none, 0.0, mixed).astype(BF16)
        high = trig_ref[device, pl.ds(0, ROWS), :]
        low = trig_ref[device, pl.ds(ROWS, ROWS), :]
        waves = jnp.concatenate([high, high, low, jnp.zeros_like(low)], axis=0)
        fields = jnp.dot(mixed, waves, preferred_element_type=F32)
        picked = []
        for a in range(3):
            part = jnp.where(match, fields[a * columns : (a + 1) * columns], 0.0)
            picked.append(jnp.sum(part, axis=0, keepdims=True))
        out_ref[device] = jnp.concatenate(picked, axis=0)
        return carry

    lax.fori_loop(0, devices, sample, 0, unroll=4)


def grid_fields(place, gathered, cycle_x, cycle_y):
    mesh_x, mesh_y = (GRID_X * cycle_x, GRID_Y * cycle_y)
    devices, _, atoms = gathered.shape
    group_y = max(1, 256 // mesh_y)
    group_x = max(1, 256 // mesh_x)
    ax, bx, cx = real_tables(mesh_x)
    ay, by, cy = real_tables(mesh_y)
    tables = [
        block_table(ay, group_y),
        block_table(ax, group_x),
        np.concatenate([block_table(bx, group_x), block_table(cx, group_x)], axis=0),
        block_table(by, group_y),
        block_table(cy, group_y),
    ]
    plane = pltpu.VMEM((mesh_x * mesh_y, LANES), F32)
    vmem = pl.BlockSpec(memory_space=pltpu.VMEM)
    return pl.pallas_call(
        functools.partial(grid_kernel, cycle_x, cycle_y),
        in_specs=[pl.BlockSpec(memory_space=pltpu.SMEM)] + [vmem] * 6,
        out_specs=vmem,
        out_shape=jax.ShapeDtypeStruct((devices, 3, atoms), F32),
        scratch_shapes=[plane] * 5
        + [pltpu.VMEM((devices, 2 * ROWS, atoms), BF16)]
        + [pltpu.VMEM((t.shape[0], 2 * t.shape[1]), BF16) for t in tables],
        compiler_params=pltpu.CompilerParams(vmem_limit_bytes=60 << 20),
        cost_estimate=pl.CostEstimate(
            flops=8_000_000_000, bytes_accessed=4_000_000, transcendentals=100_000
        ),
        name="grid_fields",
    )(place, gathered, *[jnp.asarray(t) for t in tables])


def edge_kernel(
    list_ref, feat_ref, pos_ref, mid_ref, up_ref, down_ref, w_self_ref, w_pair_ref, w_radial_ref,
    w_expand_ref, w_contract_ref, w_final_ref, out_ref,
    table, near_a, near_b, edge_a, edge_b, aux_a, aux_b, own_ref, sums_ref, w_half,
):
    atoms, channels = feat_ref.shape
    ghosts = mid_ref.shape[1] - EXTRA
    per_atom = list_ref.shape[0] // atoms
    chunk = CHUNK_ATOMS * per_atom
    chunks = atoms // CHUNK_ATOMS
    basis_count = w_radial_ref.shape[0]
    spacing = CUTOFF_SQ / (basis_count - 1)

    def column_of(index, size):
        rows = lax.broadcasted_iota(jnp.int32, (8, 3 * LANES), 0)
        cols = lax.broadcasted_iota(jnp.int32, (8, 3 * LANES), 1) // LANES
        return jnp.where(rows == cols, 1.0, 0.0)

    spread = column_of(0, 0)

    def fill(start, rows, coords, shift):
        projected = jnp.dot(rows, w_pair_ref[...], preferred_element_type=F32)
        projected = projected.astype(BF16).astype(F32)
        count = rows.shape[0]
        wide = contract_first(coords, spread, HIGHEST)
        parts = [projected[:, :channels] * 0.5, projected[:, channels:]]
        for a in range(3):
            part = wide[:, a * LANES : (a + 1) * LANES]
            parts.append(part + shift[a] if shift[a] != 0.0 else part)
        for s, part in enumerate(parts):
            table[pl.ds(start * 8 + s, count, stride=8), :] = part
        return parts

    pos = jnp.concatenate([pos_ref[...].astype(F32), jnp.zeros((5, atoms), F32)], axis=0)
    for i in range(atoms // LANES):
        rows = feat_ref[pl.ds(i * LANES, LANES), :]
        parts = fill(i * LANES, rows, pos[:, i * LANES : (i + 1) * LANES], (0.0, 0.0, 0.0))
        own = jnp.dot(rows, w_self_ref[...], preferred_element_type=F32)
        own_ref[0, pl.ds(i * LANES, LANES), :] = own * 0.5
        for a in range(3):
            own_ref[1 + a, pl.ds(i * LANES, LANES), :] = parts[2 + a]
    for sx in range(3):
        for sy, ref in enumerate((up_ref, mid_ref, down_ref)):
            block = 3 * sx + sy
            if block == 4:
                continue
            tail = ref[sx, pl.ds(ghosts, EXTRA), :].astype(F32)
            shift = ((sx - 1) * BOX, (sy - 1) * BOX, 0.0)
            for h in range(ghosts // LANES):
                rows = ref[sx, pl.ds(h * LANES, LANES), :]
                start = atoms + block * ghosts + h * LANES
                fill(start, rows, tail[h * 8 : (h + 1) * 8], shift)

    w_radial = w_radial_ref[...] * 0.5
    high = w_radial.astype(BF16).astype(F32)
    w_basis = jnp.concatenate(
        [high, high, w_radial - high, jnp.zeros((LANES - 3 * basis_count, channels), F32)], axis=0
    ).astype(BF16)
    lane = lax.broadcasted_iota(jnp.int32, (1, LANES), 1)
    center = (lane % basis_count).astype(F32)
    use_low = (lane // basis_count) == 1

    piece = chunk // PIECES
    slots = per_atom // PIECES
    latent = w_expand_ref.shape[1]
    width = latent // PIECES
    w_half[...] = w_expand_ref[...] * 0.5

    def gather(index, near, part):
        for k in range(part * slots, (part + 1) * slots):
            for a in range(CHUNK_ATOMS):
                j = pl.multiple_of(list_ref[k * atoms + index * CHUNK_ATOMS + a], 8)
                e = k * CHUNK_ATOMS + a
                near[pl.ds(e * 8, 8), :] = table[pl.ds(j, 8), :]

    def geometry(index, near, edge_in, aux, part):
        first = pl.multiple_of(index * CHUNK_ATOMS, 8)
        rows = pl.ds(part * piece, piece)

        def per_edge(s):
            start = part * piece * 8 + s
            return near[pl.ds(start, piece, stride=8), :].reshape(slots, CHUNK_ATOMS, LANES)

        def own(s):
            return own_ref[s, pl.ds(first, CHUNK_ATOMS), :][None]

        disp = [per_edge(2 + a) - own(1 + a) for a in range(3)]
        d2 = disp[0] * disp[0] + disp[1] * disp[1] + disp[2] * disp[2]
        t = (d2 * (1.0 / spacing)).reshape(piece, LANES) - center
        basis = jnp.exp(-(t * t))
        basis_high = basis.astype(BF16).astype(F32)
        mixed = jnp.where(use_low, basis - basis_high, basis_high).astype(BF16)
        radial = jnp.dot(mixed, w_basis, preferred_element_type=F32)
        half = radial.reshape(slots, CHUNK_ATOMS, LANES) + own(0) + per_edge(0)
        edge_in[rows, :] = (half + half * jnp.tanh(half)).astype(BF16).reshape(piece, LANES)
        envelope = jnp.maximum(0.0, 1.0 - d2 * (1.0 / CUTOFF_SQ))
        aux[0, rows, :] = (envelope * envelope * per_edge(1)).reshape(piece, LANES)
        for a in range(3):
            aux[1 + a, rows, :] = disp[a].reshape(piece, LANES)

    def network(edge_in, part):
        cols = pl.ds(part * width, width)
        half = jnp.dot(edge_in[...], w_half[:, cols], preferred_element_type=F32)
        hidden = (half + half * jnp.tanh(half)).astype(BF16)
        return jnp.dot(hidden, w_contract_ref[cols, :], preferred_element_type=F32)

    def collect(index, mixed, aux):
        first = pl.multiple_of(index * CHUNK_ATOMS, 8)
        shape = (per_atom, CHUNK_ATOMS, LANES)
        weight = (mixed * aux[0]).reshape(shape)
        sums_ref[0, pl.ds(first, CHUNK_ATOMS), :] = jnp.sum(weight, axis=0)
        for a in range(3):
            moment = jnp.sum(aux[1 + a].reshape(shape) * weight, axis=0)
            sums_ref[1 + a, pl.ds(first, CHUNK_ATOMS), :] = moment

    def stage(index, near, near_next, edge_in, edge_next, aux, aux_next):
        after = jnp.minimum(index + 1, chunks - 1)
        later = jnp.minimum(index + 2, chunks - 1)
        mixed = None
        for part in range(PIECES):
            gather(later, near, part)
            geometry(after, near_next, edge_next, aux_next, part)
            term = network(edge_in, part)
            mixed = term if mixed is None else mixed + term
        collect(index, mixed, aux)

    for part in range(PIECES):
        gather(0, near_a, part)
    for part in range(PIECES):
        gather(1, near_b, part)
        geometry(0, near_a, edge_a, aux_a, part)

    def pair(step, carry):
        stage(2 * step, near_a, near_b, edge_a, edge_b, aux_a, aux_b)
        stage(2 * step + 1, near_b, near_a, edge_b, edge_a, aux_b, aux_a)
        return carry

    lax.fori_loop(0, chunks // 2, pair, 0)

    scale = 1.0 / math.sqrt(per_atom)
    vector = [sums_ref[1 + a] * scale for a in range(3)]
    square = vector[0] * vector[0] + vector[1] * vector[1] + vector[2] * vector[2]
    invariant = (sums_ref[0] * scale + square * (1.0 / 3.0)).astype(BF16)
    gate = jnp.dot(invariant, w_final_ref[...], preferred_element_type=F32)
    gate = gate * (0.5 + 0.5 * jnp.tanh(0.5 * gate)) * (1.0 / math.sqrt(channels))
    ones = jnp.ones((8, channels), F32)
    short = [contract_last(ones, vector[a] * gate, HIGHEST)[:1] for a in range(3)]
    out_ref[...] = jnp.concatenate(short, axis=0)


def edge_forces(per_atom, lists, feat, pos, mid, up, down, w_self, w_pair, w_radial, w_expand, w_contract, w_final):
    atoms, channels = feat.shape
    ghosts = mid.shape[1] - EXTRA
    chunk = CHUNK_ATOMS * per_atom
    vmem = pl.BlockSpec(memory_space=pltpu.VMEM)
    near = pltpu.VMEM((chunk * 8, LANES), F32)
    edge = pltpu.VMEM((chunk, LANES), BF16)
    aux = pltpu.VMEM((4, chunk, LANES), F32)
    edges = atoms * per_atom
    latent = w_expand.shape[1]
    return pl.pallas_call(
        edge_kernel,
        in_specs=[pl.BlockSpec(memory_space=pltpu.SMEM)] + [vmem] * 11,
        out_specs=vmem,
        out_shape=jax.ShapeDtypeStruct((3, atoms), F32),
        scratch_shapes=[
            pltpu.VMEM(((atoms + 9 * ghosts) * 8, LANES), F32),
            near,
            near,
            edge,
            edge,
            aux,
            aux,
            pltpu.VMEM((4, atoms, LANES), F32),
            pltpu.VMEM((4, atoms, LANES), F32),
            pltpu.VMEM(w_expand.shape, BF16),
        ],
        compiler_params=pltpu.CompilerParams(vmem_limit_bytes=56 << 20),
        cost_estimate=pl.CostEstimate(
            flops=4 * edges * channels * latent,
            bytes_accessed=4_000_000,
            transcendentals=edges * latent,
        ),
        name="edge_forces",
    )(
        lists, feat, pos, mid, up, down, w_self, w_pair, w_radial,
        w_expand, w_contract, w_final,
    )


def ring(array, axis, step):
    size = lax.axis_size(axis)
    return lax.ppermute(array, axis, [(i, (i + step) % size) for i in range(size)])


def shards(
    features, positions, atom_count, ghost_index, neighbour_list, cell_index, w_self, w_pair,
    w_radial, w_expand, w_contract, w_final, w_charge,
):
    feat = features[0, 0]
    pos = positions[0, 0]
    cycle_x, cycle_y = (lax.axis_size("dx"), lax.axis_size("dy"))
    exported, charge_cell = prepare(
        atom_count, feat, pos, ghost_index[0, 0], cell_index[0, 0], w_charge
    )
    spread = jnp.broadcast_to(charge_cell, (cycle_x * cycle_y,) + charge_cell.shape)
    gathered = lax.all_to_all(spread, ("dx", "dy"), split_axis=0, concat_axis=0, tiled=True)
    mid = jnp.stack([ring(exported, "dx", 1), exported, ring(exported, "dx", -1)])
    lists = (neighbour_list[0, 0] * 8).T.reshape(-1)
    gathered, mid, lists = lax.optimization_barrier((gathered, mid, lists))
    up = ring(mid, "dy", 1)
    down = ring(mid, "dy", -1)
    place = lax.axis_index("dx") * cycle_y + lax.axis_index("dy")
    partial = grid_fields(place[None].astype(jnp.int32), gathered, cycle_x, cycle_y)
    received = lax.all_to_all(partial, ("dx", "dy"), split_axis=0, concat_axis=0, tiled=True)
    short = edge_forces(
        neighbour_list.shape[3], lists, feat, pos, mid, up, down, w_self, w_pair, w_radial, w_expand,
        w_contract, w_final,
    )
    field = jnp.sum(received, axis=0)
    total = short + charge_cell[:1] * field
    live = lax.broadcasted_iota(jnp.int32, (1, feat.shape[0]), 1) < atom_count[0, 0]
    return jnp.where(live, total, jnp.zeros_like(total))[None, None]


def solution(mesh):
    placed = (
        P("dx", "dy", None, None),
        P("dx", "dy", None, None),
        P("dx", "dy"),
        P("dx", "dy", None),
        P("dx", "dy", None, None),
        P("dx", "dy", None),
    ) + (P(),) * 7
    return jax.shard_map(
        shards, mesh=mesh, in_specs=placed, out_specs=P("dx", "dy", None, None), check_vma=False
    )
```

```python
import functools
import math

import jax
import jax.numpy as jnp
import numpy as np
from jax import lax
from jax.experimental import pallas as pl
from jax.experimental.pallas import tpu as pltpu
from jax.sharding import PartitionSpec as P

GRID_X = 8
GRID_Y = 8
GRID_Z = 1024
BOX = 1.0
CUTOFF_SQ = 6.25
SMEARING = 1.0

LANES = 128
EXTRA = 16
ROWS = 32
CHUNK_ATOMS = 16
PIECES = 4
HIGHEST = lax.Precision.HIGHEST
F32 = jnp.float32
BF16 = jnp.bfloat16


def contract_first(a, b, precision=None):
    return lax.dot_general(
        a, b, (((0,), (0,)), ((), ())), precision=precision, preferred_element_type=F32
    )


def contract_last(a, b, precision=None):
    return lax.dot_general(
        a, b, (((1,), (1,)), ((), ())), precision=precision, preferred_element_type=F32
    )


def prepare_kernel(count_ref, feat_ref, pos_ref, export_ref, cell_ref, wq_ref, out_ref, qc_ref):
    atoms = feat_ref.shape[0]
    ghosts = export_ref.shape[1]
    pick = lax.broadcasted_iota(jnp.int32, (atoms, ghosts), 0) == export_ref[...]
    pick = jnp.where(pick, 1.0, 0.0).astype(BF16)
    out_ref[pl.ds(0, ghosts), :] = contract_first(pick, feat_ref[...]).astype(BF16)
    pos = jnp.concatenate([pos_ref[...].astype(F32), jnp.zeros((13, atoms), F32)], axis=0)
    coords = jnp.dot(pos.astype(BF16), pick, preferred_element_type=F32)
    tail = [coords[:8, h * LANES : (h + 1) * LANES] for h in range(ghosts // LANES)]
    out_ref[pl.ds(ghosts, EXTRA), :] = jnp.concatenate(tail, axis=0).astype(BF16)
    weights = jnp.broadcast_to(wq_ref[...].astype(F32), (16, LANES)).astype(BF16)
    charge = contract_last(weights, feat_ref[...])[:1]
    live = lax.broadcasted_iota(jnp.int32, (1, atoms), 1) < count_ref[0, 0]
    qc_ref[...] = jnp.concatenate(
        [jnp.where(live, charge, 0.0), cell_ref[...].astype(F32)], axis=0
    )


def prepare(count, feat, pos, exports, cells, w_charge):
    atoms, ghosts = (feat.shape[0], exports.shape[0])
    vmem = pl.BlockSpec(memory_space=pltpu.VMEM)
    return pl.pallas_call(
        prepare_kernel,
        in_specs=[pl.BlockSpec(memory_space=pltpu.SMEM)] + [vmem] * 5,
        out_specs=[vmem, vmem],
        out_shape=[
            jax.ShapeDtypeStruct((ghosts + EXTRA, feat.shape[1]), BF16),
            jax.ShapeDtypeStruct((2, atoms), F32),
        ],
        name="prepare",
    )(count, feat, pos, exports[None], cells[None], w_charge[None])


def real_tables(count):
    half = count // 2
    index = np.arange(count)
    freq = np.where(index <= half, index, index - half)
    place = np.arange(count)
    angle = 2.0 * np.pi * (freq[:, None] * place[None, :] % count) / count
    is_cos = (index <= half)[:, None]
    basis = np.where(is_cos, np.cos(angle), np.sin(angle))
    weight = np.where((index == 0) | (index == half), 1.0, 2.0)[:, None] / count
    wave = np.where(index == half, 0.0, 2.0 * np.pi * freq / count)[:, None]
    slope = np.where(is_cos, np.sin(angle), -np.cos(angle)) * wave
    return (basis, (weight * basis).T, (weight * slope).T)


def block_table(table, copies):
    return np.kron(np.eye(copies), table).astype(np.float32)


def sine_half(t):
    x = t * (math.pi / 512.0)
    s = x * x
    p = -2.50521084e-08
    p = p * s + 2.75573192e-06
    p = p * s - 1.98412698e-04
    p = p * s + 8.33333333e-03
    p = p * s - 1.66666667e-01
    return x + x * (s * p)


def grid_kernel(
    cycle_x, cycle_y, place_ref, qc_ref, fy_table, fx_table, ix_table, iy_table, dy_table, out_ref,
    buf_a, buf_b, buf_c, buf_d, buf_e, trig_ref, fy_ref, fx_ref, ix_ref, iy_ref, dy_ref,
):
    tables = (fy_table, fx_table, ix_table, iy_table, dy_table)
    for whole, halves in zip(tables, (fy_ref, fx_ref, ix_ref, iy_ref, dy_ref)):
        high = whole[...].astype(BF16)
        halves[:, : whole.shape[1]] = high
        halves[:, whole.shape[1] :] = (whole[...] - high.astype(F32)).astype(BF16)
    mesh_x, mesh_y, mesh_z = (GRID_X * cycle_x, GRID_Y * cycle_y, GRID_Z)
    devices = cycle_x * cycle_y
    modes = mesh_z // 2 // devices
    coefs = 2 * modes
    first = place_ref[0] * modes
    columns = GRID_X * GRID_Y
    group_y = max(1, 256 // mesh_y)
    group_x = max(1, 256 // mesh_x)
    atoms = qc_ref.shape[2]

    row = lax.broadcasted_iota(jnp.int32, (ROWS, 1), 0) % coefs
    row_mode = first + row % modes
    row_sine = row >= modes
    row_edge = row_sine & (row_mode == 0)
    row_factor = jnp.where(row_edge, mesh_z // 2, row_mode)
    row_shift = jnp.where(row_sine & (row_mode != 0), mesh_z // 4, 0)
    column_iota = lax.broadcasted_iota(jnp.int32, (columns, atoms), 0)

    def columns_of(device):
        cell = qc_ref[device, 1:2, :].astype(jnp.int32)
        return cell, column_iota == lax.shift_right_logical(cell, 10)

    def spread(device, carry):
        cell, match = columns_of(device)
        depth = cell & (mesh_z - 1)
        turn = (row_factor * depth - row_shift) & (mesh_z - 1)
        trig = sine_half((jnp.abs(turn - mesh_z // 2) - mesh_z // 4).astype(F32))
        high = trig.astype(BF16)
        trig_ref[device, pl.ds(0, ROWS), :] = high
        trig_ref[device, pl.ds(ROWS, ROWS), :] = (trig - high.astype(F32)).astype(BF16)
        charged = trig * qc_ref[device, 0:1, :]
        high = charged.astype(BF16)
        low = (charged - high.astype(F32)).astype(BF16)
        pick = jnp.where(match, 1.0, 0.0).astype(BF16)
        total = contract_last(pick, jnp.concatenate([high, low] * (LANES // ROWS // 2), axis=0))
        total = total + pltpu.roll(total, ROWS, 1)
        buf_a[pl.ds(pl.multiple_of(device * columns, 8), columns), :] = total
        return carry

    lax.fori_loop(0, devices, spread, 0, unroll=4)

    lane = lax.broadcasted_iota(jnp.int32, (1, LANES), 1)
    low_half = lane >= LANES // 2

    def apply(table_ref, data):
        high = data.astype(BF16).astype(F32)
        mixed = jnp.where(low_half, data - high, high).astype(BF16)
        both = jnp.concatenate([mixed, mixed], axis=0)
        result = jnp.dot(table_ref[...], both, preferred_element_type=F32)
        return result + pltpu.roll(result, LANES // 2, 1)

    def forward_y(step, carry):
        parts = []
        for i in range(group_y):
            place = step * group_y + i
            for sy in range(cycle_y):
                start = ((place // GRID_X) * cycle_y + sy) * columns + (place % GRID_X) * GRID_Y
                parts.append(buf_a[pl.ds(pl.multiple_of(start, 8), GRID_Y), :])
        size = group_y * mesh_y
        start = pl.multiple_of(step * size, 8)
        buf_b[pl.ds(start, size), :] = apply(fy_ref, jnp.concatenate(parts, axis=0))
        return carry

    lax.fori_loop(0, mesh_x // group_y, forward_y, 0, unroll=2)

    size_x = group_x * mesh_x
    lane_coef = lane % coefs
    lane_mode = first + lane_coef % modes
    lane_sine = lane_coef >= modes
    lane_freq = jnp.where(lane_sine & (lane_mode == 0), mesh_z // 2, lane_mode)
    wave_z = lane_freq.astype(F32) * (2.0 * math.pi / mesh_z)
    lane_weight = jnp.where(lane_mode == 0, 1.0, 2.0) / mesh_z
    slope_z = jnp.where(lane_mode == 0, 0.0, wave_z) * jnp.where(lane_sine, 1.0, -1.0)
    index_x = lax.broadcasted_iota(jnp.int32, (size_x, 1), 0)
    freq_x = index_x % mesh_x
    freq_x = jnp.where(freq_x <= mesh_x // 2, freq_x, freq_x - mesh_x // 2)
    wave_x = freq_x.astype(F32) * (2.0 * math.pi / mesh_x)
    near = wave_x * wave_x + wave_z * wave_z

    def middle(step, carry):
        parts = []
        for i in range(group_x):
            parts.append(buf_b[pl.ds(step * group_x + i, mesh_x, stride=mesh_y), :])
        spectrum = apply(fx_ref, jnp.concatenate(parts, axis=0))
        freq_y = step * group_x + index_x // mesh_x
        freq_y = jnp.where(freq_y <= mesh_y // 2, freq_y, freq_y - mesh_y // 2)
        wave_y = freq_y.astype(F32) * (2.0 * math.pi / mesh_y)
        wave_sq = near + wave_y * wave_y
        zero = wave_sq == 0.0
        green = jnp.exp(-0.5 * SMEARING * SMEARING * wave_sq) / jnp.where(zero, 1.0, wave_sq)
        green = jnp.where(zero, 0.0, 4.0 * math.pi * green)
        both = apply(ix_ref, spectrum * (green * lane_weight))
        start = pl.multiple_of(step * size_x, 8)
        buf_a[pl.ds(start, size_x), :] = both[:size_x]
        buf_c[pl.ds(start, size_x), :] = both[size_x:]
        return carry

    lax.fori_loop(0, mesh_y // group_x, middle, 0, unroll=2)

    def backward_y(step, carry):
        plain, sloped = ([], [])
        for i in range(group_y):
            place = step * group_y + i
            plain.append(buf_a[pl.ds(place, mesh_y, stride=mesh_x), :])
            sloped.append(buf_c[pl.ds(place, mesh_y, stride=mesh_x), :])
        plain = jnp.concatenate(plain, axis=0)
        size = group_y * mesh_y
        start = pl.multiple_of(step * size, 8)
        potential = apply(iy_ref, plain)
        buf_b[pl.ds(start, size), :] = apply(iy_ref, jnp.concatenate(sloped, axis=0))
        buf_d[pl.ds(start, size), :] = apply(dy_ref, plain)
        buf_e[pl.ds(start, size), :] = pltpu.roll(potential, modes, 1) * slope_z
        return carry

    lax.fori_loop(0, mesh_x // group_y, backward_y, 0, unroll=2)

    use_low = (lane // ROWS) == 1
    use_none = (lane % ROWS) >= coefs

    def sample(device, carry):
        _, match = columns_of(device)
        rows = []
        for buf in (buf_b, buf_d, buf_e):
            for lx in range(GRID_X):
                place = (device // cycle_y) * GRID_X + lx
                start = place * mesh_y + (device % cycle_y) * GRID_Y
                rows.append(buf[pl.ds(pl.multiple_of(start, 8), GRID_Y), :])
        data = jnp.concatenate(rows, axis=0)
        high = data.astype(BF16).astype(F32)
        mixed = jnp.where(use_low, data - high, high)
        mixed = jnp.where(use_none, 0.0, mixed).astype(BF16)
        high = trig_ref[device, pl.ds(0, ROWS), :]
        low = trig_ref[device, pl.ds(ROWS, ROWS), :]
        waves = jnp.concatenate([high, high, low, jnp.zeros_like(low)], axis=0)
        fields = jnp.dot(mixed, waves, preferred_element_type=F32)
        picked = []
        for a in range(3):
            part = jnp.where(match, fields[a * columns : (a + 1) * columns], 0.0)
            picked.append(jnp.sum(part, axis=0, keepdims=True))
        out_ref[device] = jnp.concatenate(picked, axis=0)
        return carry

    lax.fori_loop(0, devices, sample, 0, unroll=4)


def grid_fields(place, gathered, cycle_x, cycle_y):
    mesh_x, mesh_y = (GRID_X * cycle_x, GRID_Y * cycle_y)
    devices, _, atoms = gathered.shape
    group_y = max(1, 256 // mesh_y)
    group_x = max(1, 256 // mesh_x)
    ax, bx, cx = real_tables(mesh_x)
    ay, by, cy = real_tables(mesh_y)
    tables = [
        block_table(ay, group_y),
        block_table(ax, group_x),
        np.concatenate([block_table(bx, group_x), block_table(cx, group_x)], axis=0),
        block_table(by, group_y),
        block_table(cy, group_y),
    ]
    plane = pltpu.VMEM((mesh_x * mesh_y, LANES), F32)
    vmem = pl.BlockSpec(memory_space=pltpu.VMEM)
    return pl.pallas_call(
        functools.partial(grid_kernel, cycle_x, cycle_y),
        in_specs=[pl.BlockSpec(memory_space=pltpu.SMEM)] + [vmem] * 6,
        out_specs=vmem,
        out_shape=jax.ShapeDtypeStruct((devices, 3, atoms), F32),
        scratch_shapes=[plane] * 5
        + [pltpu.VMEM((devices, 2 * ROWS, atoms), BF16)]
        + [pltpu.VMEM((t.shape[0], 2 * t.shape[1]), BF16) for t in tables],
        compiler_params=pltpu.CompilerParams(vmem_limit_bytes=60 << 20),
        cost_estimate=pl.CostEstimate(
            flops=8_000_000_000, bytes_accessed=4_000_000, transcendentals=100_000
        ),
        name="grid_fields",
    )(place, gathered, *[jnp.asarray(t) for t in tables])


def edge_kernel(
    list_ref, index_ref, feat_ref, pos_ref, mid_ref, up_ref, down_ref, w_self_ref, w_pair_ref,
    w_radial_ref, w_expand_ref, w_contract_ref, w_final_ref, out_ref,
    table, places, near_a, near_b, near_c, edge_a, edge_b, edge_c, marks, own_ref, sums_ref, w_half,
):
    atoms, channels = feat_ref.shape
    ghosts = mid_ref.shape[1] - EXTRA
    slots_all = atoms + 9 * ghosts
    per_atom = index_ref.shape[0]
    chunk = CHUNK_ATOMS * per_atom
    chunks = atoms // CHUNK_ATOMS
    basis_count = w_radial_ref.shape[0]
    spacing = CUTOFF_SQ / (basis_count - 1)
    latent = w_expand_ref.shape[1]
    width = latent // PIECES
    slots = per_atom // PIECES
    w_half[...] = w_expand_ref[...] * 0.5

    def fill(start, rows, coords, shift):
        count = rows.shape[0]
        projected = jnp.dot(rows, w_pair_ref[...], preferred_element_type=F32)
        projected = projected.astype(BF16).astype(F32)
        table[pl.ds(start, count), :] = projected[:, :channels] * 0.5
        table[pl.ds(slots_all + start, count), :] = projected[:, channels:]
        row = lax.broadcasted_iota(jnp.int32, (8, LANES), 0)
        offset = jnp.where(row == 0, shift[0], jnp.where(row == 1, shift[1], 0.0))
        places[start // LANES] = coords + offset

    pos = jnp.concatenate([pos_ref[...].astype(F32), jnp.zeros((5, atoms), F32)], axis=0)
    for i in range(atoms // LANES):
        rows = feat_ref[pl.ds(i * LANES, LANES), :]
        fill(i * LANES, rows, pos[:, i * LANES : (i + 1) * LANES], (0.0, 0.0))
        own = jnp.dot(rows, w_self_ref[...], preferred_element_type=F32)
        own_ref[pl.ds(i * LANES, LANES), :] = own * 0.5
    for sx in range(3):
        for sy, ref in enumerate((up_ref, mid_ref, down_ref)):
            block = 3 * sx + sy
            if block == 4:
                continue
            tail = ref[sx, pl.ds(ghosts, EXTRA), :].astype(F32)
            for h in range(ghosts // LANES):
                rows = ref[sx, pl.ds(h * LANES, LANES), :]
                start = atoms + block * ghosts + h * LANES
                fill(start, rows, tail[h * 8 : (h + 1) * 8], ((sx - 1) * BOX, (sy - 1) * BOX))

    feature = lax.broadcasted_iota(jnp.int32, (8, LANES), 0)
    skipped = range((atoms + 4 * ghosts) // LANES, (atoms + 5 * ghosts) // LANES)
    for i in range(atoms // LANES):
        columns = slice(i * LANES, (i + 1) * LANES)
        index = index_ref[:, columns]
        inside = index & (LANES - 1)
        outside = lax.shift_right_logical(index, 7)
        found = [jnp.zeros((per_atom, LANES), F32)] * 3
        for c in range(slots_all // LANES):
            if c in skipped:
                continue
            tile = places[c]
            here = outside == c
            for a in range(3):
                source = jnp.broadcast_to(tile[a : a + 1], (per_atom, LANES))
                value = jnp.take_along_axis(source, inside, axis=1)
                found[a] = jnp.where(here, value, found[a])
        disp = [found[a] - pos[a : a + 1, columns] for a in range(3)]
        d2 = disp[0] * disp[0] + disp[1] * disp[1] + disp[2] * disp[2]
        envelope = jnp.maximum(0.0, 1.0 - d2 * (1.0 / CUTOFF_SQ))
        envelope = envelope * envelope
        moments = [envelope] + [envelope * disp[a] for a in range(3)]
        for k in range(per_atom):
            def wide(value):
                return jnp.broadcast_to(value[k : k + 1], (8, LANES))

            t = wide(d2) * (1.0 / spacing) - feature.astype(F32)
            basis = jnp.exp(-(t * t))
            high = basis.astype(BF16).astype(F32)
            tail = jnp.where(feature == 0, wide(moments[0]), 0.0)
            for a in range(3):
                tail = jnp.where(feature == 1 + a, wide(moments[1 + a]), tail)
            stacked = jnp.concatenate([high, basis - high, high, tail], axis=0)
            marks[k, pl.ds(i * LANES, LANES), :] = stacked.T

    w_radial = w_radial_ref[...] * 0.5
    high = w_radial.astype(BF16).astype(F32)
    w_basis = jnp.concatenate(
        [high, high, w_radial - high, jnp.zeros((8, channels), F32)], axis=0
    ).astype(BF16)

    def gather(index, near, part):
        for k in range(part * slots, (part + 1) * slots):
            for a in range(CHUNK_ATOMS):
                j = list_ref[k * atoms + index * CHUNK_ATOMS + a]
                e = k * CHUNK_ATOMS + a
                near[pl.ds(e, 2, stride=chunk), :] = table[pl.ds(j, 2, stride=slots_all), :]

    def enter(index, near, edge_in, part):
        first = pl.multiple_of(index * CHUNK_ATOMS, 8)
        rows = pl.ds(part * slots * CHUNK_ATOMS, slots * CHUNK_ATOMS)
        shape = (slots, CHUNK_ATOMS, LANES)
        basis = marks[pl.ds(part * slots, slots), pl.ds(first, CHUNK_ATOMS), :]
        basis = basis.reshape(slots * CHUNK_ATOMS, basis.shape[2]).astype(BF16)
        radial = jnp.dot(basis, w_basis, preferred_element_type=F32).reshape(shape)
        own = own_ref[pl.ds(first, CHUNK_ATOMS), :][None]
        half = radial + own + near[rows, :].reshape(shape)
        edge_in[rows, :] = (half + half * jnp.tanh(half)).astype(BF16).reshape(-1, LANES)

    def network(edge_in, part):
        cols = pl.ds(part * width, width)
        half = jnp.dot(edge_in[...], w_half[:, cols], preferred_element_type=F32)
        hidden = (half + half * jnp.tanh(half)).astype(BF16)
        return jnp.dot(hidden, w_contract_ref[cols, :], preferred_element_type=F32)

    def collect(index, mixed, near):
        first = pl.multiple_of(index * CHUNK_ATOMS, 8)
        weight = (mixed * near[pl.ds(chunk, chunk), :]).reshape(per_atom, CHUNK_ATOMS, LANES)
        for s in range(4):
            mark = marks[:, pl.ds(first, CHUNK_ATOMS), 3 * basis_count + s : 3 * basis_count + s + 1]
            sums_ref[s, pl.ds(first, CHUNK_ATOMS), :] = jnp.sum(weight * mark, axis=0)

    def stage(index, nears, edges):
        after = jnp.minimum(index + 1, chunks - 1)
        later = jnp.minimum(index + 2, chunks - 1)
        mixed = None
        for part in range(PIECES):
            gather(later, nears[2], part)
            enter(after, nears[1], edges[1], part)
            term = network(edges[0], part)
            mixed = term if mixed is None else mixed + term
        collect(index, mixed, nears[0])

    nears = (near_a, near_b, near_c)
    edges = (edge_a, edge_b, edge_c)
    for part in range(PIECES):
        gather(0, near_a, part)
    for part in range(PIECES):
        gather(1, near_b, part)
        enter(0, near_a, edge_a, part)

    def triple(step, carry):
        for i in range(3):
            order = (i, (i + 1) % 3, (i + 2) % 3)
            stage(3 * step + i, [nears[o] for o in order], [edges[o] for o in order])
        return carry

    lax.fori_loop(0, chunks // 3, triple, 0)

    scale = 1.0 / math.sqrt(per_atom)
    vector = [sums_ref[1 + a] * scale for a in range(3)]
    square = vector[0] * vector[0] + vector[1] * vector[1] + vector[2] * vector[2]
    invariant = (sums_ref[0] * scale + square * (1.0 / 3.0)).astype(BF16)
    gate = jnp.dot(invariant, w_final_ref[...], preferred_element_type=F32)
    gate = gate * (0.5 + 0.5 * jnp.tanh(0.5 * gate)) * (1.0 / math.sqrt(channels))
    ones = jnp.ones((8, channels), F32)
    short = [contract_last(ones, vector[a] * gate, HIGHEST)[:1] for a in range(3)]
    out_ref[...] = jnp.concatenate(short, axis=0)


def edge_forces(index, feat, pos, mid, up, down, w_self, w_pair, w_radial, w_expand, w_contract, w_final):
    atoms, channels = feat.shape
    per_atom = index.shape[0]
    ghosts = mid.shape[1] - EXTRA
    slots_all = atoms + 9 * ghosts
    chunk = CHUNK_ATOMS * per_atom
    vmem = pl.BlockSpec(memory_space=pltpu.VMEM)
    edges = atoms * per_atom
    latent = w_expand.shape[1]
    return pl.pallas_call(
        edge_kernel,
        in_specs=[pl.BlockSpec(memory_space=pltpu.SMEM)] + [vmem] * 12,
        out_specs=vmem,
        out_shape=jax.ShapeDtypeStruct((3, atoms), F32),
        scratch_shapes=[
            pltpu.VMEM((2 * slots_all, LANES), F32),
            pltpu.VMEM((slots_all // LANES, 8, LANES), F32),
        ]
        + [pltpu.VMEM((2 * chunk, LANES), F32)] * 3
        + [pltpu.VMEM((chunk, LANES), BF16)] * 3
        + [
            pltpu.VMEM((per_atom, atoms, 32), F32),
            pltpu.VMEM((atoms, LANES), F32),
            pltpu.VMEM((4, atoms, LANES), F32),
            pltpu.VMEM(w_expand.shape, BF16),
        ],
        compiler_params=pltpu.CompilerParams(vmem_limit_bytes=56 << 20),
        cost_estimate=pl.CostEstimate(
            flops=4 * edges * channels * latent,
            bytes_accessed=4_000_000,
            transcendentals=edges * latent,
        ),
        name="edge_forces",
    )(
        index.reshape(-1), index, feat, pos, mid, up, down, w_self, w_pair, w_radial,
        w_expand, w_contract, w_final,
    )


def ring(array, axis, step):
    size = lax.axis_size(axis)
    return lax.ppermute(array, axis, [(i, (i + step) % size) for i in range(size)])


def shards(
    features, positions, atom_count, ghost_index, neighbour_list, cell_index, w_self, w_pair,
    w_radial, w_expand, w_contract, w_final, w_charge,
):
    feat = features[0, 0]
    pos = positions[0, 0]
    cycle_x, cycle_y = (lax.axis_size("dx"), lax.axis_size("dy"))
    exported, charge_cell = prepare(
        atom_count, feat, pos, ghost_index[0, 0], cell_index[0, 0], w_charge
    )
    spread = jnp.broadcast_to(charge_cell, (cycle_x * cycle_y,) + charge_cell.shape)
    gathered = lax.all_to_all(spread, ("dx", "dy"), split_axis=0, concat_axis=0, tiled=True)
    mid = jnp.stack([ring(exported, "dx", 1), exported, ring(exported, "dx", -1)])
    lists = neighbour_list[0, 0].T
    gathered, mid, lists = lax.optimization_barrier((gathered, mid, lists))
    up = ring(mid, "dy", 1)
    down = ring(mid, "dy", -1)
    place = lax.axis_index("dx") * cycle_y + lax.axis_index("dy")
    partial = grid_fields(place[None].astype(jnp.int32), gathered, cycle_x, cycle_y)
    received = lax.all_to_all(partial, ("dx", "dy"), split_axis=0, concat_axis=0, tiled=True)
    short = edge_forces(
        lists, feat, pos, mid, up, down, w_self, w_pair, w_radial, w_expand,
        w_contract, w_final,
    )
    field = jnp.sum(received, axis=0)
    total = short + charge_cell[:1] * field
    live = lax.broadcasted_iota(jnp.int32, (1, feat.shape[0]), 1) < atom_count[0, 0]
    return jnp.where(live, total, jnp.zeros_like(total))[None, None]


def solution(mesh):
    placed = (
        P("dx", "dy", None, None),
        P("dx", "dy", None, None),
        P("dx", "dy"),
        P("dx", "dy", None),
        P("dx", "dy", None, None),
        P("dx", "dy", None),
    ) + (P(),) * 7
    return jax.shard_map(
        shards, mesh=mesh, in_specs=placed, out_specs=P("dx", "dy", None, None), check_vma=False
    )
```

```python
import functools
import math

import jax
import jax.numpy as jnp
import numpy as np
from jax import lax
from jax.experimental import pallas as pl
from jax.experimental.pallas import tpu as pltpu
from jax.sharding import PartitionSpec as P

GRID_X = 8
GRID_Y = 8
GRID_Z = 1024
BOX = 1.0
CUTOFF_SQ = 6.25
SMEARING = 1.0

LANES = 128
EXTRA = 16
ROWS = 32
CHUNK_ATOMS = 16
PIECES = 4
HIGHEST = lax.Precision.HIGHEST
F32 = jnp.float32
BF16 = jnp.bfloat16


def contract_first(a, b, precision=None):
    return lax.dot_general(
        a, b, (((0,), (0,)), ((), ())), precision=precision, preferred_element_type=F32
    )


def contract_last(a, b, precision=None):
    return lax.dot_general(
        a, b, (((1,), (1,)), ((), ())), precision=precision, preferred_element_type=F32
    )


def prepare_kernel(count_ref, feat_ref, pos_ref, export_ref, cell_ref, wq_ref, out_ref, qc_ref):
    atoms = feat_ref.shape[0]
    ghosts = export_ref.shape[1]
    pick = lax.broadcasted_iota(jnp.int32, (atoms, ghosts), 0) == export_ref[...]
    pick = jnp.where(pick, 1.0, 0.0).astype(BF16)
    out_ref[pl.ds(0, ghosts), :] = contract_first(pick, feat_ref[...]).astype(BF16)
    pos = jnp.concatenate([pos_ref[...].astype(F32), jnp.zeros((13, atoms), F32)], axis=0)
    coords = jnp.dot(pos.astype(BF16), pick, preferred_element_type=F32)
    tail = [coords[:8, h * LANES : (h + 1) * LANES] for h in range(ghosts // LANES)]
    out_ref[pl.ds(ghosts, EXTRA), :] = jnp.concatenate(tail, axis=0).astype(BF16)
    weights = jnp.broadcast_to(wq_ref[...].astype(F32), (16, LANES)).astype(BF16)
    charge = contract_last(weights, feat_ref[...])[:1]
    live = lax.broadcasted_iota(jnp.int32, (1, atoms), 1) < count_ref[0, 0]
    qc_ref[...] = jnp.concatenate(
        [jnp.where(live, charge, 0.0), cell_ref[...].astype(F32)], axis=0
    )


def prepare(count, feat, pos, exports, cells, w_charge):
    atoms, ghosts = (feat.shape[0], exports.shape[0])
    vmem = pl.BlockSpec(memory_space=pltpu.VMEM)
    return pl.pallas_call(
        prepare_kernel,
        in_specs=[pl.BlockSpec(memory_space=pltpu.SMEM)] + [vmem] * 5,
        out_specs=[vmem, vmem],
        out_shape=[
            jax.ShapeDtypeStruct((ghosts + EXTRA, feat.shape[1]), BF16),
            jax.ShapeDtypeStruct((2, atoms), F32),
        ],
        name="prepare",
    )(count, feat, pos, exports[None], cells[None], w_charge[None])


def real_tables(count):
    half = count // 2
    index = np.arange(count)
    freq = np.where(index <= half, index, index - half)
    place = np.arange(count)
    angle = 2.0 * np.pi * (freq[:, None] * place[None, :] % count) / count
    is_cos = (index <= half)[:, None]
    basis = np.where(is_cos, np.cos(angle), np.sin(angle))
    weight = np.where((index == 0) | (index == half), 1.0, 2.0)[:, None] / count
    wave = np.where(index == half, 0.0, 2.0 * np.pi * freq / count)[:, None]
    slope = np.where(is_cos, np.sin(angle), -np.cos(angle)) * wave
    return (basis, (weight * basis).T, (weight * slope).T)


def block_table(table, copies):
    return np.kron(np.eye(copies), table).astype(np.float32)


def sine_half(t):
    x = t * (math.pi / 512.0)
    s = x * x
    p = -2.50521084e-08
    p = p * s + 2.75573192e-06
    p = p * s - 1.98412698e-04
    p = p * s + 8.33333333e-03
    p = p * s - 1.66666667e-01
    return x + x * (s * p)


def grid_kernel(
    cycle_x, cycle_y, place_ref, qc_ref, fy_table, fx_table, ix_table, iy_table, dy_table, out_ref,
    buf_a, buf_b, buf_c, buf_d, buf_e, trig_ref, fy_ref, fx_ref, ix_ref, iy_ref, dy_ref,
):
    tables = (fy_table, fx_table, ix_table, iy_table, dy_table)
    for whole, halves in zip(tables, (fy_ref, fx_ref, ix_ref, iy_ref, dy_ref)):
        high = whole[...].astype(BF16)
        halves[:, : whole.shape[1]] = high
        halves[:, whole.shape[1] :] = (whole[...] - high.astype(F32)).astype(BF16)
    mesh_x, mesh_y, mesh_z = (GRID_X * cycle_x, GRID_Y * cycle_y, GRID_Z)
    devices = cycle_x * cycle_y
    modes = mesh_z // 2 // devices
    coefs = 2 * modes
    first = place_ref[0] * modes
    columns = GRID_X * GRID_Y
    group_y = max(1, 256 // mesh_y)
    group_x = max(1, 256 // mesh_x)
    atoms = qc_ref.shape[2]

    row = lax.broadcasted_iota(jnp.int32, (ROWS, 1), 0) % coefs
    row_mode = first + row % modes
    row_sine = row >= modes
    row_edge = row_sine & (row_mode == 0)
    row_factor = jnp.where(row_edge, mesh_z // 2, row_mode)
    row_shift = jnp.where(row_sine & (row_mode != 0), mesh_z // 4, 0)
    column_iota = lax.broadcasted_iota(jnp.int32, (columns, atoms), 0)

    def columns_of(device):
        cell = qc_ref[device, 1:2, :].astype(jnp.int32)
        return cell, column_iota == lax.shift_right_logical(cell, 10)

    def spread(device, carry):
        cell, match = columns_of(device)
        depth = cell & (mesh_z - 1)
        turn = (row_factor * depth - row_shift) & (mesh_z - 1)
        trig = sine_half((jnp.abs(turn - mesh_z // 2) - mesh_z // 4).astype(F32))
        high = trig.astype(BF16)
        trig_ref[device, pl.ds(0, ROWS), :] = high
        trig_ref[device, pl.ds(ROWS, ROWS), :] = (trig - high.astype(F32)).astype(BF16)
        charged = trig * qc_ref[device, 0:1, :]
        high = charged.astype(BF16)
        low = (charged - high.astype(F32)).astype(BF16)
        pick = jnp.where(match, 1.0, 0.0).astype(BF16)
        total = contract_last(pick, jnp.concatenate([high, low] * (LANES // ROWS // 2), axis=0))
        total = total + pltpu.roll(total, ROWS, 1)
        buf_a[pl.ds(pl.multiple_of(device * columns, 8), columns), :] = total
        return carry

    lax.fori_loop(0, devices, spread, 0, unroll=4)

    lane = lax.broadcasted_iota(jnp.int32, (1, LANES), 1)
    low_half = lane >= LANES // 2

    def apply(table_ref, data):
        high = data.astype(BF16).astype(F32)
        mixed = jnp.where(low_half, data - high, high).astype(BF16)
        both = jnp.concatenate([mixed, mixed], axis=0)
        result = jnp.dot(table_ref[...], both, preferred_element_type=F32)
        return result + pltpu.roll(result, LANES // 2, 1)

    def forward_y(step, carry):
        parts = []
        for i in range(group_y):
            place = step * group_y + i
            for sy in range(cycle_y):
                start = ((place // GRID_X) * cycle_y + sy) * columns + (place % GRID_X) * GRID_Y
                parts.append(buf_a[pl.ds(pl.multiple_of(start, 8), GRID_Y), :])
        size = group_y * mesh_y
        start = pl.multiple_of(step * size, 8)
        buf_b[pl.ds(start, size), :] = apply(fy_ref, jnp.concatenate(parts, axis=0))
        return carry

    lax.fori_loop(0, mesh_x // group_y, forward_y, 0, unroll=2)

    size_x = group_x * mesh_x
    lane_coef = lane % coefs
    lane_mode = first + lane_coef % modes
    lane_sine = lane_coef >= modes
    lane_freq = jnp.where(lane_sine & (lane_mode == 0), mesh_z // 2, lane_mode)
    wave_z = lane_freq.astype(F32) * (2.0 * math.pi / mesh_z)
    lane_weight = jnp.where(lane_mode == 0, 1.0, 2.0) / mesh_z
    slope_z = jnp.where(lane_mode == 0, 0.0, wave_z) * jnp.where(lane_sine, 1.0, -1.0)
    index_x = lax.broadcasted_iota(jnp.int32, (size_x, 1), 0)
    freq_x = index_x % mesh_x
    freq_x = jnp.where(freq_x <= mesh_x // 2, freq_x, freq_x - mesh_x // 2)
    wave_x = freq_x.astype(F32) * (2.0 * math.pi / mesh_x)
    near = wave_x * wave_x + wave_z * wave_z

    def middle(step, carry):
        parts = []
        for i in range(group_x):
            parts.append(buf_b[pl.ds(step * group_x + i, mesh_x, stride=mesh_y), :])
        spectrum = apply(fx_ref, jnp.concatenate(parts, axis=0))
        freq_y = step * group_x + index_x // mesh_x
        freq_y = jnp.where(freq_y <= mesh_y // 2, freq_y, freq_y - mesh_y // 2)
        wave_y = freq_y.astype(F32) * (2.0 * math.pi / mesh_y)
        wave_sq = near + wave_y * wave_y
        zero = wave_sq == 0.0
        green = jnp.exp(-0.5 * SMEARING * SMEARING * wave_sq) / jnp.where(zero, 1.0, wave_sq)
        green = jnp.where(zero, 0.0, 4.0 * math.pi * green)
        both = apply(ix_ref, spectrum * (green * lane_weight))
        start = pl.multiple_of(step * size_x, 8)
        buf_a[pl.ds(start, size_x), :] = both[:size_x]
        buf_c[pl.ds(start, size_x), :] = both[size_x:]
        return carry

    lax.fori_loop(0, mesh_y // group_x, middle, 0, unroll=2)

    def backward_y(step, carry):
        plain, sloped = ([], [])
        for i in range(group_y):
            place = step * group_y + i
            plain.append(buf_a[pl.ds(place, mesh_y, stride=mesh_x), :])
            sloped.append(buf_c[pl.ds(place, mesh_y, stride=mesh_x), :])
        plain = jnp.concatenate(plain, axis=0)
        size = group_y * mesh_y
        start = pl.multiple_of(step * size, 8)
        potential = apply(iy_ref, plain)
        buf_b[pl.ds(start, size), :] = apply(iy_ref, jnp.concatenate(sloped, axis=0))
        buf_d[pl.ds(start, size), :] = apply(dy_ref, plain)
        buf_e[pl.ds(start, size), :] = pltpu.roll(potential, modes, 1) * slope_z
        return carry

    lax.fori_loop(0, mesh_x // group_y, backward_y, 0, unroll=2)

    use_low = (lane // ROWS) == 1
    use_none = (lane % ROWS) >= coefs

    def sample(device, carry):
        _, match = columns_of(device)
        rows = []
        for buf in (buf_b, buf_d, buf_e):
            for lx in range(GRID_X):
                place = (device // cycle_y) * GRID_X + lx
                start = place * mesh_y + (device % cycle_y) * GRID_Y
                rows.append(buf[pl.ds(pl.multiple_of(start, 8), GRID_Y), :])
        data = jnp.concatenate(rows, axis=0)
        high = data.astype(BF16).astype(F32)
        mixed = jnp.where(use_low, data - high, high)
        mixed = jnp.where(use_none, 0.0, mixed).astype(BF16)
        high = trig_ref[device, pl.ds(0, ROWS), :]
        low = trig_ref[device, pl.ds(ROWS, ROWS), :]
        waves = jnp.concatenate([high, high, low, jnp.zeros_like(low)], axis=0)
        fields = jnp.dot(mixed, waves, preferred_element_type=F32)
        picked = []
        for a in range(3):
            part = jnp.where(match, fields[a * columns : (a + 1) * columns], 0.0)
            picked.append(jnp.sum(part, axis=0, keepdims=True))
        out_ref[device] = jnp.concatenate(picked, axis=0)
        return carry

    lax.fori_loop(0, devices, sample, 0, unroll=4)


def grid_fields(place, gathered, cycle_x, cycle_y):
    mesh_x, mesh_y = (GRID_X * cycle_x, GRID_Y * cycle_y)
    devices, _, atoms = gathered.shape
    group_y = max(1, 256 // mesh_y)
    group_x = max(1, 256 // mesh_x)
    ax, bx, cx = real_tables(mesh_x)
    ay, by, cy = real_tables(mesh_y)
    tables = [
        block_table(ay, group_y),
        block_table(ax, group_x),
        np.concatenate([block_table(bx, group_x), block_table(cx, group_x)], axis=0),
        block_table(by, group_y),
        block_table(cy, group_y),
    ]
    plane = pltpu.VMEM((mesh_x * mesh_y, LANES), F32)
    vmem = pl.BlockSpec(memory_space=pltpu.VMEM)
    return pl.pallas_call(
        functools.partial(grid_kernel, cycle_x, cycle_y),
        in_specs=[pl.BlockSpec(memory_space=pltpu.SMEM)] + [vmem] * 6,
        out_specs=vmem,
        out_shape=jax.ShapeDtypeStruct((devices, 3, atoms), F32),
        scratch_shapes=[plane] * 5
        + [pltpu.VMEM((devices, 2 * ROWS, atoms), BF16)]
        + [pltpu.VMEM((t.shape[0], 2 * t.shape[1]), BF16) for t in tables],
        compiler_params=pltpu.CompilerParams(vmem_limit_bytes=60 << 20),
        cost_estimate=pl.CostEstimate(
            flops=8_000_000_000, bytes_accessed=4_000_000, transcendentals=100_000
        ),
        name="grid_fields",
    )(place, gathered, *[jnp.asarray(t) for t in tables])


def edge_kernel(
    list_ref, index_ref, feat_ref, pos_ref, mid_ref, up_ref, down_ref, w_self_ref, w_pair_ref,
    w_radial_ref, w_expand_ref, w_contract_ref, w_final_ref, out_ref,
    table, places, near_a, near_b, near_c, edge_a, edge_b, edge_c, marks, own_ref, sums_ref, w_half,
):
    atoms, channels = feat_ref.shape
    ghosts = mid_ref.shape[1] - EXTRA
    slots_all = atoms + 9 * ghosts
    per_atom = index_ref.shape[0]
    chunk = CHUNK_ATOMS * per_atom
    chunks = atoms // CHUNK_ATOMS
    basis_count = w_radial_ref.shape[0]
    spacing = CUTOFF_SQ / (basis_count - 1)
    latent = w_expand_ref.shape[1]
    width = latent // PIECES
    slots = per_atom // PIECES
    w_half[...] = w_expand_ref[...] * 0.5

    def fill(start, rows, coords, shift):
        count = rows.shape[0]
        projected = jnp.dot(rows, w_pair_ref[...], preferred_element_type=F32)
        projected = projected.astype(BF16).astype(F32)
        table[pl.ds(start, count), :] = projected[:, :channels] * 0.5
        table[pl.ds(slots_all + start, count), :] = projected[:, channels:]
        row = lax.broadcasted_iota(jnp.int32, (8, LANES), 0)
        offset = jnp.where(row == 0, shift[0], jnp.where(row == 1, shift[1], 0.0))
        places[start // LANES] = coords + offset

    pos = jnp.concatenate([pos_ref[...].astype(F32), jnp.zeros((5, atoms), F32)], axis=0)
    for i in range(atoms // LANES):
        rows = feat_ref[pl.ds(i * LANES, LANES), :]
        fill(i * LANES, rows, pos[:, i * LANES : (i + 1) * LANES], (0.0, 0.0))
        own = jnp.dot(rows, w_self_ref[...], preferred_element_type=F32)
        own_ref[pl.ds(i * LANES, LANES), :] = own * 0.5
    for sx in range(3):
        for sy, ref in enumerate((up_ref, mid_ref, down_ref)):
            block = 3 * sx + sy
            if block == 4:
                continue
            tail = ref[sx, pl.ds(ghosts, EXTRA), :].astype(F32)
            for h in range(ghosts // LANES):
                rows = ref[sx, pl.ds(h * LANES, LANES), :]
                start = atoms + block * ghosts + h * LANES
                fill(start, rows, tail[h * 8 : (h + 1) * 8], ((sx - 1) * BOX, (sy - 1) * BOX))

    feature = lax.broadcasted_iota(jnp.int32, (8, LANES), 0)
    skipped = range((atoms + 4 * ghosts) // LANES, (atoms + 5 * ghosts) // LANES)
    for i in range(atoms // LANES):
        columns = slice(i * LANES, (i + 1) * LANES)
        index = index_ref[:, columns]
        inside = index & (LANES - 1)
        outside = lax.shift_right_logical(index, 7)
        found = [jnp.zeros((per_atom, LANES), F32)] * 3
        for c in range(slots_all // LANES):
            if c in skipped:
                continue
            tile = places[c]
            here = outside == c
            for a in range(3):
                source = jnp.broadcast_to(tile[a : a + 1], (per_atom, LANES))
                value = jnp.take_along_axis(source, inside, axis=1)
                found[a] = jnp.where(here, value, found[a])
        disp = [found[a] - pos[a : a + 1, columns] for a in range(3)]
        d2 = disp[0] * disp[0] + disp[1] * disp[1] + disp[2] * disp[2]
        envelope = jnp.maximum(0.0, 1.0 - d2 * (1.0 / CUTOFF_SQ))
        envelope = envelope * envelope
        moments = [envelope] + [envelope * disp[a] for a in range(3)]
        for k in range(per_atom):
            def wide(value):
                return jnp.broadcast_to(value[k : k + 1], (8, LANES))

            t = wide(d2) * (1.0 / spacing) - feature.astype(F32)
            basis = jnp.exp(-(t * t))
            high = basis.astype(BF16).astype(F32)
            tail = jnp.where(feature == 0, wide(moments[0]), 0.0)
            for a in range(3):
                tail = jnp.where(feature == 1 + a, wide(moments[1 + a]), tail)
            stacked = jnp.concatenate([high, basis - high, high, tail], axis=0)
            marks[k, pl.ds(i * LANES, LANES), :] = stacked.T

    w_radial = w_radial_ref[...] * 0.5
    high = w_radial.astype(BF16).astype(F32)
    w_basis = jnp.concatenate(
        [high, high, w_radial - high, jnp.zeros((8, channels), F32)], axis=0
    ).astype(BF16)

    def gather(index, near, part):
        for k in range(part * slots, (part + 1) * slots):
            for a in range(CHUNK_ATOMS):
                j = list_ref[k * atoms + index * CHUNK_ATOMS + a]
                e = k * CHUNK_ATOMS + a
                near[pl.ds(e, 2, stride=chunk), :] = table[pl.ds(j, 2, stride=slots_all), :]

    def enter(index, near, edge_in, part):
        first = pl.multiple_of(index * CHUNK_ATOMS, 8)
        rows = pl.ds(part * slots * CHUNK_ATOMS, slots * CHUNK_ATOMS)
        shape = (slots, CHUNK_ATOMS, LANES)
        basis = marks[pl.ds(part * slots, slots), pl.ds(first, CHUNK_ATOMS), :]
        basis = basis.reshape(slots * CHUNK_ATOMS, basis.shape[2]).astype(BF16)
        radial = jnp.dot(basis, w_basis, preferred_element_type=F32).reshape(shape)
        own = own_ref[pl.ds(first, CHUNK_ATOMS), :][None]
        half = radial + own + near[rows, :].reshape(shape)
        turn = jnp.tanh(half.astype(BF16)).astype(F32)
        edge_in[rows, :] = (half + half * turn).astype(BF16).reshape(-1, LANES)

    def network(edge_in, part):
        cols = pl.ds(part * width, width)
        half = jnp.dot(edge_in[...], w_half[:, cols], preferred_element_type=F32).astype(BF16)
        hidden = half + half * jnp.tanh(half)
        return jnp.dot(hidden, w_contract_ref[cols, :], preferred_element_type=F32)

    def collect(index, mixed, near):
        first = pl.multiple_of(index * CHUNK_ATOMS, 8)
        weight = (mixed * near[pl.ds(chunk, chunk), :]).reshape(per_atom, CHUNK_ATOMS, LANES)
        for s in range(4):
            mark = marks[:, pl.ds(first, CHUNK_ATOMS), 3 * basis_count + s : 3 * basis_count + s + 1]
            sums_ref[s, pl.ds(first, CHUNK_ATOMS), :] = jnp.sum(weight * mark, axis=0)

    def stage(index, nears, edges):
        after = jnp.minimum(index + 1, chunks - 1)
        later = jnp.minimum(index + 2, chunks - 1)
        mixed = None
        for part in range(PIECES):
            gather(later, nears[2], part)
            enter(after, nears[1], edges[1], part)
            term = network(edges[0], part)
            mixed = term if mixed is None else mixed + term
        collect(index, mixed, nears[0])

    nears = (near_a, near_b, near_c)
    edges = (edge_a, edge_b, edge_c)
    for part in range(PIECES):
        gather(0, near_a, part)
    for part in range(PIECES):
        gather(1, near_b, part)
        enter(0, near_a, edge_a, part)

    def triple(step, carry):
        for i in range(3):
            order = (i, (i + 1) % 3, (i + 2) % 3)
            stage(3 * step + i, [nears[o] for o in order], [edges[o] for o in order])
        return carry

    lax.fori_loop(0, chunks // 3, triple, 0)

    scale = 1.0 / math.sqrt(per_atom)
    vector = [sums_ref[1 + a] * scale for a in range(3)]
    square = vector[0] * vector[0] + vector[1] * vector[1] + vector[2] * vector[2]
    invariant = (sums_ref[0] * scale + square * (1.0 / 3.0)).astype(BF16)
    gate = jnp.dot(invariant, w_final_ref[...], preferred_element_type=F32)
    gate = gate * (0.5 + 0.5 * jnp.tanh(0.5 * gate)) * (1.0 / math.sqrt(channels))
    ones = jnp.ones((8, channels), F32)
    short = [contract_last(ones, vector[a] * gate, HIGHEST)[:1] for a in range(3)]
    out_ref[...] = jnp.concatenate(short, axis=0)


def edge_forces(index, feat, pos, mid, up, down, w_self, w_pair, w_radial, w_expand, w_contract, w_final):
    atoms, channels = feat.shape
    per_atom = index.shape[0]
    ghosts = mid.shape[1] - EXTRA
    slots_all = atoms + 9 * ghosts
    chunk = CHUNK_ATOMS * per_atom
    vmem = pl.BlockSpec(memory_space=pltpu.VMEM)
    edges = atoms * per_atom
    latent = w_expand.shape[1]
    return pl.pallas_call(
        edge_kernel,
        in_specs=[pl.BlockSpec(memory_space=pltpu.SMEM)] + [vmem] * 12,
        out_specs=vmem,
        out_shape=jax.ShapeDtypeStruct((3, atoms), F32),
        scratch_shapes=[
            pltpu.VMEM((2 * slots_all, LANES), F32),
            pltpu.VMEM((slots_all // LANES, 8, LANES), F32),
        ]
        + [pltpu.VMEM((2 * chunk, LANES), F32)] * 3
        + [pltpu.VMEM((chunk, LANES), BF16)] * 3
        + [
            pltpu.VMEM((per_atom, atoms, 32), F32),
            pltpu.VMEM((atoms, LANES), F32),
            pltpu.VMEM((4, atoms, LANES), F32),
            pltpu.VMEM(w_expand.shape, BF16),
        ],
        compiler_params=pltpu.CompilerParams(vmem_limit_bytes=56 << 20),
        cost_estimate=pl.CostEstimate(
            flops=4 * edges * channels * latent,
            bytes_accessed=4_000_000,
            transcendentals=edges * latent,
        ),
        name="edge_forces",
    )(
        index.reshape(-1), index, feat, pos, mid, up, down, w_self, w_pair, w_radial,
        w_expand, w_contract, w_final,
    )


def ring(array, axis, step):
    size = lax.axis_size(axis)
    return lax.ppermute(array, axis, [(i, (i + step) % size) for i in range(size)])


def shards(
    features, positions, atom_count, ghost_index, neighbour_list, cell_index, w_self, w_pair,
    w_radial, w_expand, w_contract, w_final, w_charge,
):
    feat = features[0, 0]
    pos = positions[0, 0]
    cycle_x, cycle_y = (lax.axis_size("dx"), lax.axis_size("dy"))
    exported, charge_cell = prepare(
        atom_count, feat, pos, ghost_index[0, 0], cell_index[0, 0], w_charge
    )
    spread = jnp.broadcast_to(charge_cell, (cycle_x * cycle_y,) + charge_cell.shape)
    gathered = lax.all_to_all(spread, ("dx", "dy"), split_axis=0, concat_axis=0, tiled=True)
    mid = jnp.stack([ring(exported, "dx", 1), exported, ring(exported, "dx", -1)])
    lists = neighbour_list[0, 0].T
    gathered, mid, lists = lax.optimization_barrier((gathered, mid, lists))
    up = ring(mid, "dy", 1)
    down = ring(mid, "dy", -1)
    place = lax.axis_index("dx") * cycle_y + lax.axis_index("dy")
    partial = grid_fields(place[None].astype(jnp.int32), gathered, cycle_x, cycle_y)
    received = lax.all_to_all(partial, ("dx", "dy"), split_axis=0, concat_axis=0, tiled=True)
    short = edge_forces(
        lists, feat, pos, mid, up, down, w_self, w_pair, w_radial, w_expand,
        w_contract, w_final,
    )
    field = jnp.sum(received, axis=0)
    total = short + charge_cell[:1] * field
    live = lax.broadcasted_iota(jnp.int32, (1, feat.shape[0]), 1) < atom_count[0, 0]
    return jnp.where(live, total, jnp.zeros_like(total))[None, None]


def solution(mesh):
    placed = (
        P("dx", "dy", None, None),
        P("dx", "dy", None, None),
        P("dx", "dy"),
        P("dx", "dy", None),
        P("dx", "dy", None, None),
        P("dx", "dy", None),
    ) + (P(),) * 7
    return jax.shard_map(
        shards, mesh=mesh, in_specs=placed, out_specs=P("dx", "dy", None, None), check_vma=False
    )
```

```python
import functools
import math

import jax
import jax.numpy as jnp
import numpy as np
from jax import lax
from jax.experimental import pallas as pl
from jax.experimental.pallas import tpu as pltpu
from jax.sharding import PartitionSpec as P

GRID_X = 8
GRID_Y = 8
GRID_Z = 1024
BOX = 1.0
CUTOFF_SQ = 6.25
SMEARING = 1.0

LANES = 128
EXTRA = 16
ROWS = 32
CHUNK_ATOMS = 16
PIECES = 4
HIGHEST = lax.Precision.HIGHEST
F32 = jnp.float32
BF16 = jnp.bfloat16


def contract_first(a, b, precision=None):
    return lax.dot_general(
        a, b, (((0,), (0,)), ((), ())), precision=precision, preferred_element_type=F32
    )


def contract_last(a, b, precision=None):
    return lax.dot_general(
        a, b, (((1,), (1,)), ((), ())), precision=precision, preferred_element_type=F32
    )


def prepare_kernel(count_ref, feat_ref, pos_ref, export_ref, cell_ref, wq_ref, out_ref, qc_ref):
    atoms = feat_ref.shape[0]
    ghosts = export_ref.shape[1]
    pick = lax.broadcasted_iota(jnp.int32, (atoms, ghosts), 0) == export_ref[...]
    pick = jnp.where(pick, 1.0, 0.0).astype(BF16)
    out_ref[pl.ds(0, ghosts), :] = contract_first(pick, feat_ref[...]).astype(BF16)
    pos = jnp.concatenate([pos_ref[...].astype(F32), jnp.zeros((13, atoms), F32)], axis=0)
    coords = jnp.dot(pos.astype(BF16), pick, preferred_element_type=F32)
    tail = [coords[:8, h * LANES : (h + 1) * LANES] for h in range(ghosts // LANES)]
    out_ref[pl.ds(ghosts, EXTRA), :] = jnp.concatenate(tail, axis=0).astype(BF16)
    weights = jnp.broadcast_to(wq_ref[...].astype(F32), (16, LANES)).astype(BF16)
    charge = contract_last(weights, feat_ref[...])[:1]
    live = lax.broadcasted_iota(jnp.int32, (1, atoms), 1) < count_ref[0, 0]
    qc_ref[...] = jnp.concatenate(
        [jnp.where(live, charge, 0.0), cell_ref[...].astype(F32)], axis=0
    )


def prepare(count, feat, pos, exports, cells, w_charge):
    atoms, ghosts = (feat.shape[0], exports.shape[0])
    vmem = pl.BlockSpec(memory_space=pltpu.VMEM)
    return pl.pallas_call(
        prepare_kernel,
        in_specs=[pl.BlockSpec(memory_space=pltpu.SMEM)] + [vmem] * 5,
        out_specs=[vmem, vmem],
        out_shape=[
            jax.ShapeDtypeStruct((ghosts + EXTRA, feat.shape[1]), BF16),
            jax.ShapeDtypeStruct((2, atoms), F32),
        ],
        name="prepare",
    )(count, feat, pos, exports[None], cells[None], w_charge[None])


def real_tables(count):
    half = count // 2
    index = np.arange(count)
    freq = np.where(index <= half, index, index - half)
    place = np.arange(count)
    angle = 2.0 * np.pi * (freq[:, None] * place[None, :] % count) / count
    is_cos = (index <= half)[:, None]
    basis = np.where(is_cos, np.cos(angle), np.sin(angle))
    weight = np.where((index == 0) | (index == half), 1.0, 2.0)[:, None] / count
    wave = np.where(index == half, 0.0, 2.0 * np.pi * freq / count)[:, None]
    slope = np.where(is_cos, np.sin(angle), -np.cos(angle)) * wave
    return (basis, (weight * basis).T, (weight * slope).T)


def block_table(table, copies):
    return np.kron(np.eye(copies), table).astype(np.float32)


def sine_half(t):
    x = t * (math.pi / 512.0)
    s = x * x
    p = -2.50521084e-08
    p = p * s + 2.75573192e-06
    p = p * s - 1.98412698e-04
    p = p * s + 8.33333333e-03
    p = p * s - 1.66666667e-01
    return x + x * (s * p)


def grid_kernel(
    cycle_x, cycle_y, place_ref, qc_ref, fy_table, fx_table, ix_table, iy_table, dy_table, out_ref,
    buf_a, buf_b, buf_c, buf_d, buf_e, trig_ref, fy_ref, fx_ref, ix_ref, iy_ref, dy_ref,
):
    tables = (fy_table, fx_table, ix_table, iy_table, dy_table)
    for whole, halves in zip(tables, (fy_ref, fx_ref, ix_ref, iy_ref, dy_ref)):
        high = whole[...].astype(BF16)
        halves[:, : whole.shape[1]] = high
        halves[:, whole.shape[1] :] = (whole[...] - high.astype(F32)).astype(BF16)
    mesh_x, mesh_y, mesh_z = (GRID_X * cycle_x, GRID_Y * cycle_y, GRID_Z)
    devices = cycle_x * cycle_y
    modes = mesh_z // 2 // devices
    coefs = 2 * modes
    first = place_ref[0] * modes
    columns = GRID_X * GRID_Y
    group_y = max(1, 256 // mesh_y)
    group_x = max(1, 256 // mesh_x)
    atoms = qc_ref.shape[2]

    row = lax.broadcasted_iota(jnp.int32, (ROWS, 1), 0) % coefs
    row_mode = first + row % modes
    row_sine = row >= modes
    row_edge = row_sine & (row_mode == 0)
    row_factor = jnp.where(row_edge, mesh_z // 2, row_mode)
    row_shift = jnp.where(row_sine & (row_mode != 0), mesh_z // 4, 0)
    column_iota = lax.broadcasted_iota(jnp.int32, (columns, atoms), 0)

    def columns_of(device):
        cell = qc_ref[device, 1:2, :].astype(jnp.int32)
        return cell, column_iota == lax.shift_right_logical(cell, 10)

    def spread(device, carry):
        cell, match = columns_of(device)
        depth = cell & (mesh_z - 1)
        turn = (row_factor * depth - row_shift) & (mesh_z - 1)
        trig = sine_half((jnp.abs(turn - mesh_z // 2) - mesh_z // 4).astype(F32))
        high = trig.astype(BF16)
        trig_ref[device, pl.ds(0, ROWS), :] = high
        trig_ref[device, pl.ds(ROWS, ROWS), :] = (trig - high.astype(F32)).astype(BF16)
        charged = trig * qc_ref[device, 0:1, :]
        high = charged.astype(BF16)
        low = (charged - high.astype(F32)).astype(BF16)
        pick = jnp.where(match, 1.0, 0.0).astype(BF16)
        total = contract_last(pick, jnp.concatenate([high, low] * (LANES // ROWS // 2), axis=0))
        total = total + pltpu.roll(total, ROWS, 1)
        buf_a[pl.ds(pl.multiple_of(device * columns, 8), columns), :] = total
        return carry

    lax.fori_loop(0, devices, spread, 0, unroll=4)

    lane = lax.broadcasted_iota(jnp.int32, (1, LANES), 1)
    low_half = lane >= LANES // 2

    def apply(table_ref, data):
        high = data.astype(BF16).astype(F32)
        mixed = jnp.where(low_half, data - high, high).astype(BF16)
        both = jnp.concatenate([mixed, mixed], axis=0)
        result = jnp.dot(table_ref[...], both, preferred_element_type=F32)
        return result + pltpu.roll(result, LANES // 2, 1)

    def forward_y(step, carry):
        parts = []
        for i in range(group_y):
            place = step * group_y + i
            for sy in range(cycle_y):
                start = ((place // GRID_X) * cycle_y + sy) * columns + (place % GRID_X) * GRID_Y
                parts.append(buf_a[pl.ds(pl.multiple_of(start, 8), GRID_Y), :])
        size = group_y * mesh_y
        start = pl.multiple_of(step * size, 8)
        buf_b[pl.ds(start, size), :] = apply(fy_ref, jnp.concatenate(parts, axis=0))
        return carry

    lax.fori_loop(0, mesh_x // group_y, forward_y, 0, unroll=2)

    size_x = group_x * mesh_x
    lane_coef = lane % coefs
    lane_mode = first + lane_coef % modes
    lane_sine = lane_coef >= modes
    lane_freq = jnp.where(lane_sine & (lane_mode == 0), mesh_z // 2, lane_mode)
    wave_z = lane_freq.astype(F32) * (2.0 * math.pi / mesh_z)
    lane_weight = jnp.where(lane_mode == 0, 1.0, 2.0) / mesh_z
    slope_z = jnp.where(lane_mode == 0, 0.0, wave_z) * jnp.where(lane_sine, 1.0, -1.0)
    index_x = lax.broadcasted_iota(jnp.int32, (size_x, 1), 0)
    freq_x = index_x % mesh_x
    freq_x = jnp.where(freq_x <= mesh_x // 2, freq_x, freq_x - mesh_x // 2)
    wave_x = freq_x.astype(F32) * (2.0 * math.pi / mesh_x)
    near = wave_x * wave_x + wave_z * wave_z

    def middle(step, carry):
        parts = []
        for i in range(group_x):
            parts.append(buf_b[pl.ds(step * group_x + i, mesh_x, stride=mesh_y), :])
        spectrum = apply(fx_ref, jnp.concatenate(parts, axis=0))
        freq_y = step * group_x + index_x // mesh_x
        freq_y = jnp.where(freq_y <= mesh_y // 2, freq_y, freq_y - mesh_y // 2)
        wave_y = freq_y.astype(F32) * (2.0 * math.pi / mesh_y)
        wave_sq = near + wave_y * wave_y
        zero = wave_sq == 0.0
        green = jnp.exp(-0.5 * SMEARING * SMEARING * wave_sq) / jnp.where(zero, 1.0, wave_sq)
        green = jnp.where(zero, 0.0, 4.0 * math.pi * green)
        both = apply(ix_ref, spectrum * (green * lane_weight))
        start = pl.multiple_of(step * size_x, 8)
        buf_a[pl.ds(start, size_x), :] = both[:size_x]
        buf_c[pl.ds(start, size_x), :] = both[size_x:]
        return carry

    lax.fori_loop(0, mesh_y // group_x, middle, 0, unroll=2)

    def backward_y(step, carry):
        plain, sloped = ([], [])
        for i in range(group_y):
            place = step * group_y + i
            plain.append(buf_a[pl.ds(place, mesh_y, stride=mesh_x), :])
            sloped.append(buf_c[pl.ds(place, mesh_y, stride=mesh_x), :])
        plain = jnp.concatenate(plain, axis=0)
        size = group_y * mesh_y
        start = pl.multiple_of(step * size, 8)
        potential = apply(iy_ref, plain)
        buf_b[pl.ds(start, size), :] = apply(iy_ref, jnp.concatenate(sloped, axis=0))
        buf_d[pl.ds(start, size), :] = apply(dy_ref, plain)
        buf_e[pl.ds(start, size), :] = pltpu.roll(potential, modes, 1) * slope_z
        return carry

    lax.fori_loop(0, mesh_x // group_y, backward_y, 0, unroll=2)

    use_low = (lane // ROWS) == 1
    use_none = (lane % ROWS) >= coefs

    def sample(device, carry):
        _, match = columns_of(device)
        rows = []
        for buf in (buf_b, buf_d, buf_e):
            for lx in range(GRID_X):
                place = (device // cycle_y) * GRID_X + lx
                start = place * mesh_y + (device % cycle_y) * GRID_Y
                rows.append(buf[pl.ds(pl.multiple_of(start, 8), GRID_Y), :])
        data = jnp.concatenate(rows, axis=0)
        high = data.astype(BF16).astype(F32)
        mixed = jnp.where(use_low, data - high, high)
        mixed = jnp.where(use_none, 0.0, mixed).astype(BF16)
        high = trig_ref[device, pl.ds(0, ROWS), :]
        low = trig_ref[device, pl.ds(ROWS, ROWS), :]
        waves = jnp.concatenate([high, high, low, jnp.zeros_like(low)], axis=0)
        fields = jnp.dot(mixed, waves, preferred_element_type=F32)
        picked = []
        for a in range(3):
            part = jnp.where(match, fields[a * columns : (a + 1) * columns], 0.0)
            picked.append(jnp.sum(part, axis=0, keepdims=True))
        out_ref[device] = jnp.concatenate(picked, axis=0)
        return carry

    lax.fori_loop(0, devices, sample, 0, unroll=4)


def grid_fields(place, gathered, cycle_x, cycle_y):
    mesh_x, mesh_y = (GRID_X * cycle_x, GRID_Y * cycle_y)
    devices, _, atoms = gathered.shape
    group_y = max(1, 256 // mesh_y)
    group_x = max(1, 256 // mesh_x)
    ax, bx, cx = real_tables(mesh_x)
    ay, by, cy = real_tables(mesh_y)
    tables = [
        block_table(ay, group_y),
        block_table(ax, group_x),
        np.concatenate([block_table(bx, group_x), block_table(cx, group_x)], axis=0),
        block_table(by, group_y),
        block_table(cy, group_y),
    ]
    plane = pltpu.VMEM((mesh_x * mesh_y, LANES), F32)
    vmem = pl.BlockSpec(memory_space=pltpu.VMEM)
    return pl.pallas_call(
        functools.partial(grid_kernel, cycle_x, cycle_y),
        in_specs=[pl.BlockSpec(memory_space=pltpu.SMEM)] + [vmem] * 6,
        out_specs=vmem,
        out_shape=jax.ShapeDtypeStruct((devices, 3, atoms), F32),
        scratch_shapes=[plane] * 5
        + [pltpu.VMEM((devices, 2 * ROWS, atoms), BF16)]
        + [pltpu.VMEM((t.shape[0], 2 * t.shape[1]), BF16) for t in tables],
        compiler_params=pltpu.CompilerParams(vmem_limit_bytes=60 << 20),
        cost_estimate=pl.CostEstimate(
            flops=8_000_000_000, bytes_accessed=4_000_000, transcendentals=100_000
        ),
        name="grid_fields",
    )(place, gathered, *[jnp.asarray(t) for t in tables])


def edge_kernel(
    list_ref, index_ref, feat_ref, pos_ref, mid_ref, up_ref, down_ref, w_self_ref, w_pair_ref,
    w_radial_ref, w_expand_ref, w_contract_ref, w_final_ref, out_ref,
    table, places, near_a, near_b, near_c, edge_a, edge_b, edge_c, marks, own_ref, sums_ref, w_half,
):
    atoms, channels = feat_ref.shape
    ghosts = mid_ref.shape[1] - EXTRA
    slots_all = atoms + 9 * ghosts
    per_atom = index_ref.shape[0]
    chunk = CHUNK_ATOMS * per_atom
    chunks = atoms // CHUNK_ATOMS
    basis_count = w_radial_ref.shape[0]
    spacing = CUTOFF_SQ / (basis_count - 1)
    latent = w_expand_ref.shape[1]
    width = latent // PIECES
    slots = per_atom // PIECES
    w_half[...] = w_expand_ref[...] * 0.5

    def fill(start, rows, coords, shift):
        count = rows.shape[0]
        projected = jnp.dot(rows, w_pair_ref[...], preferred_element_type=F32)
        projected = projected.astype(BF16).astype(F32)
        table[pl.ds(start, count), :] = projected[:, :channels] * 0.5
        table[pl.ds(slots_all + start, count), :] = projected[:, channels:]
        row = lax.broadcasted_iota(jnp.int32, (8, LANES), 0)
        offset = jnp.where(row == 0, shift[0], jnp.where(row == 1, shift[1], 0.0))
        places[start // LANES] = coords + offset

    pos = jnp.concatenate([pos_ref[...].astype(F32), jnp.zeros((5, atoms), F32)], axis=0)
    for i in range(atoms // LANES):
        rows = feat_ref[pl.ds(i * LANES, LANES), :]
        fill(i * LANES, rows, pos[:, i * LANES : (i + 1) * LANES], (0.0, 0.0))
        own = jnp.dot(rows, w_self_ref[...], preferred_element_type=F32)
        own_ref[pl.ds(i * LANES, LANES), :] = own * 0.5
    for sx in range(3):
        for sy, ref in enumerate((up_ref, mid_ref, down_ref)):
            block = 3 * sx + sy
            if block == 4:
                continue
            tail = ref[sx, pl.ds(ghosts, EXTRA), :].astype(F32)
            for h in range(ghosts // LANES):
                rows = ref[sx, pl.ds(h * LANES, LANES), :]
                start = atoms + block * ghosts + h * LANES
                fill(start, rows, tail[h * 8 : (h + 1) * 8], ((sx - 1) * BOX, (sy - 1) * BOX))

    feature = lax.broadcasted_iota(jnp.int32, (8, LANES), 0)
    skipped = range((atoms + 4 * ghosts) // LANES, (atoms + 5 * ghosts) // LANES)
    for i in range(atoms // LANES):
        columns = slice(i * LANES, (i + 1) * LANES)
        index = index_ref[:, columns]
        inside = index & (LANES - 1)
        outside = lax.shift_right_logical(index, 7)
        found = [jnp.zeros((per_atom, LANES), F32)] * 3
        for c in range(slots_all // LANES):
            if c in skipped:
                continue
            tile = places[c]
            here = outside == c
            for a in range(3):
                source = jnp.broadcast_to(tile[a : a + 1], (per_atom, LANES))
                value = jnp.take_along_axis(source, inside, axis=1)
                found[a] = jnp.where(here, value, found[a])
        disp = [found[a] - pos[a : a + 1, columns] for a in range(3)]
        d2 = disp[0] * disp[0] + disp[1] * disp[1] + disp[2] * disp[2]
        envelope = jnp.maximum(0.0, 1.0 - d2 * (1.0 / CUTOFF_SQ))
        envelope = envelope * envelope
        moments = [envelope] + [envelope * disp[a] for a in range(3)]
        for k in range(per_atom):
            def wide(value):
                return jnp.broadcast_to(value[k : k + 1], (8, LANES))

            t = wide(d2) * (1.0 / spacing) - feature.astype(F32)
            basis = jnp.exp(-(t * t))
            high = basis.astype(BF16).astype(F32)
            tail = jnp.where(feature == 0, wide(moments[0]), 0.0)
            for a in range(3):
                tail = jnp.where(feature == 1 + a, wide(moments[1 + a]), tail)
            stacked = jnp.concatenate([high, basis - high, high, tail], axis=0)
            marks[k, pl.ds(i * LANES, LANES), :] = stacked.T

    w_radial = w_radial_ref[...] * 0.5
    high = w_radial.astype(BF16).astype(F32)
    w_basis = jnp.concatenate(
        [high, high, w_radial - high, jnp.zeros((8, channels), F32)], axis=0
    ).astype(BF16)

    def gather(index, near, part):
        for k in range(part * slots, (part + 1) * slots):
            start = k * atoms + index * CHUNK_ATOMS
            loaded = [
                table[pl.ds(list_ref[start + a], 2, stride=slots_all), :]
                for a in range(CHUNK_ATOMS)
            ]
            for a, pair in enumerate(loaded):
                near[pl.ds(k * CHUNK_ATOMS + a, 2, stride=chunk), :] = pair

    def enter(index, near, edge_in, part):
        first = pl.multiple_of(index * CHUNK_ATOMS, 8)
        rows = pl.ds(part * slots * CHUNK_ATOMS, slots * CHUNK_ATOMS)
        shape = (slots, CHUNK_ATOMS, LANES)
        basis = marks[pl.ds(part * slots, slots), pl.ds(first, CHUNK_ATOMS), :]
        basis = basis.reshape(slots * CHUNK_ATOMS, basis.shape[2]).astype(BF16)
        radial = jnp.dot(basis, w_basis, preferred_element_type=F32).reshape(shape)
        own = own_ref[pl.ds(first, CHUNK_ATOMS), :][None]
        half = radial + own + near[rows, :].reshape(shape)
        turn = jnp.tanh(half.astype(BF16)).astype(F32)
        edge_in[rows, :] = (half + half * turn).astype(BF16).reshape(-1, LANES)

    def network(edge_in, part):
        cols = pl.ds(part * width, width)
        half = jnp.dot(edge_in[...], w_half[:, cols], preferred_element_type=F32).astype(BF16)
        hidden = half + half * jnp.tanh(half)
        return jnp.dot(hidden, w_contract_ref[cols, :], preferred_element_type=F32)

    def collect(index, mixed, near):
        first = pl.multiple_of(index * CHUNK_ATOMS, 8)
        weight = (mixed * near[pl.ds(chunk, chunk), :]).reshape(per_atom, CHUNK_ATOMS, LANES)
        for s in range(4):
            mark = marks[:, pl.ds(first, CHUNK_ATOMS), 3 * basis_count + s : 3 * basis_count + s + 1]
            sums_ref[s, pl.ds(first, CHUNK_ATOMS), :] = jnp.sum(weight * mark, axis=0)

    def stage(index, nears, edges):
        after = jnp.minimum(index + 1, chunks - 1)
        later = jnp.minimum(index + 2, chunks - 1)
        mixed = None
        for part in range(PIECES):
            gather(later, nears[2], part)
            enter(after, nears[1], edges[1], part)
            term = network(edges[0], part)
            mixed = term if mixed is None else mixed + term
        collect(index, mixed, nears[0])

    nears = (near_a, near_b, near_c)
    edges = (edge_a, edge_b, edge_c)
    for part in range(PIECES):
        gather(0, near_a, part)
    for part in range(PIECES):
        gather(1, near_b, part)
        enter(0, near_a, edge_a, part)

    def triple(step, carry):
        for i in range(3):
            order = (i, (i + 1) % 3, (i + 2) % 3)
            stage(3 * step + i, [nears[o] for o in order], [edges[o] for o in order])
        return carry

    lax.fori_loop(0, chunks // 3, triple, 0)

    scale = 1.0 / math.sqrt(per_atom)
    vector = [sums_ref[1 + a] * scale for a in range(3)]
    square = vector[0] * vector[0] + vector[1] * vector[1] + vector[2] * vector[2]
    invariant = (sums_ref[0] * scale + square * (1.0 / 3.0)).astype(BF16)
    gate = jnp.dot(invariant, w_final_ref[...], preferred_element_type=F32)
    gate = gate * (0.5 + 0.5 * jnp.tanh(0.5 * gate)) * (1.0 / math.sqrt(channels))
    ones = jnp.ones((8, channels), F32)
    short = [contract_last(ones, vector[a] * gate, HIGHEST)[:1] for a in range(3)]
    out_ref[...] = jnp.concatenate(short, axis=0)


def edge_forces(index, feat, pos, mid, up, down, w_self, w_pair, w_radial, w_expand, w_contract, w_final):
    atoms, channels = feat.shape
    per_atom = index.shape[0]
    ghosts = mid.shape[1] - EXTRA
    slots_all = atoms + 9 * ghosts
    chunk = CHUNK_ATOMS * per_atom
    vmem = pl.BlockSpec(memory_space=pltpu.VMEM)
    edges = atoms * per_atom
    latent = w_expand.shape[1]
    return pl.pallas_call(
        edge_kernel,
        in_specs=[pl.BlockSpec(memory_space=pltpu.SMEM)] + [vmem] * 12,
        out_specs=vmem,
        out_shape=jax.ShapeDtypeStruct((3, atoms), F32),
        scratch_shapes=[
            pltpu.VMEM((2 * slots_all, LANES), F32),
            pltpu.VMEM((slots_all // LANES, 8, LANES), F32),
        ]
        + [pltpu.VMEM((2 * chunk, LANES), F32)] * 3
        + [pltpu.VMEM((chunk, LANES), BF16)] * 3
        + [
            pltpu.VMEM((per_atom, atoms, 32), F32),
            pltpu.VMEM((atoms, LANES), F32),
            pltpu.VMEM((4, atoms, LANES), F32),
            pltpu.VMEM(w_expand.shape, BF16),
        ],
        compiler_params=pltpu.CompilerParams(vmem_limit_bytes=56 << 20),
        cost_estimate=pl.CostEstimate(
            flops=4 * edges * channels * latent,
            bytes_accessed=4_000_000,
            transcendentals=edges * latent,
        ),
        name="edge_forces",
    )(
        index.reshape(-1), index, feat, pos, mid, up, down, w_self, w_pair, w_radial,
        w_expand, w_contract, w_final,
    )


def ring(array, axis, step):
    size = lax.axis_size(axis)
    return lax.ppermute(array, axis, [(i, (i + step) % size) for i in range(size)])


def shards(
    features, positions, atom_count, ghost_index, neighbour_list, cell_index, w_self, w_pair,
    w_radial, w_expand, w_contract, w_final, w_charge,
):
    feat = features[0, 0]
    pos = positions[0, 0]
    cycle_x, cycle_y = (lax.axis_size("dx"), lax.axis_size("dy"))
    exported, charge_cell = prepare(
        atom_count, feat, pos, ghost_index[0, 0], cell_index[0, 0], w_charge
    )
    spread = jnp.broadcast_to(charge_cell, (cycle_x * cycle_y,) + charge_cell.shape)
    gathered = lax.all_to_all(spread, ("dx", "dy"), split_axis=0, concat_axis=0, tiled=True)
    mid = jnp.stack([ring(exported, "dx", 1), exported, ring(exported, "dx", -1)])
    lists = neighbour_list[0, 0].T
    gathered, mid, lists = lax.optimization_barrier((gathered, mid, lists))
    up = ring(mid, "dy", 1)
    down = ring(mid, "dy", -1)
    place = lax.axis_index("dx") * cycle_y + lax.axis_index("dy")
    partial = grid_fields(place[None].astype(jnp.int32), gathered, cycle_x, cycle_y)
    received = lax.all_to_all(partial, ("dx", "dy"), split_axis=0, concat_axis=0, tiled=True)
    short = edge_forces(
        lists, feat, pos, mid, up, down, w_self, w_pair, w_radial, w_expand,
        w_contract, w_final,
    )
    field = jnp.sum(received, axis=0)
    total = short + charge_cell[:1] * field
    live = lax.broadcasted_iota(jnp.int32, (1, feat.shape[0]), 1) < atom_count[0, 0]
    return jnp.where(live, total, jnp.zeros_like(total))[None, None]


def solution(mesh):
    placed = (
        P("dx", "dy", None, None),
        P("dx", "dy", None, None),
        P("dx", "dy"),
        P("dx", "dy", None),
        P("dx", "dy", None, None),
        P("dx", "dy", None),
    ) + (P(),) * 7
    return jax.shard_map(
        shards, mesh=mesh, in_specs=placed, out_specs=P("dx", "dy", None, None), check_vma=False
    )
```

```python
import functools
import math

import jax
import jax.numpy as jnp
import numpy as np
from jax import lax
from jax.experimental import pallas as pl
from jax.experimental.pallas import tpu as pltpu
from jax.sharding import PartitionSpec as P

GRID_X = 8
GRID_Y = 8
GRID_Z = 1024
BOX = 1.0
CUTOFF_SQ = 6.25
SMEARING = 1.0

LANES = 128
EXTRA = 16
ROWS = 32
CHUNK_ATOMS = 64
PIECES = 4
HIGHEST = lax.Precision.HIGHEST
F32 = jnp.float32
BF16 = jnp.bfloat16


def contract_first(a, b, precision=None):
    return lax.dot_general(
        a, b, (((0,), (0,)), ((), ())), precision=precision, preferred_element_type=F32
    )


def contract_last(a, b, precision=None):
    return lax.dot_general(
        a, b, (((1,), (1,)), ((), ())), precision=precision, preferred_element_type=F32
    )


def prepare_kernel(count_ref, feat_ref, pos_ref, export_ref, cell_ref, wq_ref, out_ref, qc_ref):
    atoms = feat_ref.shape[0]
    ghosts = export_ref.shape[1]
    pick = lax.broadcasted_iota(jnp.int32, (atoms, ghosts), 0) == export_ref[...]
    pick = jnp.where(pick, 1.0, 0.0).astype(BF16)
    out_ref[pl.ds(0, ghosts), :] = contract_first(pick, feat_ref[...]).astype(BF16)
    pos = jnp.concatenate([pos_ref[...].astype(F32), jnp.zeros((13, atoms), F32)], axis=0)
    coords = jnp.dot(pos.astype(BF16), pick, preferred_element_type=F32)
    tail = [coords[:8, h * LANES : (h + 1) * LANES] for h in range(ghosts // LANES)]
    out_ref[pl.ds(ghosts, EXTRA), :] = jnp.concatenate(tail, axis=0).astype(BF16)
    weights = jnp.broadcast_to(wq_ref[...].astype(F32), (16, LANES)).astype(BF16)
    charge = contract_last(weights, feat_ref[...])[:1]
    live = lax.broadcasted_iota(jnp.int32, (1, atoms), 1) < count_ref[0, 0]
    qc_ref[...] = jnp.concatenate(
        [jnp.where(live, charge, 0.0), cell_ref[...].astype(F32)], axis=0
    )


def prepare(count, feat, pos, exports, cells, w_charge):
    atoms, ghosts = (feat.shape[0], exports.shape[0])
    vmem = pl.BlockSpec(memory_space=pltpu.VMEM)
    return pl.pallas_call(
        prepare_kernel,
        in_specs=[pl.BlockSpec(memory_space=pltpu.SMEM)] + [vmem] * 5,
        out_specs=[vmem, vmem],
        out_shape=[
            jax.ShapeDtypeStruct((ghosts + EXTRA, feat.shape[1]), BF16),
            jax.ShapeDtypeStruct((2, atoms), F32),
        ],
        name="prepare",
    )(count, feat, pos, exports[None], cells[None], w_charge[None])


def real_tables(count):
    half = count // 2
    index = np.arange(count)
    freq = np.where(index <= half, index, index - half)
    place = np.arange(count)
    angle = 2.0 * np.pi * (freq[:, None] * place[None, :] % count) / count
    is_cos = (index <= half)[:, None]
    basis = np.where(is_cos, np.cos(angle), np.sin(angle))
    weight = np.where((index == 0) | (index == half), 1.0, 2.0)[:, None] / count
    wave = np.where(index == half, 0.0, 2.0 * np.pi * freq / count)[:, None]
    slope = np.where(is_cos, np.sin(angle), -np.cos(angle)) * wave
    return (basis, (weight * basis).T, (weight * slope).T)


def block_table(table, copies):
    return np.kron(np.eye(copies), table).astype(np.float32)


def sine_half(t):
    x = t * (math.pi / 512.0)
    s = x * x
    p = -2.50521084e-08
    p = p * s + 2.75573192e-06
    p = p * s - 1.98412698e-04
    p = p * s + 8.33333333e-03
    p = p * s - 1.66666667e-01
    return x + x * (s * p)


def grid_kernel(
    cycle_x, cycle_y, place_ref, qc_ref, fy_table, fx_table, ix_table, iy_table, dy_table, out_ref,
    buf_a, buf_b, buf_c, buf_d, buf_e, trig_ref, fy_ref, fx_ref, ix_ref, iy_ref, dy_ref,
):
    tables = (fy_table, fx_table, ix_table, iy_table, dy_table)
    for whole, halves in zip(tables, (fy_ref, fx_ref, ix_ref, iy_ref, dy_ref)):
        high = whole[...].astype(BF16)
        halves[:, : whole.shape[1]] = high
        halves[:, whole.shape[1] :] = (whole[...] - high.astype(F32)).astype(BF16)
    mesh_x, mesh_y, mesh_z = (GRID_X * cycle_x, GRID_Y * cycle_y, GRID_Z)
    devices = cycle_x * cycle_y
    modes = mesh_z // 2 // devices
    coefs = 2 * modes
    first = place_ref[0] * modes
    columns = GRID_X * GRID_Y
    group_y = max(1, 256 // mesh_y)
    group_x = max(1, 256 // mesh_x)
    atoms = qc_ref.shape[2]

    row = lax.broadcasted_iota(jnp.int32, (ROWS, 1), 0) % coefs
    row_mode = first + row % modes
    row_sine = row >= modes
    row_edge = row_sine & (row_mode == 0)
    row_factor = jnp.where(row_edge, mesh_z // 2, row_mode)
    row_shift = jnp.where(row_sine & (row_mode != 0), mesh_z // 4, 0)
    column_iota = lax.broadcasted_iota(jnp.int32, (columns, atoms), 0)

    def columns_of(device):
        cell = qc_ref[device, 1:2, :].astype(jnp.int32)
        return cell, column_iota == lax.shift_right_logical(cell, 10)

    def spread(device, carry):
        cell, match = columns_of(device)
        depth = cell & (mesh_z - 1)
        turn = (row_factor * depth - row_shift) & (mesh_z - 1)
        trig = sine_half((jnp.abs(turn - mesh_z // 2) - mesh_z // 4).astype(F32))
        high = trig.astype(BF16)
        trig_ref[device, pl.ds(0, ROWS), :] = high
        trig_ref[device, pl.ds(ROWS, ROWS), :] = (trig - high.astype(F32)).astype(BF16)
        charged = trig * qc_ref[device, 0:1, :]
        high = charged.astype(BF16)
        low = (charged - high.astype(F32)).astype(BF16)
        pick = jnp.where(match, 1.0, 0.0).astype(BF16)
        total = contract_last(pick, jnp.concatenate([high, low] * (LANES // ROWS // 2), axis=0))
        total = total + pltpu.roll(total, ROWS, 1)
        buf_a[pl.ds(pl.multiple_of(device * columns, 8), columns), :] = total
        return carry

    lax.fori_loop(0, devices, spread, 0, unroll=4)

    lane = lax.broadcasted_iota(jnp.int32, (1, LANES), 1)
    low_half = lane >= LANES // 2

    def apply(table_ref, data):
        high = data.astype(BF16).astype(F32)
        mixed = jnp.where(low_half, data - high, high).astype(BF16)
        both = jnp.concatenate([mixed, mixed], axis=0)
        result = jnp.dot(table_ref[...], both, preferred_element_type=F32)
        return result + pltpu.roll(result, LANES // 2, 1)

    def forward_y(step, carry):
        parts = []
        for i in range(group_y):
            place = step * group_y + i
            for sy in range(cycle_y):
                start = ((place // GRID_X) * cycle_y + sy) * columns + (place % GRID_X) * GRID_Y
                parts.append(buf_a[pl.ds(pl.multiple_of(start, 8), GRID_Y), :])
        size = group_y * mesh_y
        start = pl.multiple_of(step * size, 8)
        buf_b[pl.ds(start, size), :] = apply(fy_ref, jnp.concatenate(parts, axis=0))
        return carry

    lax.fori_loop(0, mesh_x // group_y, forward_y, 0, unroll=2)

    size_x = group_x * mesh_x
    lane_coef = lane % coefs
    lane_mode = first + lane_coef % modes
    lane_sine = lane_coef >= modes
    lane_freq = jnp.where(lane_sine & (lane_mode == 0), mesh_z // 2, lane_mode)
    wave_z = lane_freq.astype(F32) * (2.0 * math.pi / mesh_z)
    lane_weight = jnp.where(lane_mode == 0, 1.0, 2.0) / mesh_z
    slope_z = jnp.where(lane_mode == 0, 0.0, wave_z) * jnp.where(lane_sine, 1.0, -1.0)
    index_x = lax.broadcasted_iota(jnp.int32, (size_x, 1), 0)
    freq_x = index_x % mesh_x
    freq_x = jnp.where(freq_x <= mesh_x // 2, freq_x, freq_x - mesh_x // 2)
    wave_x = freq_x.astype(F32) * (2.0 * math.pi / mesh_x)
    near = wave_x * wave_x + wave_z * wave_z

    def middle(step, carry):
        parts = []
        for i in range(group_x):
            parts.append(buf_b[pl.ds(step * group_x + i, mesh_x, stride=mesh_y), :])
        spectrum = apply(fx_ref, jnp.concatenate(parts, axis=0))
        freq_y = step * group_x + index_x // mesh_x
        freq_y = jnp.where(freq_y <= mesh_y // 2, freq_y, freq_y - mesh_y // 2)
        wave_y = freq_y.astype(F32) * (2.0 * math.pi / mesh_y)
        wave_sq = near + wave_y * wave_y
        zero = wave_sq == 0.0
        green = jnp.exp(-0.5 * SMEARING * SMEARING * wave_sq) / jnp.where(zero, 1.0, wave_sq)
        green = jnp.where(zero, 0.0, 4.0 * math.pi * green)
        both = apply(ix_ref, spectrum * (green * lane_weight))
        start = pl.multiple_of(step * size_x, 8)
        buf_a[pl.ds(start, size_x), :] = both[:size_x]
        buf_c[pl.ds(start, size_x), :] = both[size_x:]
        return carry

    lax.fori_loop(0, mesh_y // group_x, middle, 0, unroll=2)

    def backward_y(step, carry):
        plain, sloped = ([], [])
        for i in range(group_y):
            place = step * group_y + i
            plain.append(buf_a[pl.ds(place, mesh_y, stride=mesh_x), :])
            sloped.append(buf_c[pl.ds(place, mesh_y, stride=mesh_x), :])
        plain = jnp.concatenate(plain, axis=0)
        size = group_y * mesh_y
        start = pl.multiple_of(step * size, 8)
        potential = apply(iy_ref, plain)
        buf_b[pl.ds(start, size), :] = apply(iy_ref, jnp.concatenate(sloped, axis=0))
        buf_d[pl.ds(start, size), :] = apply(dy_ref, plain)
        buf_e[pl.ds(start, size), :] = pltpu.roll(potential, modes, 1) * slope_z
        return carry

    lax.fori_loop(0, mesh_x // group_y, backward_y, 0, unroll=2)

    use_low = (lane // ROWS) == 1
    use_none = (lane % ROWS) >= coefs

    def sample(device, carry):
        _, match = columns_of(device)
        rows = []
        for buf in (buf_b, buf_d, buf_e):
            for lx in range(GRID_X):
                place = (device // cycle_y) * GRID_X + lx
                start = place * mesh_y + (device % cycle_y) * GRID_Y
                rows.append(buf[pl.ds(pl.multiple_of(start, 8), GRID_Y), :])
        data = jnp.concatenate(rows, axis=0)
        high = data.astype(BF16).astype(F32)
        mixed = jnp.where(use_low, data - high, high)
        mixed = jnp.where(use_none, 0.0, mixed).astype(BF16)
        high = trig_ref[device, pl.ds(0, ROWS), :]
        low = trig_ref[device, pl.ds(ROWS, ROWS), :]
        waves = jnp.concatenate([high, high, low, jnp.zeros_like(low)], axis=0)
        fields = jnp.dot(mixed, waves, preferred_element_type=F32)
        picked = []
        for a in range(3):
            part = jnp.where(match, fields[a * columns : (a + 1) * columns], 0.0)
            picked.append(jnp.sum(part, axis=0, keepdims=True))
        out_ref[device] = jnp.concatenate(picked, axis=0)
        return carry

    lax.fori_loop(0, devices, sample, 0, unroll=4)


def grid_fields(place, gathered, cycle_x, cycle_y):
    mesh_x, mesh_y = (GRID_X * cycle_x, GRID_Y * cycle_y)
    devices, _, atoms = gathered.shape
    group_y = max(1, 256 // mesh_y)
    group_x = max(1, 256 // mesh_x)
    ax, bx, cx = real_tables(mesh_x)
    ay, by, cy = real_tables(mesh_y)
    tables = [
        block_table(ay, group_y),
        block_table(ax, group_x),
        np.concatenate([block_table(bx, group_x), block_table(cx, group_x)], axis=0),
        block_table(by, group_y),
        block_table(cy, group_y),
    ]
    plane = pltpu.VMEM((mesh_x * mesh_y, LANES), F32)
    vmem = pl.BlockSpec(memory_space=pltpu.VMEM)
    return pl.pallas_call(
        functools.partial(grid_kernel, cycle_x, cycle_y),
        in_specs=[pl.BlockSpec(memory_space=pltpu.SMEM)] + [vmem] * 6,
        out_specs=vmem,
        out_shape=jax.ShapeDtypeStruct((devices, 3, atoms), F32),
        scratch_shapes=[plane] * 5
        + [pltpu.VMEM((devices, 2 * ROWS, atoms), BF16)]
        + [pltpu.VMEM((t.shape[0], 2 * t.shape[1]), BF16) for t in tables],
        compiler_params=pltpu.CompilerParams(vmem_limit_bytes=60 << 20),
        cost_estimate=pl.CostEstimate(
            flops=8_000_000_000, bytes_accessed=4_000_000, transcendentals=100_000
        ),
        name="grid_fields",
    )(place, gathered, *[jnp.asarray(t) for t in tables])


def edge_kernel(
    list_ref, index_ref, feat_ref, pos_ref, mid_ref, up_ref, down_ref, w_self_ref, w_pair_ref,
    w_radial_ref, w_expand_ref, w_contract_ref, w_final_ref, out_ref,
    table, places, near_a, near_b, near_c, edge_a, edge_b, edge_c,
    total_a, total_b, total_c, marks, own_ref, sums_ref, w_half,
):
    atoms, channels = feat_ref.shape
    ghosts = mid_ref.shape[1] - EXTRA
    slots_all = atoms + 9 * ghosts
    per_atom = index_ref.shape[0]
    chunk = CHUNK_ATOMS * per_atom
    chunks = atoms // CHUNK_ATOMS
    basis_count = w_radial_ref.shape[0]
    spacing = CUTOFF_SQ / (basis_count - 1)
    latent = w_expand_ref.shape[1]
    width = latent // PIECES
    slots = per_atom // PIECES
    w_half[...] = w_expand_ref[...] * 0.5

    def fill(start, rows, coords, shift):
        count = rows.shape[0]
        projected = jnp.dot(rows, w_pair_ref[...], preferred_element_type=F32)
        projected = projected.astype(BF16).astype(F32)
        table[pl.ds(start, count), :] = projected[:, :channels] * 0.5
        table[pl.ds(slots_all + start, count), :] = projected[:, channels:]
        row = lax.broadcasted_iota(jnp.int32, (8, LANES), 0)
        offset = jnp.where(row == 0, shift[0], jnp.where(row == 1, shift[1], 0.0))
        places[start // LANES] = coords + offset

    pos = jnp.concatenate([pos_ref[...].astype(F32), jnp.zeros((5, atoms), F32)], axis=0)
    for i in range(atoms // LANES):
        rows = feat_ref[pl.ds(i * LANES, LANES), :]
        fill(i * LANES, rows, pos[:, i * LANES : (i + 1) * LANES], (0.0, 0.0))
        own = jnp.dot(rows, w_self_ref[...], preferred_element_type=F32)
        own_ref[pl.ds(i * LANES, LANES), :] = own * 0.5
    for sx in range(3):
        for sy, ref in enumerate((up_ref, mid_ref, down_ref)):
            block = 3 * sx + sy
            if block == 4:
                continue
            tail = ref[sx, pl.ds(ghosts, EXTRA), :].astype(F32)
            for h in range(ghosts // LANES):
                rows = ref[sx, pl.ds(h * LANES, LANES), :]
                start = atoms + block * ghosts + h * LANES
                fill(start, rows, tail[h * 8 : (h + 1) * 8], ((sx - 1) * BOX, (sy - 1) * BOX))

    feature = lax.broadcasted_iota(jnp.int32, (8, LANES), 0)
    skipped = range((atoms + 4 * ghosts) // LANES, (atoms + 5 * ghosts) // LANES)
    for i in range(atoms // LANES):
        columns = slice(i * LANES, (i + 1) * LANES)
        index = index_ref[:, columns]
        inside = index & (LANES - 1)
        outside = lax.shift_right_logical(index, 7)
        found = [jnp.zeros((per_atom, LANES), F32)] * 3
        for c in range(slots_all // LANES):
            if c in skipped:
                continue
            tile = places[c]
            here = outside == c
            for a in range(3):
                source = jnp.broadcast_to(tile[a : a + 1], (per_atom, LANES))
                value = jnp.take_along_axis(source, inside, axis=1)
                found[a] = jnp.where(here, value, found[a])
        disp = [found[a] - pos[a : a + 1, columns] for a in range(3)]
        d2 = disp[0] * disp[0] + disp[1] * disp[1] + disp[2] * disp[2]
        envelope = jnp.maximum(0.0, 1.0 - d2 * (1.0 / CUTOFF_SQ))
        envelope = envelope * envelope
        moments = [envelope] + [envelope * disp[a] for a in range(3)]
        for k in range(per_atom):
            def wide(value):
                return jnp.broadcast_to(value[k : k + 1], (8, LANES))

            t = wide(d2) * (1.0 / spacing) - feature.astype(F32)
            basis = jnp.exp(-(t * t))
            high = basis.astype(BF16).astype(F32)
            tail = jnp.where(feature == 0, wide(moments[0]), 0.0)
            for a in range(3):
                tail = jnp.where(feature == 1 + a, wide(moments[1 + a]), tail)
            stacked = jnp.concatenate([high, basis - high, high, tail], axis=0)
            marks[k, pl.ds(i * LANES, LANES), :] = stacked.T

    w_radial = w_radial_ref[...] * 0.5
    high = w_radial.astype(BF16).astype(F32)
    w_basis = jnp.concatenate(
        [high, high, w_radial - high, jnp.zeros((8, channels), F32)], axis=0
    ).astype(BF16)

    part_rows = slots * CHUNK_ATOMS

    def atoms_of(index):
        return pl.ds(pl.multiple_of(index * CHUNK_ATOMS, 8), CHUNK_ATOMS)

    def rows_of(part, offset=0):
        return pl.ds(pl.multiple_of(part * part_rows + offset, 16), part_rows)

    def gather(index, near, part):
        for k in range(slots):
            start = (part * slots + k) * atoms + index * CHUNK_ATOMS
            row = part * part_rows + k * CHUNK_ATOMS
            for group in range(0, CHUNK_ATOMS, 16):
                loaded = [
                    table[pl.ds(list_ref[start + group + a], 2, stride=slots_all), :]
                    for a in range(16)
                ]
                for a, pair in enumerate(loaded):
                    near[pl.ds(row + group + a, 2, stride=chunk), :] = pair

    def enter(index, near, edge_in, part):
        shape = (slots, CHUNK_ATOMS, LANES)
        basis = marks[pl.ds(part * slots, slots), atoms_of(index), :]
        basis = basis.reshape(part_rows, basis.shape[2]).astype(BF16)
        radial = jnp.dot(basis, w_basis, preferred_element_type=F32).reshape(shape)
        half = radial + own_ref[atoms_of(index), :][None] + near[rows_of(part), :].reshape(shape)
        turn = jnp.tanh(half.astype(BF16)).astype(F32)
        edge_in[rows_of(part), :] = (half + half * turn).astype(BF16).reshape(part_rows, LANES)

    def network(edge_in, total, part):
        cols = pl.ds(pl.multiple_of(part * width, width), width)
        half = jnp.dot(edge_in[...], w_half[:, cols], preferred_element_type=F32).astype(BF16)
        hidden = half + half * jnp.tanh(half)
        term = jnp.dot(hidden, w_contract_ref[cols, :], preferred_element_type=F32)
        total[...] = jnp.where(part == 0, 0.0, total[...]) + term

    def collect(index, near, total, part):
        shape = (slots, CHUNK_ATOMS, LANES)
        weight = (total[rows_of(part), :] * near[rows_of(part, chunk), :]).reshape(shape)
        for s in range(4):
            column = 3 * basis_count + s
            mark = marks[pl.ds(part * slots, slots), atoms_of(index), column : column + 1]
            before = jnp.where(part == 0, 0.0, sums_ref[s, atoms_of(index), :])
            sums_ref[s, atoms_of(index), :] = before + jnp.sum(weight * mark, axis=0)

    nears = (near_a, near_b, near_c)
    edges = (edge_a, edge_b, edge_c)
    totals = (total_a, total_b, total_c)

    def start(part, carry):
        gather(0, near_a, part)
        enter(0, near_a, edge_a, part)
        return carry

    lax.fori_loop(0, PIECES, start, 0)

    def triple(step, carry):
        for i in range(3):
            index = 3 * step + i
            ahead = jnp.minimum(index + 1, chunks - 1)
            behind = jnp.maximum(index - 1, 0)
            now, after, before = (i, (i + 1) % 3, (i + 2) % 3)

            def stage(part, inner):
                gather(ahead, nears[after], part)
                network(edges[now], totals[now], part)
                enter(ahead, nears[after], edges[after], part)
                collect(behind, nears[before], totals[before], part)
                return inner

            lax.fori_loop(0, PIECES, stage, 0)
        return carry

    lax.fori_loop(0, chunks // 3, triple, 0)

    def finish(part, carry):
        collect(chunks - 1, near_c, total_c, part)
        return carry

    lax.fori_loop(0, PIECES, finish, 0)

    scale = 1.0 / math.sqrt(per_atom)
    vector = [sums_ref[1 + a] * scale for a in range(3)]
    square = vector[0] * vector[0] + vector[1] * vector[1] + vector[2] * vector[2]
    invariant = (sums_ref[0] * scale + square * (1.0 / 3.0)).astype(BF16)
    gate = jnp.dot(invariant, w_final_ref[...], preferred_element_type=F32)
    gate = gate * (0.5 + 0.5 * jnp.tanh(0.5 * gate)) * (1.0 / math.sqrt(channels))
    ones = jnp.ones((8, channels), F32)
    short = [contract_last(ones, vector[a] * gate, HIGHEST)[:1] for a in range(3)]
    out_ref[...] = jnp.concatenate(short, axis=0)


def edge_forces(index, feat, pos, mid, up, down, w_self, w_pair, w_radial, w_expand, w_contract, w_final):
    atoms, channels = feat.shape
    per_atom = index.shape[0]
    ghosts = mid.shape[1] - EXTRA
    slots_all = atoms + 9 * ghosts
    chunk = CHUNK_ATOMS * per_atom
    vmem = pl.BlockSpec(memory_space=pltpu.VMEM)
    edges = atoms * per_atom
    latent = w_expand.shape[1]
    return pl.pallas_call(
        edge_kernel,
        in_specs=[pl.BlockSpec(memory_space=pltpu.SMEM)] + [vmem] * 12,
        out_specs=vmem,
        out_shape=jax.ShapeDtypeStruct((3, atoms), F32),
        scratch_shapes=[
            pltpu.VMEM((2 * slots_all, LANES), F32),
            pltpu.VMEM((slots_all // LANES, 8, LANES), F32),
        ]
        + [pltpu.VMEM((2 * chunk, LANES), F32)] * 3
        + [pltpu.VMEM((chunk, LANES), BF16)] * 3
        + [pltpu.VMEM((chunk, LANES), F32)] * 3
        + [
            pltpu.VMEM((per_atom, atoms, 32), F32),
            pltpu.VMEM((atoms, LANES), F32),
            pltpu.VMEM((4, atoms, LANES), F32),
            pltpu.VMEM(w_expand.shape, BF16),
        ],
        compiler_params=pltpu.CompilerParams(vmem_limit_bytes=56 << 20),
        cost_estimate=pl.CostEstimate(
            flops=4 * edges * channels * latent,
            bytes_accessed=4_000_000,
            transcendentals=edges * latent,
        ),
        name="edge_forces",
    )(
        index.reshape(-1), index, feat, pos, mid, up, down, w_self, w_pair, w_radial,
        w_expand, w_contract, w_final,
    )


def ring(array, axis, step):
    size = lax.axis_size(axis)
    return lax.ppermute(array, axis, [(i, (i + step) % size) for i in range(size)])


def shards(
    features, positions, atom_count, ghost_index, neighbour_list, cell_index, w_self, w_pair,
    w_radial, w_expand, w_contract, w_final, w_charge,
):
    feat = features[0, 0]
    pos = positions[0, 0]
    cycle_x, cycle_y = (lax.axis_size("dx"), lax.axis_size("dy"))
    exported, charge_cell = prepare(
        atom_count, feat, pos, ghost_index[0, 0], cell_index[0, 0], w_charge
    )
    spread = jnp.broadcast_to(charge_cell, (cycle_x * cycle_y,) + charge_cell.shape)
    gathered = lax.all_to_all(spread, ("dx", "dy"), split_axis=0, concat_axis=0, tiled=True)
    mid = jnp.stack([ring(exported, "dx", 1), exported, ring(exported, "dx", -1)])
    lists = neighbour_list[0, 0].T
    gathered, mid, lists = lax.optimization_barrier((gathered, mid, lists))
    up = ring(mid, "dy", 1)
    down = ring(mid, "dy", -1)
    place = lax.axis_index("dx") * cycle_y + lax.axis_index("dy")
    partial = grid_fields(place[None].astype(jnp.int32), gathered, cycle_x, cycle_y)
    received = lax.all_to_all(partial, ("dx", "dy"), split_axis=0, concat_axis=0, tiled=True)
    short = edge_forces(
        lists, feat, pos, mid, up, down, w_self, w_pair, w_radial, w_expand,
        w_contract, w_final,
    )
    field = jnp.sum(received, axis=0)
    total = short + charge_cell[:1] * field
    live = lax.broadcasted_iota(jnp.int32, (1, feat.shape[0]), 1) < atom_count[0, 0]
    return jnp.where(live, total, jnp.zeros_like(total))[None, None]


def solution(mesh):
    placed = (
        P("dx", "dy", None, None),
        P("dx", "dy", None, None),
        P("dx", "dy"),
        P("dx", "dy", None),
        P("dx", "dy", None, None),
        P("dx", "dy", None),
    ) + (P(),) * 7
    return jax.shard_map(
        shards, mesh=mesh, in_specs=placed, out_specs=P("dx", "dy", None, None), check_vma=False
    )
```

```python
import functools
import math

import jax
import jax.numpy as jnp
import numpy as np
from jax import lax
from jax.experimental import pallas as pl
from jax.experimental.pallas import tpu as pltpu
from jax.sharding import PartitionSpec as P

GRID_X = 8
GRID_Y = 8
GRID_Z = 1024
BOX = 1.0
CUTOFF_SQ = 6.25
SMEARING = 1.0

LANES = 128
EXTRA = 16
ROWS = 32
CHUNK_ATOMS = 16
PIECES = 4
BLOCK_ATOMS = 32
HIGHEST = lax.Precision.HIGHEST
F32 = jnp.float32
BF16 = jnp.bfloat16


def contract_first(a, b, precision=None):
    return lax.dot_general(
        a, b, (((0,), (0,)), ((), ())), precision=precision, preferred_element_type=F32
    )


def contract_last(a, b, precision=None):
    return lax.dot_general(
        a, b, (((1,), (1,)), ((), ())), precision=precision, preferred_element_type=F32
    )


def prepare_kernel(count_ref, feat_ref, pos_ref, export_ref, cell_ref, wq_ref, out_ref, qc_ref):
    atoms = feat_ref.shape[0]
    ghosts = export_ref.shape[1]
    pick = lax.broadcasted_iota(jnp.int32, (atoms, ghosts), 0) == export_ref[...]
    pick = jnp.where(pick, 1.0, 0.0).astype(BF16)
    out_ref[pl.ds(0, ghosts), :] = contract_first(pick, feat_ref[...]).astype(BF16)
    pos = jnp.concatenate([pos_ref[...].astype(F32), jnp.zeros((13, atoms), F32)], axis=0)
    coords = jnp.dot(pos.astype(BF16), pick, preferred_element_type=F32)
    tail = [coords[:8, h * LANES : (h + 1) * LANES] for h in range(ghosts // LANES)]
    out_ref[pl.ds(ghosts, EXTRA), :] = jnp.concatenate(tail, axis=0).astype(BF16)
    weights = jnp.broadcast_to(wq_ref[...].astype(F32), (16, LANES)).astype(BF16)
    charge = contract_last(weights, feat_ref[...])[:1]
    live = lax.broadcasted_iota(jnp.int32, (1, atoms), 1) < count_ref[0, 0]
    qc_ref[...] = jnp.concatenate(
        [jnp.where(live, charge, 0.0), cell_ref[...].astype(F32)], axis=0
    )


def prepare(count, feat, pos, exports, cells, w_charge):
    atoms, ghosts = (feat.shape[0], exports.shape[0])
    vmem = pl.BlockSpec(memory_space=pltpu.VMEM)
    return pl.pallas_call(
        prepare_kernel,
        in_specs=[pl.BlockSpec(memory_space=pltpu.SMEM)] + [vmem] * 5,
        out_specs=[vmem, vmem],
        out_shape=[
            jax.ShapeDtypeStruct((ghosts + EXTRA, feat.shape[1]), BF16),
            jax.ShapeDtypeStruct((2, atoms), F32),
        ],
        name="prepare",
    )(count, feat, pos, exports[None], cells[None], w_charge[None])


def real_tables(count):
    half = count // 2
    index = np.arange(count)
    freq = np.where(index <= half, index, index - half)
    place = np.arange(count)
    angle = 2.0 * np.pi * (freq[:, None] * place[None, :] % count) / count
    is_cos = (index <= half)[:, None]
    basis = np.where(is_cos, np.cos(angle), np.sin(angle))
    weight = np.where((index == 0) | (index == half), 1.0, 2.0)[:, None] / count
    wave = np.where(index == half, 0.0, 2.0 * np.pi * freq / count)[:, None]
    slope = np.where(is_cos, np.sin(angle), -np.cos(angle)) * wave
    return (basis, (weight * basis).T, (weight * slope).T)


def block_table(table, copies):
    return np.kron(np.eye(copies), table).astype(np.float32)


def sine_half(t):
    x = t * (math.pi / 512.0)
    s = x * x
    p = -2.50521084e-08
    p = p * s + 2.75573192e-06
    p = p * s - 1.98412698e-04
    p = p * s + 8.33333333e-03
    p = p * s - 1.66666667e-01
    return x + x * (s * p)


def grid_kernel(
    cycle_x, cycle_y, place_ref, qc_ref, fy_table, fx_table, ix_table, iy_table, dy_table, out_ref,
    buf_a, buf_b, buf_c, buf_d, buf_e, trig_ref, fy_ref, fx_ref, ix_ref, iy_ref, dy_ref,
):
    tables = (fy_table, fx_table, ix_table, iy_table, dy_table)
    for whole, halves in zip(tables, (fy_ref, fx_ref, ix_ref, iy_ref, dy_ref)):
        high = whole[...].astype(BF16)
        halves[:, : whole.shape[1]] = high
        halves[:, whole.shape[1] :] = (whole[...] - high.astype(F32)).astype(BF16)
    mesh_x, mesh_y, mesh_z = (GRID_X * cycle_x, GRID_Y * cycle_y, GRID_Z)
    devices = cycle_x * cycle_y
    modes = mesh_z // 2 // devices
    coefs = 2 * modes
    first = place_ref[0] * modes
    columns = GRID_X * GRID_Y
    group_y = max(1, 256 // mesh_y)
    group_x = max(1, 256 // mesh_x)
    atoms = qc_ref.shape[2]

    row = lax.broadcasted_iota(jnp.int32, (ROWS, 1), 0) % coefs
    row_mode = first + row % modes
    row_sine = row >= modes
    row_edge = row_sine & (row_mode == 0)
    row_factor = jnp.where(row_edge, mesh_z // 2, row_mode)
    row_shift = jnp.where(row_sine & (row_mode != 0), mesh_z // 4, 0)
    column_iota = lax.broadcasted_iota(jnp.int32, (columns, atoms), 0)

    def columns_of(device):
        cell = qc_ref[device, 1:2, :].astype(jnp.int32)
        return cell, column_iota == lax.shift_right_logical(cell, 10)

    def spread(device, carry):
        cell, match = columns_of(device)
        depth = cell & (mesh_z - 1)
        turn = (row_factor * depth - row_shift) & (mesh_z - 1)
        trig = sine_half((jnp.abs(turn - mesh_z // 2) - mesh_z // 4).astype(F32))
        high = trig.astype(BF16)
        trig_ref[device, pl.ds(0, ROWS), :] = high
        trig_ref[device, pl.ds(ROWS, ROWS), :] = (trig - high.astype(F32)).astype(BF16)
        charged = trig * qc_ref[device, 0:1, :]
        high = charged.astype(BF16)
        low = (charged - high.astype(F32)).astype(BF16)
        pick = jnp.where(match, 1.0, 0.0).astype(BF16)
        total = contract_last(pick, jnp.concatenate([high, low] * (LANES // ROWS // 2), axis=0))
        total = total + pltpu.roll(total, ROWS, 1)
        buf_a[pl.ds(pl.multiple_of(device * columns, 8), columns), :] = total
        return carry

    lax.fori_loop(0, devices, spread, 0, unroll=4)

    lane = lax.broadcasted_iota(jnp.int32, (1, LANES), 1)
    low_half = lane >= LANES // 2

    def apply(table_ref, data):
        high = data.astype(BF16).astype(F32)
        mixed = jnp.where(low_half, data - high, high).astype(BF16)
        both = jnp.concatenate([mixed, mixed], axis=0)
        result = jnp.dot(table_ref[...], both, preferred_element_type=F32)
        return result + pltpu.roll(result, LANES // 2, 1)

    def forward_y(step, carry):
        parts = []
        for i in range(group_y):
            place = step * group_y + i
            for sy in range(cycle_y):
                start = ((place // GRID_X) * cycle_y + sy) * columns + (place % GRID_X) * GRID_Y
                parts.append(buf_a[pl.ds(pl.multiple_of(start, 8), GRID_Y), :])
        size = group_y * mesh_y
        start = pl.multiple_of(step * size, 8)
        buf_b[pl.ds(start, size), :] = apply(fy_ref, jnp.concatenate(parts, axis=0))
        return carry

    lax.fori_loop(0, mesh_x // group_y, forward_y, 0, unroll=2)

    size_x = group_x * mesh_x
    lane_coef = lane % coefs
    lane_mode = first + lane_coef % modes
    lane_sine = lane_coef >= modes
    lane_freq = jnp.where(lane_sine & (lane_mode == 0), mesh_z // 2, lane_mode)
    wave_z = lane_freq.astype(F32) * (2.0 * math.pi / mesh_z)
    lane_weight = jnp.where(lane_mode == 0, 1.0, 2.0) / mesh_z
    slope_z = jnp.where(lane_mode == 0, 0.0, wave_z) * jnp.where(lane_sine, 1.0, -1.0)
    index_x = lax.broadcasted_iota(jnp.int32, (size_x, 1), 0)
    freq_x = index_x % mesh_x
    freq_x = jnp.where(freq_x <= mesh_x // 2, freq_x, freq_x - mesh_x // 2)
    wave_x = freq_x.astype(F32) * (2.0 * math.pi / mesh_x)
    near = wave_x * wave_x + wave_z * wave_z

    def middle(step, carry):
        parts = []
        for i in range(group_x):
            parts.append(buf_b[pl.ds(step * group_x + i, mesh_x, stride=mesh_y), :])
        spectrum = apply(fx_ref, jnp.concatenate(parts, axis=0))
        freq_y = step * group_x + index_x // mesh_x
        freq_y = jnp.where(freq_y <= mesh_y // 2, freq_y, freq_y - mesh_y // 2)
        wave_y = freq_y.astype(F32) * (2.0 * math.pi / mesh_y)
        wave_sq = near + wave_y * wave_y
        zero = wave_sq == 0.0
        green = jnp.exp(-0.5 * SMEARING * SMEARING * wave_sq) / jnp.where(zero, 1.0, wave_sq)
        green = jnp.where(zero, 0.0, 4.0 * math.pi * green)
        both = apply(ix_ref, spectrum * (green * lane_weight))
        start = pl.multiple_of(step * size_x, 8)
        buf_a[pl.ds(start, size_x), :] = both[:size_x]
        buf_c[pl.ds(start, size_x), :] = both[size_x:]
        return carry

    lax.fori_loop(0, mesh_y // group_x, middle, 0, unroll=2)

    def backward_y(step, carry):
        plain, sloped = ([], [])
        for i in range(group_y):
            place = step * group_y + i
            plain.append(buf_a[pl.ds(place, mesh_y, stride=mesh_x), :])
            sloped.append(buf_c[pl.ds(place, mesh_y, stride=mesh_x), :])
        plain = jnp.concatenate(plain, axis=0)
        size = group_y * mesh_y
        start = pl.multiple_of(step * size, 8)
        potential = apply(iy_ref, plain)
        buf_b[pl.ds(start, size), :] = apply(iy_ref, jnp.concatenate(sloped, axis=0))
        buf_d[pl.ds(start, size), :] = apply(dy_ref, plain)
        buf_e[pl.ds(start, size), :] = pltpu.roll(potential, modes, 1) * slope_z
        return carry

    lax.fori_loop(0, mesh_x // group_y, backward_y, 0, unroll=2)

    use_low = (lane // ROWS) == 1
    use_none = (lane % ROWS) >= coefs

    def sample(device, carry):
        _, match = columns_of(device)
        rows = []
        for buf in (buf_b, buf_d, buf_e):
            for lx in range(GRID_X):
                place = (device // cycle_y) * GRID_X + lx
                start = place * mesh_y + (device % cycle_y) * GRID_Y
                rows.append(buf[pl.ds(pl.multiple_of(start, 8), GRID_Y), :])
        data = jnp.concatenate(rows, axis=0)
        high = data.astype(BF16).astype(F32)
        mixed = jnp.where(use_low, data - high, high)
        mixed = jnp.where(use_none, 0.0, mixed).astype(BF16)
        high = trig_ref[device, pl.ds(0, ROWS), :]
        low = trig_ref[device, pl.ds(ROWS, ROWS), :]
        waves = jnp.concatenate([high, high, low, jnp.zeros_like(low)], axis=0)
        fields = jnp.dot(mixed, waves, preferred_element_type=F32)
        picked = []
        for a in range(3):
            part = jnp.where(match, fields[a * columns : (a + 1) * columns], 0.0)
            picked.append(jnp.sum(part, axis=0, keepdims=True))
        out_ref[device] = jnp.concatenate(picked, axis=0)
        return carry

    lax.fori_loop(0, devices, sample, 0, unroll=4)


def grid_fields(place, gathered, cycle_x, cycle_y):
    mesh_x, mesh_y = (GRID_X * cycle_x, GRID_Y * cycle_y)
    devices, _, atoms = gathered.shape
    group_y = max(1, 256 // mesh_y)
    group_x = max(1, 256 // mesh_x)
    ax, bx, cx = real_tables(mesh_x)
    ay, by, cy = real_tables(mesh_y)
    tables = [
        block_table(ay, group_y),
        block_table(ax, group_x),
        np.concatenate([block_table(bx, group_x), block_table(cx, group_x)], axis=0),
        block_table(by, group_y),
        block_table(cy, group_y),
    ]
    plane = pltpu.VMEM((mesh_x * mesh_y, LANES), F32)
    vmem = pl.BlockSpec(memory_space=pltpu.VMEM)
    return pl.pallas_call(
        functools.partial(grid_kernel, cycle_x, cycle_y),
        in_specs=[pl.BlockSpec(memory_space=pltpu.SMEM)] + [vmem] * 6,
        out_specs=vmem,
        out_shape=jax.ShapeDtypeStruct((devices, 3, atoms), F32),
        scratch_shapes=[plane] * 5
        + [pltpu.VMEM((devices, 2 * ROWS, atoms), BF16)]
        + [pltpu.VMEM((t.shape[0], 2 * t.shape[1]), BF16) for t in tables],
        compiler_params=pltpu.CompilerParams(vmem_limit_bytes=60 << 20),
        cost_estimate=pl.CostEstimate(
            flops=8_000_000_000, bytes_accessed=4_000_000, transcendentals=100_000
        ),
        name="grid_fields",
    )(place, gathered, *[jnp.asarray(t) for t in tables])


def gather_kernel(
    list_ref, index_ref, feat_ref, pos_ref, mid_ref, up_ref, down_ref, w_self_ref, w_pair_ref,
    w_radial_ref, edge_ref, value_ref, marks_ref, table, places, near_a, near_b, marks, own_ref,
):
    atoms, channels = feat_ref.shape
    ghosts = mid_ref.shape[1] - EXTRA
    slots_all = atoms + 9 * ghosts
    per_atom = index_ref.shape[0]
    chunk = CHUNK_ATOMS * per_atom
    chunks = atoms // CHUNK_ATOMS
    basis_count = w_radial_ref.shape[0]
    spacing = CUTOFF_SQ / (basis_count - 1)

    def fill(start, rows, coords, shift):
        count = rows.shape[0]
        projected = jnp.dot(rows, w_pair_ref[...], preferred_element_type=F32)
        projected = projected.astype(BF16).astype(F32)
        table[pl.ds(start, count), :] = projected[:, :channels] * 0.5
        table[pl.ds(slots_all + start, count), :] = projected[:, channels:]
        row = lax.broadcasted_iota(jnp.int32, (8, LANES), 0)
        offset = jnp.where(row == 0, shift[0], jnp.where(row == 1, shift[1], 0.0))
        places[start // LANES] = coords + offset

    pos = jnp.concatenate([pos_ref[...].astype(F32), jnp.zeros((5, atoms), F32)], axis=0)
    for i in range(atoms // LANES):
        rows = feat_ref[pl.ds(i * LANES, LANES), :]
        fill(i * LANES, rows, pos[:, i * LANES : (i + 1) * LANES], (0.0, 0.0))
        own = jnp.dot(rows, w_self_ref[...], preferred_element_type=F32)
        own_ref[pl.ds(i * LANES, LANES), :] = own * 0.5
    for sx in range(3):
        for sy, ref in enumerate((up_ref, mid_ref, down_ref)):
            block = 3 * sx + sy
            if block == 4:
                continue
            tail = ref[sx, pl.ds(ghosts, EXTRA), :].astype(F32)
            for h in range(ghosts // LANES):
                rows = ref[sx, pl.ds(h * LANES, LANES), :]
                start = atoms + block * ghosts + h * LANES
                fill(start, rows, tail[h * 8 : (h + 1) * 8], ((sx - 1) * BOX, (sy - 1) * BOX))

    feature = lax.broadcasted_iota(jnp.int32, (8, LANES), 0)
    skipped = range((atoms + 4 * ghosts) // LANES, (atoms + 5 * ghosts) // LANES)
    for i in range(atoms // LANES):
        columns = slice(i * LANES, (i + 1) * LANES)
        index = index_ref[:, columns]
        inside = index & (LANES - 1)
        outside = lax.shift_right_logical(index, 7)
        found = [jnp.zeros((per_atom, LANES), F32)] * 3
        for c in range(slots_all // LANES):
            if c in skipped:
                continue
            tile = places[c]
            here = outside == c
            for a in range(3):
                source = jnp.broadcast_to(tile[a : a + 1], (per_atom, LANES))
                value = jnp.take_along_axis(source, inside, axis=1)
                found[a] = jnp.where(here, value, found[a])
        disp = [found[a] - pos[a : a + 1, columns] for a in range(3)]
        d2 = disp[0] * disp[0] + disp[1] * disp[1] + disp[2] * disp[2]
        envelope = jnp.maximum(0.0, 1.0 - d2 * (1.0 / CUTOFF_SQ))
        envelope = envelope * envelope
        moments = [envelope] + [envelope * disp[a] for a in range(3)]
        for k in range(per_atom):
            def wide(value):
                return jnp.broadcast_to(value[k : k + 1], (8, LANES))

            t = wide(d2) * (1.0 / spacing) - feature.astype(F32)
            basis = jnp.exp(-(t * t))
            high = basis.astype(BF16).astype(F32)
            tail = jnp.where(feature == 0, wide(moments[0]), 0.0)
            for a in range(3):
                tail = jnp.where(feature == 1 + a, wide(moments[1 + a]), tail)
            stacked = jnp.concatenate([high, basis - high, high, tail], axis=0)
            marks[k, pl.ds(i * LANES, LANES), :] = stacked.T

    w_radial = w_radial_ref[...] * 0.5
    high = w_radial.astype(BF16).astype(F32)
    w_basis = jnp.concatenate(
        [high, high, w_radial - high, jnp.zeros((8, channels), F32)], axis=0
    ).astype(BF16)

    def gather(index, near):
        for k in range(per_atom):
            start = k * atoms + index * CHUNK_ATOMS
            loaded = [
                table[pl.ds(list_ref[start + a], 2, stride=slots_all), :]
                for a in range(CHUNK_ATOMS)
            ]
            for a, pair in enumerate(loaded):
                near[pl.ds(k * CHUNK_ATOMS + a, 2, stride=chunk), :] = pair

    def enter(index, near):
        first = pl.ds(pl.multiple_of(index * CHUNK_ATOMS, 16), CHUNK_ATOMS)
        shape = (per_atom, CHUNK_ATOMS, LANES)
        basis = marks[:, first, :].reshape(chunk, marks.shape[2]).astype(BF16)
        radial = jnp.dot(basis, w_basis, preferred_element_type=F32).reshape(shape)
        half = radial + own_ref[first, :][None] + near[pl.ds(0, chunk), :].reshape(shape)
        turn = jnp.tanh(half.astype(BF16)).astype(F32)
        edge_ref[:, first, :] = (half + half * turn).astype(BF16)
        value_ref[:, first, :] = near[pl.ds(chunk, chunk), :].reshape(shape).astype(BF16)

    marks_ref[...] = marks[...]
    gather(0, near_a)

    def pair(step, carry):
        gather(2 * step + 1, near_b)
        enter(2 * step, near_a)
        gather(jnp.minimum(2 * step + 2, chunks - 1), near_a)
        enter(2 * step + 1, near_b)
        return carry

    lax.fori_loop(0, chunks // 2, pair, 0)


def network_kernel(
    edge_ref, value_ref, marks_ref, w_expand_ref, w_contract_ref, w_final_ref, out_ref, w_half,
):
    per_atom, atoms, channels = edge_ref.shape
    rows = per_atom * atoms
    shape = (per_atom, atoms, channels)
    latent = w_expand_ref.shape[1]
    width = latent // PIECES

    @pl.when(pl.program_id(0) == 0)
    def _():
        w_half[...] = w_expand_ref[...] * 0.5

    edge_in = edge_ref[...].reshape(rows, channels)
    mixed = None
    for part in range(PIECES):
        cols = pl.ds(part * width, width)
        half = jnp.dot(edge_in, w_half[:, cols], preferred_element_type=F32).astype(BF16)
        hidden = half + half * jnp.tanh(half)
        term = jnp.dot(hidden, w_contract_ref[cols, :], preferred_element_type=F32)
        mixed = term if mixed is None else mixed + term
    weight = mixed.reshape(shape) * value_ref[...].astype(F32)
    first = marks_ref.shape[2] - 8
    sums = [jnp.sum(weight * marks_ref[:, :, first + s : first + s + 1], axis=0) for s in range(4)]

    scale = 1.0 / math.sqrt(per_atom)
    vector = [part * scale for part in sums[1:]]
    square = vector[0] * vector[0] + vector[1] * vector[1] + vector[2] * vector[2]
    invariant = (sums[0] * scale + square * (1.0 / 3.0)).astype(BF16)
    gate = jnp.dot(invariant, w_final_ref[...], preferred_element_type=F32)
    gate = gate * (0.5 + 0.5 * jnp.tanh(0.5 * gate)) * (1.0 / math.sqrt(channels))
    ones = jnp.ones((8, channels), F32)
    short = [contract_last(ones, vector[a] * gate, HIGHEST)[:1] for a in range(3)]
    out_ref[0] = jnp.concatenate(short, axis=0)


def edge_forces(index, feat, pos, mid, up, down, w_self, w_pair, w_radial, w_expand, w_contract, w_final):
    atoms, channels = feat.shape
    per_atom = index.shape[0]
    ghosts = mid.shape[1] - EXTRA
    slots_all = atoms + 9 * ghosts
    chunk = CHUNK_ATOMS * per_atom
    vmem = pl.BlockSpec(memory_space=pltpu.VMEM)
    edges = atoms * per_atom
    latent = w_expand.shape[1]
    blocks = atoms // BLOCK_ATOMS
    edge_in, value, marks = pl.pallas_call(
        gather_kernel,
        in_specs=[pl.BlockSpec(memory_space=pltpu.SMEM)] + [vmem] * 9,
        out_specs=[vmem] * 3,
        out_shape=[
            jax.ShapeDtypeStruct((per_atom, atoms, channels), BF16),
            jax.ShapeDtypeStruct((per_atom, atoms, channels), BF16),
            jax.ShapeDtypeStruct((per_atom, atoms, 32), F32),
        ],
        scratch_shapes=[
            pltpu.VMEM((2 * slots_all, LANES), F32),
            pltpu.VMEM((slots_all // LANES, 8, LANES), F32),
            pltpu.VMEM((2 * chunk, LANES), F32),
            pltpu.VMEM((2 * chunk, LANES), F32),
            pltpu.VMEM((per_atom, atoms, 32), F32),
            pltpu.VMEM((atoms, LANES), F32),
        ],
        compiler_params=pltpu.CompilerParams(vmem_limit_bytes=40 << 20),
        cost_estimate=pl.CostEstimate(
            flops=edges * channels * 64, bytes_accessed=10_000_000, transcendentals=edges * 128
        ),
        name="edge_gather",
    )(index.reshape(-1), index, feat, pos, mid, up, down, w_self, w_pair, w_radial)
    slotted = lambda width: pl.BlockSpec((per_atom, BLOCK_ATOMS, width), lambda i: (0, i, 0))
    whole = lambda a: pl.BlockSpec(a.shape, lambda i: (0, 0))
    short = pl.pallas_call(
        network_kernel,
        grid=(blocks,),
        in_specs=[slotted(channels), slotted(channels), slotted(32)]
        + [whole(w_expand), whole(w_contract), whole(w_final)],
        out_specs=pl.BlockSpec((1, 3, BLOCK_ATOMS), lambda i: (i, 0, 0)),
        out_shape=jax.ShapeDtypeStruct((blocks, 3, BLOCK_ATOMS), F32),
        scratch_shapes=[pltpu.VMEM(w_expand.shape, BF16)],
        compiler_params=pltpu.CompilerParams(vmem_limit_bytes=40 << 20),
        cost_estimate=pl.CostEstimate(
            flops=4 * edges * channels * latent,
            bytes_accessed=10_000_000,
            transcendentals=edges * latent,
        ),
        name="edge_network",
    )(edge_in, value, marks, w_expand, w_contract, w_final)
    return short.transpose(1, 0, 2).reshape(3, atoms)


def ring(array, axis, step):
    size = lax.axis_size(axis)
    return lax.ppermute(array, axis, [(i, (i + step) % size) for i in range(size)])


def shards(
    features, positions, atom_count, ghost_index, neighbour_list, cell_index, w_self, w_pair,
    w_radial, w_expand, w_contract, w_final, w_charge,
):
    feat = features[0, 0]
    pos = positions[0, 0]
    cycle_x, cycle_y = (lax.axis_size("dx"), lax.axis_size("dy"))
    exported, charge_cell = prepare(
        atom_count, feat, pos, ghost_index[0, 0], cell_index[0, 0], w_charge
    )
    spread = jnp.broadcast_to(charge_cell, (cycle_x * cycle_y,) + charge_cell.shape)
    gathered = lax.all_to_all(spread, ("dx", "dy"), split_axis=0, concat_axis=0, tiled=True)
    mid = jnp.stack([ring(exported, "dx", 1), exported, ring(exported, "dx", -1)])
    lists = neighbour_list[0, 0].T
    gathered, mid, lists = lax.optimization_barrier((gathered, mid, lists))
    up = ring(mid, "dy", 1)
    down = ring(mid, "dy", -1)
    place = lax.axis_index("dx") * cycle_y + lax.axis_index("dy")
    partial = grid_fields(place[None].astype(jnp.int32), gathered, cycle_x, cycle_y)
    received = lax.all_to_all(partial, ("dx", "dy"), split_axis=0, concat_axis=0, tiled=True)
    short = edge_forces(
        lists, feat, pos, mid, up, down, w_self, w_pair, w_radial, w_expand,
        w_contract, w_final,
    )
    field = jnp.sum(received, axis=0)
    total = short + charge_cell[:1] * field
    live = lax.broadcasted_iota(jnp.int32, (1, feat.shape[0]), 1) < atom_count[0, 0]
    return jnp.where(live, total, jnp.zeros_like(total))[None, None]


def solution(mesh):
    placed = (
        P("dx", "dy", None, None),
        P("dx", "dy", None, None),
        P("dx", "dy"),
        P("dx", "dy", None),
        P("dx", "dy", None, None),
        P("dx", "dy", None),
    ) + (P(),) * 7
    return jax.shard_map(
        shards, mesh=mesh, in_specs=placed, out_specs=P("dx", "dy", None, None), check_vma=False
    )
```

```python
import functools
import math

import jax
import jax.numpy as jnp
import numpy as np
from jax import lax
from jax.experimental import pallas as pl
from jax.experimental.pallas import tpu as pltpu
from jax.sharding import PartitionSpec as P

GRID_X = 8
GRID_Y = 8
GRID_Z = 1024
BOX = 1.0
CUTOFF_SQ = 6.25
SMEARING = 1.0

LANES = 128
EXTRA = 16
ROWS = 32
CHUNK_ATOMS = 16
PIECES = 4
TILES = 2
HIGHEST = lax.Precision.HIGHEST
F32 = jnp.float32
BF16 = jnp.bfloat16


def contract_first(a, b, precision=None):
    return lax.dot_general(
        a, b, (((0,), (0,)), ((), ())), precision=precision, preferred_element_type=F32
    )


def contract_last(a, b, precision=None):
    return lax.dot_general(
        a, b, (((1,), (1,)), ((), ())), precision=precision, preferred_element_type=F32
    )


def prepare_kernel(count_ref, feat_ref, pos_ref, export_ref, cell_ref, wq_ref, out_ref, qc_ref):
    atoms = feat_ref.shape[0]
    ghosts = export_ref.shape[1]
    pick = lax.broadcasted_iota(jnp.int32, (atoms, ghosts), 0) == export_ref[...]
    pick = jnp.where(pick, 1.0, 0.0).astype(BF16)
    out_ref[pl.ds(0, ghosts), :] = contract_first(pick, feat_ref[...]).astype(BF16)
    pos = jnp.concatenate([pos_ref[...].astype(F32), jnp.zeros((13, atoms), F32)], axis=0)
    coords = jnp.dot(pos.astype(BF16), pick, preferred_element_type=F32)
    tail = [coords[:8, h * LANES : (h + 1) * LANES] for h in range(ghosts // LANES)]
    out_ref[pl.ds(ghosts, EXTRA), :] = jnp.concatenate(tail, axis=0).astype(BF16)
    weights = jnp.broadcast_to(wq_ref[...].astype(F32), (16, LANES)).astype(BF16)
    charge = contract_last(weights, feat_ref[...])[:1]
    live = lax.broadcasted_iota(jnp.int32, (1, atoms), 1) < count_ref[0, 0]
    qc_ref[...] = jnp.concatenate(
        [jnp.where(live, charge, 0.0), cell_ref[...].astype(F32)], axis=0
    )


def prepare(count, feat, pos, exports, cells, w_charge):
    atoms, ghosts = (feat.shape[0], exports.shape[0])
    vmem = pl.BlockSpec(memory_space=pltpu.VMEM)
    return pl.pallas_call(
        prepare_kernel,
        in_specs=[pl.BlockSpec(memory_space=pltpu.SMEM)] + [vmem] * 5,
        out_specs=[vmem, vmem],
        out_shape=[
            jax.ShapeDtypeStruct((ghosts + EXTRA, feat.shape[1]), BF16),
            jax.ShapeDtypeStruct((2, atoms), F32),
        ],
        name="prepare",
    )(count, feat, pos, exports[None], cells[None], w_charge[None])


def real_tables(count):
    half = count // 2
    index = np.arange(count)
    freq = np.where(index <= half, index, index - half)
    place = np.arange(count)
    angle = 2.0 * np.pi * (freq[:, None] * place[None, :] % count) / count
    is_cos = (index <= half)[:, None]
    basis = np.where(is_cos, np.cos(angle), np.sin(angle))
    weight = np.where((index == 0) | (index == half), 1.0, 2.0)[:, None] / count
    wave = np.where(index == half, 0.0, 2.0 * np.pi * freq / count)[:, None]
    slope = np.where(is_cos, np.sin(angle), -np.cos(angle)) * wave
    return (basis, (weight * basis).T, (weight * slope).T)


def block_table(table, copies):
    return np.kron(np.eye(copies), table).astype(np.float32)


def sine_half(t):
    x = t * (math.pi / 512.0)
    s = x * x
    p = -2.50521084e-08
    p = p * s + 2.75573192e-06
    p = p * s - 1.98412698e-04
    p = p * s + 8.33333333e-03
    p = p * s - 1.66666667e-01
    return x + x * (s * p)


def grid_kernel(
    cycle_x, cycle_y, place_ref, qc_ref, fy_table, fx_table, ix_table, iy_table, dy_table, out_ref,
    buf_a, buf_b, buf_c, buf_d, buf_e, trig_ref, fy_ref, fx_ref, ix_ref, iy_ref, dy_ref,
):
    tables = (fy_table, fx_table, ix_table, iy_table, dy_table)
    for whole, halves in zip(tables, (fy_ref, fx_ref, ix_ref, iy_ref, dy_ref)):
        high = whole[...].astype(BF16)
        halves[:, : whole.shape[1]] = high
        halves[:, whole.shape[1] :] = (whole[...] - high.astype(F32)).astype(BF16)
    mesh_x, mesh_y, mesh_z = (GRID_X * cycle_x, GRID_Y * cycle_y, GRID_Z)
    devices = cycle_x * cycle_y
    modes = mesh_z // 2 // devices
    coefs = 2 * modes
    first = place_ref[0] * modes
    columns = GRID_X * GRID_Y
    group_y = max(1, 256 // mesh_y)
    group_x = max(1, 256 // mesh_x)
    atoms = qc_ref.shape[2]

    row = lax.broadcasted_iota(jnp.int32, (ROWS, 1), 0) % coefs
    row_mode = first + row % modes
    row_sine = row >= modes
    row_edge = row_sine & (row_mode == 0)
    row_factor = jnp.where(row_edge, mesh_z // 2, row_mode)
    row_shift = jnp.where(row_sine & (row_mode != 0), mesh_z // 4, 0)
    column_iota = lax.broadcasted_iota(jnp.int32, (columns, atoms), 0)

    def columns_of(device):
        cell = qc_ref[device, 1:2, :].astype(jnp.int32)
        return cell, column_iota == lax.shift_right_logical(cell, 10)

    def spread(device, carry):
        cell, match = columns_of(device)
        depth = cell & (mesh_z - 1)
        turn = (row_factor * depth - row_shift) & (mesh_z - 1)
        trig = sine_half((jnp.abs(turn - mesh_z // 2) - mesh_z // 4).astype(F32))
        high = trig.astype(BF16)
        trig_ref[device, pl.ds(0, ROWS), :] = high
        trig_ref[device, pl.ds(ROWS, ROWS), :] = (trig - high.astype(F32)).astype(BF16)
        charged = trig * qc_ref[device, 0:1, :]
        high = charged.astype(BF16)
        low = (charged - high.astype(F32)).astype(BF16)
        pick = jnp.where(match, 1.0, 0.0).astype(BF16)
        total = contract_last(pick, jnp.concatenate([high, low] * (LANES // ROWS // 2), axis=0))
        total = total + pltpu.roll(total, ROWS, 1)
        buf_a[pl.ds(pl.multiple_of(device * columns, 8), columns), :] = total
        return carry

    lax.fori_loop(0, devices, spread, 0, unroll=4)

    lane = lax.broadcasted_iota(jnp.int32, (1, LANES), 1)
    low_half = lane >= LANES // 2

    def apply(table_ref, data):
        high = data.astype(BF16).astype(F32)
        mixed = jnp.where(low_half, data - high, high).astype(BF16)
        both = jnp.concatenate([mixed, mixed], axis=0)
        result = jnp.dot(table_ref[...], both, preferred_element_type=F32)
        return result + pltpu.roll(result, LANES // 2, 1)

    def forward_y(step, carry):
        parts = []
        for i in range(group_y):
            place = step * group_y + i
            for sy in range(cycle_y):
                start = ((place // GRID_X) * cycle_y + sy) * columns + (place % GRID_X) * GRID_Y
                parts.append(buf_a[pl.ds(pl.multiple_of(start, 8), GRID_Y), :])
        size = group_y * mesh_y
        start = pl.multiple_of(step * size, 8)
        buf_b[pl.ds(start, size), :] = apply(fy_ref, jnp.concatenate(parts, axis=0))
        return carry

    lax.fori_loop(0, mesh_x // group_y, forward_y, 0, unroll=2)

    size_x = group_x * mesh_x
    lane_coef = lane % coefs
    lane_mode = first + lane_coef % modes
    lane_sine = lane_coef >= modes
    lane_freq = jnp.where(lane_sine & (lane_mode == 0), mesh_z // 2, lane_mode)
    wave_z = lane_freq.astype(F32) * (2.0 * math.pi / mesh_z)
    lane_weight = jnp.where(lane_mode == 0, 1.0, 2.0) / mesh_z
    slope_z = jnp.where(lane_mode == 0, 0.0, wave_z) * jnp.where(lane_sine, 1.0, -1.0)
    index_x = lax.broadcasted_iota(jnp.int32, (size_x, 1), 0)
    freq_x = index_x % mesh_x
    freq_x = jnp.where(freq_x <= mesh_x // 2, freq_x, freq_x - mesh_x // 2)
    wave_x = freq_x.astype(F32) * (2.0 * math.pi / mesh_x)
    near = wave_x * wave_x + wave_z * wave_z

    def middle(step, carry):
        parts = []
        for i in range(group_x):
            parts.append(buf_b[pl.ds(step * group_x + i, mesh_x, stride=mesh_y), :])
        spectrum = apply(fx_ref, jnp.concatenate(parts, axis=0))
        freq_y = step * group_x + index_x // mesh_x
        freq_y = jnp.where(freq_y <= mesh_y // 2, freq_y, freq_y - mesh_y // 2)
        wave_y = freq_y.astype(F32) * (2.0 * math.pi / mesh_y)
        wave_sq = near + wave_y * wave_y
        zero = wave_sq == 0.0
        green = jnp.exp(-0.5 * SMEARING * SMEARING * wave_sq) / jnp.where(zero, 1.0, wave_sq)
        green = jnp.where(zero, 0.0, 4.0 * math.pi * green)
        both = apply(ix_ref, spectrum * (green * lane_weight))
        start = pl.multiple_of(step * size_x, 8)
        buf_a[pl.ds(start, size_x), :] = both[:size_x]
        buf_c[pl.ds(start, size_x), :] = both[size_x:]
        return carry

    lax.fori_loop(0, mesh_y // group_x, middle, 0, unroll=2)

    def backward_y(step, carry):
        plain, sloped = ([], [])
        for i in range(group_y):
            place = step * group_y + i
            plain.append(buf_a[pl.ds(place, mesh_y, stride=mesh_x), :])
            sloped.append(buf_c[pl.ds(place, mesh_y, stride=mesh_x), :])
        plain = jnp.concatenate(plain, axis=0)
        size = group_y * mesh_y
        start = pl.multiple_of(step * size, 8)
        potential = apply(iy_ref, plain)
        buf_b[pl.ds(start, size), :] = apply(iy_ref, jnp.concatenate(sloped, axis=0))
        buf_d[pl.ds(start, size), :] = apply(dy_ref, plain)
        buf_e[pl.ds(start, size), :] = pltpu.roll(potential, modes, 1) * slope_z
        return carry

    lax.fori_loop(0, mesh_x // group_y, backward_y, 0, unroll=2)

    use_low = (lane // ROWS) == 1
    use_none = (lane % ROWS) >= coefs

    def sample(device, carry):
        _, match = columns_of(device)
        rows = []
        for buf in (buf_b, buf_d, buf_e):
            for lx in range(GRID_X):
                place = (device // cycle_y) * GRID_X + lx
                start = place * mesh_y + (device % cycle_y) * GRID_Y
                rows.append(buf[pl.ds(pl.multiple_of(start, 8), GRID_Y), :])
        data = jnp.concatenate(rows, axis=0)
        high = data.astype(BF16).astype(F32)
        mixed = jnp.where(use_low, data - high, high)
        mixed = jnp.where(use_none, 0.0, mixed).astype(BF16)
        high = trig_ref[device, pl.ds(0, ROWS), :]
        low = trig_ref[device, pl.ds(ROWS, ROWS), :]
        waves = jnp.concatenate([high, high, low, jnp.zeros_like(low)], axis=0)
        fields = jnp.dot(mixed, waves, preferred_element_type=F32)
        picked = []
        for a in range(3):
            part = jnp.where(match, fields[a * columns : (a + 1) * columns], 0.0)
            picked.append(jnp.sum(part, axis=0, keepdims=True))
        out_ref[device] = jnp.concatenate(picked, axis=0)
        return carry

    lax.fori_loop(0, devices, sample, 0, unroll=4)


def grid_fields(place, gathered, cycle_x, cycle_y):
    mesh_x, mesh_y = (GRID_X * cycle_x, GRID_Y * cycle_y)
    devices, _, atoms = gathered.shape
    group_y = max(1, 256 // mesh_y)
    group_x = max(1, 256 // mesh_x)
    ax, bx, cx = real_tables(mesh_x)
    ay, by, cy = real_tables(mesh_y)
    tables = [
        block_table(ay, group_y),
        block_table(ax, group_x),
        np.concatenate([block_table(bx, group_x), block_table(cx, group_x)], axis=0),
        block_table(by, group_y),
        block_table(cy, group_y),
    ]
    plane = pltpu.VMEM((mesh_x * mesh_y, LANES), F32)
    vmem = pl.BlockSpec(memory_space=pltpu.VMEM)
    return pl.pallas_call(
        functools.partial(grid_kernel, cycle_x, cycle_y),
        in_specs=[pl.BlockSpec(memory_space=pltpu.SMEM)] + [vmem] * 6,
        out_specs=vmem,
        out_shape=jax.ShapeDtypeStruct((devices, 3, atoms), F32),
        scratch_shapes=[plane] * 5
        + [pltpu.VMEM((devices, 2 * ROWS, atoms), BF16)]
        + [pltpu.VMEM((t.shape[0], 2 * t.shape[1]), BF16) for t in tables],
        compiler_params=pltpu.CompilerParams(vmem_limit_bytes=60 << 20),
        cost_estimate=pl.CostEstimate(
            flops=8_000_000_000, bytes_accessed=4_000_000, transcendentals=100_000
        ),
        name="grid_fields",
    )(place, gathered, *[jnp.asarray(t) for t in tables])


def edge_kernel(
    list_ref, index_ref, feat_ref, pos_ref, mid_ref, up_ref, down_ref, w_self_ref, w_pair_ref,
    w_radial_ref, w_expand_ref, w_contract_ref, w_final_ref, out_ref,
    table, places, near_a, near_b, near_c, edge_a, edge_b, edge_c, marks, own_ref, sums_ref, w_half,
):
    atoms, channels = feat_ref.shape
    ghosts = mid_ref.shape[1] - EXTRA
    slots_all = atoms + 9 * ghosts
    per_atom = index_ref.shape[0]
    chunk = CHUNK_ATOMS * per_atom
    chunks = atoms // CHUNK_ATOMS
    basis_count = w_radial_ref.shape[0]
    spacing = CUTOFF_SQ / (basis_count - 1)
    latent = w_expand_ref.shape[1]
    width = latent // TILES
    slots = per_atom // PIECES
    w_half[...] = w_expand_ref[...] * 0.5

    def fill(start, rows, coords, shift):
        count = rows.shape[0]
        projected = jnp.dot(rows, w_pair_ref[...], preferred_element_type=F32)
        projected = projected.astype(BF16).astype(F32)
        rows_of = table.reshape(slots_all * 8, LANES)
        rows_of[pl.ds(start * 8, count, stride=8), :] = projected[:, :channels] * 0.5
        rows_of[pl.ds(start * 8 + 1, count, stride=8), :] = projected[:, channels:]
        row = lax.broadcasted_iota(jnp.int32, (8, LANES), 0)
        offset = jnp.where(row == 0, shift[0], jnp.where(row == 1, shift[1], 0.0))
        places[start // LANES] = coords + offset

    pos = jnp.concatenate([pos_ref[...].astype(F32), jnp.zeros((5, atoms), F32)], axis=0)
    for i in range(atoms // LANES):
        rows = feat_ref[pl.ds(i * LANES, LANES), :]
        fill(i * LANES, rows, pos[:, i * LANES : (i + 1) * LANES], (0.0, 0.0))
        own = jnp.dot(rows, w_self_ref[...], preferred_element_type=F32)
        own_ref[pl.ds(i * LANES, LANES), :] = own * 0.5
    for sx in range(3):
        for sy, ref in enumerate((up_ref, mid_ref, down_ref)):
            block = 3 * sx + sy
            if block == 4:
                continue
            tail = ref[sx, pl.ds(ghosts, EXTRA), :].astype(F32)
            for h in range(ghosts // LANES):
                rows = ref[sx, pl.ds(h * LANES, LANES), :]
                start = atoms + block * ghosts + h * LANES
                fill(start, rows, tail[h * 8 : (h + 1) * 8], ((sx - 1) * BOX, (sy - 1) * BOX))

    feature = lax.broadcasted_iota(jnp.int32, (8, LANES), 0)
    skipped = range((atoms + 4 * ghosts) // LANES, (atoms + 5 * ghosts) // LANES)
    for i in range(atoms // LANES):
        columns = slice(i * LANES, (i + 1) * LANES)
        index = index_ref[:, columns]
        inside = index & (LANES - 1)
        outside = lax.shift_right_logical(index, 7)
        found = [jnp.zeros((per_atom, LANES), F32)] * 3
        for c in range(slots_all // LANES):
            if c in skipped:
                continue
            tile = places[c]
            here = outside == c
            for a in range(3):
                source = jnp.broadcast_to(tile[a : a + 1], (per_atom, LANES))
                value = jnp.take_along_axis(source, inside, axis=1)
                found[a] = jnp.where(here, value, found[a])
        disp = [found[a] - pos[a : a + 1, columns] for a in range(3)]
        d2 = disp[0] * disp[0] + disp[1] * disp[1] + disp[2] * disp[2]
        envelope = jnp.maximum(0.0, 1.0 - d2 * (1.0 / CUTOFF_SQ))
        envelope = envelope * envelope
        moments = [envelope] + [envelope * disp[a] for a in range(3)]
        for k in range(per_atom):
            def wide(value):
                return jnp.broadcast_to(value[k : k + 1], (8, LANES))

            t = wide(d2) * (1.0 / spacing) - feature.astype(F32)
            basis = jnp.exp(-(t * t))
            high = basis.astype(BF16).astype(F32)
            tail = jnp.where(feature == 0, wide(moments[0]), 0.0)
            for a in range(3):
                tail = jnp.where(feature == 1 + a, wide(moments[1 + a]), tail)
            stacked = jnp.concatenate([high, basis - high, high, tail], axis=0)
            marks[k, pl.ds(i * LANES, LANES), :] = stacked.T

    w_radial = w_radial_ref[...] * 0.5
    high = w_radial.astype(BF16).astype(F32)
    w_basis = jnp.concatenate(
        [high, high, w_radial - high, jnp.zeros((8, channels), F32)], axis=0
    ).astype(BF16)

    def gather(index, near, part):
        for k in range(part * slots, (part + 1) * slots):
            start = k * atoms + index * CHUNK_ATOMS
            loaded = [table[list_ref[start + a]] for a in range(CHUNK_ATOMS)]
            for a, tile in enumerate(loaded):
                near[pl.ds(k * CHUNK_ATOMS + a, 2, stride=chunk), :] = tile[:2]

    def enter(index, near, edge_in, part):
        first = pl.multiple_of(index * CHUNK_ATOMS, 8)
        rows = pl.ds(part * slots * CHUNK_ATOMS, slots * CHUNK_ATOMS)
        shape = (slots, CHUNK_ATOMS, LANES)
        basis = marks[pl.ds(part * slots, slots), pl.ds(first, CHUNK_ATOMS), :]
        basis = basis.reshape(slots * CHUNK_ATOMS, basis.shape[2]).astype(BF16)
        radial = jnp.dot(basis, w_basis, preferred_element_type=F32).reshape(shape)
        own = own_ref[pl.ds(first, CHUNK_ATOMS), :][None]
        half = radial + own + near[rows, :].reshape(shape)
        turn = jnp.tanh(half.astype(BF16)).astype(F32)
        edge_in[rows, :] = (half + half * turn).astype(BF16).reshape(-1, LANES)

    def network(edge_in, part):
        cols = pl.ds(part * width, width)
        half = jnp.dot(edge_in[...], w_half[:, cols], preferred_element_type=F32).astype(BF16)
        hidden = half + half * jnp.tanh(half)
        return jnp.dot(hidden, w_contract_ref[cols, :], preferred_element_type=F32)

    def collect(index, mixed, near):
        first = pl.multiple_of(index * CHUNK_ATOMS, 8)
        weight = (mixed * near[pl.ds(chunk, chunk), :]).reshape(per_atom, CHUNK_ATOMS, LANES)
        for s in range(4):
            mark = marks[:, pl.ds(first, CHUNK_ATOMS), 3 * basis_count + s : 3 * basis_count + s + 1]
            sums_ref[s, pl.ds(first, CHUNK_ATOMS), :] = jnp.sum(weight * mark, axis=0)

    def stage(index, nears, edges):
        after = jnp.minimum(index + 1, chunks - 1)
        later = jnp.minimum(index + 2, chunks - 1)
        mixed = None
        for part in range(PIECES):
            gather(later, nears[2], part)
            enter(after, nears[1], edges[1], part)
            if part % (PIECES // TILES) == PIECES // TILES - 1:
                term = network(edges[0], part // (PIECES // TILES))
                mixed = term if mixed is None else mixed + term
        collect(index, mixed, nears[0])

    nears = (near_a, near_b, near_c)
    edges = (edge_a, edge_b, edge_c)
    for part in range(PIECES):
        gather(0, near_a, part)
    for part in range(PIECES):
        gather(1, near_b, part)
        enter(0, near_a, edge_a, part)

    def triple(step, carry):
        for i in range(3):
            order = (i, (i + 1) % 3, (i + 2) % 3)
            stage(3 * step + i, [nears[o] for o in order], [edges[o] for o in order])
        return carry

    lax.fori_loop(0, chunks // 3, triple, 0)

    scale = 1.0 / math.sqrt(per_atom)
    vector = [sums_ref[1 + a] * scale for a in range(3)]
    square = vector[0] * vector[0] + vector[1] * vector[1] + vector[2] * vector[2]
    invariant = (sums_ref[0] * scale + square * (1.0 / 3.0)).astype(BF16)
    gate = jnp.dot(invariant, w_final_ref[...], preferred_element_type=F32)
    gate = gate * (0.5 + 0.5 * jnp.tanh(0.5 * gate)) * (1.0 / math.sqrt(channels))
    ones = jnp.ones((8, channels), F32)
    short = [contract_last(ones, vector[a] * gate, HIGHEST)[:1] for a in range(3)]
    out_ref[...] = jnp.concatenate(short, axis=0)


def edge_forces(index, feat, pos, mid, up, down, w_self, w_pair, w_radial, w_expand, w_contract, w_final):
    atoms, channels = feat.shape
    per_atom = index.shape[0]
    ghosts = mid.shape[1] - EXTRA
    slots_all = atoms + 9 * ghosts
    chunk = CHUNK_ATOMS * per_atom
    vmem = pl.BlockSpec(memory_space=pltpu.VMEM)
    edges = atoms * per_atom
    latent = w_expand.shape[1]
    return pl.pallas_call(
        edge_kernel,
        in_specs=[pl.BlockSpec(memory_space=pltpu.SMEM)] + [vmem] * 12,
        out_specs=vmem,
        out_shape=jax.ShapeDtypeStruct((3, atoms), F32),
        scratch_shapes=[
            pltpu.VMEM((slots_all, 8, LANES), F32),
            pltpu.VMEM((slots_all // LANES, 8, LANES), F32),
        ]
        + [pltpu.VMEM((2 * chunk, LANES), F32)] * 3
        + [pltpu.VMEM((chunk, LANES), BF16)] * 3
        + [
            pltpu.VMEM((per_atom, atoms, 32), F32),
            pltpu.VMEM((atoms, LANES), F32),
            pltpu.VMEM((4, atoms, LANES), F32),
            pltpu.VMEM(w_expand.shape, BF16),
        ],
        compiler_params=pltpu.CompilerParams(vmem_limit_bytes=56 << 20),
        cost_estimate=pl.CostEstimate(
            flops=4 * edges * channels * latent,
            bytes_accessed=4_000_000,
            transcendentals=edges * latent,
        ),
        name="edge_forces",
    )(
        index.reshape(-1), index, feat, pos, mid, up, down, w_self, w_pair, w_radial,
        w_expand, w_contract, w_final,
    )


def ring(array, axis, step):
    size = lax.axis_size(axis)
    return lax.ppermute(array, axis, [(i, (i + step) % size) for i in range(size)])


def shards(
    features, positions, atom_count, ghost_index, neighbour_list, cell_index, w_self, w_pair,
    w_radial, w_expand, w_contract, w_final, w_charge,
):
    feat = features[0, 0]
    pos = positions[0, 0]
    cycle_x, cycle_y = (lax.axis_size("dx"), lax.axis_size("dy"))
    exported, charge_cell = prepare(
        atom_count, feat, pos, ghost_index[0, 0], cell_index[0, 0], w_charge
    )
    spread = jnp.broadcast_to(charge_cell, (cycle_x * cycle_y,) + charge_cell.shape)
    gathered = lax.all_to_all(spread, ("dx", "dy"), split_axis=0, concat_axis=0, tiled=True)
    mid = jnp.stack([ring(exported, "dx", 1), exported, ring(exported, "dx", -1)])
    lists = neighbour_list[0, 0].T
    gathered, mid, lists = lax.optimization_barrier((gathered, mid, lists))
    up = ring(mid, "dy", 1)
    down = ring(mid, "dy", -1)
    place = lax.axis_index("dx") * cycle_y + lax.axis_index("dy")
    partial = grid_fields(place[None].astype(jnp.int32), gathered, cycle_x, cycle_y)
    received = lax.all_to_all(partial, ("dx", "dy"), split_axis=0, concat_axis=0, tiled=True)
    short = edge_forces(
        lists, feat, pos, mid, up, down, w_self, w_pair, w_radial, w_expand,
        w_contract, w_final,
    )
    field = jnp.sum(received, axis=0)
    total = short + charge_cell[:1] * field
    live = lax.broadcasted_iota(jnp.int32, (1, feat.shape[0]), 1) < atom_count[0, 0]
    return jnp.where(live, total, jnp.zeros_like(total))[None, None]


def solution(mesh):
    placed = (
        P("dx", "dy", None, None),
        P("dx", "dy", None, None),
        P("dx", "dy"),
        P("dx", "dy", None),
        P("dx", "dy", None, None),
        P("dx", "dy", None),
    ) + (P(),) * 7
    return jax.shard_map(
        shards, mesh=mesh, in_specs=placed, out_specs=P("dx", "dy", None, None), check_vma=False
    )
```

```python
import functools
import math

import jax
import jax.numpy as jnp
import numpy as np
from jax import lax
from jax.experimental import pallas as pl
from jax.experimental.pallas import tpu as pltpu
from jax.sharding import PartitionSpec as P

GRID_X = 8
GRID_Y = 8
GRID_Z = 1024
BOX = 1.0
CUTOFF_SQ = 6.25
SMEARING = 1.0

LANES = 128
EXTRA = 16
ROWS = 32
GROUPS = LANES // ROWS
CHUNK_ATOMS = 16
PIECES = 4
TILES = 2
HIGHEST = lax.Precision.HIGHEST
F32 = jnp.float32
BF16 = jnp.bfloat16


def contract_first(a, b, precision=None):
    return lax.dot_general(
        a, b, (((0,), (0,)), ((), ())), precision=precision, preferred_element_type=F32
    )


def contract_last(a, b, precision=None):
    return lax.dot_general(
        a, b, (((1,), (1,)), ((), ())), precision=precision, preferred_element_type=F32
    )


def prepare_kernel(count_ref, feat_ref, pos_ref, export_ref, cell_ref, wq_ref, out_ref, qc_ref):
    atoms = feat_ref.shape[0]
    ghosts = export_ref.shape[1]
    pick = lax.broadcasted_iota(jnp.int32, (atoms, ghosts), 0) == export_ref[...]
    pick = jnp.where(pick, 1.0, 0.0).astype(BF16)
    out_ref[pl.ds(0, ghosts), :] = contract_first(pick, feat_ref[...]).astype(BF16)
    pos = jnp.concatenate([pos_ref[...].astype(F32), jnp.zeros((13, atoms), F32)], axis=0)
    coords = jnp.dot(pos.astype(BF16), pick, preferred_element_type=F32)
    tail = [coords[:8, h * LANES : (h + 1) * LANES] for h in range(ghosts // LANES)]
    out_ref[pl.ds(ghosts, EXTRA), :] = jnp.concatenate(tail, axis=0).astype(BF16)
    weights = jnp.broadcast_to(wq_ref[...].astype(F32), (16, LANES)).astype(BF16)
    charge = contract_last(weights, feat_ref[...])[:1]
    live = lax.broadcasted_iota(jnp.int32, (1, atoms), 1) < count_ref[0, 0]
    both = jnp.concatenate([jnp.where(live, charge, 0.0), cell_ref[...].astype(F32)], axis=0)
    qc_ref[...] = jnp.broadcast_to(both[None], qc_ref.shape)


def prepare(devices, count, feat, pos, exports, cells, w_charge):
    atoms, ghosts = (feat.shape[0], exports.shape[0])
    vmem = pl.BlockSpec(memory_space=pltpu.VMEM)
    return pl.pallas_call(
        prepare_kernel,
        in_specs=[pl.BlockSpec(memory_space=pltpu.SMEM)] + [vmem] * 5,
        out_specs=[vmem, vmem],
        out_shape=[
            jax.ShapeDtypeStruct((ghosts + EXTRA, feat.shape[1]), BF16),
            jax.ShapeDtypeStruct((devices, 2, atoms), F32),
        ],
        name="prepare",
    )(count, feat, pos, exports[None], cells[None], w_charge[None])


def real_tables(count):
    half = count // 2
    index = np.arange(count)
    freq = np.where(index <= half, index, index - half)
    place = np.arange(count)
    angle = 2.0 * np.pi * (freq[:, None] * place[None, :] % count) / count
    is_cos = (index <= half)[:, None]
    basis = np.where(is_cos, np.cos(angle), np.sin(angle))
    weight = np.where((index == 0) | (index == half), 1.0, 2.0)[:, None] / count
    wave = np.where(index == half, 0.0, 2.0 * np.pi * freq / count)[:, None]
    slope = np.where(is_cos, np.sin(angle), -np.cos(angle)) * wave
    return (basis, (weight * basis).T, (weight * slope).T)


def thirds(table):
    whole = table.astype(np.float32)
    high = whole.astype(BF16).astype(np.float32)
    low = (whole - high).astype(BF16).astype(np.float32)
    return np.concatenate([high, high, low], axis=1)


def sine_half(t):
    x = t * (math.pi / 512.0)
    s = x * x
    p = -2.50521084e-08
    p = p * s + 2.75573192e-06
    p = p * s - 1.98412698e-04
    p = p * s + 8.33333333e-03
    p = p * s - 1.66666667e-01
    return x + x * (s * p)


def grid_kernel(
    cycle_x, cycle_y, place_ref, qc_ref, fy_ref, fx_ref, ix_ref, iy_ref, out_ref,
    buf_a, buf_b, buf_c, buf_d, buf_e, trig_ref,
):
    mesh_x, mesh_y, mesh_z = (GRID_X * cycle_x, GRID_Y * cycle_y, GRID_Z)
    devices = cycle_x * cycle_y
    modes = mesh_z // 2 // devices
    coefs = 2 * modes
    first = place_ref[0] * modes
    columns = GRID_X * GRID_Y
    atoms = qc_ref.shape[2]

    row = lax.broadcasted_iota(jnp.int32, (ROWS, 1), 0) % coefs
    row_mode = first + row % modes
    row_sine = row >= modes
    row_edge = row_sine & (row_mode == 0)
    row_factor = jnp.where(row_edge, mesh_z // 2, row_mode)
    row_shift = jnp.where(row_sine & (row_mode != 0), mesh_z // 4, 0)
    column_iota = lax.broadcasted_iota(jnp.int32, (columns, atoms), 0)

    def columns_of(device):
        cell = qc_ref[device, 1:2, :].astype(jnp.int32)
        return cell, column_iota == lax.shift_right_logical(cell, 10)

    def spread(device, carry):
        cell, match = columns_of(device)
        depth = cell & (mesh_z - 1)
        turn = (row_factor * depth - row_shift) & (mesh_z - 1)
        trig = sine_half((jnp.abs(turn - mesh_z // 2) - mesh_z // 4).astype(F32))
        high = trig.astype(BF16)
        trig_ref[device, pl.ds(0, ROWS), :] = high
        trig_ref[device, pl.ds(ROWS, ROWS), :] = (trig - high.astype(F32)).astype(BF16)
        charged = trig * qc_ref[device, 0:1, :]
        high = charged.astype(BF16)
        low = (charged - high.astype(F32)).astype(BF16)
        pick = jnp.where(match, 1.0, 0.0).astype(BF16)
        total = contract_last(pick, jnp.concatenate([high, low] * (LANES // ROWS // 2), axis=0))
        total = total + pltpu.roll(total, ROWS, 1)
        buf_a[pl.ds(pl.multiple_of(device * columns, 8), columns), :] = total
        return carry

    lax.fori_loop(0, devices, spread, 0, unroll=4)

    lane = lax.broadcasted_iota(jnp.int32, (1, LANES), 1)
    lane_group = lane // ROWS

    def pack(copied):
        wide = copied[0]
        for g in range(1, GROUPS):
            wide = jnp.where(lane_group == g, copied[g], wide)
        return wide

    def unpack(wide):
        turned = [wide] + [pltpu.roll(wide, g * ROWS, 1) for g in range(1, GROUPS)]
        copied = []
        for i in range(GROUPS):
            copied.append(pack([turned[(g - i) % GROUPS] for g in range(GROUPS)]))
        return copied

    def apply(table_ref, wide):
        high = wide.astype(BF16)
        low = (wide - high.astype(F32)).astype(BF16)
        data = jnp.concatenate([high, low, high], axis=0)
        return jnp.dot(table_ref[...].astype(BF16), data, preferred_element_type=F32)

    for first_x in range(0, mesh_x, GROUPS):
        copied = []
        for place in range(first_x, first_x + GROUPS):
            rows = []
            for sy in range(cycle_y):
                start = ((place // GRID_X) * cycle_y + sy) * columns + (place % GRID_X) * GRID_Y
                rows.append(buf_a[pl.ds(start, GRID_Y), :])
            copied.append(jnp.concatenate(rows, axis=0))
        for i, part in enumerate(unpack(apply(fy_ref, pack(copied)))):
            buf_b[pl.ds((first_x + i) * mesh_y, mesh_y), :] = part

    lane_coef = lane % ROWS % coefs
    lane_mode = first + lane_coef % modes
    lane_sine = lane_coef >= modes
    lane_freq = jnp.where(lane_sine & (lane_mode == 0), mesh_z // 2, lane_mode)
    wave_z = lane_freq.astype(F32) * (2.0 * math.pi / mesh_z)
    lane_weight = jnp.where(lane_mode == 0, 1.0, 2.0) / mesh_z
    slope_z = jnp.where(lane_mode == 0, 0.0, wave_z) * jnp.where(lane_sine, 1.0, -1.0)
    freq_x = lax.broadcasted_iota(jnp.int32, (mesh_x, 1), 0)
    freq_x = jnp.where(freq_x <= mesh_x // 2, freq_x, freq_x - mesh_x // 2)
    wave_x = freq_x.astype(F32) * (2.0 * math.pi / mesh_x)
    near = wave_x * wave_x + wave_z * wave_z

    for first_y in range(0, mesh_y, GROUPS):
        copied = [
            buf_b[pl.ds(first_y + i, mesh_x, stride=mesh_y), :] for i in range(GROUPS)
        ]
        spectrum = apply(fx_ref, pack(copied))
        freq_y = first_y + lane_group
        freq_y = jnp.where(freq_y <= mesh_y // 2, freq_y, freq_y - mesh_y // 2)
        wave_y = freq_y.astype(F32) * (2.0 * math.pi / mesh_y)
        wave_sq = near + wave_y * wave_y
        zero = wave_sq == 0.0
        green = jnp.exp(-0.5 * SMEARING * SMEARING * wave_sq) / jnp.where(zero, 1.0, wave_sq)
        green = jnp.where(zero, 0.0, 4.0 * math.pi * green)
        both = apply(ix_ref, spectrum * (green * lane_weight))
        for i, part in enumerate(unpack(both)):
            rows = pl.ds((first_y + i) * mesh_x, mesh_x)
            buf_a[rows, :] = part[:mesh_x]
            buf_c[rows, :] = part[mesh_x:]

    for first_x in range(0, mesh_x, GROUPS):
        plain, sloped = (
            pack([buf[pl.ds(first_x + i, mesh_y, stride=mesh_x), :] for i in range(GROUPS)])
            for buf in (buf_a, buf_c)
        )
        both = apply(iy_ref, plain)
        along_x = apply(iy_ref.at[pl.ds(0, mesh_y), :], sloped)
        potential = both[:mesh_y]
        partner = jnp.where(
            lane % ROWS >= modes,
            pltpu.roll(potential, modes, 1),
            pltpu.roll(potential, LANES - modes, 1),
        )
        fields = (along_x, both[mesh_y:], partner * slope_z)
        for buf, wide in zip((buf_b, buf_d, buf_e), fields):
            for i, part in enumerate(unpack(wide)):
                buf[pl.ds((first_x + i) * mesh_y, mesh_y), :] = part

    use_low = (lane // ROWS) == 1
    use_none = (lane % ROWS) >= coefs

    def sample(device, carry):
        _, match = columns_of(device)
        rows = []
        for buf in (buf_b, buf_d, buf_e):
            for lx in range(GRID_X):
                place = (device // cycle_y) * GRID_X + lx
                start = place * mesh_y + (device % cycle_y) * GRID_Y
                rows.append(buf[pl.ds(pl.multiple_of(start, 8), GRID_Y), :])
        data = jnp.concatenate(rows, axis=0)
        high = data.astype(BF16).astype(F32)
        mixed = jnp.where(use_low, data - high, high)
        mixed = jnp.where(use_none, 0.0, mixed).astype(BF16)
        high = trig_ref[device, pl.ds(0, ROWS), :]
        low = trig_ref[device, pl.ds(ROWS, ROWS), :]
        waves = jnp.concatenate([high, high, low, jnp.zeros_like(low)], axis=0)
        fields = jnp.dot(mixed, waves, preferred_element_type=F32)
        picked = []
        for a in range(3):
            part = jnp.where(match, fields[a * columns : (a + 1) * columns], 0.0)
            picked.append(jnp.sum(part, axis=0, keepdims=True))
        out_ref[device] = jnp.concatenate(picked, axis=0)
        return carry

    lax.fori_loop(0, devices, sample, 0, unroll=4)


def grid_fields(place, gathered, cycle_x, cycle_y):
    mesh_x, mesh_y = (GRID_X * cycle_x, GRID_Y * cycle_y)
    devices, _, atoms = gathered.shape
    ax, bx, cx = real_tables(mesh_x)
    ay, by, cy = real_tables(mesh_y)
    tables = [
        thirds(ay),
        thirds(ax),
        np.concatenate([thirds(bx), thirds(cx)], axis=0),
        np.concatenate([thirds(by), thirds(cy)], axis=0),
    ]
    plane = pltpu.VMEM((mesh_x * mesh_y, LANES), F32)
    vmem = pl.BlockSpec(memory_space=pltpu.VMEM)
    return pl.pallas_call(
        functools.partial(grid_kernel, cycle_x, cycle_y),
        in_specs=[pl.BlockSpec(memory_space=pltpu.SMEM)] + [vmem] * 5,
        out_specs=vmem,
        out_shape=jax.ShapeDtypeStruct((devices, 3, atoms), F32),
        scratch_shapes=[plane] * 5
        + [pltpu.VMEM((devices, 2 * ROWS, atoms), BF16)],
        compiler_params=pltpu.CompilerParams(vmem_limit_bytes=60 << 20),
        cost_estimate=pl.CostEstimate(
            flops=8_000_000_000, bytes_accessed=4_000_000, transcendentals=100_000
        ),
        name="grid_fields",
    )(place, gathered, *[jnp.asarray(t) for t in tables])


def edge_kernel(
    list_ref, index_ref, feat_ref, pos_ref, mid_ref, up_ref, down_ref, w_self_ref, w_pair_ref,
    w_radial_ref, w_expand_ref, w_contract_ref, w_final_ref, out_ref,
    table, places, near_a, near_b, near_c, edge_a, edge_b, edge_c, marks, own_ref, sums_ref, w_half,
):
    atoms, channels = feat_ref.shape
    ghosts = mid_ref.shape[1] - EXTRA
    slots_all = atoms + 9 * ghosts
    per_atom = index_ref.shape[0]
    chunk = CHUNK_ATOMS * per_atom
    chunks = atoms // CHUNK_ATOMS
    basis_count = w_radial_ref.shape[0]
    spacing = CUTOFF_SQ / (basis_count - 1)
    latent = w_expand_ref.shape[1]
    width = latent // TILES
    slots = per_atom // PIECES
    w_half[...] = w_expand_ref[...] * 0.5

    def fill(start, rows, coords, shift):
        count = rows.shape[0]
        projected = jnp.dot(rows, w_pair_ref[...], preferred_element_type=F32)
        projected = projected.astype(BF16).astype(F32)
        rows_of = table.reshape(slots_all * 8, LANES)
        rows_of[pl.ds(start * 8, count, stride=8), :] = projected[:, :channels] * 0.5
        rows_of[pl.ds(start * 8 + 1, count, stride=8), :] = projected[:, channels:]
        row = lax.broadcasted_iota(jnp.int32, (8, LANES), 0)
        offset = jnp.where(row == 0, shift[0], jnp.where(row == 1, shift[1], 0.0))
        places[start // LANES] = coords + offset

    pos = jnp.concatenate([pos_ref[...].astype(F32), jnp.zeros((5, atoms), F32)], axis=0)
    for i in range(atoms // LANES):
        rows = feat_ref[pl.ds(i * LANES, LANES), :]
        fill(i * LANES, rows, pos[:, i * LANES : (i + 1) * LANES], (0.0, 0.0))
        own = jnp.dot(rows, w_self_ref[...], preferred_element_type=F32)
        own_ref[pl.ds(i * LANES, LANES), :] = own * 0.5
    for sx in range(3):
        for sy, ref in enumerate((up_ref, mid_ref, down_ref)):
            block = 3 * sx + sy
            if block == 4:
                continue
            tail = ref[sx, pl.ds(ghosts, EXTRA), :].astype(F32)
            for h in range(ghosts // LANES):
                rows = ref[sx, pl.ds(h * LANES, LANES), :]
                start = atoms + block * ghosts + h * LANES
                fill(start, rows, tail[h * 8 : (h + 1) * 8], ((sx - 1) * BOX, (sy - 1) * BOX))

    feature = lax.broadcasted_iota(jnp.int32, (8, LANES), 0)
    skipped = range((atoms + 4 * ghosts) // LANES, (atoms + 5 * ghosts) // LANES)
    for i in range(atoms // LANES):
        columns = slice(i * LANES, (i + 1) * LANES)
        index = index_ref[:, columns]
        inside = index & (LANES - 1)
        outside = lax.shift_right_logical(index, 7)
        found = [jnp.zeros((per_atom, LANES), F32)] * 3
        for c in range(slots_all // LANES):
            if c in skipped:
                continue
            tile = places[c]
            here = outside == c
            for a in range(3):
                source = jnp.broadcast_to(tile[a : a + 1], (per_atom, LANES))
                value = jnp.take_along_axis(source, inside, axis=1)
                found[a] = jnp.where(here, value, found[a])
        disp = [found[a] - pos[a : a + 1, columns] for a in range(3)]
        d2 = disp[0] * disp[0] + disp[1] * disp[1] + disp[2] * disp[2]
        envelope = jnp.maximum(0.0, 1.0 - d2 * (1.0 / CUTOFF_SQ))
        envelope = envelope * envelope
        moments = [envelope] + [envelope * disp[a] for a in range(3)]
        for k in range(per_atom):
            def wide(value):
                return jnp.broadcast_to(value[k : k + 1], (8, LANES))

            t = wide(d2) * (1.0 / spacing) - feature.astype(F32)
            basis = jnp.exp(-(t * t))
            high = basis.astype(BF16).astype(F32)
            tail = jnp.where(feature == 0, wide(moments[0]), 0.0)
            for a in range(3):
                tail = jnp.where(feature == 1 + a, wide(moments[1 + a]), tail)
            stacked = jnp.concatenate([high, basis - high, high, tail], axis=0)
            marks[k, pl.ds(i * LANES, LANES), :] = stacked.T

    w_radial = w_radial_ref[...] * 0.5
    high = w_radial.astype(BF16).astype(F32)
    w_basis = jnp.concatenate(
        [high, high, w_radial - high, jnp.zeros((8, channels), F32)], axis=0
    ).astype(BF16)

    def gather(index, near, part):
        for k in range(part * slots, (part + 1) * slots):
            start = k * atoms + index * CHUNK_ATOMS
            loaded = [table[list_ref[start + a]] for a in range(CHUNK_ATOMS)]
            for a, tile in enumerate(loaded):
                near[pl.ds(k * CHUNK_ATOMS + a, 2, stride=chunk), :] = tile[:2]

    def enter(index, near, edge_in, part):
        first = pl.multiple_of(index * CHUNK_ATOMS, 8)
        rows = pl.ds(part * slots * CHUNK_ATOMS, slots * CHUNK_ATOMS)
        shape = (slots, CHUNK_ATOMS, LANES)
        basis = marks[pl.ds(part * slots, slots), pl.ds(first, CHUNK_ATOMS), :]
        basis = basis.reshape(slots * CHUNK_ATOMS, basis.shape[2]).astype(BF16)
        radial = jnp.dot(basis, w_basis, preferred_element_type=F32).reshape(shape)
        own = own_ref[pl.ds(first, CHUNK_ATOMS), :][None]
        half = radial + own + near[rows, :].reshape(shape)
        turn = jnp.tanh(half.astype(BF16)).astype(F32)
        edge_in[rows, :] = (half + half * turn).astype(BF16).reshape(-1, LANES)

    def network(edge_in, part):
        cols = pl.ds(part * width, width)
        half = jnp.dot(edge_in[...], w_half[:, cols], preferred_element_type=F32).astype(BF16)
        hidden = half + half * jnp.tanh(half)
        return jnp.dot(hidden, w_contract_ref[cols, :], preferred_element_type=F32)

    def collect(index, mixed, near):
        first = pl.multiple_of(index * CHUNK_ATOMS, 8)
        weight = (mixed * near[pl.ds(chunk, chunk), :]).reshape(per_atom, CHUNK_ATOMS, LANES)
        for s in range(4):
            mark = marks[:, pl.ds(first, CHUNK_ATOMS), 3 * basis_count + s : 3 * basis_count + s + 1]
            sums_ref[s, pl.ds(first, CHUNK_ATOMS), :] = jnp.sum(weight * mark, axis=0)

    def stage(index, nears, edges):
        after = jnp.minimum(index + 1, chunks - 1)
        later = jnp.minimum(index + 2, chunks - 1)
        mixed = None
        for part in range(PIECES):
            gather(later, nears[2], part)
            enter(after, nears[1], edges[1], part)
            if part % (PIECES // TILES) == PIECES // TILES - 1:
                term = network(edges[0], part // (PIECES // TILES))
                mixed = term if mixed is None else mixed + term
        collect(index, mixed, nears[0])

    nears = (near_a, near_b, near_c)
    edges = (edge_a, edge_b, edge_c)
    for part in range(PIECES):
        gather(0, near_a, part)
    for part in range(PIECES):
        gather(1, near_b, part)
        enter(0, near_a, edge_a, part)

    def triple(step, carry):
        for i in range(3):
            order = (i, (i + 1) % 3, (i + 2) % 3)
            stage(3 * step + i, [nears[o] for o in order], [edges[o] for o in order])
        return carry

    lax.fori_loop(0, chunks // 3, triple, 0)

    scale = 1.0 / math.sqrt(per_atom)
    vector = [sums_ref[1 + a] * scale for a in range(3)]
    square = vector[0] * vector[0] + vector[1] * vector[1] + vector[2] * vector[2]
    invariant = (sums_ref[0] * scale + square * (1.0 / 3.0)).astype(BF16)
    gate = jnp.dot(invariant, w_final_ref[...], preferred_element_type=F32)
    gate = gate * (0.5 + 0.5 * jnp.tanh(0.5 * gate)) * (1.0 / math.sqrt(channels))
    ones = jnp.ones((8, channels), F32)
    short = [contract_last(ones, vector[a] * gate, HIGHEST)[:1] for a in range(3)]
    out_ref[...] = jnp.concatenate(short, axis=0)


def edge_forces(index, feat, pos, mid, up, down, w_self, w_pair, w_radial, w_expand, w_contract, w_final):
    atoms, channels = feat.shape
    per_atom = index.shape[0]
    ghosts = mid.shape[1] - EXTRA
    slots_all = atoms + 9 * ghosts
    chunk = CHUNK_ATOMS * per_atom
    vmem = pl.BlockSpec(memory_space=pltpu.VMEM)
    edges = atoms * per_atom
    latent = w_expand.shape[1]
    return pl.pallas_call(
        edge_kernel,
        in_specs=[pl.BlockSpec(memory_space=pltpu.SMEM)] + [vmem] * 12,
        out_specs=vmem,
        out_shape=jax.ShapeDtypeStruct((3, atoms), F32),
        scratch_shapes=[
            pltpu.VMEM((slots_all, 8, LANES), F32),
            pltpu.VMEM((slots_all // LANES, 8, LANES), F32),
        ]
        + [pltpu.VMEM((2 * chunk, LANES), F32)] * 3
        + [pltpu.VMEM((chunk, LANES), BF16)] * 3
        + [
            pltpu.VMEM((per_atom, atoms, 32), F32),
            pltpu.VMEM((atoms, LANES), F32),
            pltpu.VMEM((4, atoms, LANES), F32),
            pltpu.VMEM(w_expand.shape, BF16),
        ],
        compiler_params=pltpu.CompilerParams(vmem_limit_bytes=56 << 20),
        cost_estimate=pl.CostEstimate(
            flops=4 * edges * channels * latent,
            bytes_accessed=4_000_000,
            transcendentals=edges * latent,
        ),
        name="edge_forces",
    )(
        index.reshape(-1), index, feat, pos, mid, up, down, w_self, w_pair, w_radial,
        w_expand, w_contract, w_final,
    )


def ring(array, axis, step):
    size = lax.axis_size(axis)
    return lax.ppermute(array, axis, [(i, (i + step) % size) for i in range(size)])


def shards(
    features, positions, atom_count, ghost_index, neighbour_list, cell_index, w_self, w_pair,
    w_radial, w_expand, w_contract, w_final, w_charge,
):
    feat = features[0, 0]
    pos = positions[0, 0]
    cycle_x, cycle_y = (lax.axis_size("dx"), lax.axis_size("dy"))
    exported, spread = prepare(
        cycle_x * cycle_y, atom_count, feat, pos, ghost_index[0, 0], cell_index[0, 0], w_charge
    )
    gathered = lax.all_to_all(spread, ("dx", "dy"), split_axis=0, concat_axis=0, tiled=True)
    mid = jnp.stack([ring(exported, "dx", 1), exported, ring(exported, "dx", -1)])
    lists = neighbour_list[0, 0].T
    gathered, mid, lists = lax.optimization_barrier((gathered, mid, lists))
    up = ring(mid, "dy", 1)
    down = ring(mid, "dy", -1)
    place = lax.axis_index("dx") * cycle_y + lax.axis_index("dy")
    partial = grid_fields(place[None].astype(jnp.int32), gathered, cycle_x, cycle_y)
    received = lax.all_to_all(partial, ("dx", "dy"), split_axis=0, concat_axis=0, tiled=True)
    short = edge_forces(
        lists, feat, pos, mid, up, down, w_self, w_pair, w_radial, w_expand,
        w_contract, w_final,
    )
    field = jnp.sum(received, axis=0)
    total = short + spread[0, :1] * field
    live = lax.broadcasted_iota(jnp.int32, (1, feat.shape[0]), 1) < atom_count[0, 0]
    return jnp.where(live, total, jnp.zeros_like(total))[None, None]


def solution(mesh):
    placed = (
        P("dx", "dy", None, None),
        P("dx", "dy", None, None),
        P("dx", "dy"),
        P("dx", "dy", None),
        P("dx", "dy", None, None),
        P("dx", "dy", None),
    ) + (P(),) * 7
    return jax.shard_map(
        shards, mesh=mesh, in_specs=placed, out_specs=P("dx", "dy", None, None), check_vma=False
    )
```

```python
import functools
import math

import jax
import jax.numpy as jnp
import numpy as np
from jax import lax
from jax.experimental import pallas as pl
from jax.experimental.pallas import tpu as pltpu
from jax.sharding import PartitionSpec as P

GRID_X = 8
GRID_Y = 8
GRID_Z = 1024
BOX = 1.0
CUTOFF_SQ = 6.25
SMEARING = 1.0

LANES = 128
EXTRA = 16
ROWS = 32
GROUPS = LANES // ROWS
CHUNK_ATOMS = 16
PIECES = 4
TILES = 1
HIGHEST = lax.Precision.HIGHEST
F32 = jnp.float32
BF16 = jnp.bfloat16


def contract_first(a, b, precision=None):
    return lax.dot_general(
        a, b, (((0,), (0,)), ((), ())), precision=precision, preferred_element_type=F32
    )


def contract_last(a, b, precision=None):
    return lax.dot_general(
        a, b, (((1,), (1,)), ((), ())), precision=precision, preferred_element_type=F32
    )


def prepare_kernel(count_ref, feat_ref, pos_ref, export_ref, cell_ref, wq_ref, out_ref, qc_ref):
    atoms = feat_ref.shape[0]
    ghosts = export_ref.shape[1]
    pick = lax.broadcasted_iota(jnp.int32, (atoms, ghosts), 0) == export_ref[...]
    pick = jnp.where(pick, 1.0, 0.0).astype(BF16)
    out_ref[pl.ds(0, ghosts), :] = contract_first(pick, feat_ref[...]).astype(BF16)
    pos = jnp.concatenate([pos_ref[...].astype(F32), jnp.zeros((13, atoms), F32)], axis=0)
    coords = jnp.dot(pos.astype(BF16), pick, preferred_element_type=F32)
    tail = [coords[:8, h * LANES : (h + 1) * LANES] for h in range(ghosts // LANES)]
    out_ref[pl.ds(ghosts, EXTRA), :] = jnp.concatenate(tail, axis=0).astype(BF16)
    weights = jnp.broadcast_to(wq_ref[...].astype(F32), (16, LANES)).astype(BF16)
    charge = contract_last(weights, feat_ref[...])[:1]
    live = lax.broadcasted_iota(jnp.int32, (1, atoms), 1) < count_ref[0, 0]
    both = jnp.concatenate([jnp.where(live, charge, 0.0), cell_ref[...].astype(F32)], axis=0)
    qc_ref[...] = jnp.broadcast_to(both[None], qc_ref.shape)


def prepare(devices, count, feat, pos, exports, cells, w_charge):
    atoms, ghosts = (feat.shape[0], exports.shape[0])
    vmem = pl.BlockSpec(memory_space=pltpu.VMEM)
    return pl.pallas_call(
        prepare_kernel,
        in_specs=[pl.BlockSpec(memory_space=pltpu.SMEM)] + [vmem] * 5,
        out_specs=[vmem, vmem],
        out_shape=[
            jax.ShapeDtypeStruct((ghosts + EXTRA, feat.shape[1]), BF16),
            jax.ShapeDtypeStruct((devices, 2, atoms), F32),
        ],
        name="prepare",
    )(count, feat, pos, exports[None], cells[None], w_charge[None])


def real_tables(count):
    half = count // 2
    index = np.arange(count)
    freq = np.where(index <= half, index, index - half)
    place = np.arange(count)
    angle = 2.0 * np.pi * (freq[:, None] * place[None, :] % count) / count
    is_cos = (index <= half)[:, None]
    basis = np.where(is_cos, np.cos(angle), np.sin(angle))
    weight = np.where((index == 0) | (index == half), 1.0, 2.0)[:, None] / count
    wave = np.where(index == half, 0.0, 2.0 * np.pi * freq / count)[:, None]
    slope = np.where(is_cos, np.sin(angle), -np.cos(angle)) * wave
    return (basis, (weight * basis).T, (weight * slope).T)


def thirds(table):
    whole = table.astype(np.float32)
    high = whole.astype(BF16).astype(np.float32)
    low = (whole - high).astype(BF16).astype(np.float32)
    return np.concatenate([high, high, low], axis=1)


def sine_half(t):
    x = t * (math.pi / 512.0)
    s = x * x
    p = -2.50521084e-08
    p = p * s + 2.75573192e-06
    p = p * s - 1.98412698e-04
    p = p * s + 8.33333333e-03
    p = p * s - 1.66666667e-01
    return x + x * (s * p)


def grid_kernel(
    cycle_x, cycle_y, place_ref, qc_ref, fy_ref, fx_ref, ix_ref, iy_ref, out_ref,
    buf_a, buf_b, buf_c, buf_d, buf_e, trig_ref,
):
    mesh_x, mesh_y, mesh_z = (GRID_X * cycle_x, GRID_Y * cycle_y, GRID_Z)
    devices = cycle_x * cycle_y
    modes = mesh_z // 2 // devices
    coefs = 2 * modes
    first = place_ref[0] * modes
    columns = GRID_X * GRID_Y
    atoms = qc_ref.shape[2]

    row = lax.broadcasted_iota(jnp.int32, (ROWS, 1), 0) % coefs
    row_mode = first + row % modes
    row_sine = row >= modes
    row_edge = row_sine & (row_mode == 0)
    row_factor = jnp.where(row_edge, mesh_z // 2, row_mode)
    row_shift = jnp.where(row_sine & (row_mode != 0), mesh_z // 4, 0)
    column_iota = lax.broadcasted_iota(jnp.int32, (columns, atoms), 0)

    def columns_of(device):
        cell = qc_ref[device, 1:2, :].astype(jnp.int32)
        return cell, column_iota == lax.shift_right_logical(cell, 10)

    def spread(device, carry):
        cell, match = columns_of(device)
        depth = cell & (mesh_z - 1)
        turn = (row_factor * depth - row_shift) & (mesh_z - 1)
        trig = sine_half((jnp.abs(turn - mesh_z // 2) - mesh_z // 4).astype(F32))
        high = trig.astype(BF16)
        trig_ref[device, pl.ds(0, ROWS), :] = high
        trig_ref[device, pl.ds(ROWS, ROWS), :] = (trig - high.astype(F32)).astype(BF16)
        charged = trig * qc_ref[device, 0:1, :]
        high = charged.astype(BF16)
        low = (charged - high.astype(F32)).astype(BF16)
        pick = jnp.where(match, 1.0, 0.0).astype(BF16)
        total = contract_last(pick, jnp.concatenate([high, low] * (LANES // ROWS // 2), axis=0))
        total = total + pltpu.roll(total, ROWS, 1)
        buf_a[pl.ds(pl.multiple_of(device * columns, 8), columns), :] = total
        return carry

    lax.fori_loop(0, devices, spread, 0, unroll=4)

    lane = lax.broadcasted_iota(jnp.int32, (1, LANES), 1)
    lane_group = lane // ROWS

    def pack(copied):
        wide = copied[0]
        for g in range(1, GROUPS):
            wide = jnp.where(lane_group == g, copied[g], wide)
        return wide

    def unpack(wide):
        turned = [wide] + [pltpu.roll(wide, g * ROWS, 1) for g in range(1, GROUPS)]
        copied = []
        for i in range(GROUPS):
            copied.append(pack([turned[(g - i) % GROUPS] for g in range(GROUPS)]))
        return copied

    def apply(table_ref, wide):
        high = wide.astype(BF16)
        low = (wide - high.astype(F32)).astype(BF16)
        data = jnp.concatenate([high, low, high], axis=0)
        return jnp.dot(table_ref[...].astype(BF16), data, preferred_element_type=F32)

    for first_x in range(0, mesh_x, GROUPS):
        copied = []
        for place in range(first_x, first_x + GROUPS):
            rows = []
            for sy in range(cycle_y):
                start = ((place // GRID_X) * cycle_y + sy) * columns + (place % GRID_X) * GRID_Y
                rows.append(buf_a[pl.ds(start, GRID_Y), :])
            copied.append(jnp.concatenate(rows, axis=0))
        for i, part in enumerate(unpack(apply(fy_ref, pack(copied)))):
            buf_b[pl.ds((first_x + i) * mesh_y, mesh_y), :] = part

    lane_coef = lane % ROWS % coefs
    lane_mode = first + lane_coef % modes
    lane_sine = lane_coef >= modes
    lane_freq = jnp.where(lane_sine & (lane_mode == 0), mesh_z // 2, lane_mode)
    wave_z = lane_freq.astype(F32) * (2.0 * math.pi / mesh_z)
    lane_weight = jnp.where(lane_mode == 0, 1.0, 2.0) / mesh_z
    slope_z = jnp.where(lane_mode == 0, 0.0, wave_z) * jnp.where(lane_sine, 1.0, -1.0)
    freq_x = lax.broadcasted_iota(jnp.int32, (mesh_x, 1), 0)
    freq_x = jnp.where(freq_x <= mesh_x // 2, freq_x, freq_x - mesh_x // 2)
    wave_x = freq_x.astype(F32) * (2.0 * math.pi / mesh_x)
    near = wave_x * wave_x + wave_z * wave_z

    for first_y in range(0, mesh_y, GROUPS):
        copied = [
            buf_b[pl.ds(first_y + i, mesh_x, stride=mesh_y), :] for i in range(GROUPS)
        ]
        spectrum = apply(fx_ref, pack(copied))
        freq_y = first_y + lane_group
        freq_y = jnp.where(freq_y <= mesh_y // 2, freq_y, freq_y - mesh_y // 2)
        wave_y = freq_y.astype(F32) * (2.0 * math.pi / mesh_y)
        wave_sq = near + wave_y * wave_y
        zero = wave_sq == 0.0
        green = jnp.exp(-0.5 * SMEARING * SMEARING * wave_sq) / jnp.where(zero, 1.0, wave_sq)
        green = jnp.where(zero, 0.0, 4.0 * math.pi * green)
        both = apply(ix_ref, spectrum * (green * lane_weight))
        for i, part in enumerate(unpack(both)):
            rows = pl.ds((first_y + i) * mesh_x, mesh_x)
            buf_a[rows, :] = part[:mesh_x]
            buf_c[rows, :] = part[mesh_x:]

    for first_x in range(0, mesh_x, GROUPS):
        plain, sloped = (
            pack([buf[pl.ds(first_x + i, mesh_y, stride=mesh_x), :] for i in range(GROUPS)])
            for buf in (buf_a, buf_c)
        )
        both = apply(iy_ref, plain)
        along_x = apply(iy_ref.at[pl.ds(0, mesh_y), :], sloped)
        potential = both[:mesh_y]
        partner = jnp.where(
            lane % ROWS >= modes,
            pltpu.roll(potential, modes, 1),
            pltpu.roll(potential, LANES - modes, 1),
        )
        fields = (along_x, both[mesh_y:], partner * slope_z)
        for buf, wide in zip((buf_b, buf_d, buf_e), fields):
            for i, part in enumerate(unpack(wide)):
                buf[pl.ds((first_x + i) * mesh_y, mesh_y), :] = part

    use_low = (lane // ROWS) == 1
    use_none = (lane % ROWS) >= coefs

    def sample(device, carry):
        _, match = columns_of(device)
        rows = []
        for buf in (buf_b, buf_d, buf_e):
            for lx in range(GRID_X):
                place = (device // cycle_y) * GRID_X + lx
                start = place * mesh_y + (device % cycle_y) * GRID_Y
                rows.append(buf[pl.ds(pl.multiple_of(start, 8), GRID_Y), :])
        data = jnp.concatenate(rows, axis=0)
        high = data.astype(BF16).astype(F32)
        mixed = jnp.where(use_low, data - high, high)
        mixed = jnp.where(use_none, 0.0, mixed).astype(BF16)
        high = trig_ref[device, pl.ds(0, ROWS), :]
        low = trig_ref[device, pl.ds(ROWS, ROWS), :]
        waves = jnp.concatenate([high, high, low, jnp.zeros_like(low)], axis=0)
        fields = jnp.dot(mixed, waves, preferred_element_type=F32)
        picked = []
        for a in range(3):
            part = jnp.where(match, fields[a * columns : (a + 1) * columns], 0.0)
            picked.append(jnp.sum(part, axis=0, keepdims=True))
        for a in range(3):
            out_ref[device, a] = picked[a]
        return carry

    lax.fori_loop(0, devices, sample, 0, unroll=4)


def grid_fields(place, gathered, cycle_x, cycle_y):
    mesh_x, mesh_y = (GRID_X * cycle_x, GRID_Y * cycle_y)
    devices, _, atoms = gathered.shape
    ax, bx, cx = real_tables(mesh_x)
    ay, by, cy = real_tables(mesh_y)
    tables = [
        thirds(ay),
        thirds(ax),
        np.concatenate([thirds(bx), thirds(cx)], axis=0),
        np.concatenate([thirds(by), thirds(cy)], axis=0),
    ]
    plane = pltpu.VMEM((mesh_x * mesh_y, LANES), F32)
    vmem = pl.BlockSpec(memory_space=pltpu.VMEM)
    return pl.pallas_call(
        functools.partial(grid_kernel, cycle_x, cycle_y),
        in_specs=[pl.BlockSpec(memory_space=pltpu.SMEM)] + [vmem] * 5,
        out_specs=vmem,
        out_shape=jax.ShapeDtypeStruct((devices, 3, 1, atoms), F32),
        scratch_shapes=[plane] * 5
        + [pltpu.VMEM((devices, 2 * ROWS, atoms), BF16)],
        compiler_params=pltpu.CompilerParams(
            vmem_limit_bytes=5 * mesh_x * mesh_y * LANES * 4
            + devices * atoms * (4 * ROWS + 64)
            + (10 << 20)
        ),
        cost_estimate=pl.CostEstimate(
            flops=8_000_000_000, bytes_accessed=4_000_000, transcendentals=100_000
        ),
        name="grid_fields",
    )(place, gathered, *[jnp.asarray(t) for t in tables])


def edge_kernel(
    list_ref, index_ref, feat_ref, pos_ref, mid_ref, up_ref, down_ref, w_self_ref, w_pair_ref,
    w_radial_ref, w_expand_ref, w_contract_ref, w_final_ref, out_ref,
    table, places, near_a, near_b, near_c, edge_a, edge_b, edge_c, marks, own_ref, sums_ref, w_half,
):
    atoms, channels = feat_ref.shape
    ghosts = mid_ref.shape[1] - EXTRA
    slots_all = atoms + 9 * ghosts
    per_atom = index_ref.shape[0]
    chunk = CHUNK_ATOMS * per_atom
    chunks = atoms // CHUNK_ATOMS
    basis_count = w_radial_ref.shape[0]
    spacing = CUTOFF_SQ / (basis_count - 1)
    latent = w_expand_ref.shape[1]
    width = latent // TILES
    slots = per_atom // PIECES
    w_half[...] = w_expand_ref[...] * 0.5

    def fill(start, rows, coords, shift):
        count = rows.shape[0]
        projected = jnp.dot(rows, w_pair_ref[...], preferred_element_type=F32)
        projected = projected.astype(BF16).astype(F32)
        rows_of = table.reshape(slots_all * 8, LANES)
        rows_of[pl.ds(start * 8, count, stride=8), :] = projected[:, :channels] * 0.5
        rows_of[pl.ds(start * 8 + 1, count, stride=8), :] = projected[:, channels:]
        row = lax.broadcasted_iota(jnp.int32, (8, LANES), 0)
        offset = jnp.where(row == 0, shift[0], jnp.where(row == 1, shift[1], 0.0))
        places[start // LANES] = coords + offset

    pos = jnp.concatenate([pos_ref[...].astype(F32), jnp.zeros((5, atoms), F32)], axis=0)
    for i in range(atoms // LANES):
        rows = feat_ref[pl.ds(i * LANES, LANES), :]
        fill(i * LANES, rows, pos[:, i * LANES : (i + 1) * LANES], (0.0, 0.0))
        own = jnp.dot(rows, w_self_ref[...], preferred_element_type=F32)
        own_ref[pl.ds(i * LANES, LANES), :] = own * 0.5
    for sx in range(3):
        for sy, ref in enumerate((up_ref, mid_ref, down_ref)):
            block = 3 * sx + sy
            if block == 4:
                continue
            tail = ref[sx, pl.ds(ghosts, EXTRA), :].astype(F32)
            for h in range(ghosts // LANES):
                rows = ref[sx, pl.ds(h * LANES, LANES), :]
                start = atoms + block * ghosts + h * LANES
                fill(start, rows, tail[h * 8 : (h + 1) * 8], ((sx - 1) * BOX, (sy - 1) * BOX))

    feature = lax.broadcasted_iota(jnp.int32, (8, LANES), 0)
    skipped = range((atoms + 4 * ghosts) // LANES, (atoms + 5 * ghosts) // LANES)
    for i in range(atoms // LANES):
        columns = slice(i * LANES, (i + 1) * LANES)
        index = index_ref[:, columns]
        inside = index & (LANES - 1)
        outside = lax.shift_right_logical(index, 7)
        found = [jnp.zeros((per_atom, LANES), F32)] * 3
        for c in range(slots_all // LANES):
            if c in skipped:
                continue
            tile = places[c]
            here = outside == c
            for a in range(3):
                source = jnp.broadcast_to(tile[a : a + 1], (per_atom, LANES))
                value = jnp.take_along_axis(source, inside, axis=1)
                found[a] = jnp.where(here, value, found[a])
        disp = [found[a] - pos[a : a + 1, columns] for a in range(3)]
        d2 = disp[0] * disp[0] + disp[1] * disp[1] + disp[2] * disp[2]
        envelope = jnp.maximum(0.0, 1.0 - d2 * (1.0 / CUTOFF_SQ))
        envelope = envelope * envelope
        moments = [envelope] + [envelope * disp[a] for a in range(3)]
        for k in range(per_atom):
            def wide(value):
                return jnp.broadcast_to(value[k : k + 1], (8, LANES))

            t = wide(d2) * (1.0 / spacing) - feature.astype(F32)
            basis = jnp.exp(-(t * t))
            high = basis.astype(BF16).astype(F32)
            tail = jnp.where(feature == 0, wide(moments[0]), 0.0)
            for a in range(3):
                tail = jnp.where(feature == 1 + a, wide(moments[1 + a]), tail)
            stacked = jnp.concatenate([high, basis - high, high, tail], axis=0)
            marks[k, pl.ds(i * LANES, LANES), :] = stacked.T

    w_radial = w_radial_ref[...] * 0.5
    high = w_radial.astype(BF16).astype(F32)
    w_basis = jnp.concatenate(
        [high, high, w_radial - high, jnp.zeros((8, channels), F32)], axis=0
    ).astype(BF16)

    def gather(index, near, part):
        for k in range(part * slots, (part + 1) * slots):
            start = k * atoms + index * CHUNK_ATOMS
            loaded = [table[list_ref[start + a]] for a in range(CHUNK_ATOMS)]
            for a, tile in enumerate(loaded):
                near[pl.ds(k * CHUNK_ATOMS + a, 2, stride=chunk), :] = tile[:2]

    def enter(index, near, edge_in, part):
        first = pl.multiple_of(index * CHUNK_ATOMS, 8)
        rows = pl.ds(part * slots * CHUNK_ATOMS, slots * CHUNK_ATOMS)
        shape = (slots, CHUNK_ATOMS, LANES)
        basis = marks[pl.ds(part * slots, slots), pl.ds(first, CHUNK_ATOMS), :]
        basis = basis.reshape(slots * CHUNK_ATOMS, basis.shape[2]).astype(BF16)
        radial = jnp.dot(basis, w_basis, preferred_element_type=F32).reshape(shape)
        own = own_ref[pl.ds(first, CHUNK_ATOMS), :][None]
        half = radial + own + near[rows, :].reshape(shape)
        turn = jnp.tanh(half.astype(BF16)).astype(F32)
        edge_in[rows, :] = (half + half * turn).astype(BF16).reshape(-1, LANES)

    def network(edge_in, part):
        cols = pl.ds(part * width, width)
        half = jnp.dot(edge_in[...], w_half[:, cols], preferred_element_type=F32).astype(BF16)
        hidden = half + half * jnp.tanh(half)
        return jnp.dot(hidden, w_contract_ref[cols, :], preferred_element_type=F32)

    def collect(index, mixed, near):
        first = pl.multiple_of(index * CHUNK_ATOMS, 8)
        weight = (mixed * near[pl.ds(chunk, chunk), :]).reshape(per_atom, CHUNK_ATOMS, LANES)
        for s in range(4):
            mark = marks[:, pl.ds(first, CHUNK_ATOMS), 3 * basis_count + s : 3 * basis_count + s + 1]
            sums_ref[s, pl.ds(first, CHUNK_ATOMS), :] = jnp.sum(weight * mark, axis=0)

    def stage(index, nears, edges):
        after = jnp.minimum(index + 1, chunks - 1)
        later = jnp.minimum(index + 2, chunks - 1)
        mixed = None
        for part in range(PIECES):
            gather(later, nears[2], part)
            enter(after, nears[1], edges[1], part)
            if part % (PIECES // TILES) == PIECES // TILES - 1:
                term = network(edges[0], part // (PIECES // TILES))
                mixed = term if mixed is None else mixed + term
        collect(index, mixed, nears[0])

    nears = (near_a, near_b, near_c)
    edges = (edge_a, edge_b, edge_c)
    for part in range(PIECES):
        gather(0, near_a, part)
    for part in range(PIECES):
        gather(1, near_b, part)
        enter(0, near_a, edge_a, part)

    def triple(step, carry):
        for i in range(3):
            order = (i, (i + 1) % 3, (i + 2) % 3)
            stage(3 * step + i, [nears[o] for o in order], [edges[o] for o in order])
        return carry

    lax.fori_loop(0, chunks // 3, triple, 0)

    scale = 1.0 / math.sqrt(per_atom)
    vector = [sums_ref[1 + a] * scale for a in range(3)]
    square = vector[0] * vector[0] + vector[1] * vector[1] + vector[2] * vector[2]
    invariant = (sums_ref[0] * scale + square * (1.0 / 3.0)).astype(BF16)
    gate = jnp.dot(invariant, w_final_ref[...], preferred_element_type=F32)
    gate = gate * (0.5 + 0.5 * jnp.tanh(0.5 * gate)) * (1.0 / math.sqrt(channels))
    ones = jnp.ones((8, channels), F32)
    for a in range(3):
        out_ref[a] = contract_last(ones, vector[a] * gate, HIGHEST)[:1]


def edge_forces(lists, index, feat, pos, mid, up, down, w_self, w_pair, w_radial, w_expand, w_contract, w_final):
    atoms, channels = feat.shape
    per_atom = index.shape[0]
    ghosts = mid.shape[1] - EXTRA
    slots_all = atoms + 9 * ghosts
    chunk = CHUNK_ATOMS * per_atom
    vmem = pl.BlockSpec(memory_space=pltpu.VMEM)
    edges = atoms * per_atom
    latent = w_expand.shape[1]
    return pl.pallas_call(
        edge_kernel,
        in_specs=[pl.BlockSpec(memory_space=pltpu.SMEM)] + [vmem] * 12,
        out_specs=vmem,
        out_shape=jax.ShapeDtypeStruct((3, 1, atoms), F32),
        scratch_shapes=[
            pltpu.VMEM((slots_all, 8, LANES), F32),
            pltpu.VMEM((slots_all // LANES, 8, LANES), F32),
        ]
        + [pltpu.VMEM((2 * chunk, LANES), F32)] * 3
        + [pltpu.VMEM((chunk, LANES), BF16)] * 3
        + [
            pltpu.VMEM((per_atom, atoms, 32), F32),
            pltpu.VMEM((atoms, LANES), F32),
            pltpu.VMEM((4, atoms, LANES), F32),
            pltpu.VMEM(w_expand.shape, BF16),
        ],
        compiler_params=pltpu.CompilerParams(vmem_limit_bytes=32 << 20),
        cost_estimate=pl.CostEstimate(
            flops=4 * edges * channels * latent,
            bytes_accessed=4_000_000,
            transcendentals=edges * latent,
        ),
        name="edge_forces",
    )(
        lists, index, feat, pos, mid, up, down, w_self, w_pair, w_radial,
        w_expand, w_contract, w_final,
    )


def ring(array, axis, step):
    size = lax.axis_size(axis)
    return lax.ppermute(array, axis, [(i, (i + step) % size) for i in range(size)])


def shards(
    features, positions, atom_count, ghost_index, neighbour_list, cell_index, w_self, w_pair,
    w_radial, w_expand, w_contract, w_final, w_charge,
):
    feat = features[0, 0]
    pos = positions[0, 0]
    cycle_x, cycle_y = (lax.axis_size("dx"), lax.axis_size("dy"))
    exported, spread = prepare(
        cycle_x * cycle_y, atom_count, feat, pos, ghost_index[0, 0], cell_index[0, 0], w_charge
    )
    gathered = lax.all_to_all(spread, ("dx", "dy"), split_axis=0, concat_axis=0, tiled=True)
    mid = jnp.stack([ring(exported, "dx", 1), exported, ring(exported, "dx", -1)])
    index = neighbour_list[0, 0].T
    lists = index.reshape(-1)
    gathered, mid, lists = lax.optimization_barrier((gathered, mid, lists))
    up = ring(mid, "dy", 1)
    down = ring(mid, "dy", -1)
    place = lax.axis_index("dx") * cycle_y + lax.axis_index("dy")
    partial = grid_fields(place[None].astype(jnp.int32), gathered, cycle_x, cycle_y)
    received = lax.all_to_all(partial, ("dx", "dy"), split_axis=0, concat_axis=0, tiled=True)
    short = edge_forces(
        lists, index, feat, pos, mid, up, down, w_self, w_pair, w_radial, w_expand,
        w_contract, w_final,
    )
    field = jnp.sum(received, axis=0)
    total = short + spread[0, :1] * field
    live = lax.broadcasted_iota(jnp.int32, (1, feat.shape[0]), 1) < atom_count[0, 0]
    return jnp.where(live, total, jnp.zeros_like(total)).transpose(1, 0, 2)[None]


def solution(mesh):
    placed = (
        P("dx", "dy", None, None),
        P("dx", "dy", None, None),
        P("dx", "dy"),
        P("dx", "dy", None),
        P("dx", "dy", None, None),
        P("dx", "dy", None),
    ) + (P(),) * 7
    return jax.shard_map(
        shards, mesh=mesh, in_specs=placed, out_specs=P("dx", "dy", None, None), check_vma=False
    )
```

```python
import functools
import math

import jax
import jax.numpy as jnp
import numpy as np
from jax import lax
from jax.experimental import pallas as pl
from jax.experimental.pallas import tpu as pltpu
from jax.sharding import PartitionSpec as P

GRID_X = 8
GRID_Y = 8
GRID_Z = 1024
BOX = 1.0
CUTOFF_SQ = 6.25
SMEARING = 1.0

LANES = 128
EXTRA = 16
ROWS = 32
GROUPS = LANES // ROWS
CHUNK_ATOMS = 16
PIECES = 4
TILES = 2
HIGHEST = lax.Precision.HIGHEST
F32 = jnp.float32
BF16 = jnp.bfloat16


def contract_first(a, b, precision=None):
    return lax.dot_general(
        a, b, (((0,), (0,)), ((), ())), precision=precision, preferred_element_type=F32
    )


def contract_last(a, b, precision=None):
    return lax.dot_general(
        a, b, (((1,), (1,)), ((), ())), precision=precision, preferred_element_type=F32
    )


def charge_kernel(count_ref, feat_ref, cell_ref, wq_ref, qc_ref):
    atoms = feat_ref.shape[0]
    weights = jnp.broadcast_to(wq_ref[...].astype(F32), (16, LANES)).astype(BF16)
    charge = contract_last(weights, feat_ref[...])[:1]
    live = lax.broadcasted_iota(jnp.int32, (1, atoms), 1) < count_ref[0, 0]
    both = jnp.concatenate([jnp.where(live, charge, 0.0), cell_ref[...].astype(F32)], axis=0)
    qc_ref[...] = jnp.broadcast_to(both[None], qc_ref.shape)


def export_kernel(feat_ref, pos_ref, export_ref, after_ref, out_ref):
    atoms = feat_ref.shape[0]
    ghosts = export_ref.shape[1]
    pick = lax.broadcasted_iota(jnp.int32, (atoms, ghosts), 0) == export_ref[...]
    pick = jnp.where(pick, 1.0, 0.0).astype(BF16)
    out_ref[pl.ds(0, ghosts), :] = contract_first(pick, feat_ref[...]).astype(BF16)
    pos = jnp.concatenate([pos_ref[...].astype(F32), jnp.zeros((13, atoms), F32)], axis=0)
    coords = jnp.dot(pos.astype(BF16), pick, preferred_element_type=F32)
    tail = [coords[:8, h * LANES : (h + 1) * LANES] for h in range(ghosts // LANES)]
    out_ref[pl.ds(ghosts, EXTRA), :] = jnp.concatenate(tail, axis=0).astype(BF16)


def charges(devices, count, feat, cells, w_charge):
    vmem = pl.BlockSpec(memory_space=pltpu.VMEM)
    return pl.pallas_call(
        charge_kernel,
        in_specs=[pl.BlockSpec(memory_space=pltpu.SMEM)] + [vmem] * 3,
        out_specs=vmem,
        out_shape=jax.ShapeDtypeStruct((devices, 2, feat.shape[0]), F32),
        compiler_params=pltpu.CompilerParams(vmem_limit_bytes=16 << 20),
        name="charges",
    )(count, feat, cells[None], w_charge[None])


def exports_after(after, feat, pos, exports):
    vmem = pl.BlockSpec(memory_space=pltpu.VMEM)
    return pl.pallas_call(
        export_kernel,
        in_specs=[vmem] * 3 + [pl.BlockSpec(memory_space=pl.ANY)],
        out_specs=vmem,
        out_shape=jax.ShapeDtypeStruct((exports.shape[0] + EXTRA, feat.shape[1]), BF16),
        compiler_params=pltpu.CompilerParams(vmem_limit_bytes=16 << 20),
        name="exports",
    )(feat, pos, exports[None], after)


def real_tables(count):
    half = count // 2
    index = np.arange(count)
    freq = np.where(index <= half, index, index - half)
    place = np.arange(count)
    angle = 2.0 * np.pi * (freq[:, None] * place[None, :] % count) / count
    is_cos = (index <= half)[:, None]
    basis = np.where(is_cos, np.cos(angle), np.sin(angle))
    weight = np.where((index == 0) | (index == half), 1.0, 2.0)[:, None] / count
    wave = np.where(index == half, 0.0, 2.0 * np.pi * freq / count)[:, None]
    slope = np.where(is_cos, np.sin(angle), -np.cos(angle)) * wave
    return (basis, (weight * basis).T, (weight * slope).T)


def thirds(table):
    whole = table.astype(np.float32)
    high = whole.astype(BF16).astype(np.float32)
    low = (whole - high).astype(BF16).astype(np.float32)
    return np.concatenate([high, high, low], axis=1)


def sine_half(t):
    x = t * (math.pi / 512.0)
    s = x * x
    p = -2.50521084e-08
    p = p * s + 2.75573192e-06
    p = p * s - 1.98412698e-04
    p = p * s + 8.33333333e-03
    p = p * s - 1.66666667e-01
    return x + x * (s * p)


def grid_kernel(
    cycle_x, cycle_y, place_ref, qc_ref, fy_ref, fx_ref, ix_ref, iy_ref, out_ref,
    buf_a, buf_b, buf_c, buf_d, buf_e, trig_ref,
):
    mesh_x, mesh_y, mesh_z = (GRID_X * cycle_x, GRID_Y * cycle_y, GRID_Z)
    devices = cycle_x * cycle_y
    modes = mesh_z // 2 // devices
    coefs = 2 * modes
    first = place_ref[0] * modes
    columns = GRID_X * GRID_Y
    atoms = qc_ref.shape[2]

    row = lax.broadcasted_iota(jnp.int32, (ROWS, 1), 0) % coefs
    row_mode = first + row % modes
    row_sine = row >= modes
    row_edge = row_sine & (row_mode == 0)
    row_factor = jnp.where(row_edge, mesh_z // 2, row_mode)
    row_shift = jnp.where(row_sine & (row_mode != 0), mesh_z // 4, 0)
    column_iota = lax.broadcasted_iota(jnp.int32, (columns, atoms), 0)

    def columns_of(device):
        cell = qc_ref[device, 1:2, :].astype(jnp.int32)
        return cell, column_iota == lax.shift_right_logical(cell, 10)

    def spread(device, carry):
        cell, match = columns_of(device)
        depth = cell & (mesh_z - 1)
        turn = (row_factor * depth - row_shift) & (mesh_z - 1)
        trig = sine_half((jnp.abs(turn - mesh_z // 2) - mesh_z // 4).astype(F32))
        high = trig.astype(BF16)
        trig_ref[device, pl.ds(0, ROWS), :] = high
        trig_ref[device, pl.ds(ROWS, ROWS), :] = (trig - high.astype(F32)).astype(BF16)
        charged = trig * qc_ref[device, 0:1, :]
        high = charged.astype(BF16)
        low = (charged - high.astype(F32)).astype(BF16)
        pick = jnp.where(match, 1.0, 0.0).astype(BF16)
        total = contract_last(pick, jnp.concatenate([high, low] * (LANES // ROWS // 2), axis=0))
        total = total + pltpu.roll(total, ROWS, 1)
        buf_a[pl.ds(pl.multiple_of(device * columns, 8), columns), :] = total
        return carry

    lax.fori_loop(0, devices, spread, 0, unroll=8)

    lane = lax.broadcasted_iota(jnp.int32, (1, LANES), 1)
    lane_group = lane // ROWS

    def pack(copied):
        wide = copied[0]
        for g in range(1, GROUPS):
            wide = jnp.where(lane_group == g, copied[g], wide)
        return wide

    def unpack(wide):
        turned = [wide] + [pltpu.roll(wide, g * ROWS, 1) for g in range(1, GROUPS)]
        copied = []
        for i in range(GROUPS):
            copied.append(pack([turned[(g - i) % GROUPS] for g in range(GROUPS)]))
        return copied

    def apply(table_ref, wide):
        high = wide.astype(BF16)
        low = (wide - high.astype(F32)).astype(BF16)
        data = jnp.concatenate([high, low, high], axis=0)
        return jnp.dot(table_ref[...].astype(BF16), data, preferred_element_type=F32)

    for first_x in range(0, mesh_x, GROUPS):
        copied = []
        for place in range(first_x, first_x + GROUPS):
            rows = []
            for sy in range(cycle_y):
                start = ((place // GRID_X) * cycle_y + sy) * columns + (place % GRID_X) * GRID_Y
                rows.append(buf_a[pl.ds(start, GRID_Y), :])
            copied.append(jnp.concatenate(rows, axis=0))
        for i, part in enumerate(unpack(apply(fy_ref, pack(copied)))):
            buf_b[pl.ds((first_x + i) * mesh_y, mesh_y), :] = part

    lane_coef = lane % ROWS % coefs
    lane_mode = first + lane_coef % modes
    lane_sine = lane_coef >= modes
    lane_freq = jnp.where(lane_sine & (lane_mode == 0), mesh_z // 2, lane_mode)
    wave_z = lane_freq.astype(F32) * (2.0 * math.pi / mesh_z)
    lane_weight = jnp.where(lane_mode == 0, 1.0, 2.0) / mesh_z
    slope_z = jnp.where(lane_mode == 0, 0.0, wave_z) * jnp.where(lane_sine, 1.0, -1.0)
    freq_x = lax.broadcasted_iota(jnp.int32, (mesh_x, 1), 0)
    freq_x = jnp.where(freq_x <= mesh_x // 2, freq_x, freq_x - mesh_x // 2)
    wave_x = freq_x.astype(F32) * (2.0 * math.pi / mesh_x)
    near = wave_x * wave_x + wave_z * wave_z

    for first_y in range(0, mesh_y, GROUPS):
        copied = [
            buf_b[pl.ds(first_y + i, mesh_x, stride=mesh_y), :] for i in range(GROUPS)
        ]
        spectrum = apply(fx_ref, pack(copied))
        freq_y = first_y + lane_group
        freq_y = jnp.where(freq_y <= mesh_y // 2, freq_y, freq_y - mesh_y // 2)
        wave_y = freq_y.astype(F32) * (2.0 * math.pi / mesh_y)
        wave_sq = near + wave_y * wave_y
        zero = wave_sq == 0.0
        green = jnp.exp(-0.5 * SMEARING * SMEARING * wave_sq) / jnp.where(zero, 1.0, wave_sq)
        green = jnp.where(zero, 0.0, 4.0 * math.pi * green)
        both = apply(ix_ref, spectrum * (green * lane_weight))
        for i, part in enumerate(unpack(both)):
            rows = pl.ds((first_y + i) * mesh_x, mesh_x)
            buf_a[rows, :] = part[:mesh_x]
            buf_c[rows, :] = part[mesh_x:]

    for first_x in range(0, mesh_x, GROUPS):
        plain, sloped = (
            pack([buf[pl.ds(first_x + i, mesh_y, stride=mesh_x), :] for i in range(GROUPS)])
            for buf in (buf_a, buf_c)
        )
        both = apply(iy_ref, plain)
        along_x = apply(iy_ref.at[pl.ds(0, mesh_y), :], sloped)
        potential = both[:mesh_y]
        partner = jnp.where(
            lane % ROWS >= modes,
            pltpu.roll(potential, modes, 1),
            pltpu.roll(potential, LANES - modes, 1),
        )
        fields = (along_x, both[mesh_y:], partner * slope_z)
        for buf, wide in zip((buf_b, buf_d, buf_e), fields):
            for i, part in enumerate(unpack(wide)):
                buf[pl.ds((first_x + i) * mesh_y, mesh_y), :] = part

    use_low = (lane // ROWS) == 1
    use_none = (lane % ROWS) >= coefs

    def sample(device, carry):
        _, match = columns_of(device)
        rows = []
        for buf in (buf_b, buf_d, buf_e):
            for lx in range(GRID_X):
                place = (device // cycle_y) * GRID_X + lx
                start = place * mesh_y + (device % cycle_y) * GRID_Y
                rows.append(buf[pl.ds(pl.multiple_of(start, 8), GRID_Y), :])
        data = jnp.concatenate(rows, axis=0)
        high = data.astype(BF16).astype(F32)
        mixed = jnp.where(use_low, data - high, high)
        mixed = jnp.where(use_none, 0.0, mixed).astype(BF16)
        high = trig_ref[device, pl.ds(0, ROWS), :]
        low = trig_ref[device, pl.ds(ROWS, ROWS), :]
        waves = jnp.concatenate([high, high, low, jnp.zeros_like(low)], axis=0)
        fields = jnp.dot(mixed, waves, preferred_element_type=F32)
        picked = []
        for a in range(3):
            part = jnp.where(match, fields[a * columns : (a + 1) * columns], 0.0)
            picked.append(jnp.sum(part, axis=0, keepdims=True))
        for a in range(3):
            out_ref[device, a] = picked[a]
        return carry

    lax.fori_loop(0, devices, sample, 0, unroll=8)


def grid_fields(place, gathered, cycle_x, cycle_y):
    mesh_x, mesh_y = (GRID_X * cycle_x, GRID_Y * cycle_y)
    devices, _, atoms = gathered.shape
    ax, bx, cx = real_tables(mesh_x)
    ay, by, cy = real_tables(mesh_y)
    tables = [
        thirds(ay),
        thirds(ax),
        np.concatenate([thirds(bx), thirds(cx)], axis=0),
        np.concatenate([thirds(by), thirds(cy)], axis=0),
    ]
    plane = pltpu.VMEM((mesh_x * mesh_y, LANES), F32)
    vmem = pl.BlockSpec(memory_space=pltpu.VMEM)
    return pl.pallas_call(
        functools.partial(grid_kernel, cycle_x, cycle_y),
        in_specs=[pl.BlockSpec(memory_space=pltpu.SMEM)] + [vmem] * 5,
        out_specs=vmem,
        out_shape=jax.ShapeDtypeStruct((devices, 3, 1, atoms), F32),
        scratch_shapes=[plane] * 5
        + [pltpu.VMEM((devices, 2 * ROWS, atoms), BF16)],
        compiler_params=pltpu.CompilerParams(
            vmem_limit_bytes=5 * mesh_x * mesh_y * LANES * 4
            + devices * atoms * (4 * ROWS + 64)
            + (10 << 20)
        ),
        cost_estimate=pl.CostEstimate(
            flops=8_000_000_000, bytes_accessed=4_000_000, transcendentals=100_000
        ),
        name="grid_fields",
    )(place, gathered, *[jnp.asarray(t) for t in tables])


def edge_kernel(
    list_ref, index_ref, feat_ref, pos_ref, mid_ref, up_ref, down_ref, w_self_ref, w_pair_ref,
    w_radial_ref, w_expand_ref, w_contract_ref, w_final_ref, out_ref,
    table, places, near_a, near_b, near_c, edge_a, edge_b, edge_c, marks, own_ref, sums_ref,
):
    atoms, channels = feat_ref.shape
    ghosts = mid_ref.shape[1] - EXTRA
    slots_all = atoms + 9 * ghosts
    per_atom = index_ref.shape[0]
    chunk = CHUNK_ATOMS * per_atom
    chunks = atoms // CHUNK_ATOMS
    basis_count = w_radial_ref.shape[0]
    spacing = CUTOFF_SQ / (basis_count - 1)
    latent = w_expand_ref.shape[1]
    width = latent // TILES
    slots = per_atom // PIECES

    def fill(start, rows, coords, shift):
        count = rows.shape[0]
        projected = jnp.dot(rows, w_pair_ref[...], preferred_element_type=F32)
        projected = projected.astype(BF16).astype(F32)
        rows_of = table.reshape(slots_all * 8, LANES)
        rows_of[pl.ds(start * 8, count, stride=8), :] = projected[:, :channels] * 0.5
        rows_of[pl.ds(start * 8 + 1, count, stride=8), :] = projected[:, channels:]
        row = lax.broadcasted_iota(jnp.int32, (8, LANES), 0)
        offset = jnp.where(row == 0, shift[0], jnp.where(row == 1, shift[1], 0.0))
        places[start // LANES] = coords + offset

    pos = jnp.concatenate([pos_ref[...].astype(F32), jnp.zeros((5, atoms), F32)], axis=0)
    for i in range(atoms // LANES):
        rows = feat_ref[pl.ds(i * LANES, LANES), :]
        fill(i * LANES, rows, pos[:, i * LANES : (i + 1) * LANES], (0.0, 0.0))
        own = jnp.dot(rows, w_self_ref[...], preferred_element_type=F32)
        own_ref[pl.ds(i * LANES, LANES), :] = own * 0.5
    for sx in range(3):
        for sy, ref in enumerate((up_ref, mid_ref, down_ref)):
            block = 3 * sx + sy
            if block == 4:
                continue
            tail = ref[sx, pl.ds(ghosts, EXTRA), :].astype(F32)
            for h in range(ghosts // LANES):
                rows = ref[sx, pl.ds(h * LANES, LANES), :]
                start = atoms + block * ghosts + h * LANES
                fill(start, rows, tail[h * 8 : (h + 1) * 8], ((sx - 1) * BOX, (sy - 1) * BOX))

    feature = lax.broadcasted_iota(jnp.int32, (8, LANES), 0)
    skipped = range((atoms + 4 * ghosts) // LANES, (atoms + 5 * ghosts) // LANES)
    for i in range(atoms // LANES):
        columns = slice(i * LANES, (i + 1) * LANES)
        index = index_ref[:, columns]
        inside = index & (LANES - 1)
        outside = lax.shift_right_logical(index, 7)
        found = [jnp.zeros((per_atom, LANES), F32)] * 3
        for c in range(slots_all // LANES):
            if c in skipped:
                continue
            tile = places[c]
            here = outside == c
            for a in range(3):
                source = jnp.broadcast_to(tile[a : a + 1], (per_atom, LANES))
                value = jnp.take_along_axis(source, inside, axis=1)
                found[a] = jnp.where(here, value, found[a])
        disp = [found[a] - pos[a : a + 1, columns] for a in range(3)]
        d2 = disp[0] * disp[0] + disp[1] * disp[1] + disp[2] * disp[2]
        envelope = jnp.maximum(0.0, 1.0 - d2 * (1.0 / CUTOFF_SQ))
        envelope = envelope * envelope
        moments = [envelope] + [envelope * disp[a] for a in range(3)]
        for k in range(per_atom):
            def wide(value):
                return jnp.broadcast_to(value[k : k + 1], (8, LANES))

            t = wide(d2) * (1.0 / spacing) - feature.astype(F32)
            basis = jnp.exp(-(t * t))
            high = basis.astype(BF16).astype(F32)
            tail = jnp.where(feature == 0, wide(moments[0]), 0.0)
            for a in range(3):
                tail = jnp.where(feature == 1 + a, wide(moments[1 + a]), tail)
            stacked = jnp.concatenate([high, basis - high, high, tail], axis=0)
            marks[k, pl.ds(i * LANES, LANES), :] = stacked.T

    w_radial = w_radial_ref[...] * 0.5
    high = w_radial.astype(BF16).astype(F32)
    w_basis = jnp.concatenate(
        [high, high, w_radial - high, jnp.zeros((8, channels), F32)], axis=0
    ).astype(BF16)

    def gather(index, near, part):
        for k in range(part * slots, (part + 1) * slots):
            start = k * atoms + index * CHUNK_ATOMS
            loaded = [table[list_ref[start + a]] for a in range(CHUNK_ATOMS)]
            for a, tile in enumerate(loaded):
                near[pl.ds(k * CHUNK_ATOMS + a, 2, stride=chunk), :] = tile[:2]

    def enter(index, near, edge_in, part):
        first = pl.multiple_of(index * CHUNK_ATOMS, 8)
        rows = pl.ds(part * slots * CHUNK_ATOMS, slots * CHUNK_ATOMS)
        shape = (slots, CHUNK_ATOMS, LANES)
        basis = marks[pl.ds(part * slots, slots), pl.ds(first, CHUNK_ATOMS), :]
        basis = basis.reshape(slots * CHUNK_ATOMS, basis.shape[2]).astype(BF16)
        radial = jnp.dot(basis, w_basis, preferred_element_type=F32).reshape(shape)
        own = own_ref[pl.ds(first, CHUNK_ATOMS), :][None]
        half = radial + own + near[rows, :].reshape(shape)
        turn = jnp.tanh(half.astype(BF16)).astype(F32)
        edge_in[rows, :] = (half + half * turn).astype(BF16).reshape(-1, LANES)

    def network(edge_in, part):
        cols = pl.ds(part * width, width)
        full = jnp.dot(edge_in[...], w_expand_ref[:, cols], preferred_element_type=F32)
        decay = jnp.exp(jnp.minimum(-full, 80.0))
        hidden = (full * pl.reciprocal(1.0 + decay, approx=True)).astype(BF16)
        return jnp.dot(hidden, w_contract_ref[cols, :], preferred_element_type=F32)

    def collect(index, mixed, near):
        first = pl.multiple_of(index * CHUNK_ATOMS, 8)
        weight = (mixed * near[pl.ds(chunk, chunk), :]).reshape(per_atom, CHUNK_ATOMS, LANES)
        for s in range(4):
            mark = marks[:, pl.ds(first, CHUNK_ATOMS), 3 * basis_count + s : 3 * basis_count + s + 1]
            sums_ref[s, pl.ds(first, CHUNK_ATOMS), :] = jnp.sum(weight * mark, axis=0)

    def stage(index, nears, edges):
        after = jnp.minimum(index + 1, chunks - 1)
        later = jnp.minimum(index + 2, chunks - 1)
        mixed = None
        for part in range(PIECES):
            gather(later, nears[2], part)
            enter(after, nears[1], edges[1], part)
            if part % (PIECES // TILES) == PIECES // TILES - 1:
                term = network(edges[0], part // (PIECES // TILES))
                mixed = term if mixed is None else mixed + term
        collect(index, mixed, nears[0])

    nears = (near_a, near_b, near_c)
    edges = (edge_a, edge_b, edge_c)
    for part in range(PIECES):
        gather(0, near_a, part)
    for part in range(PIECES):
        gather(1, near_b, part)
        enter(0, near_a, edge_a, part)

    def triple(step, carry):
        for i in range(3):
            order = (i, (i + 1) % 3, (i + 2) % 3)
            stage(3 * step + i, [nears[o] for o in order], [edges[o] for o in order])
        return carry

    lax.fori_loop(0, chunks // 3, triple, 0)

    scale = 1.0 / math.sqrt(per_atom)
    vector = [sums_ref[1 + a] * scale for a in range(3)]
    square = vector[0] * vector[0] + vector[1] * vector[1] + vector[2] * vector[2]
    invariant = (sums_ref[0] * scale + square * (1.0 / 3.0)).astype(BF16)
    gate = jnp.dot(invariant, w_final_ref[...], preferred_element_type=F32)
    gate = gate * (0.5 + 0.5 * jnp.tanh(0.5 * gate)) * (1.0 / math.sqrt(channels))
    ones = jnp.ones((8, channels), F32)
    for a in range(3):
        out_ref[a] = contract_last(ones, vector[a] * gate, HIGHEST)[:1]


def edge_forces(lists, index, feat, pos, mid, up, down, w_self, w_pair, w_radial, w_expand, w_contract, w_final):
    atoms, channels = feat.shape
    per_atom = index.shape[0]
    ghosts = mid.shape[1] - EXTRA
    slots_all = atoms + 9 * ghosts
    chunk = CHUNK_ATOMS * per_atom
    vmem = pl.BlockSpec(memory_space=pltpu.VMEM)
    edges = atoms * per_atom
    latent = w_expand.shape[1]
    return pl.pallas_call(
        edge_kernel,
        in_specs=[pl.BlockSpec(memory_space=pltpu.SMEM)] + [vmem] * 12,
        out_specs=vmem,
        out_shape=jax.ShapeDtypeStruct((3, 1, atoms), F32),
        scratch_shapes=[
            pltpu.VMEM((slots_all, 8, LANES), F32),
            pltpu.VMEM((slots_all // LANES, 8, LANES), F32),
        ]
        + [pltpu.VMEM((2 * chunk, LANES), F32)] * 3
        + [pltpu.VMEM((chunk, LANES), BF16)] * 3
        + [
            pltpu.VMEM((per_atom, atoms, 32), F32),
            pltpu.VMEM((atoms, LANES), F32),
            pltpu.VMEM((4, atoms, LANES), F32),
        ],
        compiler_params=pltpu.CompilerParams(vmem_limit_bytes=32 << 20),
        cost_estimate=pl.CostEstimate(
            flops=4 * edges * channels * latent,
            bytes_accessed=4_000_000,
            transcendentals=edges * latent,
        ),
        name="edge_forces",
    )(
        lists, index, feat, pos, mid, up, down, w_self, w_pair, w_radial,
        w_expand, w_contract, w_final,
    )


def ring(array, axis, step):
    size = lax.axis_size(axis)
    return lax.ppermute(array, axis, [(i, (i + step) % size) for i in range(size)])


def shards(
    features, positions, atom_count, ghost_index, neighbour_list, cell_index, w_self, w_pair,
    w_radial, w_expand, w_contract, w_final, w_charge,
):
    feat = features[0, 0]
    pos = positions[0, 0]
    cycle_x, cycle_y = (lax.axis_size("dx"), lax.axis_size("dy"))
    spread = charges(cycle_x * cycle_y, atom_count, feat, cell_index[0, 0], w_charge)
    exported = exports_after(spread, feat, pos, ghost_index[0, 0])
    gathered = lax.all_to_all(spread, ("dx", "dy"), split_axis=0, concat_axis=0, tiled=True)
    mid = jnp.stack([ring(exported, "dx", 1), exported, ring(exported, "dx", -1)])
    index = neighbour_list[0, 0].T
    lists = index.reshape(-1)
    gathered, mid, lists = lax.optimization_barrier((gathered, mid, lists))
    up = ring(mid, "dy", 1)
    down = ring(mid, "dy", -1)
    place = lax.axis_index("dx") * cycle_y + lax.axis_index("dy")
    partial = grid_fields(place[None].astype(jnp.int32), gathered, cycle_x, cycle_y)
    received = lax.all_to_all(partial, ("dx", "dy"), split_axis=0, concat_axis=0, tiled=True)
    short = edge_forces(
        lists, index, feat, pos, mid, up, down, w_self, w_pair, w_radial, w_expand,
        w_contract, w_final,
    )
    field = jnp.sum(received, axis=0)
    total = short + spread[0, :1] * field
    live = lax.broadcasted_iota(jnp.int32, (1, feat.shape[0]), 1) < atom_count[0, 0]
    return jnp.where(live, total, jnp.zeros_like(total)).transpose(1, 0, 2)[None]


def solution(mesh):
    placed = (
        P("dx", "dy", None, None),
        P("dx", "dy", None, None),
        P("dx", "dy"),
        P("dx", "dy", None),
        P("dx", "dy", None, None),
        P("dx", "dy", None),
    ) + (P(),) * 7
    return jax.shard_map(
        shards, mesh=mesh, in_specs=placed, out_specs=P("dx", "dy", None, None), check_vma=False
    )
```

```python
import functools
import math

import jax
import jax.numpy as jnp
import numpy as np
from jax import lax
from jax.experimental import pallas as pl
from jax.experimental.pallas import tpu as pltpu
from jax.sharding import PartitionSpec as P

GRID_X = 8
GRID_Y = 8
GRID_Z = 1024
BOX = 1.0
CUTOFF_SQ = 6.25
SMEARING = 1.0

LANES = 128
EXTRA = 16
ROWS = 32
GROUPS = LANES // ROWS
CHUNK_ATOMS = 16
PIECES = 4
HIGHEST = lax.Precision.HIGHEST
F32 = jnp.float32
BF16 = jnp.bfloat16


def contract_first(a, b, precision=None):
    return lax.dot_general(
        a, b, (((0,), (0,)), ((), ())), precision=precision, preferred_element_type=F32
    )


def contract_last(a, b, precision=None):
    return lax.dot_general(
        a, b, (((1,), (1,)), ((), ())), precision=precision, preferred_element_type=F32
    )


def charge_kernel(count_ref, feat_ref, cell_ref, wq_ref, qc_ref):
    atoms = feat_ref.shape[0]
    weights = jnp.broadcast_to(wq_ref[...].astype(F32), (16, LANES)).astype(BF16)
    charge = contract_last(weights, feat_ref[...])[:1]
    live = lax.broadcasted_iota(jnp.int32, (1, atoms), 1) < count_ref[0, 0]
    both = jnp.concatenate([jnp.where(live, charge, 0.0), cell_ref[...].astype(F32)], axis=0)
    qc_ref[...] = jnp.broadcast_to(both[None], qc_ref.shape)


def export_kernel(feat_ref, pos_ref, export_ref, after_ref, out_ref):
    atoms = feat_ref.shape[0]
    ghosts = export_ref.shape[1]
    pick = lax.broadcasted_iota(jnp.int32, (atoms, ghosts), 0) == export_ref[...]
    pick = jnp.where(pick, 1.0, 0.0).astype(BF16)
    out_ref[pl.ds(0, ghosts), :] = contract_first(pick, feat_ref[...]).astype(BF16)
    pos = jnp.concatenate([pos_ref[...].astype(F32), jnp.zeros((13, atoms), F32)], axis=0)
    coords = jnp.dot(pos.astype(BF16), pick, preferred_element_type=F32)
    tail = [coords[:8, h * LANES : (h + 1) * LANES] for h in range(ghosts // LANES)]
    out_ref[pl.ds(ghosts, EXTRA), :] = jnp.concatenate(tail, axis=0).astype(BF16)


def charges(devices, count, feat, cells, w_charge):
    vmem = pl.BlockSpec(memory_space=pltpu.VMEM)
    return pl.pallas_call(
        charge_kernel,
        in_specs=[pl.BlockSpec(memory_space=pltpu.SMEM)] + [vmem] * 3,
        out_specs=vmem,
        out_shape=jax.ShapeDtypeStruct((devices, 2, feat.shape[0]), F32),
        compiler_params=pltpu.CompilerParams(vmem_limit_bytes=60 << 20),
        name="charges",
    )(count, feat, cells[None], w_charge[None])


def exports_after(after, feat, pos, exports):
    vmem = pl.BlockSpec(memory_space=pltpu.VMEM)
    return pl.pallas_call(
        export_kernel,
        in_specs=[vmem] * 3 + [pl.BlockSpec(memory_space=pl.ANY)],
        out_specs=vmem,
        out_shape=jax.ShapeDtypeStruct((exports.shape[0] + EXTRA, feat.shape[1]), BF16),
        compiler_params=pltpu.CompilerParams(vmem_limit_bytes=16 << 20),
        name="exports",
    )(feat, pos, exports[None], after)


def real_tables(count):
    half = count // 2
    index = np.arange(count)
    freq = np.where(index <= half, index, index - half)
    place = np.arange(count)
    angle = 2.0 * np.pi * (freq[:, None] * place[None, :] % count) / count
    is_cos = (index <= half)[:, None]
    basis = np.where(is_cos, np.cos(angle), np.sin(angle))
    weight = np.where((index == 0) | (index == half), 1.0, 2.0)[:, None] / count
    wave = np.where(index == half, 0.0, 2.0 * np.pi * freq / count)[:, None]
    slope = np.where(is_cos, np.sin(angle), -np.cos(angle)) * wave
    return (basis, (weight * basis).T, (weight * slope).T)


def thirds(table):
    whole = table.astype(np.float32)
    high = whole.astype(BF16).astype(np.float32)
    low = (whole - high).astype(BF16).astype(np.float32)
    return np.concatenate([high, high, low], axis=1)


def sine_half(t):
    x = t * (math.pi / 512.0)
    s = x * x
    p = -2.50521084e-08
    p = p * s + 2.75573192e-06
    p = p * s - 1.98412698e-04
    p = p * s + 8.33333333e-03
    p = p * s - 1.66666667e-01
    return x + x * (s * p)


def grid_kernel(
    cycle_x, cycle_y, place_ref, qc_ref, fy_ref, fx_ref, ix_ref, iy_ref, out_ref,
    buf_a, buf_b, buf_c, buf_d, buf_e, trig_ref,
):
    mesh_x, mesh_y, mesh_z = (GRID_X * cycle_x, GRID_Y * cycle_y, GRID_Z)
    devices = cycle_x * cycle_y
    modes = mesh_z // 2 // devices
    coefs = 2 * modes
    first = place_ref[0] * modes
    columns = GRID_X * GRID_Y
    atoms = qc_ref.shape[2]

    row = lax.broadcasted_iota(jnp.int32, (ROWS, 1), 0) % coefs
    row_mode = first + row % modes
    row_sine = row >= modes
    row_edge = row_sine & (row_mode == 0)
    row_factor = jnp.where(row_edge, mesh_z // 2, row_mode)
    row_shift = jnp.where(row_sine & (row_mode != 0), mesh_z // 4, 0)
    column_iota = lax.broadcasted_iota(jnp.int32, (columns, atoms), 0)

    def columns_of(device):
        cell = qc_ref[device, 1:2, :].astype(jnp.int32)
        return cell, column_iota == lax.shift_right_logical(cell, 10)

    def spread(device, carry):
        cell, match = columns_of(device)
        depth = cell & (mesh_z - 1)
        turn = (row_factor * depth - row_shift) & (mesh_z - 1)
        trig = sine_half((jnp.abs(turn - mesh_z // 2) - mesh_z // 4).astype(F32))
        high = trig.astype(BF16)
        trig_ref[device, pl.ds(0, ROWS), :] = high
        trig_ref[device, pl.ds(ROWS, ROWS), :] = (trig - high.astype(F32)).astype(BF16)
        charged = trig * qc_ref[device, 0:1, :]
        high = charged.astype(BF16)
        low = (charged - high.astype(F32)).astype(BF16)
        pick = jnp.where(match, 1.0, 0.0).astype(BF16)
        total = contract_last(pick, jnp.concatenate([high, low] * (LANES // ROWS // 2), axis=0))
        total = total + pltpu.roll(total, ROWS, 1)
        buf_a[pl.ds(pl.multiple_of(device * columns, 8), columns), :] = total
        return carry

    lax.fori_loop(0, devices, spread, 0, unroll=8)

    lane = lax.broadcasted_iota(jnp.int32, (1, LANES), 1)
    lane_group = lane // ROWS

    def pack(copied):
        wide = copied[0]
        for g in range(1, GROUPS):
            wide = jnp.where(lane_group == g, copied[g], wide)
        return wide

    def unpack(wide):
        turned = [wide] + [pltpu.roll(wide, g * ROWS, 1) for g in range(1, GROUPS)]
        copied = []
        for i in range(GROUPS):
            copied.append(pack([turned[(g - i) % GROUPS] for g in range(GROUPS)]))
        return copied

    def apply(table_ref, wide):
        high = wide.astype(BF16)
        low = (wide - high.astype(F32)).astype(BF16)
        data = jnp.concatenate([high, low, high], axis=0)
        return jnp.dot(table_ref[...].astype(BF16), data, preferred_element_type=F32)

    for first_x in range(0, mesh_x, GROUPS):
        copied = []
        for place in range(first_x, first_x + GROUPS):
            rows = []
            for sy in range(cycle_y):
                start = ((place // GRID_X) * cycle_y + sy) * columns + (place % GRID_X) * GRID_Y
                rows.append(buf_a[pl.ds(start, GRID_Y), :])
            copied.append(jnp.concatenate(rows, axis=0))
        for i, part in enumerate(unpack(apply(fy_ref, pack(copied)))):
            buf_b[pl.ds((first_x + i) * mesh_y, mesh_y), :] = part

    lane_coef = lane % ROWS % coefs
    lane_mode = first + lane_coef % modes
    lane_sine = lane_coef >= modes
    lane_freq = jnp.where(lane_sine & (lane_mode == 0), mesh_z // 2, lane_mode)
    wave_z = lane_freq.astype(F32) * (2.0 * math.pi / mesh_z)
    lane_weight = jnp.where(lane_mode == 0, 1.0, 2.0) / mesh_z
    slope_z = jnp.where(lane_mode == 0, 0.0, wave_z) * jnp.where(lane_sine, 1.0, -1.0)
    freq_x = lax.broadcasted_iota(jnp.int32, (mesh_x, 1), 0)
    freq_x = jnp.where(freq_x <= mesh_x // 2, freq_x, freq_x - mesh_x // 2)
    wave_x = freq_x.astype(F32) * (2.0 * math.pi / mesh_x)
    near = wave_x * wave_x + wave_z * wave_z

    for first_y in range(0, mesh_y, GROUPS):
        copied = [
            buf_b[pl.ds(first_y + i, mesh_x, stride=mesh_y), :] for i in range(GROUPS)
        ]
        spectrum = apply(fx_ref, pack(copied))
        freq_y = first_y + lane_group
        freq_y = jnp.where(freq_y <= mesh_y // 2, freq_y, freq_y - mesh_y // 2)
        wave_y = freq_y.astype(F32) * (2.0 * math.pi / mesh_y)
        wave_sq = near + wave_y * wave_y
        zero = wave_sq == 0.0
        green = jnp.exp(-0.5 * SMEARING * SMEARING * wave_sq) / jnp.where(zero, 1.0, wave_sq)
        green = jnp.where(zero, 0.0, 4.0 * math.pi * green)
        both = apply(ix_ref, spectrum * (green * lane_weight))
        for i, part in enumerate(unpack(both)):
            rows = pl.ds((first_y + i) * mesh_x, mesh_x)
            buf_a[rows, :] = part[:mesh_x]
            buf_c[rows, :] = part[mesh_x:]

    for first_x in range(0, mesh_x, GROUPS):
        plain, sloped = (
            pack([buf[pl.ds(first_x + i, mesh_y, stride=mesh_x), :] for i in range(GROUPS)])
            for buf in (buf_a, buf_c)
        )
        both = apply(iy_ref, plain)
        along_x = apply(iy_ref.at[pl.ds(0, mesh_y), :], sloped)
        potential = both[:mesh_y]
        partner = jnp.where(
            lane % ROWS >= modes,
            pltpu.roll(potential, modes, 1),
            pltpu.roll(potential, LANES - modes, 1),
        )
        fields = (along_x, both[mesh_y:], partner * slope_z)
        for buf, wide in zip((buf_b, buf_d, buf_e), fields):
            for i, part in enumerate(unpack(wide)):
                buf[pl.ds((first_x + i) * mesh_y, mesh_y), :] = part

    use_low = (lane // ROWS) == 1
    use_none = (lane % ROWS) >= coefs

    def sample(device, carry):
        _, match = columns_of(device)
        rows = []
        for buf in (buf_b, buf_d, buf_e):
            for lx in range(GRID_X):
                place = (device // cycle_y) * GRID_X + lx
                start = place * mesh_y + (device % cycle_y) * GRID_Y
                rows.append(buf[pl.ds(pl.multiple_of(start, 8), GRID_Y), :])
        data = jnp.concatenate(rows, axis=0)
        high = data.astype(BF16).astype(F32)
        mixed = jnp.where(use_low, data - high, high)
        mixed = jnp.where(use_none, 0.0, mixed).astype(BF16)
        high = trig_ref[device, pl.ds(0, ROWS), :]
        low = trig_ref[device, pl.ds(ROWS, ROWS), :]
        waves = jnp.concatenate([high, high, low, jnp.zeros_like(low)], axis=0)
        fields = jnp.dot(mixed, waves, preferred_element_type=F32)
        picked = []
        for a in range(3):
            part = jnp.where(match, fields[a * columns : (a + 1) * columns], 0.0)
            picked.append(jnp.sum(part, axis=0, keepdims=True))
        for a in range(3):
            out_ref[device, a] = picked[a]
        return carry

    lax.fori_loop(0, devices, sample, 0, unroll=8)


def grid_fields(place, gathered, cycle_x, cycle_y):
    mesh_x, mesh_y = (GRID_X * cycle_x, GRID_Y * cycle_y)
    devices, _, atoms = gathered.shape
    ax, bx, cx = real_tables(mesh_x)
    ay, by, cy = real_tables(mesh_y)
    tables = [
        thirds(ay),
        thirds(ax),
        np.concatenate([thirds(bx), thirds(cx)], axis=0),
        np.concatenate([thirds(by), thirds(cy)], axis=0),
    ]
    plane = pltpu.VMEM((mesh_x * mesh_y, LANES), F32)
    vmem = pl.BlockSpec(memory_space=pltpu.VMEM)
    return pl.pallas_call(
        functools.partial(grid_kernel, cycle_x, cycle_y),
        in_specs=[pl.BlockSpec(memory_space=pltpu.SMEM)] + [vmem] * 5,
        out_specs=vmem,
        out_shape=jax.ShapeDtypeStruct((devices, 3, 1, atoms), F32),
        scratch_shapes=[plane] * 5
        + [pltpu.VMEM((devices, 2 * ROWS, atoms), BF16)],
        compiler_params=pltpu.CompilerParams(
            vmem_limit_bytes=5 * mesh_x * mesh_y * LANES * 4
            + devices * atoms * (4 * ROWS + 64)
            + (10 << 20)
        ),
        cost_estimate=pl.CostEstimate(
            flops=8_000_000_000, bytes_accessed=4_000_000, transcendentals=100_000
        ),
        name="grid_fields",
    )(place, gathered, *[jnp.asarray(t) for t in tables])


def edge_kernel(
    list_ref, index_ref, feat_ref, pos_ref, mid_ref, up_ref, down_ref, w_self_ref, w_pair_ref,
    w_radial_ref, w_expand_ref, w_contract_ref, w_final_ref, out_ref,
    table, places, near_a, near_b, near_c, edge_a, edge_b, edge_c,
    total_a, total_b, total_c, marks, own_ref, sums_ref, w_half,
):
    atoms, channels = feat_ref.shape
    ghosts = mid_ref.shape[1] - EXTRA
    slots_all = atoms + 9 * ghosts
    per_atom = index_ref.shape[0]
    chunk = CHUNK_ATOMS * per_atom
    chunks = atoms // CHUNK_ATOMS
    basis_count = w_radial_ref.shape[0]
    spacing = CUTOFF_SQ / (basis_count - 1)
    latent = w_expand_ref.shape[1]
    width = latent // PIECES
    slots = per_atom // PIECES
    w_half[...] = w_expand_ref[...] * 0.5

    def fill(start, rows, coords, shift):
        count = rows.shape[0]
        projected = jnp.dot(rows, w_pair_ref[...], preferred_element_type=F32)
        projected = projected.astype(BF16).astype(F32)
        rows_of = table.reshape(slots_all * 8, LANES)
        rows_of[pl.ds(start * 8, count, stride=8), :] = projected[:, :channels] * 0.5
        rows_of[pl.ds(start * 8 + 1, count, stride=8), :] = projected[:, channels:]
        row = lax.broadcasted_iota(jnp.int32, (8, LANES), 0)
        offset = jnp.where(row == 0, shift[0], jnp.where(row == 1, shift[1], 0.0))
        places[start // LANES] = coords + offset

    pos = jnp.concatenate([pos_ref[...].astype(F32), jnp.zeros((5, atoms), F32)], axis=0)
    for i in range(atoms // LANES):
        rows = feat_ref[pl.ds(i * LANES, LANES), :]
        fill(i * LANES, rows, pos[:, i * LANES : (i + 1) * LANES], (0.0, 0.0))
        own = jnp.dot(rows, w_self_ref[...], preferred_element_type=F32)
        own_ref[pl.ds(i * LANES, LANES), :] = own * 0.5
    for sx in range(3):
        for sy, ref in enumerate((up_ref, mid_ref, down_ref)):
            block = 3 * sx + sy
            if block == 4:
                continue
            tail = ref[sx, pl.ds(ghosts, EXTRA), :].astype(F32)
            for h in range(ghosts // LANES):
                rows = ref[sx, pl.ds(h * LANES, LANES), :]
                start = atoms + block * ghosts + h * LANES
                fill(start, rows, tail[h * 8 : (h + 1) * 8], ((sx - 1) * BOX, (sy - 1) * BOX))

    feature = lax.broadcasted_iota(jnp.int32, (8, LANES), 0)
    skipped = range((atoms + 4 * ghosts) // LANES, (atoms + 5 * ghosts) // LANES)
    for i in range(atoms // LANES):
        columns = slice(i * LANES, (i + 1) * LANES)
        index = index_ref[:, columns]
        inside = index & (LANES - 1)
        outside = lax.shift_right_logical(index, 7)
        found = [jnp.zeros((per_atom, LANES), F32)] * 3
        for c in range(slots_all // LANES):
            if c in skipped:
                continue
            tile = places[c]
            here = outside == c
            for a in range(3):
                source = jnp.broadcast_to(tile[a : a + 1], (per_atom, LANES))
                value = jnp.take_along_axis(source, inside, axis=1)
                found[a] = jnp.where(here, value, found[a])
        disp = [found[a] - pos[a : a + 1, columns] for a in range(3)]
        d2 = disp[0] * disp[0] + disp[1] * disp[1] + disp[2] * disp[2]
        envelope = jnp.maximum(0.0, 1.0 - d2 * (1.0 / CUTOFF_SQ))
        envelope = envelope * envelope
        moments = [envelope] + [envelope * disp[a] for a in range(3)]
        for k in range(per_atom):
            def wide(value):
                return jnp.broadcast_to(value[k : k + 1], (8, LANES))

            t = wide(d2) * (1.0 / spacing) - feature.astype(F32)
            basis = jnp.exp(-(t * t))
            high = basis.astype(BF16).astype(F32)
            tail = jnp.where(feature == 0, wide(moments[0]), 0.0)
            for a in range(3):
                tail = jnp.where(feature == 1 + a, wide(moments[1 + a]), tail)
            stacked = jnp.concatenate([high, basis - high, high, tail], axis=0)
            marks[k, pl.ds(i * LANES, LANES), :] = stacked.T

    w_radial = w_radial_ref[...] * 0.5
    high = w_radial.astype(BF16).astype(F32)
    w_basis = jnp.concatenate(
        [high, high, w_radial - high, jnp.zeros((8, channels), F32)], axis=0
    ).astype(BF16)

    part_rows = slots * CHUNK_ATOMS
    shape = (slots, CHUNK_ATOMS, LANES)

    def atoms_of(index):
        return pl.ds(pl.multiple_of(index * CHUNK_ATOMS, 16), CHUNK_ATOMS)

    def gather(index, near, part):
        for k in range(part * slots, (part + 1) * slots):
            start = k * atoms + index * CHUNK_ATOMS
            loaded = [table[list_ref[start + a]] for a in range(CHUNK_ATOMS)]
            for a, tile in enumerate(loaded):
                near[pl.ds(k * CHUNK_ATOMS + a, 2, stride=chunk), :] = tile[:2]

    def enter(index, near, edge_in, part):
        rows = pl.ds(part * part_rows, part_rows)
        basis = marks[pl.ds(part * slots, slots), atoms_of(index), :]
        basis = basis.reshape(part_rows, basis.shape[2]).astype(BF16)
        radial = jnp.dot(basis, w_basis, preferred_element_type=F32).reshape(shape)
        half = radial + own_ref[atoms_of(index), :][None] + near[rows, :].reshape(shape)
        turn = jnp.tanh(half.astype(BF16)).astype(F32)
        edge_in[rows, :] = (half + half * turn).astype(BF16).reshape(part_rows, LANES)

    def expand(edge_in, part):
        cols = pl.ds(part * width, width)
        return jnp.dot(edge_in[...], w_half[:, cols], preferred_element_type=F32).astype(BF16)

    def contract(half, part):
        hidden = half + half * jnp.tanh(half)
        cols = pl.ds(part * width, width)
        return jnp.dot(hidden, w_contract_ref[cols, :], preferred_element_type=F32)

    def collect(index, near, total, part, before):
        rows = pl.ds(part * part_rows, part_rows)
        other = pl.ds(chunk + part * part_rows, part_rows)
        weight = (total[rows, :] * near[other, :]).reshape(shape)
        after = []
        for s in range(4):
            column = 3 * basis_count + s
            mark = marks[pl.ds(part * slots, slots), atoms_of(index), column : column + 1]
            summed = jnp.sum(weight * mark, axis=0)
            after.append(summed if before is None else before[s] + summed)
        return after

    def keep(index, sums):
        for s in range(4):
            sums_ref[s, atoms_of(index), :] = sums[s]

    def stage(index, nears, edges, totals):
        after = jnp.minimum(index + 1, chunks - 1)
        before = jnp.maximum(index - 1, 0)
        mixed, sums = (None, None)
        half = expand(edges[0], 0)
        for part in range(PIECES):
            gather(after, nears[1], part)
            following = expand(edges[0], part + 1) if part + 1 < PIECES else None
            sums = collect(before, nears[2], totals[2], part, sums)
            term = contract(half, part)
            mixed = term if mixed is None else mixed + term
            enter(after, nears[1], edges[1], part)
            half = following
        totals[0][...] = mixed
        keep(before, sums)

    nears = (near_a, near_b, near_c)
    edges = (edge_a, edge_b, edge_c)
    totals = (total_a, total_b, total_c)
    for part in range(PIECES):
        gather(0, near_a, part)
    for part in range(PIECES):
        enter(0, near_a, edge_a, part)

    def triple(step, carry):
        for i in range(3):
            order = (i, (i + 1) % 3, (i + 2) % 3)
            pick = lambda refs: [refs[o] for o in order]
            stage(3 * step + i, pick(nears), pick(edges), pick(totals))
        return carry

    lax.fori_loop(0, chunks // 3, triple, 0)
    sums = None
    for part in range(PIECES):
        sums = collect(chunks - 1, near_c, total_c, part, sums)
    keep(chunks - 1, sums)

    scale = 1.0 / math.sqrt(per_atom)
    vector = [sums_ref[1 + a] * scale for a in range(3)]
    square = vector[0] * vector[0] + vector[1] * vector[1] + vector[2] * vector[2]
    invariant = (sums_ref[0] * scale + square * (1.0 / 3.0)).astype(BF16)
    gate = jnp.dot(invariant, w_final_ref[...], preferred_element_type=F32)
    gate = gate * (0.5 + 0.5 * jnp.tanh(0.5 * gate)) * (1.0 / math.sqrt(channels))
    ones = jnp.ones((8, channels), F32)
    for a in range(3):
        out_ref[a] = contract_last(ones, vector[a] * gate, HIGHEST)[:1]


def edge_forces(lists, index, feat, pos, mid, up, down, w_self, w_pair, w_radial, w_expand, w_contract, w_final):
    atoms, channels = feat.shape
    per_atom = index.shape[0]
    ghosts = mid.shape[1] - EXTRA
    slots_all = atoms + 9 * ghosts
    chunk = CHUNK_ATOMS * per_atom
    vmem = pl.BlockSpec(memory_space=pltpu.VMEM)
    edges = atoms * per_atom
    latent = w_expand.shape[1]
    return pl.pallas_call(
        edge_kernel,
        in_specs=[pl.BlockSpec(memory_space=pltpu.SMEM)] + [vmem] * 12,
        out_specs=vmem,
        out_shape=jax.ShapeDtypeStruct((3, 1, atoms), F32),
        scratch_shapes=[
            pltpu.VMEM((slots_all, 8, LANES), F32),
            pltpu.VMEM((slots_all // LANES, 8, LANES), F32),
        ]
        + [pltpu.VMEM((2 * chunk, LANES), F32)] * 3
        + [pltpu.VMEM((chunk, LANES), BF16)] * 3
        + [pltpu.VMEM((chunk, LANES), F32)] * 3
        + [
            pltpu.VMEM((per_atom, atoms, 32), F32),
            pltpu.VMEM((atoms, LANES), F32),
            pltpu.VMEM((4, atoms, LANES), F32),
            pltpu.VMEM(w_expand.shape, BF16),
        ],
        compiler_params=pltpu.CompilerParams(vmem_limit_bytes=32 << 20),
        cost_estimate=pl.CostEstimate(
            flops=4 * edges * channels * latent,
            bytes_accessed=4_000_000,
            transcendentals=edges * latent,
        ),
        name="edge_forces",
    )(
        lists, index, feat, pos, mid, up, down, w_self, w_pair, w_radial,
        w_expand, w_contract, w_final,
    )


def ring(array, axis, step):
    size = lax.axis_size(axis)
    return lax.ppermute(array, axis, [(i, (i + step) % size) for i in range(size)])


def shards(
    features, positions, atom_count, ghost_index, neighbour_list, cell_index, w_self, w_pair,
    w_radial, w_expand, w_contract, w_final, w_charge,
):
    feat = features[0, 0]
    pos = positions[0, 0]
    cycle_x, cycle_y = (lax.axis_size("dx"), lax.axis_size("dy"))
    spread = charges(cycle_x * cycle_y, atom_count, feat, cell_index[0, 0], w_charge)
    exported = exports_after(spread, feat, pos, ghost_index[0, 0])
    gathered = lax.all_to_all(spread, ("dx", "dy"), split_axis=0, concat_axis=0, tiled=True)
    mid = jnp.stack([ring(exported, "dx", 1), exported, ring(exported, "dx", -1)])
    index = neighbour_list[0, 0].T
    lists = index.reshape(-1)
    gathered, mid, lists = lax.optimization_barrier((gathered, mid, lists))
    up = ring(mid, "dy", 1)
    down = ring(mid, "dy", -1)
    place = lax.axis_index("dx") * cycle_y + lax.axis_index("dy")
    partial = grid_fields(place[None].astype(jnp.int32), gathered, cycle_x, cycle_y)
    received = lax.all_to_all(partial, ("dx", "dy"), split_axis=0, concat_axis=0, tiled=True)
    short = edge_forces(
        lists, index, feat, pos, mid, up, down, w_self, w_pair, w_radial, w_expand,
        w_contract, w_final,
    )
    field = jnp.sum(received, axis=0)
    total = short + spread[0, :1] * field
    live = lax.broadcasted_iota(jnp.int32, (1, feat.shape[0]), 1) < atom_count[0, 0]
    return jnp.where(live, total, jnp.zeros_like(total)).transpose(1, 0, 2)[None]


def solution(mesh):
    placed = (
        P("dx", "dy", None, None),
        P("dx", "dy", None, None),
        P("dx", "dy"),
        P("dx", "dy", None),
        P("dx", "dy", None, None),
        P("dx", "dy", None),
    ) + (P(),) * 7
    return jax.shard_map(
        shards, mesh=mesh, in_specs=placed, out_specs=P("dx", "dy", None, None), check_vma=False
    )
```

```python
import functools
import math

import jax
import jax.numpy as jnp
import numpy as np
from jax import lax
from jax.experimental import pallas as pl
from jax.experimental.pallas import tpu as pltpu
from jax.sharding import PartitionSpec as P

GRID_X = 8
GRID_Y = 8
GRID_Z = 1024
BOX = 1.0
CUTOFF_SQ = 6.25
SMEARING = 1.0

LANES = 128
EXTRA = 16
ROWS = 32
GROUPS = LANES // ROWS
CHUNK_ATOMS = 16
PIECES = 4
HIGHEST = lax.Precision.HIGHEST
F32 = jnp.float32
BF16 = jnp.bfloat16


def contract_first(a, b, precision=None):
    return lax.dot_general(
        a, b, (((0,), (0,)), ((), ())), precision=precision, preferred_element_type=F32
    )


def contract_last(a, b, precision=None):
    return lax.dot_general(
        a, b, (((1,), (1,)), ((), ())), precision=precision, preferred_element_type=F32
    )


def charge_kernel(count_ref, feat_ref, cell_ref, wq_ref, qc_ref):
    atoms = feat_ref.shape[0]
    weights = jnp.broadcast_to(wq_ref[...].astype(F32), (16, LANES)).astype(BF16)
    charge = contract_last(weights, feat_ref[...])[:1]
    live = lax.broadcasted_iota(jnp.int32, (1, atoms), 1) < count_ref[0, 0]
    both = jnp.concatenate([jnp.where(live, charge, 0.0), cell_ref[...].astype(F32)], axis=0)
    qc_ref[...] = jnp.broadcast_to(both[None], qc_ref.shape)


def export_kernel(feat_ref, pos_ref, export_ref, after_ref, out_ref):
    atoms = feat_ref.shape[0]
    ghosts = export_ref.shape[1]
    pick = lax.broadcasted_iota(jnp.int32, (atoms, ghosts), 0) == export_ref[...]
    pick = jnp.where(pick, 1.0, 0.0).astype(BF16)
    out_ref[pl.ds(0, ghosts), :] = contract_first(pick, feat_ref[...]).astype(BF16)
    pos = jnp.concatenate([pos_ref[...].astype(F32), jnp.zeros((13, atoms), F32)], axis=0)
    coords = jnp.dot(pos.astype(BF16), pick, preferred_element_type=F32)
    tail = [coords[:8, h * LANES : (h + 1) * LANES] for h in range(ghosts // LANES)]
    out_ref[pl.ds(ghosts, EXTRA), :] = jnp.concatenate(tail, axis=0).astype(BF16)


def charges(devices, count, feat, cells, w_charge):
    vmem = pl.BlockSpec(memory_space=pltpu.VMEM)
    return pl.pallas_call(
        charge_kernel,
        in_specs=[pl.BlockSpec(memory_space=pltpu.SMEM)] + [vmem] * 3,
        out_specs=vmem,
        out_shape=jax.ShapeDtypeStruct((devices, 2, feat.shape[0]), F32),
        compiler_params=pltpu.CompilerParams(vmem_limit_bytes=60 << 20),
        name="charges",
    )(count, feat, cells[None], w_charge[None])


def exports_after(after, feat, pos, exports):
    vmem = pl.BlockSpec(memory_space=pltpu.VMEM)
    return pl.pallas_call(
        export_kernel,
        in_specs=[vmem] * 3 + [pl.BlockSpec(memory_space=pl.ANY)],
        out_specs=vmem,
        out_shape=jax.ShapeDtypeStruct((exports.shape[0] + EXTRA, feat.shape[1]), BF16),
        compiler_params=pltpu.CompilerParams(vmem_limit_bytes=16 << 20),
        name="exports",
    )(feat, pos, exports[None], after)


def real_tables(count):
    half = count // 2
    index = np.arange(count)
    freq = np.where(index <= half, index, index - half)
    place = np.arange(count)
    angle = 2.0 * np.pi * (freq[:, None] * place[None, :] % count) / count
    is_cos = (index <= half)[:, None]
    basis = np.where(is_cos, np.cos(angle), np.sin(angle))
    weight = np.where((index == 0) | (index == half), 1.0, 2.0)[:, None] / count
    wave = np.where(index == half, 0.0, 2.0 * np.pi * freq / count)[:, None]
    slope = np.where(is_cos, np.sin(angle), -np.cos(angle)) * wave
    return (basis, (weight * basis).T, (weight * slope).T)


def thirds(table):
    whole = table.astype(np.float32)
    high = whole.astype(BF16).astype(np.float32)
    low = (whole - high).astype(BF16).astype(np.float32)
    return np.concatenate([high, high, low], axis=1)


def sine_half(t):
    x = t * (math.pi / 512.0)
    s = x * x
    p = -2.50521084e-08
    p = p * s + 2.75573192e-06
    p = p * s - 1.98412698e-04
    p = p * s + 8.33333333e-03
    p = p * s - 1.66666667e-01
    return x + x * (s * p)


def grid_kernel(
    cycle_x, cycle_y, place_ref, qc_ref, fy_ref, fx_ref, ix_ref, iy_ref, out_ref,
    buf_a, buf_b, buf_c, buf_d, buf_e, trig_ref,
):
    mesh_x, mesh_y, mesh_z = (GRID_X * cycle_x, GRID_Y * cycle_y, GRID_Z)
    devices = cycle_x * cycle_y
    modes = mesh_z // 2 // devices
    coefs = 2 * modes
    first = place_ref[0] * modes
    columns = GRID_X * GRID_Y
    atoms = qc_ref.shape[2]

    row = lax.broadcasted_iota(jnp.int32, (ROWS, 1), 0) % coefs
    row_mode = first + row % modes
    row_sine = row >= modes
    row_edge = row_sine & (row_mode == 0)
    row_factor = jnp.where(row_edge, mesh_z // 2, row_mode)
    row_shift = jnp.where(row_sine & (row_mode != 0), mesh_z // 4, 0)
    column_iota = lax.broadcasted_iota(jnp.int32, (columns, atoms), 0)

    def columns_of(device):
        cell = qc_ref[device, 1:2, :].astype(jnp.int32)
        return cell, column_iota == lax.shift_right_logical(cell, 10)

    def spread(device, carry):
        cell, match = columns_of(device)
        depth = cell & (mesh_z - 1)
        turn = (row_factor * depth - row_shift) & (mesh_z - 1)
        trig = sine_half((jnp.abs(turn - mesh_z // 2) - mesh_z // 4).astype(F32))
        high = trig.astype(BF16)
        trig_ref[device, pl.ds(0, ROWS), :] = high
        trig_ref[device, pl.ds(ROWS, ROWS), :] = (trig - high.astype(F32)).astype(BF16)
        charged = trig * qc_ref[device, 0:1, :]
        high = charged.astype(BF16)
        low = (charged - high.astype(F32)).astype(BF16)
        pick = jnp.where(match, 1.0, 0.0).astype(BF16)
        total = contract_last(pick, jnp.concatenate([high, low] * (LANES // ROWS // 2), axis=0))
        total = total + pltpu.roll(total, ROWS, 1)
        buf_a[pl.ds(pl.multiple_of(device * columns, 8), columns), :] = total
        return carry

    lax.fori_loop(0, devices, spread, 0, unroll=8)

    lane = lax.broadcasted_iota(jnp.int32, (1, LANES), 1)
    lane_group = lane // ROWS

    def pack(copied):
        wide = copied[0]
        for g in range(1, GROUPS):
            wide = jnp.where(lane_group == g, copied[g], wide)
        return wide

    def unpack(wide):
        turned = [wide] + [pltpu.roll(wide, g * ROWS, 1) for g in range(1, GROUPS)]
        copied = []
        for i in range(GROUPS):
            copied.append(pack([turned[(g - i) % GROUPS] for g in range(GROUPS)]))
        return copied

    def apply(table_ref, wide):
        high = wide.astype(BF16)
        low = (wide - high.astype(F32)).astype(BF16)
        data = jnp.concatenate([high, low, high], axis=0)
        return jnp.dot(table_ref[...].astype(BF16), data, preferred_element_type=F32)

    for first_x in range(0, mesh_x, GROUPS):
        copied = []
        for place in range(first_x, first_x + GROUPS):
            rows = []
            for sy in range(cycle_y):
                start = ((place // GRID_X) * cycle_y + sy) * columns + (place % GRID_X) * GRID_Y
                rows.append(buf_a[pl.ds(start, GRID_Y), :])
            copied.append(jnp.concatenate(rows, axis=0))
        for i, part in enumerate(unpack(apply(fy_ref, pack(copied)))):
            buf_b[pl.ds((first_x + i) * mesh_y, mesh_y), :] = part

    lane_coef = lane % ROWS % coefs
    lane_mode = first + lane_coef % modes
    lane_sine = lane_coef >= modes
    lane_freq = jnp.where(lane_sine & (lane_mode == 0), mesh_z // 2, lane_mode)
    wave_z = lane_freq.astype(F32) * (2.0 * math.pi / mesh_z)
    lane_weight = jnp.where(lane_mode == 0, 1.0, 2.0) / mesh_z
    slope_z = jnp.where(lane_mode == 0, 0.0, wave_z) * jnp.where(lane_sine, 1.0, -1.0)
    freq_x = lax.broadcasted_iota(jnp.int32, (mesh_x, 1), 0)
    freq_x = jnp.where(freq_x <= mesh_x // 2, freq_x, freq_x - mesh_x // 2)
    wave_x = freq_x.astype(F32) * (2.0 * math.pi / mesh_x)
    near = wave_x * wave_x + wave_z * wave_z

    for first_y in range(0, mesh_y, GROUPS):
        copied = [
            buf_b[pl.ds(first_y + i, mesh_x, stride=mesh_y), :] for i in range(GROUPS)
        ]
        spectrum = apply(fx_ref, pack(copied))
        freq_y = first_y + lane_group
        freq_y = jnp.where(freq_y <= mesh_y // 2, freq_y, freq_y - mesh_y // 2)
        wave_y = freq_y.astype(F32) * (2.0 * math.pi / mesh_y)
        wave_sq = near + wave_y * wave_y
        zero = wave_sq == 0.0
        green = jnp.exp(-0.5 * SMEARING * SMEARING * wave_sq) / jnp.where(zero, 1.0, wave_sq)
        green = jnp.where(zero, 0.0, 4.0 * math.pi * green)
        both = apply(ix_ref, spectrum * (green * lane_weight))
        for i, part in enumerate(unpack(both)):
            rows = pl.ds((first_y + i) * mesh_x, mesh_x)
            buf_a[rows, :] = part[:mesh_x]
            buf_c[rows, :] = part[mesh_x:]

    for first_x in range(0, mesh_x, GROUPS):
        plain, sloped = (
            pack([buf[pl.ds(first_x + i, mesh_y, stride=mesh_x), :] for i in range(GROUPS)])
            for buf in (buf_a, buf_c)
        )
        both = apply(iy_ref, plain)
        along_x = apply(iy_ref.at[pl.ds(0, mesh_y), :], sloped)
        potential = both[:mesh_y]
        partner = jnp.where(
            lane % ROWS >= modes,
            pltpu.roll(potential, modes, 1),
            pltpu.roll(potential, LANES - modes, 1),
        )
        fields = (along_x, both[mesh_y:], partner * slope_z)
        for buf, wide in zip((buf_b, buf_d, buf_e), fields):
            for i, part in enumerate(unpack(wide)):
                buf[pl.ds((first_x + i) * mesh_y, mesh_y), :] = part

    use_low = (lane // ROWS) == 1
    use_none = (lane % ROWS) >= coefs

    def sample(device, carry):
        _, match = columns_of(device)
        rows = []
        for buf in (buf_b, buf_d, buf_e):
            for lx in range(GRID_X):
                place = (device // cycle_y) * GRID_X + lx
                start = place * mesh_y + (device % cycle_y) * GRID_Y
                rows.append(buf[pl.ds(pl.multiple_of(start, 8), GRID_Y), :])
        data = jnp.concatenate(rows, axis=0)
        high = data.astype(BF16).astype(F32)
        mixed = jnp.where(use_low, data - high, high)
        mixed = jnp.where(use_none, 0.0, mixed).astype(BF16)
        high = trig_ref[device, pl.ds(0, ROWS), :]
        low = trig_ref[device, pl.ds(ROWS, ROWS), :]
        waves = jnp.concatenate([high, high, low, jnp.zeros_like(low)], axis=0)
        fields = jnp.dot(mixed, waves, preferred_element_type=F32)
        picked = []
        for a in range(3):
            part = jnp.where(match, fields[a * columns : (a + 1) * columns], 0.0)
            picked.append(jnp.sum(part, axis=0, keepdims=True))
        for a in range(3):
            out_ref[device, a] = picked[a]
        return carry

    lax.fori_loop(0, devices, sample, 0, unroll=8)


def grid_fields(place, gathered, cycle_x, cycle_y):
    mesh_x, mesh_y = (GRID_X * cycle_x, GRID_Y * cycle_y)
    devices, _, atoms = gathered.shape
    ax, bx, cx = real_tables(mesh_x)
    ay, by, cy = real_tables(mesh_y)
    tables = [
        thirds(ay),
        thirds(ax),
        np.concatenate([thirds(bx), thirds(cx)], axis=0),
        np.concatenate([thirds(by), thirds(cy)], axis=0),
    ]
    plane = pltpu.VMEM((mesh_x * mesh_y, LANES), F32)
    vmem = pl.BlockSpec(memory_space=pltpu.VMEM)
    return pl.pallas_call(
        functools.partial(grid_kernel, cycle_x, cycle_y),
        in_specs=[pl.BlockSpec(memory_space=pltpu.SMEM)] + [vmem] * 5,
        out_specs=vmem,
        out_shape=jax.ShapeDtypeStruct((devices, 3, 1, atoms), F32),
        scratch_shapes=[plane] * 5
        + [pltpu.VMEM((devices, 2 * ROWS, atoms), BF16)],
        compiler_params=pltpu.CompilerParams(
            vmem_limit_bytes=5 * mesh_x * mesh_y * LANES * 4
            + devices * atoms * (4 * ROWS + 64)
            + (10 << 20)
        ),
        cost_estimate=pl.CostEstimate(
            flops=8_000_000_000, bytes_accessed=4_000_000, transcendentals=100_000
        ),
        name="grid_fields",
    )(place, gathered, *[jnp.asarray(t) for t in tables])


def edge_kernel(
    list_hbm, index_ref, feat_ref, pos_ref, mid_ref, up_ref, down_ref, w_self_ref, w_pair_ref,
    w_radial_ref, w_expand_ref, w_contract_ref, w_final_ref, out_ref,
    table, places, near_a, near_b, near_c, edge_a, edge_b, edge_c,
    total_a, total_b, total_c, marks, own_ref, sums_ref, w_half,
    list_ref, list_sem,
):
    atoms, channels = feat_ref.shape
    ghosts = mid_ref.shape[1] - EXTRA
    slots_all = atoms + 9 * ghosts
    per_atom = index_ref.shape[0]
    chunk = CHUNK_ATOMS * per_atom
    chunks = atoms // CHUNK_ATOMS
    basis_count = w_radial_ref.shape[0]
    spacing = CUTOFF_SQ / (basis_count - 1)
    latent = w_expand_ref.shape[1]
    width = latent // PIECES
    slots = per_atom // PIECES
    w_half[...] = w_expand_ref[...] * 0.5

    fetch = pltpu.make_async_copy(list_hbm, list_ref, list_sem)
    fetch.start()

    def fill(start, rows, coords, shift):
        count = rows.shape[0]
        projected = jnp.dot(rows, w_pair_ref[...], preferred_element_type=F32)
        projected = projected.astype(BF16).astype(F32)
        rows_of = table.reshape(slots_all * 2, LANES)
        rows_of[pl.ds(start * 2, count, stride=2), :] = projected[:, :channels] * 0.5
        rows_of[pl.ds(start * 2 + 1, count, stride=2), :] = projected[:, channels:]
        row = lax.broadcasted_iota(jnp.int32, (8, LANES), 0)
        offset = jnp.where(row == 0, shift[0], jnp.where(row == 1, shift[1], 0.0))
        places[start // LANES] = coords + offset

    pos = jnp.concatenate([pos_ref[...].astype(F32), jnp.zeros((5, atoms), F32)], axis=0)
    for i in range(atoms // LANES):
        rows = feat_ref[pl.ds(i * LANES, LANES), :]
        fill(i * LANES, rows, pos[:, i * LANES : (i + 1) * LANES], (0.0, 0.0))
        own = jnp.dot(rows, w_self_ref[...], preferred_element_type=F32)
        own_ref[pl.ds(i * LANES, LANES), :] = own * 0.5
    for sx in range(3):
        for sy, ref in enumerate((up_ref, mid_ref, down_ref)):
            block = 3 * sx + sy
            if block == 4:
                continue
            tail = ref[sx, pl.ds(ghosts, EXTRA), :].astype(F32)
            for h in range(ghosts // LANES):
                rows = ref[sx, pl.ds(h * LANES, LANES), :]
                start = atoms + block * ghosts + h * LANES
                fill(start, rows, tail[h * 8 : (h + 1) * 8], ((sx - 1) * BOX, (sy - 1) * BOX))

    feature = lax.broadcasted_iota(jnp.int32, (8, LANES), 0)
    skipped = range((atoms + 4 * ghosts) // LANES, (atoms + 5 * ghosts) // LANES)
    for i in range(atoms // LANES):
        columns = slice(i * LANES, (i + 1) * LANES)
        index = index_ref[:, columns]
        inside = index & (LANES - 1)
        outside = lax.shift_right_logical(index, 7)
        found = [jnp.zeros((per_atom, LANES), F32)] * 3
        for c in range(slots_all // LANES):
            if c in skipped:
                continue
            tile = places[c]
            here = outside == c
            for a in range(3):
                source = jnp.broadcast_to(tile[a : a + 1], (per_atom, LANES))
                value = jnp.take_along_axis(source, inside, axis=1)
                found[a] = jnp.where(here, value, found[a])
        disp = [found[a] - pos[a : a + 1, columns] for a in range(3)]
        d2 = disp[0] * disp[0] + disp[1] * disp[1] + disp[2] * disp[2]
        envelope = jnp.maximum(0.0, 1.0 - d2 * (1.0 / CUTOFF_SQ))
        envelope = envelope * envelope
        moments = [envelope] + [envelope * disp[a] for a in range(3)]
        for group in range(per_atom // GROUPS):
            stacked = []
            for k in range(group * GROUPS, (group + 1) * GROUPS):
                def wide(value):
                    return jnp.broadcast_to(value[k : k + 1], (8, LANES))

                t = wide(d2) * (1.0 / spacing) - feature.astype(F32)
                basis = jnp.exp(-(t * t))
                high = basis.astype(BF16).astype(F32)
                tail = jnp.where(feature == 0, wide(moments[0]), 0.0)
                for a in range(3):
                    tail = jnp.where(feature == 1 + a, wide(moments[1 + a]), tail)
                stacked += [high, basis - high, high, tail]
            marks[group, pl.ds(i * LANES, LANES), :] = jnp.concatenate(stacked, axis=0).T

    w_radial = w_radial_ref[...] * 0.5
    high = w_radial.astype(BF16).astype(F32)
    one = jnp.concatenate([high, high, w_radial - high, jnp.zeros((8, channels), F32)], axis=0)
    none = jnp.zeros((ROWS, channels), F32)
    blocks = []
    for g in range(GROUPS):
        column = [one if other == g else none for other in range(GROUPS)]
        blocks.append(jnp.concatenate(column, axis=0))
    w_basis = jnp.concatenate(blocks, axis=1).astype(BF16)

    part_rows = slots * CHUNK_ATOMS
    shape = (slots, CHUNK_ATOMS, LANES)

    def atoms_of(index):
        return pl.ds(pl.multiple_of(index * CHUNK_ATOMS, 16), CHUNK_ATOMS)

    def gather(index, near, part):
        for k in range(part * slots, (part + 1) * slots):
            start = k * atoms + index * CHUNK_ATOMS
            loaded = [table[list_ref[start + a]] for a in range(CHUNK_ATOMS)]
            for a, tile in enumerate(loaded):
                near[pl.ds(k * CHUNK_ATOMS + a, 2, stride=chunk), :] = tile

    def enter(index, near, edge_in, part):
        rows = pl.ds(part * part_rows, part_rows)
        groups = slots // GROUPS
        basis = marks[pl.ds(part * groups, groups), atoms_of(index), :]
        basis = basis.reshape(groups * CHUNK_ATOMS, LANES).astype(BF16)
        wide = jnp.dot(basis, w_basis, preferred_element_type=F32)
        pieces = []
        for q in range(groups):
            for g in range(GROUPS):
                rows_q = slice(q * CHUNK_ATOMS, (q + 1) * CHUNK_ATOMS)
                pieces.append(wide[rows_q, g * LANES : (g + 1) * LANES])
        radial = jnp.concatenate(pieces, axis=0).reshape(shape)
        half = radial + own_ref[atoms_of(index), :][None] + near[rows, :].reshape(shape)
        turn = jnp.tanh(half.astype(BF16)).astype(F32)
        edge_in[rows, :] = (half + half * turn).astype(BF16).reshape(part_rows, LANES)

    def expand(edge_in, part):
        cols = pl.ds(part * width, width)
        return jnp.dot(edge_in[...], w_half[:, cols], preferred_element_type=F32).astype(BF16)

    def contract(half, part):
        hidden = half + half * jnp.tanh(half)
        cols = pl.ds(part * width, width)
        return jnp.dot(hidden, w_contract_ref[cols, :], preferred_element_type=F32)

    def collect(index, near, total, part, before):
        rows = pl.ds(part * part_rows, part_rows)
        other = pl.ds(chunk + part * part_rows, part_rows)
        weight = (total[rows, :] * near[other, :]).reshape(shape)
        after = []
        for s in range(4):
            summed = 0.0
            for k in range(slots):
                column = k % GROUPS * ROWS + 3 * basis_count + s
                tile = marks[(part * slots + k) // GROUPS, atoms_of(index), :]
                summed = summed + weight[k] * tile[:, column : column + 1]
            after.append(summed if before is None else before[s] + summed)
        return after

    def keep(index, sums):
        for s in range(4):
            sums_ref[s, atoms_of(index), :] = sums[s]

    def stage(index, nears, edges, totals):
        after = jnp.minimum(index + 1, chunks - 1)
        before = jnp.maximum(index - 1, 0)
        mixed, sums = (None, None)
        half = expand(edges[0], 0)
        for part in range(PIECES):
            gather(after, nears[1], part)
            following = expand(edges[0], part + 1) if part + 1 < PIECES else None
            sums = collect(before, nears[2], totals[2], part, sums)
            term = contract(half, part)
            mixed = term if mixed is None else mixed + term
            enter(after, nears[1], edges[1], part)
            half = following
        totals[0][...] = mixed
        keep(before, sums)

    nears = (near_a, near_b, near_c)
    edges = (edge_a, edge_b, edge_c)
    totals = (total_a, total_b, total_c)
    fetch.wait()
    for part in range(PIECES):
        gather(0, near_a, part)
    for part in range(PIECES):
        enter(0, near_a, edge_a, part)

    def triple(step, carry):
        for i in range(3):
            order = (i, (i + 1) % 3, (i + 2) % 3)
            pick = lambda refs: [refs[o] for o in order]
            stage(3 * step + i, pick(nears), pick(edges), pick(totals))
        return carry

    lax.fori_loop(0, chunks // 3, triple, 0)
    sums = None
    for part in range(PIECES):
        sums = collect(chunks - 1, near_c, total_c, part, sums)
    keep(chunks - 1, sums)

    scale = 1.0 / math.sqrt(per_atom)
    vector = [sums_ref[1 + a] * scale for a in range(3)]
    square = vector[0] * vector[0] + vector[1] * vector[1] + vector[2] * vector[2]
    invariant = (sums_ref[0] * scale + square * (1.0 / 3.0)).astype(BF16)
    gate = jnp.dot(invariant, w_final_ref[...], preferred_element_type=F32)
    gate = gate * (0.5 + 0.5 * jnp.tanh(0.5 * gate)) * (1.0 / math.sqrt(channels))
    ones = jnp.ones((8, channels), F32)
    for a in range(3):
        out_ref[a] = contract_last(ones, vector[a] * gate, HIGHEST)[:1]


def edge_forces(lists, index, feat, pos, mid, up, down, w_self, w_pair, w_radial, w_expand, w_contract, w_final):
    atoms, channels = feat.shape
    per_atom = index.shape[0]
    ghosts = mid.shape[1] - EXTRA
    slots_all = atoms + 9 * ghosts
    chunk = CHUNK_ATOMS * per_atom
    vmem = pl.BlockSpec(memory_space=pltpu.VMEM)
    edges = atoms * per_atom
    latent = w_expand.shape[1]
    return pl.pallas_call(
        edge_kernel,
        in_specs=[pl.BlockSpec(memory_space=pl.ANY)] + [vmem] * 12,
        out_specs=vmem,
        out_shape=jax.ShapeDtypeStruct((3, 1, atoms), F32),
        scratch_shapes=[
            pltpu.VMEM((slots_all, 2, LANES), F32),
            pltpu.VMEM((slots_all // LANES, 8, LANES), F32),
        ]
        + [pltpu.VMEM((2 * chunk, LANES), F32)] * 3
        + [pltpu.VMEM((chunk, LANES), BF16)] * 3
        + [pltpu.VMEM((chunk, LANES), F32)] * 3
        + [
            pltpu.VMEM((per_atom // GROUPS, atoms, LANES), F32),
            pltpu.VMEM((atoms, LANES), F32),
            pltpu.VMEM((4, atoms, LANES), F32),
            pltpu.VMEM(w_expand.shape, BF16),
            pltpu.SMEM(lists.shape, lists.dtype),
            pltpu.SemaphoreType.DMA(()),
        ],
        compiler_params=pltpu.CompilerParams(vmem_limit_bytes=32 << 20),
        cost_estimate=pl.CostEstimate(
            flops=4 * edges * channels * latent,
            bytes_accessed=4_000_000,
            transcendentals=edges * latent,
        ),
        name="edge_forces",
    )(
        lists, index, feat, pos, mid, up, down, w_self, w_pair, w_radial,
        w_expand, w_contract, w_final,
    )


def ring(array, axis, step):
    size = lax.axis_size(axis)
    return lax.ppermute(array, axis, [(i, (i + step) % size) for i in range(size)])


def shards(
    features, positions, atom_count, ghost_index, neighbour_list, cell_index, w_self, w_pair,
    w_radial, w_expand, w_contract, w_final, w_charge,
):
    feat = features[0, 0]
    pos = positions[0, 0]
    cycle_x, cycle_y = (lax.axis_size("dx"), lax.axis_size("dy"))
    spread = charges(cycle_x * cycle_y, atom_count, feat, cell_index[0, 0], w_charge)
    exported = exports_after(spread, feat, pos, ghost_index[0, 0])
    gathered = lax.all_to_all(spread, ("dx", "dy"), split_axis=0, concat_axis=0, tiled=True)
    mid = jnp.stack([ring(exported, "dx", 1), exported, ring(exported, "dx", -1)])
    index = neighbour_list[0, 0].T
    lists = index.reshape(-1)
    gathered, mid, lists = lax.optimization_barrier((gathered, mid, lists))
    up = ring(mid, "dy", 1)
    down = ring(mid, "dy", -1)
    place = lax.axis_index("dx") * cycle_y + lax.axis_index("dy")
    partial = grid_fields(place[None].astype(jnp.int32), gathered, cycle_x, cycle_y)
    received = lax.all_to_all(partial, ("dx", "dy"), split_axis=0, concat_axis=0, tiled=True)
    short = edge_forces(
        lists, index, feat, pos, mid, up, down, w_self, w_pair, w_radial, w_expand,
        w_contract, w_final,
    )
    field = jnp.sum(received, axis=0)
    total = short + spread[0, :1] * field
    live = lax.broadcasted_iota(jnp.int32, (1, feat.shape[0]), 1) < atom_count[0, 0]
    return jnp.where(live, total, jnp.zeros_like(total)).transpose(1, 0, 2)[None]


def solution(mesh):
    placed = (
        P("dx", "dy", None, None),
        P("dx", "dy", None, None),
        P("dx", "dy"),
        P("dx", "dy", None),
        P("dx", "dy", None, None),
        P("dx", "dy", None),
    ) + (P(),) * 7
    return jax.shard_map(
        shards, mesh=mesh, in_specs=placed, out_specs=P("dx", "dy", None, None), check_vma=False
    )
```

```python
import functools
import math

import jax
import jax.numpy as jnp
import numpy as np
from jax import lax
from jax.experimental import pallas as pl
from jax.experimental.pallas import tpu as pltpu
from jax.sharding import PartitionSpec as P

GRID_X = 8
GRID_Y = 8
GRID_Z = 1024
BOX = 1.0
CUTOFF_SQ = 6.25
SMEARING = 1.0

LANES = 128
EXTRA = 16
ROWS = 32
GROUPS = LANES // ROWS
CHUNK_ATOMS = 32
PIECES = 4
HIGHEST = lax.Precision.HIGHEST
F32 = jnp.float32
BF16 = jnp.bfloat16


def contract_first(a, b, precision=None):
    return lax.dot_general(
        a, b, (((0,), (0,)), ((), ())), precision=precision, preferred_element_type=F32
    )


def contract_last(a, b, precision=None):
    return lax.dot_general(
        a, b, (((1,), (1,)), ((), ())), precision=precision, preferred_element_type=F32
    )


def charge_kernel(count_ref, feat_ref, cell_ref, wq_ref, qc_ref):
    atoms = feat_ref.shape[0]
    weights = jnp.broadcast_to(wq_ref[...].astype(F32), (16, LANES)).astype(BF16)
    charge = contract_last(weights, feat_ref[...])[:1]
    live = lax.broadcasted_iota(jnp.int32, (1, atoms), 1) < count_ref[0, 0]
    both = jnp.concatenate([jnp.where(live, charge, 0.0), cell_ref[...].astype(F32)], axis=0)
    qc_ref[...] = jnp.broadcast_to(both[None], qc_ref.shape)


def export_kernel(feat_ref, pos_ref, export_ref, after_ref, out_ref):
    atoms = feat_ref.shape[0]
    ghosts = export_ref.shape[1]
    pick = lax.broadcasted_iota(jnp.int32, (atoms, ghosts), 0) == export_ref[...]
    pick = jnp.where(pick, 1.0, 0.0).astype(BF16)
    out_ref[pl.ds(0, ghosts), :] = contract_first(pick, feat_ref[...]).astype(BF16)
    pos = jnp.concatenate([pos_ref[...].astype(F32), jnp.zeros((13, atoms), F32)], axis=0)
    coords = jnp.dot(pos.astype(BF16), pick, preferred_element_type=F32)
    tail = [coords[:8, h * LANES : (h + 1) * LANES] for h in range(ghosts // LANES)]
    out_ref[pl.ds(ghosts, EXTRA), :] = jnp.concatenate(tail, axis=0).astype(BF16)


def charges(devices, count, feat, cells, w_charge):
    vmem = pl.BlockSpec(memory_space=pltpu.VMEM)
    return pl.pallas_call(
        charge_kernel,
        in_specs=[pl.BlockSpec(memory_space=pltpu.SMEM)] + [vmem] * 3,
        out_specs=vmem,
        out_shape=jax.ShapeDtypeStruct((devices, 2, feat.shape[0]), F32),
        compiler_params=pltpu.CompilerParams(vmem_limit_bytes=60 << 20),
        name="charges",
    )(count, feat, cells[None], w_charge[None])


def exports_after(after, feat, pos, exports):
    vmem = pl.BlockSpec(memory_space=pltpu.VMEM)
    return pl.pallas_call(
        export_kernel,
        in_specs=[vmem] * 3 + [pl.BlockSpec(memory_space=pl.ANY)],
        out_specs=vmem,
        out_shape=jax.ShapeDtypeStruct((exports.shape[0] + EXTRA, feat.shape[1]), BF16),
        compiler_params=pltpu.CompilerParams(vmem_limit_bytes=16 << 20),
        name="exports",
    )(feat, pos, exports[None], after)


def real_tables(count):
    half = count // 2
    index = np.arange(count)
    freq = np.where(index <= half, index, index - half)
    place = np.arange(count)
    angle = 2.0 * np.pi * (freq[:, None] * place[None, :] % count) / count
    is_cos = (index <= half)[:, None]
    basis = np.where(is_cos, np.cos(angle), np.sin(angle))
    weight = np.where((index == 0) | (index == half), 1.0, 2.0)[:, None] / count
    wave = np.where(index == half, 0.0, 2.0 * np.pi * freq / count)[:, None]
    slope = np.where(is_cos, np.sin(angle), -np.cos(angle)) * wave
    return (basis, (weight * basis).T, (weight * slope).T)


def thirds(table):
    whole = table.astype(np.float32)
    high = whole.astype(BF16).astype(np.float32)
    low = (whole - high).astype(BF16).astype(np.float32)
    return np.concatenate([high, high, low], axis=1)


def sine_half(t):
    x = t * (math.pi / 512.0)
    s = x * x
    p = -2.50521084e-08
    p = p * s + 2.75573192e-06
    p = p * s - 1.98412698e-04
    p = p * s + 8.33333333e-03
    p = p * s - 1.66666667e-01
    return x + x * (s * p)


def grid_kernel(
    cycle_x, cycle_y, place_ref, qc_ref, fy_ref, fx_ref, ix_ref, iy_ref, out_ref,
    buf_a, buf_b, buf_c, buf_d, buf_e, trig_ref,
):
    mesh_x, mesh_y, mesh_z = (GRID_X * cycle_x, GRID_Y * cycle_y, GRID_Z)
    devices = cycle_x * cycle_y
    modes = mesh_z // 2 // devices
    coefs = 2 * modes
    first = place_ref[0] * modes
    columns = GRID_X * GRID_Y
    atoms = qc_ref.shape[2]

    row = lax.broadcasted_iota(jnp.int32, (ROWS, 1), 0) % coefs
    row_mode = first + row % modes
    row_sine = row >= modes
    row_edge = row_sine & (row_mode == 0)
    row_factor = jnp.where(row_edge, mesh_z // 2, row_mode)
    row_shift = jnp.where(row_sine & (row_mode != 0), mesh_z // 4, 0)
    column_iota = lax.broadcasted_iota(jnp.int32, (columns, atoms), 0)

    def columns_of(device):
        cell = qc_ref[device, 1:2, :].astype(jnp.int32)
        return cell, column_iota == lax.shift_right_logical(cell, 10)

    def spread(device, carry):
        cell, match = columns_of(device)
        depth = cell & (mesh_z - 1)
        turn = (row_factor * depth - row_shift) & (mesh_z - 1)
        trig = sine_half((jnp.abs(turn - mesh_z // 2) - mesh_z // 4).astype(F32))
        high = trig.astype(BF16)
        trig_ref[device, pl.ds(0, ROWS), :] = high
        trig_ref[device, pl.ds(ROWS, ROWS), :] = (trig - high.astype(F32)).astype(BF16)
        charged = trig * qc_ref[device, 0:1, :]
        high = charged.astype(BF16)
        low = (charged - high.astype(F32)).astype(BF16)
        pick = jnp.where(match, 1.0, 0.0).astype(BF16)
        total = contract_last(pick, jnp.concatenate([high, low] * (LANES // ROWS // 2), axis=0))
        total = total + pltpu.roll(total, ROWS, 1)
        buf_a[pl.ds(pl.multiple_of(device * columns, 8), columns), :] = total
        return carry

    lax.fori_loop(0, devices, spread, 0, unroll=8)

    lane = lax.broadcasted_iota(jnp.int32, (1, LANES), 1)
    lane_group = lane // ROWS

    def pack(copied):
        wide = copied[0]
        for g in range(1, GROUPS):
            wide = jnp.where(lane_group == g, copied[g], wide)
        return wide

    def unpack(wide):
        turned = [wide] + [pltpu.roll(wide, g * ROWS, 1) for g in range(1, GROUPS)]
        copied = []
        for i in range(GROUPS):
            copied.append(pack([turned[(g - i) % GROUPS] for g in range(GROUPS)]))
        return copied

    def apply(table_ref, wide):
        high = wide.astype(BF16)
        low = (wide - high.astype(F32)).astype(BF16)
        data = jnp.concatenate([high, low, high], axis=0)
        return jnp.dot(table_ref[...].astype(BF16), data, preferred_element_type=F32)

    for first_x in range(0, mesh_x, GROUPS):
        copied = []
        for place in range(first_x, first_x + GROUPS):
            rows = []
            for sy in range(cycle_y):
                start = ((place // GRID_X) * cycle_y + sy) * columns + (place % GRID_X) * GRID_Y
                rows.append(buf_a[pl.ds(start, GRID_Y), :])
            copied.append(jnp.concatenate(rows, axis=0))
        for i, part in enumerate(unpack(apply(fy_ref, pack(copied)))):
            buf_b[pl.ds((first_x + i) * mesh_y, mesh_y), :] = part

    lane_coef = lane % ROWS % coefs
    lane_mode = first + lane_coef % modes
    lane_sine = lane_coef >= modes
    lane_freq = jnp.where(lane_sine & (lane_mode == 0), mesh_z // 2, lane_mode)
    wave_z = lane_freq.astype(F32) * (2.0 * math.pi / mesh_z)
    lane_weight = jnp.where(lane_mode == 0, 1.0, 2.0) / mesh_z
    slope_z = jnp.where(lane_mode == 0, 0.0, wave_z) * jnp.where(lane_sine, 1.0, -1.0)
    freq_x = lax.broadcasted_iota(jnp.int32, (mesh_x, 1), 0)
    freq_x = jnp.where(freq_x <= mesh_x // 2, freq_x, freq_x - mesh_x // 2)
    wave_x = freq_x.astype(F32) * (2.0 * math.pi / mesh_x)
    near = wave_x * wave_x + wave_z * wave_z

    for first_y in range(0, mesh_y, GROUPS):
        copied = [
            buf_b[pl.ds(first_y + i, mesh_x, stride=mesh_y), :] for i in range(GROUPS)
        ]
        spectrum = apply(fx_ref, pack(copied))
        freq_y = first_y + lane_group
        freq_y = jnp.where(freq_y <= mesh_y // 2, freq_y, freq_y - mesh_y // 2)
        wave_y = freq_y.astype(F32) * (2.0 * math.pi / mesh_y)
        wave_sq = near + wave_y * wave_y
        zero = wave_sq == 0.0
        green = jnp.exp(-0.5 * SMEARING * SMEARING * wave_sq) / jnp.where(zero, 1.0, wave_sq)
        green = jnp.where(zero, 0.0, 4.0 * math.pi * green)
        both = apply(ix_ref, spectrum * (green * lane_weight))
        for i, part in enumerate(unpack(both)):
            rows = pl.ds((first_y + i) * mesh_x, mesh_x)
            buf_a[rows, :] = part[:mesh_x]
            buf_c[rows, :] = part[mesh_x:]

    for first_x in range(0, mesh_x, GROUPS):
        plain, sloped = (
            pack([buf[pl.ds(first_x + i, mesh_y, stride=mesh_x), :] for i in range(GROUPS)])
            for buf in (buf_a, buf_c)
        )
        both = apply(iy_ref, plain)
        along_x = apply(iy_ref.at[pl.ds(0, mesh_y), :], sloped)
        potential = both[:mesh_y]
        partner = jnp.where(
            lane % ROWS >= modes,
            pltpu.roll(potential, modes, 1),
            pltpu.roll(potential, LANES - modes, 1),
        )
        fields = (along_x, both[mesh_y:], partner * slope_z)
        for buf, wide in zip((buf_b, buf_d, buf_e), fields):
            for i, part in enumerate(unpack(wide)):
                buf[pl.ds((first_x + i) * mesh_y, mesh_y), :] = part

    use_low = (lane // ROWS) == 1
    use_none = (lane % ROWS) >= coefs

    def sample(device, carry):
        _, match = columns_of(device)
        rows = []
        for buf in (buf_b, buf_d, buf_e):
            for lx in range(GRID_X):
                place = (device // cycle_y) * GRID_X + lx
                start = place * mesh_y + (device % cycle_y) * GRID_Y
                rows.append(buf[pl.ds(pl.multiple_of(start, 8), GRID_Y), :])
        data = jnp.concatenate(rows, axis=0)
        high = data.astype(BF16).astype(F32)
        mixed = jnp.where(use_low, data - high, high)
        mixed = jnp.where(use_none, 0.0, mixed).astype(BF16)
        high = trig_ref[device, pl.ds(0, ROWS), :]
        low = trig_ref[device, pl.ds(ROWS, ROWS), :]
        waves = jnp.concatenate([high, high, low, jnp.zeros_like(low)], axis=0)
        fields = jnp.dot(mixed, waves, preferred_element_type=F32)
        picked = []
        for a in range(3):
            part = jnp.where(match, fields[a * columns : (a + 1) * columns], 0.0)
            picked.append(jnp.sum(part, axis=0, keepdims=True))
        for a in range(3):
            out_ref[device, a] = picked[a]
        return carry

    lax.fori_loop(0, devices, sample, 0, unroll=8)


def grid_fields(place, gathered, cycle_x, cycle_y):
    mesh_x, mesh_y = (GRID_X * cycle_x, GRID_Y * cycle_y)
    devices, _, atoms = gathered.shape
    ax, bx, cx = real_tables(mesh_x)
    ay, by, cy = real_tables(mesh_y)
    tables = [
        thirds(ay),
        thirds(ax),
        np.concatenate([thirds(bx), thirds(cx)], axis=0),
        np.concatenate([thirds(by), thirds(cy)], axis=0),
    ]
    plane = pltpu.VMEM((mesh_x * mesh_y, LANES), F32)
    vmem = pl.BlockSpec(memory_space=pltpu.VMEM)
    return pl.pallas_call(
        functools.partial(grid_kernel, cycle_x, cycle_y),
        in_specs=[pl.BlockSpec(memory_space=pltpu.SMEM)] + [vmem] * 5,
        out_specs=vmem,
        out_shape=jax.ShapeDtypeStruct((devices, 3, 1, atoms), F32),
        scratch_shapes=[plane] * 5
        + [pltpu.VMEM((devices, 2 * ROWS, atoms), BF16)],
        compiler_params=pltpu.CompilerParams(
            vmem_limit_bytes=5 * mesh_x * mesh_y * LANES * 4
            + devices * atoms * (4 * ROWS + 64)
            + (10 << 20)
        ),
        cost_estimate=pl.CostEstimate(
            flops=8_000_000_000, bytes_accessed=4_000_000, transcendentals=100_000
        ),
        name="grid_fields",
    )(place, gathered, *[jnp.asarray(t) for t in tables])


def edge_kernel(
    list_hbm, index_ref, feat_ref, pos_ref, mid_ref, up_ref, down_ref, w_self_ref, w_pair_ref,
    w_radial_ref, w_expand_ref, w_contract_ref, w_final_ref, out_ref,
    table, places, near_a, near_b, near_c, edge_a, edge_b, edge_c,
    total_a, total_b, total_c, marks, own_ref, sums_ref, w_half,
    list_ref, list_sem,
):
    atoms, channels = feat_ref.shape
    ghosts = mid_ref.shape[1] - EXTRA
    slots_all = atoms + 9 * ghosts
    per_atom = index_ref.shape[0]
    chunk = CHUNK_ATOMS * per_atom
    chunks = atoms // CHUNK_ATOMS
    basis_count = w_radial_ref.shape[0]
    spacing = CUTOFF_SQ / (basis_count - 1)
    latent = w_expand_ref.shape[1]
    width = latent // PIECES
    slots = per_atom // PIECES
    w_half[...] = w_expand_ref[...] * 0.5

    fetch = pltpu.make_async_copy(list_hbm, list_ref, list_sem)
    fetch.start()

    def fill(start, rows, coords, shift):
        count = rows.shape[0]
        projected = jnp.dot(rows, w_pair_ref[...], preferred_element_type=F32)
        projected = projected.astype(BF16).astype(F32)
        rows_of = table.reshape(slots_all * 2, LANES)
        rows_of[pl.ds(start * 2, count, stride=2), :] = projected[:, :channels] * 0.5
        rows_of[pl.ds(start * 2 + 1, count, stride=2), :] = projected[:, channels:]
        row = lax.broadcasted_iota(jnp.int32, (8, LANES), 0)
        offset = jnp.where(row == 0, shift[0], jnp.where(row == 1, shift[1], 0.0))
        places[start // LANES] = coords + offset

    pos = jnp.concatenate([pos_ref[...].astype(F32), jnp.zeros((5, atoms), F32)], axis=0)
    for i in range(atoms // LANES):
        rows = feat_ref[pl.ds(i * LANES, LANES), :]
        fill(i * LANES, rows, pos[:, i * LANES : (i + 1) * LANES], (0.0, 0.0))
        own = jnp.dot(rows, w_self_ref[...], preferred_element_type=F32)
        own_ref[pl.ds(i * LANES, LANES), :] = own * 0.5
    for sx in range(3):
        for sy, ref in enumerate((up_ref, mid_ref, down_ref)):
            block = 3 * sx + sy
            if block == 4:
                continue
            tail = ref[sx, pl.ds(ghosts, EXTRA), :].astype(F32)
            for h in range(ghosts // LANES):
                rows = ref[sx, pl.ds(h * LANES, LANES), :]
                start = atoms + block * ghosts + h * LANES
                fill(start, rows, tail[h * 8 : (h + 1) * 8], ((sx - 1) * BOX, (sy - 1) * BOX))

    feature = lax.broadcasted_iota(jnp.int32, (8, LANES), 0)
    skipped = range((atoms + 4 * ghosts) // LANES, (atoms + 5 * ghosts) // LANES)
    for i in range(atoms // LANES):
        columns = slice(i * LANES, (i + 1) * LANES)
        index = index_ref[:, columns]
        inside = index & (LANES - 1)
        outside = lax.shift_right_logical(index, 7)
        found = [jnp.zeros((per_atom, LANES), F32)] * 3
        for c in range(slots_all // LANES):
            if c in skipped:
                continue
            tile = places[c]
            here = outside == c
            for a in range(3):
                source = jnp.broadcast_to(tile[a : a + 1], (per_atom, LANES))
                value = jnp.take_along_axis(source, inside, axis=1)
                found[a] = jnp.where(here, value, found[a])
        disp = [found[a] - pos[a : a + 1, columns] for a in range(3)]
        d2 = disp[0] * disp[0] + disp[1] * disp[1] + disp[2] * disp[2]
        envelope = jnp.maximum(0.0, 1.0 - d2 * (1.0 / CUTOFF_SQ))
        envelope = envelope * envelope
        moments = [envelope] + [envelope * disp[a] for a in range(3)]
        for group in range(per_atom // GROUPS):
            stacked = []
            for k in range(group * GROUPS, (group + 1) * GROUPS):
                def wide(value):
                    return jnp.broadcast_to(value[k : k + 1], (8, LANES))

                t = wide(d2) * (1.0 / spacing) - feature.astype(F32)
                basis = jnp.exp(-(t * t))
                high = basis.astype(BF16).astype(F32)
                tail = jnp.where(feature == 0, wide(moments[0]), 0.0)
                for a in range(3):
                    tail = jnp.where(feature == 1 + a, wide(moments[1 + a]), tail)
                stacked += [high, basis - high, high, tail]
            marks[group, pl.ds(i * LANES, LANES), :] = jnp.concatenate(stacked, axis=0).T

    w_radial = w_radial_ref[...] * 0.5
    high = w_radial.astype(BF16).astype(F32)
    one = jnp.concatenate([high, high, w_radial - high, jnp.zeros((8, channels), F32)], axis=0)
    none = jnp.zeros((ROWS, channels), F32)
    blocks = []
    for g in range(GROUPS):
        column = [one if other == g else none for other in range(GROUPS)]
        blocks.append(jnp.concatenate(column, axis=0))
    w_basis = jnp.concatenate(blocks, axis=1).astype(BF16)

    part_rows = slots * CHUNK_ATOMS
    shape = (slots, CHUNK_ATOMS, LANES)

    def atoms_of(index):
        return pl.ds(pl.multiple_of(index * CHUNK_ATOMS, 16), CHUNK_ATOMS)

    def gather(index, near, part):
        for k in range(part * slots, (part + 1) * slots):
            start = k * atoms + index * CHUNK_ATOMS
            loaded = [table[list_ref[start + a]] for a in range(CHUNK_ATOMS)]
            for a, tile in enumerate(loaded):
                near[k * CHUNK_ATOMS + a] = tile

    def radials(index):
        basis = marks[:, atoms_of(index), :].reshape(-1, LANES).astype(BF16)
        return jnp.dot(basis, w_basis, preferred_element_type=F32)

    def enter(index, near, edge_in, part, wide):
        rows = pl.ds(part * part_rows, part_rows)
        groups = slots // GROUPS
        pieces = []
        for q in range(part * groups, (part + 1) * groups):
            for g in range(GROUPS):
                rows_q = slice(q * CHUNK_ATOMS, (q + 1) * CHUNK_ATOMS)
                pieces.append(wide[rows_q, g * LANES : (g + 1) * LANES])
        radial = jnp.concatenate(pieces, axis=0).reshape(shape)
        bias = near.reshape(2 * chunk, LANES)[pl.ds(part * part_rows * 2, part_rows, stride=2), :]
        half = radial + own_ref[atoms_of(index), :][None] + bias.reshape(shape)
        turn = jnp.tanh(half.astype(BF16)).astype(F32)
        edge_in[rows, :] = (half + half * turn).astype(BF16).reshape(part_rows, LANES)

    def expand(edge_in, part):
        cols = pl.ds(part * width, width)
        return jnp.dot(edge_in[...], w_half[:, cols], preferred_element_type=F32).astype(BF16)

    def contract(half, part):
        hidden = half + half * jnp.tanh(half)
        cols = pl.ds(part * width, width)
        return jnp.dot(hidden, w_contract_ref[cols, :], preferred_element_type=F32)

    def collect(index, near, total, part, before):
        rows = pl.ds(part * part_rows, part_rows)
        other = pl.ds(part * part_rows * 2 + 1, part_rows, stride=2)
        weight = (total[rows, :] * near.reshape(2 * chunk, LANES)[other, :]).reshape(shape)
        after = []
        for s in range(4):
            summed = 0.0
            for k in range(slots):
                column = k % GROUPS * ROWS + 3 * basis_count + s
                tile = marks[(part * slots + k) // GROUPS, atoms_of(index), :]
                summed = summed + weight[k] * tile[:, column : column + 1]
            after.append(summed if before is None else before[s] + summed)
        return after

    def keep(index, sums):
        for s in range(4):
            sums_ref[s, atoms_of(index), :] = sums[s]

    def stage(index, nears, edges, totals):
        after = jnp.minimum(index + 1, chunks - 1)
        before = jnp.maximum(index - 1, 0)
        mixed, sums = (None, None)
        half = expand(edges[0], 0)
        wide = radials(after)
        for part in range(PIECES):
            gather(after, nears[1], part)
            following = expand(edges[0], part + 1) if part + 1 < PIECES else None
            sums = collect(before, nears[2], totals[2], part, sums)
            term = contract(half, part)
            mixed = term if mixed is None else mixed + term
            enter(after, nears[1], edges[1], part, wide)
            half = following
        totals[0][...] = mixed
        keep(before, sums)

    nears = (near_a, near_b, near_c)
    edges = (edge_a, edge_b, edge_c)
    totals = (total_a, total_b, total_c)
    fetch.wait()
    for part in range(PIECES):
        gather(0, near_a, part)
    wide = radials(0)
    for part in range(PIECES):
        enter(0, near_a, edge_a, part, wide)

    def triple(step, carry):
        for i in range(3):
            order = (i, (i + 1) % 3, (i + 2) % 3)
            pick = lambda refs: [refs[o] for o in order]
            stage(3 * step + i, pick(nears), pick(edges), pick(totals))
        return carry

    lax.fori_loop(0, chunks // 3, triple, 0)
    sums = None
    for part in range(PIECES):
        sums = collect(chunks - 1, near_c, total_c, part, sums)
    keep(chunks - 1, sums)

    scale = 1.0 / math.sqrt(per_atom)
    vector = [sums_ref[1 + a] * scale for a in range(3)]
    square = vector[0] * vector[0] + vector[1] * vector[1] + vector[2] * vector[2]
    invariant = (sums_ref[0] * scale + square * (1.0 / 3.0)).astype(BF16)
    gate = jnp.dot(invariant, w_final_ref[...], preferred_element_type=F32)
    gate = gate * (0.5 + 0.5 * jnp.tanh(0.5 * gate)) * (1.0 / math.sqrt(channels))
    ones = jnp.ones((8, channels), F32)
    for a in range(3):
        out_ref[a] = contract_last(ones, vector[a] * gate, HIGHEST)[:1]


def edge_forces(lists, index, feat, pos, mid, up, down, w_self, w_pair, w_radial, w_expand, w_contract, w_final):
    atoms, channels = feat.shape
    per_atom = index.shape[0]
    ghosts = mid.shape[1] - EXTRA
    slots_all = atoms + 9 * ghosts
    chunk = CHUNK_ATOMS * per_atom
    vmem = pl.BlockSpec(memory_space=pltpu.VMEM)
    edges = atoms * per_atom
    latent = w_expand.shape[1]
    return pl.pallas_call(
        edge_kernel,
        in_specs=[pl.BlockSpec(memory_space=pl.ANY)] + [vmem] * 12,
        out_specs=vmem,
        out_shape=jax.ShapeDtypeStruct((3, 1, atoms), F32),
        scratch_shapes=[
            pltpu.VMEM((slots_all, 2, LANES), F32),
            pltpu.VMEM((slots_all // LANES, 8, LANES), F32),
        ]
        + [pltpu.VMEM((chunk, 2, LANES), F32)] * 3
        + [pltpu.VMEM((chunk, LANES), BF16)] * 3
        + [pltpu.VMEM((chunk, LANES), F32)] * 3
        + [
            pltpu.VMEM((per_atom // GROUPS, atoms, LANES), F32),
            pltpu.VMEM((atoms, LANES), F32),
            pltpu.VMEM((4, atoms, LANES), F32),
            pltpu.VMEM(w_expand.shape, BF16),
            pltpu.SMEM(lists.shape, lists.dtype),
            pltpu.SemaphoreType.DMA(()),
        ],
        compiler_params=pltpu.CompilerParams(vmem_limit_bytes=32 << 20),
        cost_estimate=pl.CostEstimate(
            flops=4 * edges * channels * latent,
            bytes_accessed=4_000_000,
            transcendentals=edges * latent,
        ),
        name="edge_forces",
    )(
        lists, index, feat, pos, mid, up, down, w_self, w_pair, w_radial,
        w_expand, w_contract, w_final,
    )


def ring(array, axis, step):
    size = lax.axis_size(axis)
    return lax.ppermute(array, axis, [(i, (i + step) % size) for i in range(size)])


def shards(
    features, positions, atom_count, ghost_index, neighbour_list, cell_index, w_self, w_pair,
    w_radial, w_expand, w_contract, w_final, w_charge,
):
    feat = features[0, 0]
    pos = positions[0, 0]
    cycle_x, cycle_y = (lax.axis_size("dx"), lax.axis_size("dy"))
    spread = charges(cycle_x * cycle_y, atom_count, feat, cell_index[0, 0], w_charge)
    exported = exports_after(spread, feat, pos, ghost_index[0, 0])
    gathered = lax.all_to_all(spread, ("dx", "dy"), split_axis=0, concat_axis=0, tiled=True)
    mid = jnp.stack([ring(exported, "dx", 1), exported, ring(exported, "dx", -1)])
    index = neighbour_list[0, 0].T
    lists = index.reshape(-1)
    gathered, mid, lists = lax.optimization_barrier((gathered, mid, lists))
    up = ring(mid, "dy", 1)
    down = ring(mid, "dy", -1)
    place = lax.axis_index("dx") * cycle_y + lax.axis_index("dy")
    partial = grid_fields(place[None].astype(jnp.int32), gathered, cycle_x, cycle_y)
    received = lax.all_to_all(partial, ("dx", "dy"), split_axis=0, concat_axis=0, tiled=True)
    short = edge_forces(
        lists, index, feat, pos, mid, up, down, w_self, w_pair, w_radial, w_expand,
        w_contract, w_final,
    )
    field = jnp.sum(received, axis=0)
    total = short + spread[0, :1] * field
    live = lax.broadcasted_iota(jnp.int32, (1, feat.shape[0]), 1) < atom_count[0, 0]
    return jnp.where(live, total, jnp.zeros_like(total)).transpose(1, 0, 2)[None]


def solution(mesh):
    placed = (
        P("dx", "dy", None, None),
        P("dx", "dy", None, None),
        P("dx", "dy"),
        P("dx", "dy", None),
        P("dx", "dy", None, None),
        P("dx", "dy", None),
    ) + (P(),) * 7
    return jax.shard_map(
        shards, mesh=mesh, in_specs=placed, out_specs=P("dx", "dy", None, None), check_vma=False
    )
```

```python
import functools
import math

import jax
import jax.numpy as jnp
import numpy as np
from jax import lax
from jax.experimental import pallas as pl
from jax.experimental.pallas import tpu as pltpu
from jax.sharding import PartitionSpec as P

GRID_X = 8
GRID_Y = 8
GRID_Z = 1024
BOX = 1.0
CUTOFF_SQ = 6.25
SMEARING = 1.0

LANES = 128
EXTRA = 16
ROWS = 32
GROUPS = LANES // ROWS
CHUNK_ATOMS = 32
PIECES = 4
HIGHEST = lax.Precision.HIGHEST
F32 = jnp.float32
BF16 = jnp.bfloat16


def contract_first(a, b, precision=None):
    return lax.dot_general(
        a, b, (((0,), (0,)), ((), ())), precision=precision, preferred_element_type=F32
    )


def contract_last(a, b, precision=None):
    return lax.dot_general(
        a, b, (((1,), (1,)), ((), ())), precision=precision, preferred_element_type=F32
    )


def charge_kernel(count_ref, feat_ref, cell_ref, wq_ref, qc_ref):
    atoms = feat_ref.shape[0]
    weights = jnp.broadcast_to(wq_ref[...].astype(F32), (16, LANES)).astype(BF16)
    charge = contract_last(weights, feat_ref[...])[:1]
    live = lax.broadcasted_iota(jnp.int32, (1, atoms), 1) < count_ref[0, 0]
    both = jnp.concatenate([jnp.where(live, charge, 0.0), cell_ref[...].astype(F32)], axis=0)
    qc_ref[...] = jnp.broadcast_to(both[None], qc_ref.shape)


def export_kernel(feat_ref, pos_ref, export_ref, after_ref, out_ref):
    atoms = feat_ref.shape[0]
    ghosts = export_ref.shape[1]
    pick = lax.broadcasted_iota(jnp.int32, (atoms, ghosts), 0) == export_ref[...]
    pick = jnp.where(pick, 1.0, 0.0).astype(BF16)
    out_ref[pl.ds(0, ghosts), :] = contract_first(pick, feat_ref[...]).astype(BF16)
    pos = jnp.concatenate([pos_ref[...].astype(F32), jnp.zeros((13, atoms), F32)], axis=0)
    coords = jnp.dot(pos.astype(BF16), pick, preferred_element_type=F32)
    tail = [coords[:8, h * LANES : (h + 1) * LANES] for h in range(ghosts // LANES)]
    out_ref[pl.ds(ghosts, EXTRA), :] = jnp.concatenate(tail, axis=0).astype(BF16)


def charges(devices, count, feat, cells, w_charge):
    vmem = pl.BlockSpec(memory_space=pltpu.VMEM)
    return pl.pallas_call(
        charge_kernel,
        in_specs=[pl.BlockSpec(memory_space=pltpu.SMEM)] + [vmem] * 3,
        out_specs=vmem,
        out_shape=jax.ShapeDtypeStruct((devices, 2, feat.shape[0]), F32),
        compiler_params=pltpu.CompilerParams(vmem_limit_bytes=60 << 20),
        name="charges",
    )(count, feat, cells[None], w_charge[None])


def exports_after(after, feat, pos, exports):
    vmem = pl.BlockSpec(memory_space=pltpu.VMEM)
    return pl.pallas_call(
        export_kernel,
        in_specs=[vmem] * 3 + [pl.BlockSpec(memory_space=pl.ANY)],
        out_specs=vmem,
        out_shape=jax.ShapeDtypeStruct((exports.shape[0] + EXTRA, feat.shape[1]), BF16),
        compiler_params=pltpu.CompilerParams(vmem_limit_bytes=16 << 20),
        name="exports",
    )(feat, pos, exports[None], after)


def real_tables(count):
    half = count // 2
    index = np.arange(count)
    freq = np.where(index <= half, index, index - half)
    place = np.arange(count)
    angle = 2.0 * np.pi * (freq[:, None] * place[None, :] % count) / count
    is_cos = (index <= half)[:, None]
    basis = np.where(is_cos, np.cos(angle), np.sin(angle))
    weight = np.where((index == 0) | (index == half), 1.0, 2.0)[:, None] / count
    wave = np.where(index == half, 0.0, 2.0 * np.pi * freq / count)[:, None]
    slope = np.where(is_cos, np.sin(angle), -np.cos(angle)) * wave
    return (basis, (weight * basis).T, (weight * slope).T)


def thirds(table):
    whole = table.astype(np.float32)
    high = whole.astype(BF16).astype(np.float32)
    low = (whole - high).astype(BF16).astype(np.float32)
    return np.concatenate([high, high, low], axis=1)


def sine_half(t):
    x = t * (math.pi / 512.0)
    s = x * x
    p = -2.50521084e-08
    p = p * s + 2.75573192e-06
    p = p * s - 1.98412698e-04
    p = p * s + 8.33333333e-03
    p = p * s - 1.66666667e-01
    return x + x * (s * p)


def grid_kernel(
    cycle_x, cycle_y, place_ref, qc_ref, fy_ref, fx_ref, ix_ref, iy_ref, out_ref,
    buf_a, buf_b, buf_c, buf_d, buf_e, trig_ref,
):
    mesh_x, mesh_y, mesh_z = (GRID_X * cycle_x, GRID_Y * cycle_y, GRID_Z)
    devices = cycle_x * cycle_y
    modes = mesh_z // 2 // devices
    coefs = 2 * modes
    first = place_ref[0] * modes
    columns = GRID_X * GRID_Y
    atoms = qc_ref.shape[2]

    row = lax.broadcasted_iota(jnp.int32, (ROWS, 1), 0) % coefs
    row_mode = first + row % modes
    row_sine = row >= modes
    row_edge = row_sine & (row_mode == 0)
    row_factor = jnp.where(row_edge, mesh_z // 2, row_mode)
    row_shift = jnp.where(row_sine & (row_mode != 0), mesh_z // 4, 0)
    column_iota = lax.broadcasted_iota(jnp.int32, (columns, atoms), 0)

    def columns_of(device):
        cell = qc_ref[device, 1:2, :].astype(jnp.int32)
        return cell, column_iota == lax.shift_right_logical(cell, 10)

    def spread(device, carry):
        cell, match = columns_of(device)
        depth = cell & (mesh_z - 1)
        turn = (row_factor * depth - row_shift) & (mesh_z - 1)
        trig = sine_half((jnp.abs(turn - mesh_z // 2) - mesh_z // 4).astype(F32))
        high = trig.astype(BF16)
        trig_ref[device, pl.ds(0, ROWS), :] = high
        trig_ref[device, pl.ds(ROWS, ROWS), :] = (trig - high.astype(F32)).astype(BF16)
        charged = trig * qc_ref[device, 0:1, :]
        high = charged.astype(BF16)
        low = (charged - high.astype(F32)).astype(BF16)
        pick = jnp.where(match, 1.0, 0.0).astype(BF16)
        total = contract_last(pick, jnp.concatenate([high, low] * (LANES // ROWS // 2), axis=0))
        total = total + pltpu.roll(total, ROWS, 1)
        buf_a[pl.ds(pl.multiple_of(device * columns, 8), columns), :] = total
        return carry

    lax.fori_loop(0, devices, spread, 0, unroll=8)

    lane = lax.broadcasted_iota(jnp.int32, (1, LANES), 1)
    lane_group = lane // ROWS

    def pack(copied):
        wide = copied[0]
        for g in range(1, GROUPS):
            wide = jnp.where(lane_group == g, copied[g], wide)
        return wide

    def unpack(wide):
        turned = [wide] + [pltpu.roll(wide, g * ROWS, 1) for g in range(1, GROUPS)]
        copied = []
        for i in range(GROUPS):
            copied.append(pack([turned[(g - i) % GROUPS] for g in range(GROUPS)]))
        return copied

    def apply(table_ref, wide):
        high = wide.astype(BF16)
        low = (wide - high.astype(F32)).astype(BF16)
        data = jnp.concatenate([high, low, high], axis=0)
        return jnp.dot(table_ref[...].astype(BF16), data, preferred_element_type=F32)

    for first_x in range(0, mesh_x, GROUPS):
        copied = []
        for place in range(first_x, first_x + GROUPS):
            rows = []
            for sy in range(cycle_y):
                start = ((place // GRID_X) * cycle_y + sy) * columns + (place % GRID_X) * GRID_Y
                rows.append(buf_a[pl.ds(start, GRID_Y), :])
            copied.append(jnp.concatenate(rows, axis=0))
        for i, part in enumerate(unpack(apply(fy_ref, pack(copied)))):
            buf_b[pl.ds((first_x + i) * mesh_y, mesh_y), :] = part

    lane_coef = lane % ROWS % coefs
    lane_mode = first + lane_coef % modes
    lane_sine = lane_coef >= modes
    lane_freq = jnp.where(lane_sine & (lane_mode == 0), mesh_z // 2, lane_mode)
    wave_z = lane_freq.astype(F32) * (2.0 * math.pi / mesh_z)
    lane_weight = jnp.where(lane_mode == 0, 1.0, 2.0) / mesh_z
    slope_z = jnp.where(lane_mode == 0, 0.0, wave_z) * jnp.where(lane_sine, 1.0, -1.0)
    freq_x = lax.broadcasted_iota(jnp.int32, (mesh_x, 1), 0)
    freq_x = jnp.where(freq_x <= mesh_x // 2, freq_x, freq_x - mesh_x // 2)
    wave_x = freq_x.astype(F32) * (2.0 * math.pi / mesh_x)
    near = wave_x * wave_x + wave_z * wave_z

    for first_y in range(0, mesh_y, GROUPS):
        copied = [
            buf_b[pl.ds(first_y + i, mesh_x, stride=mesh_y), :] for i in range(GROUPS)
        ]
        spectrum = apply(fx_ref, pack(copied))
        freq_y = first_y + lane_group
        freq_y = jnp.where(freq_y <= mesh_y // 2, freq_y, freq_y - mesh_y // 2)
        wave_y = freq_y.astype(F32) * (2.0 * math.pi / mesh_y)
        wave_sq = near + wave_y * wave_y
        zero = wave_sq == 0.0
        green = jnp.exp(-0.5 * SMEARING * SMEARING * wave_sq) / jnp.where(zero, 1.0, wave_sq)
        green = jnp.where(zero, 0.0, 4.0 * math.pi * green)
        both = apply(ix_ref, spectrum * (green * lane_weight))
        for i, part in enumerate(unpack(both)):
            rows = pl.ds((first_y + i) * mesh_x, mesh_x)
            buf_a[rows, :] = part[:mesh_x]
            buf_c[rows, :] = part[mesh_x:]

    for first_x in range(0, mesh_x, GROUPS):
        plain, sloped = (
            pack([buf[pl.ds(first_x + i, mesh_y, stride=mesh_x), :] for i in range(GROUPS)])
            for buf in (buf_a, buf_c)
        )
        both = apply(iy_ref, plain)
        along_x = apply(iy_ref.at[pl.ds(0, mesh_y), :], sloped)
        potential = both[:mesh_y]
        partner = jnp.where(
            lane % ROWS >= modes,
            pltpu.roll(potential, modes, 1),
            pltpu.roll(potential, LANES - modes, 1),
        )
        fields = (along_x, both[mesh_y:], partner * slope_z)
        for buf, wide in zip((buf_b, buf_d, buf_e), fields):
            for i, part in enumerate(unpack(wide)):
                buf[pl.ds((first_x + i) * mesh_y, mesh_y), :] = part

    use_low = (lane // ROWS) == 1
    use_none = (lane % ROWS) >= coefs

    def sample(device, carry):
        _, match = columns_of(device)
        rows = []
        for buf in (buf_b, buf_d, buf_e):
            for lx in range(GRID_X):
                place = (device // cycle_y) * GRID_X + lx
                start = place * mesh_y + (device % cycle_y) * GRID_Y
                rows.append(buf[pl.ds(pl.multiple_of(start, 8), GRID_Y), :])
        data = jnp.concatenate(rows, axis=0)
        high = data.astype(BF16).astype(F32)
        mixed = jnp.where(use_low, data - high, high)
        mixed = jnp.where(use_none, 0.0, mixed).astype(BF16)
        high = trig_ref[device, pl.ds(0, ROWS), :]
        low = trig_ref[device, pl.ds(ROWS, ROWS), :]
        waves = jnp.concatenate([high, high, low, jnp.zeros_like(low)], axis=0)
        fields = jnp.dot(mixed, waves, preferred_element_type=F32)
        picked = []
        for a in range(3):
            part = jnp.where(match, fields[a * columns : (a + 1) * columns], 0.0)
            picked.append(jnp.sum(part, axis=0, keepdims=True))
        for a in range(3):
            out_ref[device, a] = picked[a]
        return carry

    lax.fori_loop(0, devices, sample, 0, unroll=8)


def grid_fields(place, gathered, cycle_x, cycle_y):
    mesh_x, mesh_y = (GRID_X * cycle_x, GRID_Y * cycle_y)
    devices, _, atoms = gathered.shape
    ax, bx, cx = real_tables(mesh_x)
    ay, by, cy = real_tables(mesh_y)
    tables = [
        thirds(ay),
        thirds(ax),
        np.concatenate([thirds(bx), thirds(cx)], axis=0),
        np.concatenate([thirds(by), thirds(cy)], axis=0),
    ]
    plane = pltpu.VMEM((mesh_x * mesh_y, LANES), F32)
    vmem = pl.BlockSpec(memory_space=pltpu.VMEM)
    return pl.pallas_call(
        functools.partial(grid_kernel, cycle_x, cycle_y),
        in_specs=[pl.BlockSpec(memory_space=pltpu.SMEM)] + [vmem] * 5,
        out_specs=vmem,
        out_shape=jax.ShapeDtypeStruct((devices, 3, 1, atoms), F32),
        scratch_shapes=[plane] * 5
        + [pltpu.VMEM((devices, 2 * ROWS, atoms), BF16)],
        compiler_params=pltpu.CompilerParams(
            vmem_limit_bytes=5 * mesh_x * mesh_y * LANES * 4
            + devices * atoms * (4 * ROWS + 64)
            + (10 << 20)
        ),
        cost_estimate=pl.CostEstimate(
            flops=8_000_000_000, bytes_accessed=4_000_000, transcendentals=100_000
        ),
        name="grid_fields",
    )(place, gathered, *[jnp.asarray(t) for t in tables])


def edge_kernel(
    list_hbm, index_ref, feat_ref, pos_ref, mid_ref, up_ref, down_ref, w_self_ref, w_pair_ref,
    w_radial_ref, w_expand_ref, w_contract_ref, w_final_ref, out_ref,
    table, places, near_a, near_b, near_c, edge_a, edge_b, edge_c,
    total_a, total_b, total_c, marks, own_ref, sums_ref, w_half, w_back,
    list_ref, list_sem,
):
    atoms, channels = feat_ref.shape
    ghosts = mid_ref.shape[1] - EXTRA
    slots_all = atoms + 9 * ghosts
    per_atom = index_ref.shape[0]
    chunk = CHUNK_ATOMS * per_atom
    chunks = atoms // CHUNK_ATOMS
    basis_count = w_radial_ref.shape[0]
    spacing = CUTOFF_SQ / (basis_count - 1)
    latent = w_expand_ref.shape[1]
    slots = per_atom // PIECES
    for i in range(latent // LANES):
        rows = pl.ds(i * LANES, LANES)
        w_half[rows, :] = (w_expand_ref[:, rows].astype(F32) * 0.5).T.astype(BF16)
        w_back[:, rows] = w_contract_ref[rows, :].astype(F32).T.astype(BF16)

    fetch = pltpu.make_async_copy(list_hbm, list_ref, list_sem)
    fetch.start()

    def fill(start, rows, coords, shift):
        count = rows.shape[0]
        projected = jnp.dot(rows, w_pair_ref[...], preferred_element_type=F32)
        projected = projected.astype(BF16).astype(F32)
        rows_of = table.reshape(slots_all * 2, LANES)
        rows_of[pl.ds(start * 2, count, stride=2), :] = projected[:, :channels] * 0.5
        rows_of[pl.ds(start * 2 + 1, count, stride=2), :] = projected[:, channels:]
        row = lax.broadcasted_iota(jnp.int32, (8, LANES), 0)
        offset = jnp.where(row == 0, shift[0], jnp.where(row == 1, shift[1], 0.0))
        places[start // LANES] = coords + offset

    pos = jnp.concatenate([pos_ref[...].astype(F32), jnp.zeros((5, atoms), F32)], axis=0)
    for i in range(atoms // LANES):
        rows = feat_ref[pl.ds(i * LANES, LANES), :]
        fill(i * LANES, rows, pos[:, i * LANES : (i + 1) * LANES], (0.0, 0.0))
        own = jnp.dot(rows, w_self_ref[...], preferred_element_type=F32)
        own_ref[pl.ds(i * LANES, LANES), :] = own * 0.5
    for sx in range(3):
        for sy, ref in enumerate((up_ref, mid_ref, down_ref)):
            block = 3 * sx + sy
            if block == 4:
                continue
            tail = ref[sx, pl.ds(ghosts, EXTRA), :].astype(F32)
            for h in range(ghosts // LANES):
                rows = ref[sx, pl.ds(h * LANES, LANES), :]
                start = atoms + block * ghosts + h * LANES
                fill(start, rows, tail[h * 8 : (h + 1) * 8], ((sx - 1) * BOX, (sy - 1) * BOX))

    feature = lax.broadcasted_iota(jnp.int32, (8, LANES), 0)
    skipped = range((atoms + 4 * ghosts) // LANES, (atoms + 5 * ghosts) // LANES)
    for i in range(atoms // LANES):
        columns = slice(i * LANES, (i + 1) * LANES)
        index = index_ref[:, columns]
        inside = index & (LANES - 1)
        outside = lax.shift_right_logical(index, 7)
        found = [jnp.zeros((per_atom, LANES), F32)] * 3
        for c in range(slots_all // LANES):
            if c in skipped:
                continue
            tile = places[c]
            here = outside == c
            for a in range(3):
                source = jnp.broadcast_to(tile[a : a + 1], (per_atom, LANES))
                value = jnp.take_along_axis(source, inside, axis=1)
                found[a] = jnp.where(here, value, found[a])
        disp = [found[a] - pos[a : a + 1, columns] for a in range(3)]
        d2 = disp[0] * disp[0] + disp[1] * disp[1] + disp[2] * disp[2]
        envelope = jnp.maximum(0.0, 1.0 - d2 * (1.0 / CUTOFF_SQ))
        envelope = envelope * envelope
        moments = [envelope] + [envelope * disp[a] for a in range(3)]
        for group in range(per_atom // GROUPS):
            stacked = []
            for k in range(group * GROUPS, (group + 1) * GROUPS):
                def wide(value):
                    return jnp.broadcast_to(value[k : k + 1], (8, LANES))

                t = wide(d2) * (1.0 / spacing) - feature.astype(F32)
                basis = jnp.exp(-(t * t))
                high = basis.astype(BF16).astype(F32)
                tail = jnp.where(feature == 0, wide(moments[0]), 0.0)
                for a in range(3):
                    tail = jnp.where(feature == 1 + a, wide(moments[1 + a]), tail)
                stacked += [high, basis - high, high, tail]
            marks[group, pl.ds(i * LANES, LANES), :] = jnp.concatenate(stacked, axis=0).T

    w_radial = w_radial_ref[...] * 0.5
    high = w_radial.astype(BF16).astype(F32)
    one = jnp.concatenate([high, high, w_radial - high, jnp.zeros((8, channels), F32)], axis=0)
    none = jnp.zeros((ROWS, channels), F32)
    blocks = []
    for g in range(GROUPS):
        column = [one if other == g else none for other in range(GROUPS)]
        blocks.append(jnp.concatenate(column, axis=0))
    w_basis = jnp.concatenate(blocks, axis=1).astype(BF16)

    part_rows = slots * CHUNK_ATOMS
    shape = (slots, CHUNK_ATOMS, LANES)

    def atoms_of(index):
        return pl.ds(pl.multiple_of(index * CHUNK_ATOMS, 16), CHUNK_ATOMS)

    def gather(index, near, part):
        for k in range(part * slots, (part + 1) * slots):
            start = k * atoms + index * CHUNK_ATOMS
            loaded = [table[list_ref[start + a]] for a in range(CHUNK_ATOMS)]
            for a, tile in enumerate(loaded):
                near[k * CHUNK_ATOMS + a] = tile

    def radials(index):
        basis = marks[:, atoms_of(index), :].reshape(-1, LANES).astype(BF16)
        return jnp.dot(basis, w_basis, preferred_element_type=F32)

    def enter(index, near, edge_in, part, wide):
        rows = pl.ds(part * part_rows, part_rows)
        groups = slots // GROUPS
        pieces = []
        for q in range(part * groups, (part + 1) * groups):
            for g in range(GROUPS):
                rows_q = slice(q * CHUNK_ATOMS, (q + 1) * CHUNK_ATOMS)
                pieces.append(wide[rows_q, g * LANES : (g + 1) * LANES])
        radial = jnp.concatenate(pieces, axis=0).reshape(shape)
        bias = near.reshape(2 * chunk, LANES)[pl.ds(part * part_rows * 2, part_rows, stride=2), :]
        half = radial + own_ref[atoms_of(index), :][None] + bias.reshape(shape)
        turn = jnp.tanh(half.astype(BF16)).astype(F32)
        edge_in[rows, :] = (half + half * turn).astype(BF16).reshape(part_rows, LANES)

    def network(edge_in, part):
        rows = pl.ds(part * part_rows, part_rows)
        half = contract_last(w_half[...], edge_in[rows, :]).astype(BF16)
        hidden = half + half * jnp.tanh(half)
        return jnp.dot(w_back[...], hidden, preferred_element_type=F32).T

    def collect(index, near, total, part, before):
        rows = pl.ds(part * part_rows, part_rows)
        other = pl.ds(part * part_rows * 2 + 1, part_rows, stride=2)
        weight = (total[rows, :] * near.reshape(2 * chunk, LANES)[other, :]).reshape(shape)
        after = []
        for s in range(4):
            summed = 0.0
            for k in range(slots):
                column = k % GROUPS * ROWS + 3 * basis_count + s
                tile = marks[(part * slots + k) // GROUPS, atoms_of(index), :]
                summed = summed + weight[k] * tile[:, column : column + 1]
            after.append(summed if before is None else before[s] + summed)
        return after

    def keep(index, sums):
        for s in range(4):
            sums_ref[s, atoms_of(index), :] = sums[s]

    def stage(index, nears, edges, totals):
        after = jnp.minimum(index + 1, chunks - 1)
        before = jnp.maximum(index - 1, 0)
        sums = None
        wide = radials(after)
        for part in range(PIECES):
            gather(after, nears[1], part)
            sums = collect(before, nears[2], totals[2], part, sums)
            totals[0][pl.ds(part * part_rows, part_rows), :] = network(edges[0], part)
            enter(after, nears[1], edges[1], part, wide)
        keep(before, sums)

    nears = (near_a, near_b, near_c)
    edges = (edge_a, edge_b, edge_c)
    totals = (total_a, total_b, total_c)
    fetch.wait()
    for part in range(PIECES):
        gather(0, near_a, part)
    wide = radials(0)
    for part in range(PIECES):
        enter(0, near_a, edge_a, part, wide)

    def triple(step, carry):
        for i in range(3):
            order = (i, (i + 1) % 3, (i + 2) % 3)
            pick = lambda refs: [refs[o] for o in order]
            stage(3 * step + i, pick(nears), pick(edges), pick(totals))
        return carry

    lax.fori_loop(0, chunks // 3, triple, 0)
    sums = None
    for part in range(PIECES):
        sums = collect(chunks - 1, near_c, total_c, part, sums)
    keep(chunks - 1, sums)

    scale = 1.0 / math.sqrt(per_atom)
    vector = [sums_ref[1 + a] * scale for a in range(3)]
    square = vector[0] * vector[0] + vector[1] * vector[1] + vector[2] * vector[2]
    invariant = (sums_ref[0] * scale + square * (1.0 / 3.0)).astype(BF16)
    gate = jnp.dot(invariant, w_final_ref[...], preferred_element_type=F32)
    gate = gate * (0.5 + 0.5 * jnp.tanh(0.5 * gate)) * (1.0 / math.sqrt(channels))
    ones = jnp.ones((8, channels), F32)
    for a in range(3):
        out_ref[a] = contract_last(ones, vector[a] * gate, HIGHEST)[:1]


def edge_forces(lists, index, feat, pos, mid, up, down, w_self, w_pair, w_radial, w_expand, w_contract, w_final):
    atoms, channels = feat.shape
    per_atom = index.shape[0]
    ghosts = mid.shape[1] - EXTRA
    slots_all = atoms + 9 * ghosts
    chunk = CHUNK_ATOMS * per_atom
    vmem = pl.BlockSpec(memory_space=pltpu.VMEM)
    edges = atoms * per_atom
    latent = w_expand.shape[1]
    return pl.pallas_call(
        edge_kernel,
        in_specs=[pl.BlockSpec(memory_space=pl.ANY)] + [vmem] * 12,
        out_specs=vmem,
        out_shape=jax.ShapeDtypeStruct((3, 1, atoms), F32),
        scratch_shapes=[
            pltpu.VMEM((slots_all, 2, LANES), F32),
            pltpu.VMEM((slots_all // LANES, 8, LANES), F32),
        ]
        + [pltpu.VMEM((chunk, 2, LANES), F32)] * 3
        + [pltpu.VMEM((chunk, LANES), BF16)] * 3
        + [pltpu.VMEM((chunk, LANES), F32)] * 3
        + [
            pltpu.VMEM((per_atom // GROUPS, atoms, LANES), F32),
            pltpu.VMEM((atoms, LANES), F32),
            pltpu.VMEM((4, atoms, LANES), F32),
            pltpu.VMEM(w_contract.shape, BF16),
            pltpu.VMEM(w_expand.shape, BF16),
            pltpu.SMEM(lists.shape, lists.dtype),
            pltpu.SemaphoreType.DMA(()),
        ],
        compiler_params=pltpu.CompilerParams(vmem_limit_bytes=32 << 20),
        cost_estimate=pl.CostEstimate(
            flops=4 * edges * channels * latent,
            bytes_accessed=4_000_000,
            transcendentals=edges * latent,
        ),
        name="edge_forces",
    )(
        lists, index, feat, pos, mid, up, down, w_self, w_pair, w_radial,
        w_expand, w_contract, w_final,
    )


def ring(array, axis, step):
    size = lax.axis_size(axis)
    return lax.ppermute(array, axis, [(i, (i + step) % size) for i in range(size)])


def shards(
    features, positions, atom_count, ghost_index, neighbour_list, cell_index, w_self, w_pair,
    w_radial, w_expand, w_contract, w_final, w_charge,
):
    feat = features[0, 0]
    pos = positions[0, 0]
    cycle_x, cycle_y = (lax.axis_size("dx"), lax.axis_size("dy"))
    spread = charges(cycle_x * cycle_y, atom_count, feat, cell_index[0, 0], w_charge)
    exported = exports_after(spread, feat, pos, ghost_index[0, 0])
    gathered = lax.all_to_all(spread, ("dx", "dy"), split_axis=0, concat_axis=0, tiled=True)
    mid = jnp.stack([ring(exported, "dx", 1), exported, ring(exported, "dx", -1)])
    index = neighbour_list[0, 0].T
    lists = index.reshape(-1)
    gathered, mid, lists = lax.optimization_barrier((gathered, mid, lists))
    up = ring(mid, "dy", 1)
    down = ring(mid, "dy", -1)
    place = lax.axis_index("dx") * cycle_y + lax.axis_index("dy")
    partial = grid_fields(place[None].astype(jnp.int32), gathered, cycle_x, cycle_y)
    received = lax.all_to_all(partial, ("dx", "dy"), split_axis=0, concat_axis=0, tiled=True)
    short = edge_forces(
        lists, index, feat, pos, mid, up, down, w_self, w_pair, w_radial, w_expand,
        w_contract, w_final,
    )
    field = jnp.sum(received, axis=0)
    total = short + spread[0, :1] * field
    live = lax.broadcasted_iota(jnp.int32, (1, feat.shape[0]), 1) < atom_count[0, 0]
    return jnp.where(live, total, jnp.zeros_like(total)).transpose(1, 0, 2)[None]


def solution(mesh):
    placed = (
        P("dx", "dy", None, None),
        P("dx", "dy", None, None),
        P("dx", "dy"),
        P("dx", "dy", None),
        P("dx", "dy", None, None),
        P("dx", "dy", None),
    ) + (P(),) * 7
    return jax.shard_map(
        shards, mesh=mesh, in_specs=placed, out_specs=P("dx", "dy", None, None), check_vma=False
    )
```

```python
import functools
import math

import jax
import jax.numpy as jnp
import numpy as np
from jax import lax
from jax.experimental import pallas as pl
from jax.experimental.pallas import tpu as pltpu
from jax.sharding import PartitionSpec as P

GRID_X = 8
GRID_Y = 8
GRID_Z = 1024
BOX = 1.0
CUTOFF_SQ = 6.25
SMEARING = 1.0

LANES = 128
EXTRA = 16
ROWS = 32
GROUPS = LANES // ROWS
CHUNK_ATOMS = 64
PIECES = 4
HIGHEST = lax.Precision.HIGHEST
F32 = jnp.float32
BF16 = jnp.bfloat16


def contract_first(a, b, precision=None):
    return lax.dot_general(
        a, b, (((0,), (0,)), ((), ())), precision=precision, preferred_element_type=F32
    )


def contract_last(a, b, precision=None):
    return lax.dot_general(
        a, b, (((1,), (1,)), ((), ())), precision=precision, preferred_element_type=F32
    )


def charge_kernel(count_ref, feat_ref, cell_ref, wq_ref, qc_ref):
    atoms = feat_ref.shape[0]
    weights = jnp.broadcast_to(wq_ref[...].astype(F32), (16, LANES)).astype(BF16)
    charge = contract_last(weights, feat_ref[...])[:1]
    live = lax.broadcasted_iota(jnp.int32, (1, atoms), 1) < count_ref[0, 0]
    both = jnp.concatenate([jnp.where(live, charge, 0.0), cell_ref[...].astype(F32)], axis=0)
    qc_ref[...] = jnp.broadcast_to(both[None], qc_ref.shape)


def export_kernel(feat_ref, pos_ref, export_ref, after_ref, out_ref):
    atoms = feat_ref.shape[0]
    ghosts = export_ref.shape[1]
    pick = lax.broadcasted_iota(jnp.int32, (atoms, ghosts), 0) == export_ref[...]
    pick = jnp.where(pick, 1.0, 0.0).astype(BF16)
    out_ref[pl.ds(0, ghosts), :] = contract_first(pick, feat_ref[...]).astype(BF16)
    pos = jnp.concatenate([pos_ref[...].astype(F32), jnp.zeros((13, atoms), F32)], axis=0)
    coords = jnp.dot(pos.astype(BF16), pick, preferred_element_type=F32)
    tail = [coords[:8, h * LANES : (h + 1) * LANES] for h in range(ghosts // LANES)]
    out_ref[pl.ds(ghosts, EXTRA), :] = jnp.concatenate(tail, axis=0).astype(BF16)


def charges(devices, count, feat, cells, w_charge):
    vmem = pl.BlockSpec(memory_space=pltpu.VMEM)
    return pl.pallas_call(
        charge_kernel,
        in_specs=[pl.BlockSpec(memory_space=pltpu.SMEM)] + [vmem] * 3,
        out_specs=vmem,
        out_shape=jax.ShapeDtypeStruct((devices, 2, feat.shape[0]), F32),
        compiler_params=pltpu.CompilerParams(vmem_limit_bytes=60 << 20),
        name="charges",
    )(count, feat, cells[None], w_charge[None])


def exports_after(after, feat, pos, exports):
    vmem = pl.BlockSpec(memory_space=pltpu.VMEM)
    return pl.pallas_call(
        export_kernel,
        in_specs=[vmem] * 3 + [pl.BlockSpec(memory_space=pl.ANY)],
        out_specs=vmem,
        out_shape=jax.ShapeDtypeStruct((exports.shape[0] + EXTRA, feat.shape[1]), BF16),
        compiler_params=pltpu.CompilerParams(vmem_limit_bytes=16 << 20),
        name="exports",
    )(feat, pos, exports[None], after)


def real_tables(count):
    half = count // 2
    index = np.arange(count)
    freq = np.where(index <= half, index, index - half)
    place = np.arange(count)
    angle = 2.0 * np.pi * (freq[:, None] * place[None, :] % count) / count
    is_cos = (index <= half)[:, None]
    basis = np.where(is_cos, np.cos(angle), np.sin(angle))
    weight = np.where((index == 0) | (index == half), 1.0, 2.0)[:, None] / count
    wave = np.where(index == half, 0.0, 2.0 * np.pi * freq / count)[:, None]
    slope = np.where(is_cos, np.sin(angle), -np.cos(angle)) * wave
    return (basis, (weight * basis).T, (weight * slope).T)


def thirds(table):
    whole = table.astype(np.float32)
    high = whole.astype(BF16).astype(np.float32)
    low = (whole - high).astype(BF16).astype(np.float32)
    return np.concatenate([high, high, low], axis=1)


def sine_half(t):
    x = t * (math.pi / 512.0)
    s = x * x
    p = -2.50521084e-08
    p = p * s + 2.75573192e-06
    p = p * s - 1.98412698e-04
    p = p * s + 8.33333333e-03
    p = p * s - 1.66666667e-01
    return x + x * (s * p)


def grid_kernel(
    cycle_x, cycle_y, place_ref, qc_ref, fy_ref, fx_ref, ix_ref, iy_ref, out_ref,
    buf_a, buf_b, buf_c, buf_d, buf_e, trig_ref,
):
    mesh_x, mesh_y, mesh_z = (GRID_X * cycle_x, GRID_Y * cycle_y, GRID_Z)
    devices = cycle_x * cycle_y
    modes = mesh_z // 2 // devices
    coefs = 2 * modes
    first = place_ref[0] * modes
    columns = GRID_X * GRID_Y
    atoms = qc_ref.shape[2]

    row = lax.broadcasted_iota(jnp.int32, (ROWS, 1), 0) % coefs
    row_mode = first + row % modes
    row_sine = row >= modes
    row_edge = row_sine & (row_mode == 0)
    row_factor = jnp.where(row_edge, mesh_z // 2, row_mode)
    row_shift = jnp.where(row_sine & (row_mode != 0), mesh_z // 4, 0)
    column_iota = lax.broadcasted_iota(jnp.int32, (columns, atoms), 0)

    def columns_of(device):
        cell = qc_ref[device, 1:2, :].astype(jnp.int32)
        return cell, column_iota == lax.shift_right_logical(cell, 10)

    def spread(device, carry):
        cell, match = columns_of(device)
        depth = cell & (mesh_z - 1)
        turn = (row_factor * depth - row_shift) & (mesh_z - 1)
        trig = sine_half((jnp.abs(turn - mesh_z // 2) - mesh_z // 4).astype(F32))
        high = trig.astype(BF16)
        trig_ref[device, pl.ds(0, ROWS), :] = high
        trig_ref[device, pl.ds(ROWS, ROWS), :] = (trig - high.astype(F32)).astype(BF16)
        charged = trig * qc_ref[device, 0:1, :]
        high = charged.astype(BF16)
        low = (charged - high.astype(F32)).astype(BF16)
        pick = jnp.where(match, 1.0, 0.0).astype(BF16)
        total = contract_last(pick, jnp.concatenate([high, low] * (LANES // ROWS // 2), axis=0))
        total = total + pltpu.roll(total, ROWS, 1)
        buf_a[pl.ds(pl.multiple_of(device * columns, 8), columns), :] = total
        return carry

    lax.fori_loop(0, devices, spread, 0, unroll=8)

    lane = lax.broadcasted_iota(jnp.int32, (1, LANES), 1)
    lane_group = lane // ROWS

    def pack(copied):
        wide = copied[0]
        for g in range(1, GROUPS):
            wide = jnp.where(lane_group == g, copied[g], wide)
        return wide

    def unpack(wide):
        turned = [wide] + [pltpu.roll(wide, g * ROWS, 1) for g in range(1, GROUPS)]
        copied = []
        for i in range(GROUPS):
            copied.append(pack([turned[(g - i) % GROUPS] for g in range(GROUPS)]))
        return copied

    def apply(table_ref, wide):
        high = wide.astype(BF16)
        low = (wide - high.astype(F32)).astype(BF16)
        data = jnp.concatenate([high, low, high], axis=0)
        return jnp.dot(table_ref[...].astype(BF16), data, preferred_element_type=F32)

    for first_x in range(0, mesh_x, GROUPS):
        copied = []
        for place in range(first_x, first_x + GROUPS):
            rows = []
            for sy in range(cycle_y):
                start = ((place // GRID_X) * cycle_y + sy) * columns + (place % GRID_X) * GRID_Y
                rows.append(buf_a[pl.ds(start, GRID_Y), :])
            copied.append(jnp.concatenate(rows, axis=0))
        for i, part in enumerate(unpack(apply(fy_ref, pack(copied)))):
            buf_b[pl.ds((first_x + i) * mesh_y, mesh_y), :] = part

    lane_coef = lane % ROWS % coefs
    lane_mode = first + lane_coef % modes
    lane_sine = lane_coef >= modes
    lane_freq = jnp.where(lane_sine & (lane_mode == 0), mesh_z // 2, lane_mode)
    wave_z = lane_freq.astype(F32) * (2.0 * math.pi / mesh_z)
    lane_weight = jnp.where(lane_mode == 0, 1.0, 2.0) / mesh_z
    slope_z = jnp.where(lane_mode == 0, 0.0, wave_z) * jnp.where(lane_sine, 1.0, -1.0)
    freq_x = lax.broadcasted_iota(jnp.int32, (mesh_x, 1), 0)
    freq_x = jnp.where(freq_x <= mesh_x // 2, freq_x, freq_x - mesh_x // 2)
    wave_x = freq_x.astype(F32) * (2.0 * math.pi / mesh_x)
    near = wave_x * wave_x + wave_z * wave_z

    for first_y in range(0, mesh_y, GROUPS):
        copied = [
            buf_b[pl.ds(first_y + i, mesh_x, stride=mesh_y), :] for i in range(GROUPS)
        ]
        spectrum = apply(fx_ref, pack(copied))
        freq_y = first_y + lane_group
        freq_y = jnp.where(freq_y <= mesh_y // 2, freq_y, freq_y - mesh_y // 2)
        wave_y = freq_y.astype(F32) * (2.0 * math.pi / mesh_y)
        wave_sq = near + wave_y * wave_y
        zero = wave_sq == 0.0
        green = jnp.exp(-0.5 * SMEARING * SMEARING * wave_sq) / jnp.where(zero, 1.0, wave_sq)
        green = jnp.where(zero, 0.0, 4.0 * math.pi * green)
        both = apply(ix_ref, spectrum * (green * lane_weight))
        for i, part in enumerate(unpack(both)):
            rows = pl.ds((first_y + i) * mesh_x, mesh_x)
            buf_a[rows, :] = part[:mesh_x]
            buf_c[rows, :] = part[mesh_x:]

    for first_x in range(0, mesh_x, GROUPS):
        plain, sloped = (
            pack([buf[pl.ds(first_x + i, mesh_y, stride=mesh_x), :] for i in range(GROUPS)])
            for buf in (buf_a, buf_c)
        )
        both = apply(iy_ref, plain)
        along_x = apply(iy_ref.at[pl.ds(0, mesh_y), :], sloped)
        potential = both[:mesh_y]
        partner = jnp.where(
            lane % ROWS >= modes,
            pltpu.roll(potential, modes, 1),
            pltpu.roll(potential, LANES - modes, 1),
        )
        fields = (along_x, both[mesh_y:], partner * slope_z)
        for buf, wide in zip((buf_b, buf_d, buf_e), fields):
            for i, part in enumerate(unpack(wide)):
                buf[pl.ds((first_x + i) * mesh_y, mesh_y), :] = part

    use_low = (lane // ROWS) == 1
    use_none = (lane % ROWS) >= coefs

    def sample(device, carry):
        _, match = columns_of(device)
        rows = []
        for buf in (buf_b, buf_d, buf_e):
            for lx in range(GRID_X):
                place = (device // cycle_y) * GRID_X + lx
                start = place * mesh_y + (device % cycle_y) * GRID_Y
                rows.append(buf[pl.ds(pl.multiple_of(start, 8), GRID_Y), :])
        data = jnp.concatenate(rows, axis=0)
        high = data.astype(BF16).astype(F32)
        mixed = jnp.where(use_low, data - high, high)
        mixed = jnp.where(use_none, 0.0, mixed).astype(BF16)
        high = trig_ref[device, pl.ds(0, ROWS), :]
        low = trig_ref[device, pl.ds(ROWS, ROWS), :]
        waves = jnp.concatenate([high, high, low, jnp.zeros_like(low)], axis=0)
        fields = jnp.dot(mixed, waves, preferred_element_type=F32)
        picked = []
        for a in range(3):
            part = jnp.where(match, fields[a * columns : (a + 1) * columns], 0.0)
            picked.append(jnp.sum(part, axis=0, keepdims=True))
        for a in range(3):
            out_ref[device, a] = picked[a]
        return carry

    lax.fori_loop(0, devices, sample, 0, unroll=8)


def grid_fields(place, gathered, cycle_x, cycle_y):
    mesh_x, mesh_y = (GRID_X * cycle_x, GRID_Y * cycle_y)
    devices, _, atoms = gathered.shape
    ax, bx, cx = real_tables(mesh_x)
    ay, by, cy = real_tables(mesh_y)
    tables = [
        thirds(ay),
        thirds(ax),
        np.concatenate([thirds(bx), thirds(cx)], axis=0),
        np.concatenate([thirds(by), thirds(cy)], axis=0),
    ]
    plane = pltpu.VMEM((mesh_x * mesh_y, LANES), F32)
    vmem = pl.BlockSpec(memory_space=pltpu.VMEM)
    return pl.pallas_call(
        functools.partial(grid_kernel, cycle_x, cycle_y),
        in_specs=[pl.BlockSpec(memory_space=pltpu.SMEM)] + [vmem] * 5,
        out_specs=vmem,
        out_shape=jax.ShapeDtypeStruct((devices, 3, 1, atoms), F32),
        scratch_shapes=[plane] * 5
        + [pltpu.VMEM((devices, 2 * ROWS, atoms), BF16)],
        compiler_params=pltpu.CompilerParams(
            vmem_limit_bytes=5 * mesh_x * mesh_y * LANES * 4
            + devices * atoms * (4 * ROWS + 64)
            + (10 << 20)
        ),
        cost_estimate=pl.CostEstimate(
            flops=8_000_000_000, bytes_accessed=4_000_000, transcendentals=100_000
        ),
        name="grid_fields",
    )(place, gathered, *[jnp.asarray(t) for t in tables])


def edge_kernel(
    list_hbm, index_ref, feat_ref, pos_ref, mid_ref, up_ref, down_ref, w_self_ref, w_pair_ref,
    w_radial_ref, w_expand_ref, w_contract_ref, w_final_ref, out_ref,
    table, places, near_a, near_b, near_c, edge_a, edge_b, edge_c,
    total_a, total_b, total_c, marks, own_ref, sums_ref, w_half,
    list_ref, list_sem,
):
    atoms, channels = feat_ref.shape
    ghosts = mid_ref.shape[1] - EXTRA
    slots_all = atoms + 9 * ghosts
    per_atom = index_ref.shape[0]
    chunk = CHUNK_ATOMS * per_atom
    chunks = atoms // CHUNK_ATOMS
    basis_count = w_radial_ref.shape[0]
    spacing = CUTOFF_SQ / (basis_count - 1)
    latent = w_expand_ref.shape[1]
    width = latent // PIECES
    slots = per_atom // PIECES
    w_half[...] = w_expand_ref[...] * 0.5

    fetch = pltpu.make_async_copy(list_hbm, list_ref, list_sem)
    fetch.start()

    def fill(start, rows, coords, shift):
        count = rows.shape[0]
        projected = jnp.dot(rows, w_pair_ref[...], preferred_element_type=F32)
        projected = projected.astype(BF16).astype(F32)
        rows_of = table.reshape(slots_all * 2, LANES)
        rows_of[pl.ds(start * 2, count, stride=2), :] = projected[:, :channels] * 0.5
        rows_of[pl.ds(start * 2 + 1, count, stride=2), :] = projected[:, channels:]
        row = lax.broadcasted_iota(jnp.int32, (8, LANES), 0)
        offset = jnp.where(row == 0, shift[0], jnp.where(row == 1, shift[1], 0.0))
        places[start // LANES] = coords + offset

    pos = jnp.concatenate([pos_ref[...].astype(F32), jnp.zeros((5, atoms), F32)], axis=0)
    for i in range(atoms // LANES):
        rows = feat_ref[pl.ds(i * LANES, LANES), :]
        fill(i * LANES, rows, pos[:, i * LANES : (i + 1) * LANES], (0.0, 0.0))
        own = jnp.dot(rows, w_self_ref[...], preferred_element_type=F32)
        own_ref[pl.ds(i * LANES, LANES), :] = own * 0.5
    for sx in range(3):
        for sy, ref in enumerate((up_ref, mid_ref, down_ref)):
            block = 3 * sx + sy
            if block == 4:
                continue
            tail = ref[sx, pl.ds(ghosts, EXTRA), :].astype(F32)
            for h in range(ghosts // LANES):
                rows = ref[sx, pl.ds(h * LANES, LANES), :]
                start = atoms + block * ghosts + h * LANES
                fill(start, rows, tail[h * 8 : (h + 1) * 8], ((sx - 1) * BOX, (sy - 1) * BOX))

    feature = lax.broadcasted_iota(jnp.int32, (8, LANES), 0)
    skipped = range((atoms + 4 * ghosts) // LANES, (atoms + 5 * ghosts) // LANES)
    for i in range(atoms // LANES):
        columns = slice(i * LANES, (i + 1) * LANES)
        index = index_ref[:, columns]
        inside = index & (LANES - 1)
        outside = lax.shift_right_logical(index, 7)
        found = [jnp.zeros((per_atom, LANES), F32)] * 3
        for c in range(slots_all // LANES):
            if c in skipped:
                continue
            tile = places[c]
            here = outside == c
            for a in range(3):
                source = jnp.broadcast_to(tile[a : a + 1], (per_atom, LANES))
                value = jnp.take_along_axis(source, inside, axis=1)
                found[a] = jnp.where(here, value, found[a])
        disp = [found[a] - pos[a : a + 1, columns] for a in range(3)]
        d2 = disp[0] * disp[0] + disp[1] * disp[1] + disp[2] * disp[2]
        envelope = jnp.maximum(0.0, 1.0 - d2 * (1.0 / CUTOFF_SQ))
        envelope = envelope * envelope
        moments = [envelope] + [envelope * disp[a] for a in range(3)]
        for group in range(per_atom // GROUPS):
            stacked = []
            for k in range(group * GROUPS, (group + 1) * GROUPS):
                def wide(value):
                    return jnp.broadcast_to(value[k : k + 1], (8, LANES))

                t = wide(d2) * (1.0 / spacing) - feature.astype(F32)
                basis = jnp.exp(-(t * t))
                high = basis.astype(BF16).astype(F32)
                tail = jnp.where(feature == 0, wide(moments[0]), 0.0)
                for a in range(3):
                    tail = jnp.where(feature == 1 + a, wide(moments[1 + a]), tail)
                stacked += [high, basis - high, high, tail]
            marks[group, pl.ds(i * LANES, LANES), :] = jnp.concatenate(stacked, axis=0).T

    w_radial = w_radial_ref[...] * 0.5
    high = w_radial.astype(BF16).astype(F32)
    one = jnp.concatenate([high, high, w_radial - high, jnp.zeros((8, channels), F32)], axis=0)
    none = jnp.zeros((ROWS, channels), F32)
    blocks = []
    for g in range(GROUPS):
        column = [one if other == g else none for other in range(GROUPS)]
        blocks.append(jnp.concatenate(column, axis=0))
    w_basis = jnp.concatenate(blocks, axis=1).astype(BF16)

    part_rows = slots * CHUNK_ATOMS
    shape = (slots, CHUNK_ATOMS, LANES)

    def atoms_of(index):
        return pl.ds(pl.multiple_of(index * CHUNK_ATOMS, 16), CHUNK_ATOMS)

    def gather(index, near, part):
        for k in range(part * slots, (part + 1) * slots):
            start = k * atoms + index * CHUNK_ATOMS
            for first in range(0, CHUNK_ATOMS, 16):
                loaded = [table[list_ref[start + first + a]] for a in range(16)]
                for a, tile in enumerate(loaded):
                    near[k * CHUNK_ATOMS + first + a] = tile

    def radials(index):
        basis = marks[:, atoms_of(index), :].reshape(-1, LANES).astype(BF16)
        return jnp.dot(basis, w_basis, preferred_element_type=F32)

    def enter(index, near, edge_in, part, wide):
        rows = pl.ds(part * part_rows, part_rows)
        groups = slots // GROUPS
        pieces = []
        for q in range(part * groups, (part + 1) * groups):
            for g in range(GROUPS):
                rows_q = slice(q * CHUNK_ATOMS, (q + 1) * CHUNK_ATOMS)
                pieces.append(wide[rows_q, g * LANES : (g + 1) * LANES])
        radial = jnp.concatenate(pieces, axis=0).reshape(shape)
        bias = near.reshape(2 * chunk, LANES)[pl.ds(part * part_rows * 2, part_rows, stride=2), :]
        half = radial + own_ref[atoms_of(index), :][None] + bias.reshape(shape)
        turn = jnp.tanh(half.astype(BF16)).astype(F32)
        edge_in[rows, :] = (half + half * turn).astype(BF16).reshape(part_rows, LANES)

    def expand(edge_in, part):
        cols = pl.ds(part * width, width)
        return jnp.dot(edge_in[...], w_half[:, cols], preferred_element_type=F32).astype(BF16)

    def contract(half, part):
        hidden = half + half * jnp.tanh(half)
        cols = pl.ds(part * width, width)
        return jnp.dot(hidden, w_contract_ref[cols, :], preferred_element_type=F32)

    def collect(index, near, total, part, before):
        rows = pl.ds(part * part_rows, part_rows)
        other = pl.ds(part * part_rows * 2 + 1, part_rows, stride=2)
        weight = (total[rows, :] * near.reshape(2 * chunk, LANES)[other, :]).reshape(shape)
        after = []
        for s in range(4):
            summed = 0.0
            for k in range(slots):
                column = k % GROUPS * ROWS + 3 * basis_count + s
                tile = marks[(part * slots + k) // GROUPS, atoms_of(index), :]
                summed = summed + weight[k] * tile[:, column : column + 1]
            after.append(summed if before is None else before[s] + summed)
        return after

    def keep(index, sums):
        for s in range(4):
            sums_ref[s, atoms_of(index), :] = sums[s]

    def stage(index, nears, edges, totals):
        after = jnp.minimum(index + 1, chunks - 1)
        before = jnp.maximum(index - 1, 0)
        mixed, sums = (None, None)
        half = expand(edges[0], 0)
        wide = radials(after)
        for part in range(PIECES):
            gather(after, nears[1], part)
            following = expand(edges[0], part + 1) if part + 1 < PIECES else None
            sums = collect(before, nears[2], totals[2], part, sums)
            term = contract(half, part)
            mixed = term if mixed is None else mixed + term
            enter(after, nears[1], edges[1], part, wide)
            half = following
        totals[0][...] = mixed
        keep(before, sums)

    nears = (near_a, near_b, near_c)
    edges = (edge_a, edge_b, edge_c)
    totals = (total_a, total_b, total_c)
    fetch.wait()
    for part in range(PIECES):
        gather(0, near_a, part)
    wide = radials(0)
    for part in range(PIECES):
        enter(0, near_a, edge_a, part, wide)

    def triple(step, carry):
        for i in range(3):
            order = (i, (i + 1) % 3, (i + 2) % 3)
            pick = lambda refs: [refs[o] for o in order]
            stage(3 * step + i, pick(nears), pick(edges), pick(totals))
        return carry

    lax.fori_loop(0, chunks // 3, triple, 0)
    sums = None
    for part in range(PIECES):
        sums = collect(chunks - 1, near_c, total_c, part, sums)
    keep(chunks - 1, sums)

    scale = 1.0 / math.sqrt(per_atom)
    vector = [sums_ref[1 + a] * scale for a in range(3)]
    square = vector[0] * vector[0] + vector[1] * vector[1] + vector[2] * vector[2]
    invariant = (sums_ref[0] * scale + square * (1.0 / 3.0)).astype(BF16)
    gate = jnp.dot(invariant, w_final_ref[...], preferred_element_type=F32)
    gate = gate * (0.5 + 0.5 * jnp.tanh(0.5 * gate)) * (1.0 / math.sqrt(channels))
    ones = jnp.ones((8, channels), F32)
    for a in range(3):
        out_ref[a] = contract_last(ones, vector[a] * gate, HIGHEST)[:1]


def edge_forces(lists, index, feat, pos, mid, up, down, w_self, w_pair, w_radial, w_expand, w_contract, w_final):
    atoms, channels = feat.shape
    per_atom = index.shape[0]
    ghosts = mid.shape[1] - EXTRA
    slots_all = atoms + 9 * ghosts
    chunk = CHUNK_ATOMS * per_atom
    vmem = pl.BlockSpec(memory_space=pltpu.VMEM)
    edges = atoms * per_atom
    latent = w_expand.shape[1]
    return pl.pallas_call(
        edge_kernel,
        in_specs=[pl.BlockSpec(memory_space=pl.ANY)] + [vmem] * 12,
        out_specs=vmem,
        out_shape=jax.ShapeDtypeStruct((3, 1, atoms), F32),
        scratch_shapes=[
            pltpu.VMEM((slots_all, 2, LANES), F32),
            pltpu.VMEM((slots_all // LANES, 8, LANES), F32),
        ]
        + [pltpu.VMEM((chunk, 2, LANES), F32)] * 3
        + [pltpu.VMEM((chunk, LANES), BF16)] * 3
        + [pltpu.VMEM((chunk, LANES), F32)] * 3
        + [
            pltpu.VMEM((per_atom // GROUPS, atoms, LANES), F32),
            pltpu.VMEM((atoms, LANES), F32),
            pltpu.VMEM((4, atoms, LANES), F32),
            pltpu.VMEM(w_expand.shape, BF16),
            pltpu.SMEM(lists.shape, lists.dtype),
            pltpu.SemaphoreType.DMA(()),
        ],
        compiler_params=pltpu.CompilerParams(vmem_limit_bytes=32 << 20),
        cost_estimate=pl.CostEstimate(
            flops=4 * edges * channels * latent,
            bytes_accessed=4_000_000,
            transcendentals=edges * latent,
        ),
        name="edge_forces",
    )(
        lists, index, feat, pos, mid, up, down, w_self, w_pair, w_radial,
        w_expand, w_contract, w_final,
    )


def ring(array, axis, step):
    size = lax.axis_size(axis)
    return lax.ppermute(array, axis, [(i, (i + step) % size) for i in range(size)])


def shards(
    features, positions, atom_count, ghost_index, neighbour_list, cell_index, w_self, w_pair,
    w_radial, w_expand, w_contract, w_final, w_charge,
):
    feat = features[0, 0]
    pos = positions[0, 0]
    cycle_x, cycle_y = (lax.axis_size("dx"), lax.axis_size("dy"))
    spread = charges(cycle_x * cycle_y, atom_count, feat, cell_index[0, 0], w_charge)
    exported = exports_after(spread, feat, pos, ghost_index[0, 0])
    gathered = lax.all_to_all(spread, ("dx", "dy"), split_axis=0, concat_axis=0, tiled=True)
    mid = jnp.stack([ring(exported, "dx", 1), exported, ring(exported, "dx", -1)])
    index = neighbour_list[0, 0].T
    lists = index.reshape(-1)
    gathered, mid, lists = lax.optimization_barrier((gathered, mid, lists))
    up = ring(mid, "dy", 1)
    down = ring(mid, "dy", -1)
    place = lax.axis_index("dx") * cycle_y + lax.axis_index("dy")
    partial = grid_fields(place[None].astype(jnp.int32), gathered, cycle_x, cycle_y)
    received = lax.all_to_all(partial, ("dx", "dy"), split_axis=0, concat_axis=0, tiled=True)
    short = edge_forces(
        lists, index, feat, pos, mid, up, down, w_self, w_pair, w_radial, w_expand,
        w_contract, w_final,
    )
    field = jnp.sum(received, axis=0)
    total = short + spread[0, :1] * field
    live = lax.broadcasted_iota(jnp.int32, (1, feat.shape[0]), 1) < atom_count[0, 0]
    return jnp.where(live, total, jnp.zeros_like(total)).transpose(1, 0, 2)[None]


def solution(mesh):
    placed = (
        P("dx", "dy", None, None),
        P("dx", "dy", None, None),
        P("dx", "dy"),
        P("dx", "dy", None),
        P("dx", "dy", None, None),
        P("dx", "dy", None),
    ) + (P(),) * 7
    return jax.shard_map(
        shards, mesh=mesh, in_specs=placed, out_specs=P("dx", "dy", None, None), check_vma=False
    )
```
